32 devices in a mesh: groups: 2 (over x), dp: 16 (over z, y, core).
Axes of the slice: x: 2, y: 2, z: 4, core: 2. Of those that a mesh axis runs over, the one named last changes fastest.
Arguments:
- context: bfloat16 [16384, 2048], P(('groups', 'dp')), parts along dimension 0, may hold values from -6 to 6
- residual: bfloat16 [16384, 4096], P(('groups', 'dp')), parts along dimension 0
- out_proj: bfloat16 [2048, 4096], P(None, 'dp'), may hold values from -0.125 to 0.125
- norm_gain: float32 [4096], replicated, may hold values from 0.5 to 1.5
- lengths: int32 [32], P(('groups', 'dp')), parts along dimension 0, may hold values from 64 to 512, as said below
- queries: bfloat16 [3584, 4096], P(('groups', 'dp')), parts along dimension 0
- pattern: int32 [32, 7], P(('groups', 'dp')), parts along dimension 0, may hold values from 0 to 1, as said below
Outputs:
- embedded: float32 [32, 4096], P(('groups', 'dp')), parts along dimension 0
- recalled: float32 [32, 4096], P(('groups', 'dp')), parts along dimension 0
- log_total: float32 [32], P(('groups', 'dp')), parts along dimension 0
The draws below stay inside these ranges and needn't reach their ends.
There are 2 independent parts, one for each index of `groups`. The reference program is written for one: setup_inputs(seed, part) draws one part's arguments, and reference() takes and returns one part's arrays. A program takes and returns all parts, laid end to end along the dimension named above; an argument that names none is the same for every part. Nothing has to cross between parts.
Inputs may be any that keep to these rules, and one draw needn't show every extreme that they name: `lengths`: token slots of a passage from its length on are padding; some passage of every draw is full. `pattern`: entry 1 marks a query block as candidates of all passages of a passage block; every row holds one or two ones, and some row two.
All inputs are finite; a program needn't handle non-finite values.
Results may differ from the reference program's by a relative error of at most 0.007.
Values may be sent and summed in bfloat16 or wider, within the bound.
No kernel may reach another device: no remote copies, remote signals or barrier semaphores. Data moves between devices by JAX's collectives and lax.ppermute only.
A program may use at most 128 MiB of HBM per device.

```python
import math
import jax
import jax.numpy as jnp
from jax import lax

D = 4096
HC = 2048
SEQ = 512
PASS_DEV = 1
PASSAGES = 16
TOKENS = 8192
QB = 256
QBLOCKS = 7
QUERIES = 1792
PBLOCKS = 16


def draw_residual(key, part):
    key = jax.random.fold_in(key, 11)
    key_rough, key_rows, key_cols = jax.random.split(key, 3)
    row_scale = jnp.exp(jax.random.uniform(key_rows, (TOKENS, 1), jnp.float32, math.log(0.3), math.log(3.0)))
    col_scale = jnp.exp(jax.random.uniform(key_cols, (1, D), jnp.float32, math.log(0.3), math.log(3.0)))
    rough_part = jax.random.normal(key_rough, (TOKENS, D), jnp.float32)
    values = rough_part * row_scale * col_scale
    return values.astype(jnp.bfloat16)


def draw_queries(key, part):
    key = jax.random.fold_in(key, 23)
    key_rough, key_rows = jax.random.split(key, 2)
    row_scale = jnp.exp(jax.random.uniform(key_rows, (QUERIES, 1), jnp.float32, math.log(0.5), math.log(2.0)))
    values = jax.random.normal(key_rough, (QUERIES, D), jnp.float32) * 0.1 * row_scale
    return values.astype(jnp.bfloat16)


def draw_lengths(key, part):
    key = jax.random.fold_in(key, 37)
    key_vals, key_full, key_short = jax.random.split(key, 3)
    shortest = max(SEQ // 8, 1)
    values = jax.random.randint(key_vals, (PASSAGES,), shortest, SEQ + 1, jnp.int32)
    full_at = jax.random.randint(key_full, (), 0, PASSAGES, jnp.int32)
    short_at = (full_at + 1 + jax.random.randint(key_short, (), 0, PASSAGES - 1, jnp.int32)) % PASSAGES
    values = values.at[full_at].set(SEQ)
    values = values.at[short_at].set(shortest)
    return values


def draw_pattern(key, part):
    key = jax.random.fold_in(key, 53)
    key_counts, key_order, key_pick = jax.random.split(key, 3)
    counts = jax.random.randint(key_counts, (PBLOCKS,), 1, 3, jnp.int32)
    counts = counts.at[jax.random.randint(key_pick, (), 0, PBLOCKS, jnp.int32)].set(2)
    scores = jax.random.randint(key_order, (PBLOCKS, QBLOCKS), 0, 1 << 20, jnp.int32) * QBLOCKS + jnp.arange(QBLOCKS, dtype=jnp.int32)[None, :]
    order_rank = jnp.argsort(jnp.argsort(scores, axis=1), axis=1)
    return (order_rank < counts[:, None]).astype(jnp.int32)


def block_scale(rng, extent, cuts, smallest, high):
    gain, own = 1.0, jax.random.fold_in(rng, 6)
    for axis_at, blocks in cuts:
        steps = jnp.exp(jax.random.uniform(jax.random.fold_in(own, axis_at), (blocks,), jnp.float32, smallest / len(cuts), high / len(cuts)))
        gain = gain * jnp.repeat(steps, extent[axis_at] // blocks).reshape([-1 if axis == axis_at else 1 for axis in range(len(extent))])
    return gain


def centred(key, extent, spread, bound, shards=(), kind=jnp.bfloat16):
    entries = spread * jax.random.normal(key, extent, jnp.float32)
    if shards:
        entries = entries * block_scale(key, extent, shards, -0.22, 0.18)
    return jnp.clip(entries, -bound, bound).astype(kind)


def setup_inputs(seed: int = 0, part: int = 0) -> dict:
    seeds = jax.random.split(jax.random.key(seed), 8)
    part_splits = jax.random.split(jax.random.fold_in(seeds[7], part), 8)
    return {
        "context": centred(part_splits[0], (TOKENS, HC), 1.0, 6.0, ((0, 16),)),
        "residual": draw_residual(jax.random.fold_in(jax.random.fold_in(seeds[7], part), 71), part),
        "out_proj": centred(seeds[2], (HC, D), HC ** -0.5, 0.125, ((1, 16),)),
        "norm_gain": jnp.clip(1.0 + 0.1 * jax.random.normal(seeds[3], (D,), jnp.float32), 0.5, 1.5),
        "lengths": draw_lengths(jax.random.fold_in(jax.random.fold_in(seeds[7], part), 71), part),
        "queries": draw_queries(jax.random.fold_in(jax.random.fold_in(seeds[7], part), 71), part),
        "pattern": draw_pattern(jax.random.fold_in(jax.random.fold_in(seeds[7], part), 71), part),
    }


def reference(context, residual, out_proj, norm_gain, lengths, queries, pattern):
    ctx_blocks = context.reshape(PASSAGES, SEQ, HC)
    res_blocks = residual.reshape(PASSAGES, SEQ, D)

    def passage_vector(items):
        ctx_block, res_block, length = items
        hidden_sum = res_block.astype(jnp.float32) + jnp.dot(ctx_block, out_proj, preferred_element_type=jnp.float32)
        normed = hidden_sum * lax.rsqrt(lax.optimization_barrier(jnp.mean(hidden_sum * hidden_sum, axis=-1, keepdims=True)) + 1e-05) * norm_gain
        valid_mask = (jnp.arange(SEQ) < length).astype(jnp.float32)
        pooled = lax.optimization_barrier(jnp.sum(normed * valid_mask[:, None], axis=0)) / length.astype(jnp.float32)
        return pooled * lax.rsqrt(jnp.mean(pooled * pooled) + 1e-06)
    embedded = lax.map(passage_vector, (ctx_blocks, res_blocks, lengths))
    emb_half = embedded.astype(jnp.bfloat16)
    temper = 1.0 / (0.02 * math.sqrt(D))
    scores = jnp.dot(emb_half, queries.T, preferred_element_type=jnp.float32) * temper
    cand_mask = jnp.repeat(jnp.repeat(pattern, PASS_DEV, axis=0), QB, axis=1) > 0
    peak_score = lax.optimization_barrier(jnp.max(jnp.where(cand_mask, scores, -jnp.inf), axis=1))
    weights = jnp.where(cand_mask, jnp.exp(scores - peak_score[:, None]), 0.0)
    totals = lax.optimization_barrier(jnp.sum(weights, axis=1))
    recalled = jnp.dot(weights.astype(jnp.bfloat16), queries, preferred_element_type=jnp.float32) / totals[:, None]
    log_total = peak_score + jnp.log(totals)
    return (embedded, recalled, log_total)
```

```python
import math

import jax
import jax.numpy as jnp
from jax import lax
from jax.sharding import PartitionSpec as P

QB = 256
LANES = 128


def per_device(context, residual, out_proj, norm_gain, lengths, queries, pattern):
    tok_rows = context.shape[0]
    features = residual.shape[1]
    passages_here = lengths.shape[0]
    seq_len = tok_rows // passages_here
    query_rows = queries.shape[0]
    blocks = pattern.shape[1]
    ranks = lax.axis_size("dp")
    me = lax.axis_index("dp")
    branch = jnp.dot(
        context,
        lax.all_gather(out_proj, "dp", axis=1, tiled=True),
        preferred_element_type=jnp.float32,
    )
    hidden_sum = residual.astype(jnp.float32) + branch
    normed = (
        hidden_sum
        * lax.rsqrt(jnp.mean(hidden_sum * hidden_sum, axis=-1, keepdims=True) + 1e-05)
        * norm_gain
    )
    shaped = normed.reshape(passages_here, seq_len, features)
    valid_mask = (jnp.arange(seq_len)[None, :] < lengths[:, None]).astype(jnp.float32)
    pooled = jnp.sum(shaped * valid_mask[:, :, None], axis=1) / lengths.astype(jnp.float32)[:, None]
    embedded = pooled * lax.rsqrt(jnp.mean(pooled * pooled, axis=-1, keepdims=True) + 1e-06)
    emb_half = embedded.astype(jnp.bfloat16)
    temper = 1.0 / (0.02 * math.sqrt(features))
    contract = (((1,), (1,)), ((), ()))

    flags = jnp.pad(pattern.astype(jnp.bfloat16), ((0, 0), (0, LANES - blocks)))
    everyone = lax.all_gather(jnp.concatenate([emb_half, flags], axis=1), "dp", axis=0, tiled=True)
    emb_all = everyone[:, :features]
    flags_all = everyone[:, features : features + blocks].astype(jnp.float32)
    scores = lax.dot_general(emb_all, queries, contract, preferred_element_type=jnp.float32) * temper
    row_block = (me * query_rows + jnp.arange(query_rows)) // QB
    picks = (row_block[None, :] == jnp.arange(blocks)[:, None]).astype(jnp.float32)
    cand_mask = jnp.dot(flags_all, picks) > 0
    low = jnp.float32(-1e30)
    peak_part = jnp.max(jnp.where(cand_mask, scores, low), axis=1, keepdims=True)
    weights = jnp.where(cand_mask, jnp.exp(scores - peak_part), 0.0)
    total_part = jnp.sum(weights, axis=1, keepdims=True)
    mix_part = jnp.dot(weights.astype(jnp.bfloat16), queries, preferred_element_type=jnp.float32)

    passages = emb_all.shape[0]
    lane = jnp.arange(LANES)[None, :]
    tail = jnp.where(lane == 0, peak_part, jnp.where(lane == 1, total_part, 0.0))
    parts = jnp.concatenate([mix_part, tail], axis=1).reshape(ranks, passages // ranks, -1)
    parts = lax.all_to_all(parts, "dp", split_axis=0, concat_axis=0, tiled=True)
    mixes, peaks, sums = parts[:, :, :features], parts[:, :, features], parts[:, :, features + 1]
    peak_score = jnp.max(peaks, axis=0)
    factor = jnp.exp(peaks - peak_score[None, :])
    totals = jnp.sum(sums * factor, axis=0)
    recalled = jnp.sum(mixes * factor[:, :, None], axis=0) / totals[:, None]
    log_total = peak_score + jnp.log(totals)
    return (embedded, recalled, log_total)


def solution(mesh):
    in_specs = (
        P(("groups", "dp"), None),
        P(("groups", "dp"), None),
        P(None, "dp"),
        P(),
        P(("groups", "dp")),
        P(("groups", "dp"), None),
        P(("groups", "dp"), None),
    )
    out_specs = (P(("groups", "dp"), None), P(("groups", "dp"), None), P(("groups", "dp")))
    return jax.shard_map(
        per_device, mesh=mesh, in_specs=in_specs, out_specs=out_specs, check_vma=False
    )
```

```python
import math

import jax
import jax.numpy as jnp
from jax import lax
from jax.sharding import PartitionSpec as P

QB = 256
LANES = 128


def per_device(context, residual, out_proj, norm_gain, lengths, queries, pattern):
    tok_rows = context.shape[0]
    features = residual.shape[1]
    passages_here = lengths.shape[0]
    seq_len = tok_rows // passages_here
    query_rows = queries.shape[0]
    blocks = pattern.shape[1]
    ranks = lax.axis_size("dp")
    me = lax.axis_index("dp")
    groups = lax.axis_size("groups")
    depth = out_proj.shape[0]
    share = depth // groups
    piece = lax.dynamic_slice_in_dim(out_proj, lax.axis_index("groups") * share, share, 0)
    pieces = lax.all_gather(piece, ("groups", "dp"), axis=0)
    pieces = pieces.reshape(groups, ranks, share, out_proj.shape[1])
    branch = jnp.einsum(
        "tgk,grkc->trc",
        context.reshape(tok_rows, groups, share),
        pieces,
        preferred_element_type=jnp.float32,
    ).reshape(tok_rows, features)
    hidden_sum = residual.astype(jnp.float32) + branch
    normed = (
        hidden_sum
        * lax.rsqrt(jnp.mean(hidden_sum * hidden_sum, axis=-1, keepdims=True) + 1e-05)
        * norm_gain
    )
    shaped = normed.reshape(passages_here, seq_len, features)
    valid_mask = (jnp.arange(seq_len)[None, :] < lengths[:, None]).astype(jnp.float32)
    pooled = jnp.sum(shaped * valid_mask[:, :, None], axis=1) / lengths.astype(jnp.float32)[:, None]
    embedded = pooled * lax.rsqrt(jnp.mean(pooled * pooled, axis=-1, keepdims=True) + 1e-06)
    emb_half = embedded.astype(jnp.bfloat16)
    temper = 1.0 / (0.02 * math.sqrt(features))
    contract = (((1,), (1,)), ((), ()))

    flags = jnp.pad(pattern.astype(jnp.bfloat16), ((0, 0), (0, LANES - blocks)))
    everyone = lax.all_gather(jnp.concatenate([emb_half, flags], axis=1), "dp", axis=0, tiled=True)
    emb_all = everyone[:, :features]
    flags_all = everyone[:, features : features + blocks].astype(jnp.float32)
    scores = lax.dot_general(emb_all, queries, contract, preferred_element_type=jnp.float32) * temper
    row_block = (me * query_rows + jnp.arange(query_rows)) // QB
    picks = (row_block[None, :] == jnp.arange(blocks)[:, None]).astype(jnp.float32)
    cand_mask = jnp.dot(flags_all, picks) > 0
    low = jnp.float32(-1e30)
    peak_part = jnp.max(jnp.where(cand_mask, scores, low), axis=1, keepdims=True)
    weights = jnp.where(cand_mask, jnp.exp(scores - peak_part), 0.0)
    total_part = jnp.sum(weights, axis=1, keepdims=True)
    mix_part = jnp.dot(weights.astype(jnp.bfloat16), queries, preferred_element_type=jnp.float32)

    passages = emb_all.shape[0]
    lane = jnp.arange(LANES)[None, :]
    tail = jnp.where(lane == 0, peak_part, jnp.where(lane == 1, total_part, 0.0))
    parts = jnp.concatenate([mix_part, tail], axis=1).reshape(ranks, passages // ranks, -1)
    parts = lax.all_to_all(parts, "dp", split_axis=0, concat_axis=0, tiled=True)
    mixes, peaks, sums = parts[:, :, :features], parts[:, :, features], parts[:, :, features + 1]
    peak_score = jnp.max(peaks, axis=0)
    factor = jnp.exp(peaks - peak_score[None, :])
    totals = jnp.sum(sums * factor, axis=0)
    recalled = jnp.sum(mixes * factor[:, :, None], axis=0) / totals[:, None]
    log_total = peak_score + jnp.log(totals)
    return (embedded, recalled, log_total)


def solution(mesh):
    in_specs = (
        P(("groups", "dp"), None),
        P(("groups", "dp"), None),
        P(None, "dp"),
        P(),
        P(("groups", "dp")),
        P(("groups", "dp"), None),
        P(("groups", "dp"), None),
    )
    out_specs = (P(("groups", "dp"), None), P(("groups", "dp"), None), P(("groups", "dp")))
    return jax.shard_map(
        per_device, mesh=mesh, in_specs=in_specs, out_specs=out_specs, check_vma=False
    )
```

```python
import functools
import math

import jax
import jax.numpy as jnp
from jax import lax
from jax.experimental import pallas as pl
from jax.experimental.pallas import tpu as pltpu
from jax.sharding import PartitionSpec as P

QB = 256
LANES = 128
CORES = 2
CYCLE = (0, 2, 4, 6, 7, 5, 3, 1)


def project_kernel(count, place, ctx, residual, *refs):
    pieces = refs[: 2 * count]
    hidden, squares, weights, extra, weight_sems, extra_sems = refs[2 * count :]
    half = weights.shape[1]
    width = weights.shape[2]
    rows = ctx.shape[0]

    def weight_copy(i):
        return pltpu.make_async_copy(pieces[i], weights.at[i], weight_sems.at[i])

    def extra_copy(j):
        start = pl.multiple_of(place[j] * width, width)
        return pltpu.make_async_copy(residual.at[:, pl.ds(start, width)], extra.at[j], extra_sems.at[j])

    for j in range(count):
        extra_copy(j).start()
        weight_copy(2 * j).start()
        weight_copy(2 * j + 1).start()
    squares[...] = jnp.zeros_like(squares)
    first = pl.multiple_of(place[count] * half, half)
    second = pl.multiple_of((1 - place[count]) * half, half)
    step = 256
    for j in range(count):
        extra_copy(j).wait()
        weight_copy(2 * j).wait()
        weight_copy(2 * j + 1).wait()

        @pl.loop(0, rows // step)
        def _(k):
            at = pl.ds(pl.multiple_of(k * step, step), step)
            total = jnp.dot(
                ctx[at, pl.ds(first, half)], weights[2 * j], preferred_element_type=jnp.float32
            )
            total += jnp.dot(
                ctx[at, pl.ds(second, half)], weights[2 * j + 1], preferred_element_type=jnp.float32
            )
            total += extra[j, at, :].astype(jnp.float32)
            hidden[j, at, :] = total
            square = total * total
            for lane in range(0, width, LANES):
                squares[at, :] += square[:, lane : lane + LANES]


def project(place, ctx, residual, pieces):
    count = len(pieces) // 2
    rows = ctx.shape[0]
    half, width = pieces[0].shape
    return pl.pallas_call(
        functools.partial(project_kernel, count),
        out_shape=(
            jax.ShapeDtypeStruct((count, rows, width), jnp.float32),
            jax.ShapeDtypeStruct((rows, LANES), jnp.float32),
        ),
        in_specs=[pl.BlockSpec(memory_space=pltpu.SMEM), pl.BlockSpec(memory_space=pltpu.VMEM)]
        + [pl.BlockSpec(memory_space=pl.ANY)] * (1 + 2 * count),
        out_specs=(pl.BlockSpec(memory_space=pltpu.VMEM), pl.BlockSpec(memory_space=pltpu.VMEM)),
        scratch_shapes=[
            pltpu.VMEM((2 * count, half, width), jnp.bfloat16),
            pltpu.VMEM((count, rows, width), jnp.bfloat16),
            pltpu.SemaphoreType.DMA((2 * count,)),
            pltpu.SemaphoreType.DMA((count,)),
        ],
        compiler_params=pltpu.CompilerParams(vmem_limit_bytes=24 << 20),
        cost_estimate=pl.CostEstimate(
            flops=2 * rows * 2 * half * width * count,
            bytes_accessed=count * width * (2 * half * 2 + rows * 6),
            transcendentals=0,
        ),
    )(place, ctx, residual, *pieces)


def pool_kernel(parts, counts, place, length, gain, *refs):
    hidden = refs[:parts]
    squares = refs[parts : 2 * parts]
    embedded = refs[2 * parts]
    blocks, rows, sems = refs[2 * parts + 1 :]
    total = sum(counts)
    width = blocks.shape[2]
    features = total * width
    at = 0
    copies = []
    for i, n in enumerate(counts):
        copies.append(pltpu.make_async_copy(hidden[i], blocks.at[pl.ds(at, n)], sems.at[i]))
        copies[-1].start()
        at += n
    square = squares[0][...]
    for i in range(1, parts):
        square += squares[i][...]
    mean = jnp.sum(square, axis=1, keepdims=True) * (1.0 / features)
    row = lax.broadcasted_iota(jnp.int32, mean.shape, 0)
    scale = jnp.where(row < length[0], lax.rsqrt(mean + 1e-05), 0.0)
    rows[...] = jnp.broadcast_to(scale, rows.shape)
    inverse = 1.0 / jnp.full((1, width), length[0], jnp.int32).astype(jnp.float32)
    at = 0
    for i, n in enumerate(counts):
        copies[i].wait()
        for j in range(at, at + n):
            halves = [
                jnp.sum(blocks[j, :, lane : lane + LANES] * rows[...], axis=0, keepdims=True)
                for lane in range(0, width, LANES)
            ]
            summed = jnp.concatenate(halves, axis=1)
            embedded[pl.ds(place[j], 1), :] = summed * gain[pl.ds(place[j], 1), :] * inverse
        at += n
    pooled = embedded[...]
    mean = jnp.sum(jnp.sum(pooled * pooled, axis=1, keepdims=True), axis=0, keepdims=True)
    embedded[...] = pooled * lax.rsqrt(mean * (1.0 / features) + 1e-06)


def pool(place, lengths, gain, hidden, squares):
    counts = tuple(part.shape[0] for part in hidden)
    total = sum(counts)
    rows, width = hidden[0].shape[1:]
    parts = len(hidden)
    return pl.pallas_call(
        functools.partial(pool_kernel, parts, counts),
        out_shape=jax.ShapeDtypeStruct((total, width), jnp.float32),
        in_specs=[pl.BlockSpec(memory_space=pltpu.SMEM)] * 2
        + [pl.BlockSpec(memory_space=pltpu.VMEM)]
        + [pl.BlockSpec(memory_space=pl.ANY)] * parts
        + [pl.BlockSpec(memory_space=pltpu.VMEM)] * parts,
        out_specs=pl.BlockSpec(memory_space=pltpu.VMEM),
        scratch_shapes=[
            pltpu.VMEM((total, rows, width), jnp.float32),
            pltpu.VMEM((rows, LANES), jnp.float32),
            pltpu.SemaphoreType.DMA((parts,)),
        ],
        compiler_params=pltpu.CompilerParams(vmem_limit_bytes=24 << 20),
    )(place, lengths, gain.reshape(total, width), *hidden, *squares)


def embed_ring(context, residual, out_proj, norm_gain, lengths):
    ranks = lax.axis_size("dp")
    me = lax.axis_index("dp")
    side = lax.axis_index("groups")
    core = me % CORES
    size = ranks // CORES
    where = [CYCLE.index(chip) for chip in range(size)]

    def ring(step):
        return [
            (CYCLE[r] * CORES + c, CYCLE[(r + step) % size] * CORES + c)
            for r in range(size)
            for c in range(CORES)
        ]

    def from_next(piece):
        return lax.ppermute(piece, "dp", ring(-1))

    def from_last(piece):
        return lax.ppermute(piece, "dp", ring(1))

    def over_x(piece):
        return lax.ppermute(piece, "groups", [(0, 1), (1, 0)])

    def other_core(piece):
        return lax.ppermute(piece, "dp", [(i, i ^ 1) for i in range(ranks)])

    half = out_proj.shape[0] // 2
    own = lax.dynamic_slice_in_dim(out_proj, side * half, half, 0)
    rest = lax.dynamic_slice_in_dim(out_proj, (1 - side) * half, half, 0)
    n1, l1 = from_next(own), from_last(own)
    own_pair = (own, rest, other_core(own), other_core(rest))
    n2, l2 = from_next(n1), from_last(l1)
    xn1 = over_x(n1)
    n3, l3 = from_next(n2), from_last(l2)
    xn2 = over_x(n2)
    n3x, l4 = from_next(xn2), from_last(l3)
    xl2 = over_x(l2)
    n4x, l3x = from_next(n3x), from_last(xl2)
    xl1 = over_x(l1)

    def both(a, b):
        return (a, b, other_core(a), other_core(b))

    batches = (
        (0, own_pair),
        (1, both(n1, xn1)),
        (2, both(n2, xn2)),
        (-2, both(l2, xl2)),
        (3, both(n3, n3x)),
        (-1, both(l1, xl1)),
        (-3, both(l3, l3x)),
        (4, both(l4, n4x)),
    )
    cycle = jnp.array(CYCLE, jnp.int32)
    at = jnp.array(where, jnp.int32)[me // CORES]

    def place_of(group):
        chips = cycle[(at + jnp.array([k for k, _ in group], jnp.int32)) % size]
        return jnp.stack([chips * CORES + core, chips * CORES + 1 - core], axis=1).reshape(-1)

    hidden, squares, places = [], [], []
    for group in (batches[:1], batches[1:3], batches[3:5], batches[5:]):
        place = place_of(group)
        pieces = [piece for _, four in group for piece in four]
        h, s = project(jnp.append(place, side), context, residual, pieces)
        hidden.append(h)
        squares.append(s)
        places.append(place)
    embedded = pool(jnp.concatenate(places), lengths, norm_gain, hidden, squares)
    return embedded.reshape(1, -1)


def embed_gather(context, residual, out_proj, norm_gain, lengths):
    tok_rows = context.shape[0]
    features = residual.shape[1]
    passages_here = lengths.shape[0]
    seq_len = tok_rows // passages_here
    branch = jnp.dot(
        context,
        lax.all_gather(out_proj, "dp", axis=1, tiled=True),
        preferred_element_type=jnp.float32,
    )
    hidden_sum = residual.astype(jnp.float32) + branch
    normed = (
        hidden_sum
        * lax.rsqrt(jnp.mean(hidden_sum * hidden_sum, axis=-1, keepdims=True) + 1e-05)
        * norm_gain
    )
    shaped = normed.reshape(passages_here, seq_len, features)
    valid_mask = (jnp.arange(seq_len)[None, :] < lengths[:, None]).astype(jnp.float32)
    pooled = jnp.sum(shaped * valid_mask[:, :, None], axis=1) / lengths.astype(jnp.float32)[:, None]
    return pooled * lax.rsqrt(jnp.mean(pooled * pooled, axis=-1, keepdims=True) + 1e-06)


def per_device(context, residual, out_proj, norm_gain, lengths, queries, pattern):
    features = residual.shape[1]
    query_rows = queries.shape[0]
    blocks = pattern.shape[1]
    ranks = lax.axis_size("dp")
    me = lax.axis_index("dp")
    if (
        ranks == CORES * len(CYCLE)
        and lax.axis_size("groups") == 2
        and lengths.shape[0] == 1
        and out_proj.shape[1] % LANES == 0
    ):
        embedded = embed_ring(context, residual, out_proj, norm_gain, lengths)
    else:
        embedded = embed_gather(context, residual, out_proj, norm_gain, lengths)
    emb_half = embedded.astype(jnp.bfloat16)
    temper = 1.0 / (0.02 * math.sqrt(features))
    contract = (((1,), (1,)), ((), ()))

    flags = jnp.pad(pattern.astype(jnp.bfloat16), ((0, 0), (0, LANES - blocks)))
    everyone = lax.all_gather(jnp.concatenate([emb_half, flags], axis=1), "dp", axis=0, tiled=True)
    emb_all = everyone[:, :features]
    flags_all = everyone[:, features : features + blocks].astype(jnp.float32)
    scores = lax.dot_general(emb_all, queries, contract, preferred_element_type=jnp.float32) * temper
    row_block = (me * query_rows + jnp.arange(query_rows)) // QB
    picks = (row_block[None, :] == jnp.arange(blocks)[:, None]).astype(jnp.float32)
    cand_mask = jnp.dot(flags_all, picks) > 0
    low = jnp.float32(-1e30)
    peak_part = jnp.max(jnp.where(cand_mask, scores, low), axis=1, keepdims=True)
    weights = jnp.where(cand_mask, jnp.exp(scores - peak_part), 0.0)
    total_part = jnp.sum(weights, axis=1, keepdims=True)
    mix_part = jnp.dot(weights.astype(jnp.bfloat16), queries, preferred_element_type=jnp.float32)

    passages = emb_all.shape[0]
    lane = jnp.arange(LANES)[None, :]
    tail = jnp.where(lane == 0, peak_part, jnp.where(lane == 1, total_part, 0.0))
    parts = jnp.concatenate([mix_part, tail], axis=1).reshape(ranks, passages // ranks, -1)
    parts = lax.all_to_all(parts, "dp", split_axis=0, concat_axis=0, tiled=True)
    mixes, peaks, sums = parts[:, :, :features], parts[:, :, features], parts[:, :, features + 1]
    peak_score = jnp.max(peaks, axis=0)
    factor = jnp.exp(peaks - peak_score[None, :])
    totals = jnp.sum(sums * factor, axis=0)
    recalled = jnp.sum(mixes * factor[:, :, None], axis=0) / totals[:, None]
    log_total = peak_score + jnp.log(totals)
    return (embedded, recalled, log_total)


def solution(mesh):
    in_specs = (
        P(("groups", "dp"), None),
        P(("groups", "dp"), None),
        P(None, "dp"),
        P(),
        P(("groups", "dp")),
        P(("groups", "dp"), None),
        P(("groups", "dp"), None),
    )
    out_specs = (P(("groups", "dp"), None), P(("groups", "dp"), None), P(("groups", "dp")))
    return jax.shard_map(
        per_device, mesh=mesh, in_specs=in_specs, out_specs=out_specs, check_vma=False
    )
```

```python
import functools
import math

import jax
import jax.numpy as jnp
from jax import lax
from jax.experimental import pallas as pl
from jax.experimental.pallas import tpu as pltpu
from jax.sharding import PartitionSpec as P

QB = 256
LANES = 128
CORES = 2
CYCLE = (0, 2, 4, 6, 7, 5, 3, 1)


def project_kernel(count, place, ctx, residual, *refs):
    pieces = refs[: 2 * count]
    hidden, squares, weights, extra, weight_sems, extra_sems = refs[2 * count :]
    half = weights.shape[1]
    width = weights.shape[2]
    rows = ctx.shape[0]

    def weight_copy(i):
        return pltpu.make_async_copy(pieces[i], weights.at[i], weight_sems.at[i])

    def extra_copy(j):
        start = pl.multiple_of(place[j] * width, width)
        return pltpu.make_async_copy(residual.at[:, pl.ds(start, width)], extra.at[j], extra_sems.at[j])

    for j in range(count):
        extra_copy(j).start()
        weight_copy(2 * j).start()
        weight_copy(2 * j + 1).start()
    squares[...] = jnp.zeros_like(squares)
    first = pl.multiple_of(place[count] * half, half)
    second = pl.multiple_of((1 - place[count]) * half, half)
    step = 256
    for j in range(count):
        extra_copy(j).wait()
        weight_copy(2 * j).wait()
        weight_copy(2 * j + 1).wait()

        @pl.loop(0, rows // step)
        def _(k):
            at = pl.ds(pl.multiple_of(k * step, step), step)
            total = jnp.dot(
                ctx[at, pl.ds(first, half)], weights[2 * j], preferred_element_type=jnp.float32
            )
            total += jnp.dot(
                ctx[at, pl.ds(second, half)], weights[2 * j + 1], preferred_element_type=jnp.float32
            )
            total += extra[j, at, :].astype(jnp.float32)
            hidden[j, at, :] = total
            square = total * total
            for lane in range(0, width, LANES):
                squares[at, :] += square[:, lane : lane + LANES]


def project(place, ctx, residual, pieces):
    count = len(pieces) // 2
    rows = ctx.shape[0]
    half, width = pieces[0].shape
    return pl.pallas_call(
        functools.partial(project_kernel, count),
        out_shape=(
            jax.ShapeDtypeStruct((count, rows, width), jnp.float32),
            jax.ShapeDtypeStruct((rows, LANES), jnp.float32),
        ),
        in_specs=[pl.BlockSpec(memory_space=pltpu.SMEM), pl.BlockSpec(memory_space=pltpu.VMEM)]
        + [pl.BlockSpec(memory_space=pl.ANY)] * (1 + 2 * count),
        out_specs=(pl.BlockSpec(memory_space=pltpu.VMEM), pl.BlockSpec(memory_space=pltpu.VMEM)),
        scratch_shapes=[
            pltpu.VMEM((2 * count, half, width), jnp.bfloat16),
            pltpu.VMEM((count, rows, width), jnp.bfloat16),
            pltpu.SemaphoreType.DMA((2 * count,)),
            pltpu.SemaphoreType.DMA((count,)),
        ],
        compiler_params=pltpu.CompilerParams(vmem_limit_bytes=24 << 20),
        cost_estimate=pl.CostEstimate(
            flops=2 * rows * 2 * half * width * count,
            bytes_accessed=count * width * (2 * half * 2 + rows * 6),
            transcendentals=0,
        ),
    )(place, ctx, residual, *pieces)


def pool_kernel(parts, counts, place, length, gain, *refs):
    hidden = refs[:parts]
    squares = refs[parts : 2 * parts]
    embedded = refs[2 * parts]
    blocks, rows, sems = refs[2 * parts + 1 :]
    total = sum(counts)
    width = blocks.shape[2]
    features = total * width
    at = 0
    copies = []
    for i, n in enumerate(counts):
        copies.append(pltpu.make_async_copy(hidden[i], blocks.at[pl.ds(at, n)], sems.at[i]))
        copies[-1].start()
        at += n
    square = squares[0][...]
    for i in range(1, parts):
        square += squares[i][...]
    mean = jnp.sum(square, axis=1, keepdims=True) * (1.0 / features)
    row = lax.broadcasted_iota(jnp.int32, mean.shape, 0)
    scale = jnp.where(row < length[0], lax.rsqrt(mean + 1e-05), 0.0)
    rows[...] = jnp.broadcast_to(scale, rows.shape)
    inverse = 1.0 / jnp.full((1, width), length[0], jnp.int32).astype(jnp.float32)
    at = 0
    for i, n in enumerate(counts):
        copies[i].wait()
        for j in range(at, at + n):
            halves = [
                jnp.sum(blocks[j, :, lane : lane + LANES] * rows[...], axis=0, keepdims=True)
                for lane in range(0, width, LANES)
            ]
            summed = jnp.concatenate(halves, axis=1)
            embedded[pl.ds(place[j], 1), :] = summed * gain[pl.ds(place[j], 1), :] * inverse
        at += n
    pooled = embedded[...]
    mean = jnp.sum(jnp.sum(pooled * pooled, axis=1, keepdims=True), axis=0, keepdims=True)
    embedded[...] = pooled * lax.rsqrt(mean * (1.0 / features) + 1e-06)


def pool(place, lengths, gain, hidden, squares):
    counts = tuple(part.shape[0] for part in hidden)
    total = sum(counts)
    rows, width = hidden[0].shape[1:]
    parts = len(hidden)
    return pl.pallas_call(
        functools.partial(pool_kernel, parts, counts),
        out_shape=jax.ShapeDtypeStruct((total, width), jnp.float32),
        in_specs=[pl.BlockSpec(memory_space=pltpu.SMEM)] * 2
        + [pl.BlockSpec(memory_space=pltpu.VMEM)]
        + [pl.BlockSpec(memory_space=pl.ANY)] * parts
        + [pl.BlockSpec(memory_space=pltpu.VMEM)] * parts,
        out_specs=pl.BlockSpec(memory_space=pltpu.VMEM),
        scratch_shapes=[
            pltpu.VMEM((total, rows, width), jnp.float32),
            pltpu.VMEM((rows, LANES), jnp.float32),
            pltpu.SemaphoreType.DMA((parts,)),
        ],
        compiler_params=pltpu.CompilerParams(vmem_limit_bytes=24 << 20),
    )(place, lengths, gain.reshape(total, width), *hidden, *squares)


def embed_ring(context, residual, out_proj, norm_gain, lengths):
    ranks = lax.axis_size("dp")
    me = lax.axis_index("dp")
    side = lax.axis_index("groups")
    core = me % CORES
    size = ranks // CORES
    where = [CYCLE.index(chip) for chip in range(size)]

    def ring(step):
        return [
            (CYCLE[r] * CORES + c, CYCLE[(r + step) % size] * CORES + c)
            for r in range(size)
            for c in range(CORES)
        ]

    def from_next(piece):
        return lax.ppermute(piece, "dp", ring(-1))

    def from_last(piece):
        return lax.ppermute(piece, "dp", ring(1))

    def over_x(piece):
        return lax.ppermute(piece, "groups", [(0, 1), (1, 0)])

    def other_core(piece):
        return lax.ppermute(piece, "dp", [(i, i ^ 1) for i in range(ranks)])

    def after(piece, *earlier):
        return lax.optimization_barrier((piece, earlier))[0]

    cycle = jnp.array(CYCLE, jnp.int32)
    at = jnp.array(where, jnp.int32)[me // CORES]

    def place_of(group):
        chips = cycle[(at + jnp.array(group, jnp.int32)) % size]
        return jnp.stack([chips * CORES + core, chips * CORES + 1 - core], axis=1).reshape(-1)

    steps = ((0,), (1, 2), (-2, 3), (-1, -3, 4))
    places = [place_of(group) for group in steps]
    hidden, squares = [], []

    def run(i, side, pieces):
        h, s = project(jnp.append(places[i], side), context, residual, pieces)
        hidden.append(h)
        squares.append(s)
        return s

    half = out_proj.shape[0] // 2
    own = lax.dynamic_slice_in_dim(out_proj, side * half, half, 0)
    n1, l1 = from_next(own), from_last(own)
    other = other_core(out_proj)
    done = run(0, 0, [out_proj[:half], out_proj[half:], other[:half], other[half:]])
    n1, l1 = after((n1, l1), done)
    n2, l2 = from_next(n1), from_last(l1)
    xn1 = over_x(n1)
    cn1, cl1 = other_core(n1), other_core(l1)
    n2, l2, xn1 = after((n2, l2, xn1), cn1, cl1)
    n3, l3 = from_next(n2), from_last(l2)
    xn2 = over_x(n2)
    cn2, cl2, cxn1 = other_core(n2), other_core(l2), other_core(xn1)
    xn2, n3, l3 = after((xn2, n3, l3), cn2, cl2, cxn1)
    n3x, l4 = from_next(xn2), from_last(l3)
    xl2 = over_x(after(l2, xn2))
    cn3, cl3, cxn2 = other_core(n3), other_core(l3), other_core(xn2)
    done = run(1, side, [n1, xn1, cn1, cxn1, n2, xn2, cn2, cxn2])
    n3x, l4, xl2 = after((n3x, l4, xl2), cn3, cl3, cxn2, done)
    n4x, l3x = from_next(n3x), from_last(xl2)
    xl1 = over_x(after(l1, xl2))
    cn3x, cl4, cxl2 = other_core(n3x), other_core(l4), other_core(xl2)
    done = run(2, side, [l2, xl2, cl2, cxl2, n3, n3x, cn3, cn3x])
    n4x, l3x, xl1 = after((n4x, l3x, xl1), cl4, done)
    cn4x, cl3x, cxl1 = other_core(n4x), other_core(l3x), other_core(xl1)
    run(3, side, [l1, xl1, cl1, cxl1, l3, l3x, cl3, cl3x, l4, n4x, cl4, cn4x])
    embedded = pool(jnp.concatenate(places), lengths, norm_gain, hidden, squares)
    return embedded.reshape(1, -1)


def embed_gather(context, residual, out_proj, norm_gain, lengths):
    tok_rows = context.shape[0]
    features = residual.shape[1]
    passages_here = lengths.shape[0]
    seq_len = tok_rows // passages_here
    branch = jnp.dot(
        context,
        lax.all_gather(out_proj, "dp", axis=1, tiled=True),
        preferred_element_type=jnp.float32,
    )
    hidden_sum = residual.astype(jnp.float32) + branch
    normed = (
        hidden_sum
        * lax.rsqrt(jnp.mean(hidden_sum * hidden_sum, axis=-1, keepdims=True) + 1e-05)
        * norm_gain
    )
    shaped = normed.reshape(passages_here, seq_len, features)
    valid_mask = (jnp.arange(seq_len)[None, :] < lengths[:, None]).astype(jnp.float32)
    pooled = jnp.sum(shaped * valid_mask[:, :, None], axis=1) / lengths.astype(jnp.float32)[:, None]
    return pooled * lax.rsqrt(jnp.mean(pooled * pooled, axis=-1, keepdims=True) + 1e-06)


def per_device(context, residual, out_proj, norm_gain, lengths, queries, pattern):
    features = residual.shape[1]
    query_rows = queries.shape[0]
    blocks = pattern.shape[1]
    ranks = lax.axis_size("dp")
    me = lax.axis_index("dp")
    if (
        ranks == CORES * len(CYCLE)
        and lax.axis_size("groups") == 2
        and lengths.shape[0] == 1
        and out_proj.shape[1] % LANES == 0
    ):
        embedded = embed_ring(context, residual, out_proj, norm_gain, lengths)
    else:
        embedded = embed_gather(context, residual, out_proj, norm_gain, lengths)
    emb_half = embedded.astype(jnp.bfloat16)
    temper = 1.0 / (0.02 * math.sqrt(features))
    contract = (((1,), (1,)), ((), ()))

    flags = jnp.pad(pattern.astype(jnp.bfloat16), ((0, 0), (0, LANES - blocks)))
    everyone = jnp.broadcast_to(
        jnp.concatenate([emb_half, flags], axis=1)[None], (ranks,) + (emb_half.shape[0], features + LANES)
    )
    everyone = lax.all_to_all(everyone, "dp", split_axis=0, concat_axis=0, tiled=True)
    everyone = everyone.reshape(-1, features + LANES)
    emb_all = everyone[:, :features]
    flags_all = everyone[:, features : features + blocks].astype(jnp.float32)
    scores = lax.dot_general(emb_all, queries, contract, preferred_element_type=jnp.float32) * temper
    row_block = (me * query_rows + jnp.arange(query_rows)) // QB
    picks = (row_block[None, :] == jnp.arange(blocks)[:, None]).astype(jnp.float32)
    cand_mask = jnp.dot(flags_all, picks) > 0
    low = jnp.float32(-1e30)
    peak_part = jnp.max(jnp.where(cand_mask, scores, low), axis=1, keepdims=True)
    weights = jnp.where(cand_mask, jnp.exp(scores - peak_part), 0.0)
    total_part = jnp.sum(weights, axis=1, keepdims=True)
    mix_part = jnp.dot(weights.astype(jnp.bfloat16), queries, preferred_element_type=jnp.float32)

    passages = emb_all.shape[0]
    lane = jnp.arange(LANES)[None, :]
    tail = jnp.where(lane == 0, peak_part, jnp.where(lane == 1, total_part, 0.0))
    parts = jnp.concatenate([mix_part, tail], axis=1).reshape(ranks, passages // ranks, -1)
    parts = lax.all_to_all(parts, "dp", split_axis=0, concat_axis=0, tiled=True)
    mixes, peaks, sums = parts[:, :, :features], parts[:, :, features], parts[:, :, features + 1]
    peak_score = jnp.max(peaks, axis=0)
    factor = jnp.exp(peaks - peak_score[None, :])
    totals = jnp.sum(sums * factor, axis=0)
    recalled = jnp.sum(mixes * factor[:, :, None], axis=0) / totals[:, None]
    log_total = peak_score + jnp.log(totals)
    return (embedded, recalled, log_total)


def solution(mesh):
    in_specs = (
        P(("groups", "dp"), None),
        P(("groups", "dp"), None),
        P(None, "dp"),
        P(),
        P(("groups", "dp")),
        P(("groups", "dp"), None),
        P(("groups", "dp"), None),
    )
    out_specs = (P(("groups", "dp"), None), P(("groups", "dp"), None), P(("groups", "dp")))
    return jax.shard_map(
        per_device, mesh=mesh, in_specs=in_specs, out_specs=out_specs, check_vma=False
    )
```

```python
import functools
import math

import jax
import jax.numpy as jnp
from jax import lax
from jax.experimental import pallas as pl
from jax.experimental.pallas import tpu as pltpu
from jax.sharding import PartitionSpec as P

QB = 256
LANES = 128
CORES = 2
STEP = 256
VMEM_BYTES = 20 << 20
LOW = -1e30
CYCLE = (0, 2, 4, 6, 7, 5, 3, 1)
WAVES = (((0,), ()), ((1,), ()), ((2,), (-1, -3)), ((-2, 3), (4,)))
LATE = (-1, -3, 4)


def column_block(distance, same_core):
    me = lax.axis_index("dp")
    core = lax.rem(me, CORES)
    chip = lax.div(me, CORES)
    z, y = lax.div(chip, 2), lax.rem(chip, 2)
    size = len(CYCLE)
    at = jnp.where(y == 0, z, size - 1 - z)
    there = lax.rem(at + (distance + size), size)
    chip = jnp.where(there < size // 2, 2 * there, 2 * (size - 1 - there) + 1)
    return chip * CORES + (core if same_core else 1 - core)


def columns(distance, same_core, width):
    return pl.ds(pl.multiple_of(column_block(distance, same_core) * width, width), width)


def half_rows(second, half):
    side = lax.axis_index("groups")
    return pl.ds(pl.multiple_of((1 - side if second else side) * half, half), half)


def copy_in(copies, source, target, sems):
    copies.append(pltpu.make_async_copy(source, target, sems.at[len(copies)]))
    copies[-1].start()
    return copies[-1]


def add_squares(squares, at, total):
    square = total * total
    for lane in range(0, total.shape[1], LANES):
        squares[at, :] += square[:, lane : lane + LANES]


def half_kernel(whole, part, sem):
    copy = pltpu.make_async_copy(whole.at[half_rows(False, part.shape[0])], part, sem)
    copy.start()
    copy.wait()


def own_half(whole):
    rows, width = whole.shape
    return pl.pallas_call(
        half_kernel,
        out_shape=jax.ShapeDtypeStruct((rows // 2, width), whole.dtype),
        in_specs=[pl.BlockSpec(memory_space=pl.ANY)],
        out_specs=pl.BlockSpec(memory_space=pl.ANY),
        scratch_shapes=[pltpu.SemaphoreType.DMA],
        compiler_params=pltpu.CompilerParams(vmem_limit_bytes=VMEM_BYTES),
    )(whole)


def wave_kernel(full, part, arrived, whole, context, other_context, residual, *refs):
    count = len(full) + len(part)
    n_pieces = 1 if whole else 2 * len(full) + len(part)
    pieces, refs = refs[:n_pieces], refs[n_pieces:]
    n_given = 2 if arrived else 0
    given, refs = refs[:n_given], refs[n_given:]
    mine, theirs, refs = refs[0], refs[1], refs[2:]
    if arrived:
        finished, refs = refs[0], refs[1:]
    squares, both, weights, extra = refs[:4]
    sems = refs[-1]
    half, width = weights.shape[2:]
    rows = context.shape[0]
    copies = []
    for who, tokens in enumerate((context, other_context)):
        for part_of in range(2):
            source = tokens.at[:, half_rows(part_of, half)]
            copy_in(copies, source, both.at[who, part_of], sems)
    at = 0
    for j in range(count):
        for part_of in range(2 if j < len(full) else 1):
            if whole:
                source = pieces[0].at[half_rows(part_of, half)]
            else:
                source = pieces[at]
                at += 1
            copy_in(copies, source, weights.at[j, part_of], sems)
    for j, distance in enumerate(full + part):
        copy_in(copies, residual.at[:, columns(distance, True, width)], extra.at[j], sems)
    if arrived:
        landed = refs[4]
        for j, distance in enumerate(arrived):
            copy_in(copies, given[0].at[j], landed.at[j], sems)
            copy_in(copies, residual.at[:, columns(distance, False, width)], extra.at[count + j], sems)
        squares[...] = given[1][...]
    else:
        squares[...] = jnp.zeros_like(squares)
    for copy in copies:
        copy.wait()
    if arrived:
        for j in range(len(arrived)):

            @pl.loop(0, rows // STEP)
            def _(k):
                at = pl.ds(pl.multiple_of(k * STEP, STEP), STEP)
                total = landed[j, at, :] + extra[count + j, at, :].astype(jnp.float32)
                finished[j, at, :] = total
                add_squares(squares, at, total)

    for j in range(count):

        @pl.loop(0, rows // STEP)
        def _(k):
            at = pl.ds(pl.multiple_of(k * STEP, STEP), STEP)

            def product(who):
                total = jnp.dot(both[who, 0, at, :], weights[j, 0], preferred_element_type=jnp.float32)
                if j < len(full):
                    total += jnp.dot(both[who, 1, at, :], weights[j, 1], preferred_element_type=jnp.float32)
                return total

            theirs[j, at, :] = product(1)
            total = product(0) + extra[j, at, :].astype(jnp.float32)
            mine[j, at, :] = total
            if j < len(full):
                add_squares(squares, at, total)


def wave(full, part, arrived, context, other_context, residual, pieces, received=None, squares=None):
    count, done = len(full) + len(part), len(arrived)
    rows = context.shape[0]
    whole = len(pieces) == 1
    half, width = pieces[0].shape
    half = half // 2 if whole else half
    given = [received, squares] if arrived else []
    blocks = jax.ShapeDtypeStruct((count, rows, width), jnp.float32)
    outs = [blocks, blocks]
    scratch = [
        pltpu.VMEM((2, 2, rows, half), jnp.bfloat16),
        pltpu.VMEM((count, 2, half, width), jnp.bfloat16),
        pltpu.VMEM((count + done, rows, width), jnp.bfloat16),
    ]
    if arrived:
        outs.append(jax.ShapeDtypeStruct((done, rows, width), jnp.float32))
        scratch.append(pltpu.VMEM((done, rows, width), jnp.float32))
    outs.append(jax.ShapeDtypeStruct((rows, LANES), jnp.float32))
    scratch.append(pltpu.SemaphoreType.DMA((4 + 3 * count + 2 * done,)))
    out = pl.pallas_call(
        functools.partial(wave_kernel, full, part, arrived, whole),
        out_shape=outs,
        in_specs=[pl.BlockSpec(memory_space=pl.ANY)] * (3 + len(pieces))
        + ([pl.BlockSpec(memory_space=pl.ANY), pl.BlockSpec(memory_space=pltpu.VMEM)] if arrived else []),
        out_specs=[pl.BlockSpec(memory_space=pltpu.VMEM)] * len(outs),
        scratch_shapes=scratch,
        compiler_params=pltpu.CompilerParams(vmem_limit_bytes=VMEM_BYTES),
        cost_estimate=pl.CostEstimate(
            flops=4 * rows * half * width * (2 * len(full) + len(part)),
            bytes_accessed=8 * rows * half + count * width * (4 * half + 10 * rows),
            transcendentals=0,
        ),
    )(context, other_context, residual, *pieces, *given)
    if arrived:
        return out
    return out[0], out[1], None, out[2]


def final_kernel(sources, late, plain, length, context, residual, squares, gain, flags, *refs):
    n_late = len(late)
    arrays = 1 + max(source for source, _, _, _ in sources)
    pieces, refs = refs[:n_late], refs[n_late:]
    hidden, refs = refs[:arrays], refs[arrays:]
    embedded, payload, second, weights, extra, blocks, scale_rows, sheet, sems = refs
    half, width = weights.shape[1:]
    rows = context.shape[0]
    total = len(sources)
    features = total * width
    copies = []
    first = [copy_in(copies, context.at[:, half_rows(True, half)], second, sems)]
    late_copies = []
    for i, slot in enumerate(late):
        source, entry, distance, same = sources[slot]
        needed = [
            copy_in(copies, pieces[i], weights.at[i], sems),
            copy_in(copies, hidden[source].at[entry], blocks.at[slot], sems),
        ]
        if not same:
            needed.append(copy_in(copies, residual.at[:, columns(distance, same, width)], extra.at[i], sems))
        late_copies.append(needed)
    plain_copies = []
    for i, slot in enumerate(plain):
        source, entry, distance, same = sources[slot]
        plain_copies.append(
            [
                copy_in(copies, hidden[source].at[entry], blocks.at[slot], sems),
                copy_in(copies, residual.at[:, columns(distance, same, width)], extra.at[n_late + i], sems),
            ]
        )
    rest = [slot for slot in range(total) if slot not in late + plain]
    rest_copies = [
        copy_in(copies, hidden[sources[slot][0]].at[sources[slot][1]], blocks.at[slot], sems) for slot in rest
    ]
    for copy in first:
        copy.wait()
    for i, slot in enumerate(late):
        for copy in late_copies[i]:
            copy.wait()
        same = sources[slot][3]

        @pl.loop(0, rows // STEP)
        def _(k):
            at = pl.ds(pl.multiple_of(k * STEP, STEP), STEP)
            value = jnp.dot(second[at, :], weights[i], preferred_element_type=jnp.float32)
            value += blocks[slot, at, :]
            if not same:
                value += extra[i, at, :].astype(jnp.float32)
            blocks[slot, at, :] = value
            add_squares(squares, at, value)

    for i, slot in enumerate(plain):
        for copy in plain_copies[i]:
            copy.wait()

        @pl.loop(0, rows // STEP)
        def _(k):
            at = pl.ds(pl.multiple_of(k * STEP, STEP), STEP)
            value = blocks[slot, at, :] + extra[n_late + i, at, :].astype(jnp.float32)
            blocks[slot, at, :] = value
            add_squares(squares, at, value)

    mean = jnp.sum(squares[...], axis=1, keepdims=True) * (1.0 / features)
    row = lax.broadcasted_iota(jnp.int32, mean.shape, 0)
    scale = jnp.where(row < length[0], lax.rsqrt(mean + 1e-05), 0.0)
    scale_rows[...] = jnp.broadcast_to(scale, scale_rows.shape)
    for copy in rest_copies:
        copy.wait()
    inverse = 1.0 / jnp.full((1, width), length[0], jnp.int32).astype(jnp.float32)
    for slot, (_, _, distance, same) in enumerate(sources):
        parts = [
            jnp.sum(blocks[slot, :, lane : lane + LANES] * scale_rows[...], axis=0, keepdims=True)
            for lane in range(0, width, LANES)
        ]
        where = columns(distance, same, width)
        embedded[:, where] = jnp.concatenate(parts, axis=1) * gain[:, where] * inverse
    pooled = embedded[...]
    mean = jnp.sum(pooled * pooled, axis=1, keepdims=True) * (1.0 / features)
    embedded[...] = pooled * lax.rsqrt(mean + 1e-06)
    lines = features // LANES
    sheet[lines:, :] = jnp.zeros((sheet.shape[0] - lines, LANES), jnp.float32)
    for line in range(lines):
        sheet[line : line + 1, :] = embedded[:, line * LANES : (line + 1) * LANES]
    sheet[lines : lines + 1, :] = flags[...]
    rounded = sheet[...].astype(jnp.bfloat16)
    for rank in range(payload.shape[0]):
        payload[rank] = rounded


def finish(sources, late, plain, lengths, context, residual, squares, gain, flags, pieces, hidden, ranks):
    rows = context.shape[0]
    half, width = pieces[0].shape
    total = len(sources)
    features = total * width
    lines = -(-(features // LANES + 1) // 16) * 16
    return pl.pallas_call(
        functools.partial(final_kernel, sources, late, plain),
        out_shape=(
            jax.ShapeDtypeStruct((1, features), jnp.float32),
            jax.ShapeDtypeStruct((ranks, lines, LANES), jnp.bfloat16),
        ),
        in_specs=[pl.BlockSpec(memory_space=pltpu.SMEM)]
        + [pl.BlockSpec(memory_space=pl.ANY)] * 2
        + [pl.BlockSpec(memory_space=pltpu.VMEM)] * 3
        + [pl.BlockSpec(memory_space=pl.ANY)] * (len(pieces) + len(hidden)),
        out_specs=(pl.BlockSpec(memory_space=pltpu.VMEM), pl.BlockSpec(memory_space=pltpu.VMEM)),
        scratch_shapes=[
            pltpu.VMEM((rows, half), jnp.bfloat16),
            pltpu.VMEM((len(late), half, width), jnp.bfloat16),
            pltpu.VMEM((len(late) + len(plain), rows, width), jnp.bfloat16),
            pltpu.VMEM((total, rows, width), jnp.float32),
            pltpu.VMEM((rows, LANES), jnp.float32),
            pltpu.VMEM((lines, LANES), jnp.float32),
            pltpu.SemaphoreType.DMA((1 + total + 2 * len(late) + len(plain),)),
        ],
        compiler_params=pltpu.CompilerParams(vmem_limit_bytes=VMEM_BYTES),
    )(lengths, context, residual, squares, gain, flags, *pieces, *hidden)


def score_kernel(lines, blocks, got, queries, other_queries, out, wide, emb, mix):
    me = lax.axis_index("dp")
    ranks = got.shape[0]
    count = queries.shape[0]
    wide[...] = got[...].astype(jnp.float32)
    for line in range(lines):
        emb[:, line * LANES : (line + 1) * LANES] = wide[:, line, :]
    half = emb[...].astype(jnp.bfloat16)
    flags = wide[:, lines, :].astype(jnp.bfloat16)
    temper = 1.0 / (0.02 * math.sqrt(lines * LANES))
    scores, masks = [], []
    for owner, rows in ((me, queries), (me + 1 - 2 * lax.rem(me, CORES), other_queries)):
        score = lax.dot_general(
            half, rows[...], (((1,), (1,)), ((), ())), preferred_element_type=jnp.float32
        )
        scores.append(score * temper)
        block = lax.broadcasted_iota(jnp.int32, (LANES, count), 0)
        row = owner * count + lax.broadcasted_iota(jnp.int32, (LANES, count), 1)
        pick = (row >= block * QB) & (row < block * QB + QB) & (block < blocks)
        pick = jnp.where(pick, 1.0, 0.0).astype(jnp.bfloat16)
        masks.append(jnp.dot(flags, pick, preferred_element_type=jnp.float32) > 0.5)
    peaks = [
        jnp.max(jnp.where(mask, score, LOW), axis=1, keepdims=True) for score, mask in zip(scores, masks)
    ]
    peak = jnp.maximum(*peaks)
    weights = [jnp.where(mask, jnp.exp(score - peak), 0.0) for score, mask in zip(scores, masks)]
    total = sum(jnp.sum(weight, axis=1, keepdims=True) for weight in weights)
    mix[...] = jnp.dot(
        weights[0].astype(jnp.bfloat16), queries[...], preferred_element_type=jnp.float32
    ) + jnp.dot(weights[1].astype(jnp.bfloat16), other_queries[...], preferred_element_type=jnp.float32)
    for line in range(lines):
        out[:, line, :] = mix[:, line * LANES : (line + 1) * LANES]
    lane = lax.broadcasted_iota(jnp.int32, (ranks, LANES), 1)
    out[:, lines, :] = jnp.where(lane == 0, peak, jnp.where(lane == 1, total, 0.0))
    for line in range(lines + 1, out.shape[1]):
        out[:, line, :] = jnp.zeros((ranks, LANES), jnp.float32)


def score(got, queries, other_queries, blocks):
    ranks = got.shape[0]
    features = queries.shape[1]
    lines = features // LANES
    return pl.pallas_call(
        functools.partial(score_kernel, lines, blocks),
        out_shape=jax.ShapeDtypeStruct((ranks, -(-(lines + 1) // 8) * 8, LANES), jnp.float32),
        in_specs=[pl.BlockSpec(memory_space=pltpu.VMEM)] * 3,
        out_specs=pl.BlockSpec(memory_space=pltpu.VMEM),
        scratch_shapes=[
            pltpu.VMEM(got.shape, jnp.float32),
            pltpu.VMEM((ranks, features), jnp.float32),
            pltpu.VMEM((ranks, features), jnp.float32),
        ],
        compiler_params=pltpu.CompilerParams(vmem_limit_bytes=VMEM_BYTES),
    )(got, queries, other_queries)


def combine_kernel(lines, got, recalled, log_total):
    stats = got[:, lines, :]
    peaks, sums = stats[:, 0:1], stats[:, 1:2]
    peak = jnp.max(peaks, axis=0, keepdims=True)
    factor = jnp.exp(peaks - peak)
    total = jnp.sum(sums * factor, axis=0, keepdims=True)
    mix = got[0, :lines, :] * factor[0:1, :]
    for rank in range(1, got.shape[0]):
        mix += got[rank, :lines, :] * factor[rank : rank + 1, :]
    mix = mix / total
    for line in range(lines):
        recalled[:, line * LANES : (line + 1) * LANES] = mix[line : line + 1, :]
    log_total[...] = peak + jnp.log(total)


def combine(got, features):
    recalled, log_total = pl.pallas_call(
        functools.partial(combine_kernel, features // LANES),
        out_shape=(
            jax.ShapeDtypeStruct((1, features), jnp.float32),
            jax.ShapeDtypeStruct((1, 1), jnp.float32),
        ),
        in_specs=[pl.BlockSpec(memory_space=pltpu.VMEM)],
        out_specs=(pl.BlockSpec(memory_space=pltpu.VMEM), pl.BlockSpec(memory_space=pltpu.VMEM)),
        compiler_params=pltpu.CompilerParams(vmem_limit_bytes=VMEM_BYTES),
    )(got)
    return recalled, log_total.reshape(1)


def on_cycle(context, residual, out_proj, norm_gain, lengths, queries, pattern):
    ranks = lax.axis_size("dp")
    size = ranks // CORES
    features = residual.shape[1]

    def ring(step):
        return [
            (CYCLE[r] * CORES + c, CYCLE[(r + step) % size] * CORES + c)
            for r in range(size)
            for c in range(CORES)
        ]

    def from_next(piece):
        return lax.ppermute(piece, "dp", ring(-1))

    def from_last(piece):
        return lax.ppermute(piece, "dp", ring(1))

    def over_x(piece):
        return lax.ppermute(piece, "groups", [(0, 1), (1, 0)])

    def other_core(piece):
        return lax.ppermute(piece, "dp", [(i, i ^ 1) for i in range(ranks)])

    wait = lax.optimization_barrier
    own = own_half(out_proj)
    n1, l1, context2 = wait((from_next(own), from_last(own), other_core(context)))

    def run(i, pieces, arrived=(), received=None, squares=None):
        full, part = WAVES[i]
        return wave(full, part, arrived, context, context2, residual, pieces, received, squares)

    h0, t0, _, sq0 = run(0, [out_proj])
    n2, l2, xn1, queries2, t0, sq0 = wait(
        (from_next(n1), from_last(l1), over_x(n1), other_core(queries), t0, sq0)
    )
    h1, t1, f0, sq1 = run(1, [n1, xn1], (0,), other_core(t0), sq0)
    n3, l3, xn2, t1, sq1 = wait((from_next(n2), from_last(l2), over_x(n2), t1, sq1))
    h2, t2, f1, sq2 = run(2, [n2, xn2, l1, l3], (1,), other_core(t1), sq1)
    n3x, l4, xl2, t2, sq2 = wait((from_next(xn2), from_last(l3), over_x(l2), t2, sq2))
    r2 = other_core(t2)
    h3, t3, f2, sq3 = run(3, [l2, xl2, n3, n3x, l4], (2,), r2, sq2)
    n4x, l3x, xl1, t3, sq3 = wait((from_next(n3x), from_last(xl2), over_x(l1), t3, sq3))
    late = [xl1, l3x, n4x]
    late += [other_core(piece) for piece in late]
    r3 = other_core(t3)

    hidden = [h0, h1, h2, h3, f0, f1, f2, r2, r3]
    sources = (
        (2, 1, -1, True),
        (2, 2, -3, True),
        (3, 2, 4, True),
        (7, 1, -1, False),
        (7, 2, -3, False),
        (8, 2, 4, False),
        (8, 0, -2, False),
        (8, 1, 3, False),
        (0, 0, 0, True),
        (1, 0, 1, True),
        (2, 0, 2, True),
        (3, 0, -2, True),
        (3, 1, 3, True),
        (4, 0, 0, False),
        (5, 0, 1, False),
        (6, 0, 2, False),
    )
    flags = jnp.pad(pattern.astype(jnp.float32), ((0, 0), (0, LANES - pattern.shape[1])))
    embedded, payload = finish(
        sources,
        (0, 1, 2, 3, 4, 5),
        (6, 7),
        lengths,
        context,
        residual,
        sq3,
        norm_gain.reshape(1, -1),
        flags,
        late,
        hidden,
        size,
    )
    same_core = [list(range(c, ranks, CORES)) for c in range(CORES)]

    def spread(blocks):
        return lax.all_to_all(blocks, "dp", 0, 0, axis_index_groups=same_core, tiled=True)

    parts = score(spread(payload), queries, queries2, pattern.shape[1])
    recalled, log_total = combine(spread(parts), features)
    return embedded, recalled, log_total


def gathered(context, residual, out_proj, norm_gain, lengths, queries, pattern):
    tok_rows = context.shape[0]
    features = residual.shape[1]
    passages_here = lengths.shape[0]
    seq_len = tok_rows // passages_here
    query_rows = queries.shape[0]
    blocks = pattern.shape[1]
    ranks = lax.axis_size("dp")
    me = lax.axis_index("dp")
    branch = jnp.dot(
        context,
        lax.all_gather(out_proj, "dp", axis=1, tiled=True),
        preferred_element_type=jnp.float32,
    )
    hidden_sum = residual.astype(jnp.float32) + branch
    normed = (
        hidden_sum
        * lax.rsqrt(jnp.mean(hidden_sum * hidden_sum, axis=-1, keepdims=True) + 1e-05)
        * norm_gain
    )
    shaped = normed.reshape(passages_here, seq_len, features)
    valid_mask = (jnp.arange(seq_len)[None, :] < lengths[:, None]).astype(jnp.float32)
    pooled = jnp.sum(shaped * valid_mask[:, :, None], axis=1) / lengths.astype(jnp.float32)[:, None]
    embedded = pooled * lax.rsqrt(jnp.mean(pooled * pooled, axis=-1, keepdims=True) + 1e-06)
    emb_half = embedded.astype(jnp.bfloat16)
    temper = 1.0 / (0.02 * math.sqrt(features))
    contract = (((1,), (1,)), ((), ()))

    flags = jnp.pad(pattern.astype(jnp.bfloat16), ((0, 0), (0, LANES - blocks)))
    everyone = lax.all_gather(jnp.concatenate([emb_half, flags], axis=1), "dp", axis=0, tiled=True)
    emb_all = everyone[:, :features]
    flags_all = everyone[:, features : features + blocks].astype(jnp.float32)
    scores = lax.dot_general(emb_all, queries, contract, preferred_element_type=jnp.float32) * temper
    row_block = (me * query_rows + jnp.arange(query_rows)) // QB
    picks = (row_block[None, :] == jnp.arange(blocks)[:, None]).astype(jnp.float32)
    cand_mask = jnp.dot(flags_all, picks) > 0
    peak_part = jnp.max(jnp.where(cand_mask, scores, LOW), axis=1, keepdims=True)
    weights = jnp.where(cand_mask, jnp.exp(scores - peak_part), 0.0)
    total_part = jnp.sum(weights, axis=1, keepdims=True)
    mix_part = jnp.dot(weights.astype(jnp.bfloat16), queries, preferred_element_type=jnp.float32)

    passages = emb_all.shape[0]
    lane = jnp.arange(LANES)[None, :]
    tail = jnp.where(lane == 0, peak_part, jnp.where(lane == 1, total_part, 0.0))
    parts = jnp.concatenate([mix_part, tail], axis=1).reshape(ranks, passages // ranks, -1)
    parts = lax.all_to_all(parts, "dp", split_axis=0, concat_axis=0, tiled=True)
    mixes, peaks, sums = parts[:, :, :features], parts[:, :, features], parts[:, :, features + 1]
    peak_score = jnp.max(peaks, axis=0)
    factor = jnp.exp(peaks - peak_score[None, :])
    totals = jnp.sum(sums * factor, axis=0)
    recalled = jnp.sum(mixes * factor[:, :, None], axis=0) / totals[:, None]
    log_total = peak_score + jnp.log(totals)
    return (embedded, recalled, log_total)


def per_device(context, residual, out_proj, norm_gain, lengths, queries, pattern):
    fits = (
        lax.axis_size("dp") == CORES * len(CYCLE)
        and lax.axis_size("groups") == 2
        and lengths.shape[0] == 1
        and out_proj.shape[1] % LANES == 0
        and out_proj.shape[0] % (2 * LANES) == 0
        and context.shape[0] % STEP == 0
        and pattern.shape[1] <= LANES
    )
    form = on_cycle if fits else gathered
    return form(context, residual, out_proj, norm_gain, lengths, queries, pattern)


def solution(mesh):
    in_specs = (
        P(("groups", "dp"), None),
        P(("groups", "dp"), None),
        P(None, "dp"),
        P(),
        P(("groups", "dp")),
        P(("groups", "dp"), None),
        P(("groups", "dp"), None),
    )
    out_specs = (P(("groups", "dp"), None), P(("groups", "dp"), None), P(("groups", "dp")))
    return jax.shard_map(
        per_device, mesh=mesh, in_specs=in_specs, out_specs=out_specs, check_vma=False
    )
```

```python
import functools
import math

import jax
import jax.numpy as jnp
from jax import lax
from jax.experimental import pallas as pl
from jax.experimental.pallas import tpu as pltpu
from jax.sharding import PartitionSpec as P

QB = 256
LANES = 128
CORES = 2
STEP = 256
VMEM_BYTES = 20 << 20
FULL_VMEM_BYTES = 60 << 20
LOW = -1e30
CYCLE = (0, 2, 4, 6, 7, 5, 3, 1)
WAVES = (((0,), ()), ((1,), ()), ((2,), (-1, -3)), ((-2, 3), (4,)))
LATE = (-1, -3, 4)


def column_block(distance, same_core):
    me = lax.axis_index("dp")
    core = lax.rem(me, CORES)
    chip = lax.div(me, CORES)
    z, y = lax.div(chip, 2), lax.rem(chip, 2)
    size = len(CYCLE)
    at = jnp.where(y == 0, z, size - 1 - z)
    core = core if same_core else 1 - core
    there = lax.rem(at + jnp.where(core == 0, size + distance, size - distance), size)
    chip = jnp.where(there < size // 2, 2 * there, 2 * (size - 1 - there) + 1)
    return chip * CORES + core


def columns(distance, same_core, width):
    return pl.ds(pl.multiple_of(column_block(distance, same_core) * width, width), width)


def half_rows(second, half):
    side = lax.axis_index("groups")
    return pl.ds(pl.multiple_of((1 - side if second else side) * half, half), half)


def copy_in(copies, source, target, sems):
    copies.append(pltpu.make_async_copy(source, target, sems.at[len(copies)]))
    copies[-1].start()
    return copies[-1]


def add_squares(squares, at, total):
    square = total * total
    for lane in range(0, total.shape[1], LANES):
        squares[at, :] += square[:, lane : lane + LANES]


def half_kernel(whole, part, sem):
    copy = pltpu.make_async_copy(whole.at[half_rows(False, part.shape[0])], part, sem)
    copy.start()
    copy.wait()


def own_half(whole):
    rows, width = whole.shape
    return pl.pallas_call(
        half_kernel,
        out_shape=jax.ShapeDtypeStruct((rows // 2, width), whole.dtype),
        in_specs=[pl.BlockSpec(memory_space=pl.ANY)],
        out_specs=pl.BlockSpec(memory_space=pl.ANY),
        scratch_shapes=[pltpu.SemaphoreType.DMA],
        compiler_params=pltpu.CompilerParams(vmem_limit_bytes=FULL_VMEM_BYTES),
    )(whole)


def wave_kernel(full, part, arrived, whole, context, other_context, residual, *refs):
    count = len(full) + len(part)
    n_pieces = 1 if whole else 2 * len(full) + len(part)
    pieces, refs = refs[:n_pieces], refs[n_pieces:]
    n_given = 2 if arrived else 0
    given, refs = refs[:n_given], refs[n_given:]
    mine, theirs, refs = refs[0], refs[1], refs[2:]
    if arrived:
        finished, refs = refs[0], refs[1:]
    squares, both, weights, extra = refs[:4]
    sems = refs[-1]
    half, width = weights.shape[2:]
    rows = context.shape[0]
    copies = []
    for who, tokens in enumerate((context, other_context)):
        for part_of in range(2):
            source = tokens.at[:, half_rows(part_of, half)]
            copy_in(copies, source, both.at[who, part_of], sems)
    at = 0
    for j in range(count):
        for part_of in range(2 if j < len(full) else 1):
            if whole:
                source = pieces[0].at[half_rows(part_of, half)]
            else:
                source = pieces[at]
                at += 1
            copy_in(copies, source, weights.at[j, part_of], sems)
    for j, distance in enumerate(full + part):
        copy_in(copies, residual.at[:, columns(distance, True, width)], extra.at[j], sems)
    if arrived:
        landed = refs[4]
        for j, distance in enumerate(arrived):
            copy_in(copies, given[0].at[j], landed.at[j], sems)
            copy_in(copies, residual.at[:, columns(distance, False, width)], extra.at[count + j], sems)
        squares[...] = given[1][...]
    else:
        squares[...] = jnp.zeros_like(squares)
    for copy in copies:
        copy.wait()
    if arrived:
        for j in range(len(arrived)):

            @pl.loop(0, rows // STEP)
            def _(k):
                at = pl.ds(pl.multiple_of(k * STEP, STEP), STEP)
                total = landed[j, at, :] + extra[count + j, at, :].astype(jnp.float32)
                finished[j, at, :] = total
                add_squares(squares, at, total)

    for j in range(count):

        @pl.loop(0, rows // STEP)
        def _(k):
            at = pl.ds(pl.multiple_of(k * STEP, STEP), STEP)

            def product(who):
                total = jnp.dot(both[who, 0, at, :], weights[j, 0], preferred_element_type=jnp.float32)
                if j < len(full):
                    total += jnp.dot(both[who, 1, at, :], weights[j, 1], preferred_element_type=jnp.float32)
                return total

            theirs[j, at, :] = product(1)
            total = product(0) + extra[j, at, :].astype(jnp.float32)
            mine[j, at, :] = total
            if j < len(full):
                add_squares(squares, at, total)


def wave(full, part, arrived, context, other_context, residual, pieces, received=None, squares=None):
    count, done = len(full) + len(part), len(arrived)
    rows = context.shape[0]
    whole = len(pieces) == 1
    half, width = pieces[0].shape
    half = half // 2 if whole else half
    given = [received, squares] if arrived else []
    blocks = jax.ShapeDtypeStruct((count, rows, width), jnp.float32)
    outs = [blocks, blocks]
    scratch = [
        pltpu.VMEM((2, 2, rows, half), jnp.bfloat16),
        pltpu.VMEM((count, 2, half, width), jnp.bfloat16),
        pltpu.VMEM((count + done, rows, width), jnp.bfloat16),
    ]
    if arrived:
        outs.append(jax.ShapeDtypeStruct((done, rows, width), jnp.float32))
        scratch.append(pltpu.VMEM((done, rows, width), jnp.float32))
    outs.append(jax.ShapeDtypeStruct((rows, LANES), jnp.float32))
    scratch.append(pltpu.SemaphoreType.DMA((4 + 3 * count + 2 * done,)))
    out = pl.pallas_call(
        functools.partial(wave_kernel, full, part, arrived, whole),
        out_shape=outs,
        in_specs=[pl.BlockSpec(memory_space=pl.ANY)] * (3 + len(pieces))
        + ([pl.BlockSpec(memory_space=pl.ANY), pl.BlockSpec(memory_space=pltpu.VMEM)] if arrived else []),
        out_specs=[pl.BlockSpec(memory_space=pltpu.VMEM)] * len(outs),
        scratch_shapes=scratch,
        compiler_params=pltpu.CompilerParams(vmem_limit_bytes=VMEM_BYTES),
        cost_estimate=pl.CostEstimate(
            flops=4 * rows * half * width * (2 * len(full) + len(part)),
            bytes_accessed=8 * rows * half + count * width * (4 * half + 10 * rows),
            transcendentals=0,
        ),
    )(context, other_context, residual, *pieces, *given)
    if arrived:
        return out
    return out[0], out[1], None, out[2]


def late_kernel(entries, context, given, *refs):
    count = len(entries)
    pieces, parts = refs[:count], refs[count : 2 * count]
    finished, squares, second, weights, landed, sems = refs[2 * count :]
    half, width = weights.shape[1:]
    rows = context.shape[0]
    copies = []
    first = copy_in(copies, context.at[:, half_rows(True, half)], second, sems)
    needed = [
        (
            copy_in(copies, pieces[i], weights.at[i], sems),
            copy_in(copies, parts[i].at[entries[i]], landed.at[i], sems),
        )
        for i in range(count)
    ]
    squares[...] = given[...]
    first.wait()
    for i in range(count):
        for copy in needed[i]:
            copy.wait()

        @pl.loop(0, rows // STEP)
        def _(k):
            at = pl.ds(pl.multiple_of(k * STEP, STEP), STEP)
            value = jnp.dot(second[at, :], weights[i], preferred_element_type=jnp.float32)
            value += landed[i, at, :]
            finished[i, at, :] = value
            add_squares(squares, at, value)


def late_half(context, squares, pieces, parts, entries):
    count = len(pieces)
    rows = context.shape[0]
    half, width = pieces[0].shape
    return pl.pallas_call(
        functools.partial(late_kernel, entries),
        out_shape=(
            jax.ShapeDtypeStruct((count, rows, width), jnp.float32),
            jax.ShapeDtypeStruct(squares.shape, jnp.float32),
        ),
        in_specs=[pl.BlockSpec(memory_space=pl.ANY), pl.BlockSpec(memory_space=pltpu.VMEM)]
        + [pl.BlockSpec(memory_space=pl.ANY)] * (2 * count),
        out_specs=(pl.BlockSpec(memory_space=pltpu.VMEM), pl.BlockSpec(memory_space=pltpu.VMEM)),
        scratch_shapes=[
            pltpu.VMEM((rows, half), jnp.bfloat16),
            pltpu.VMEM((count, half, width), jnp.bfloat16),
            pltpu.VMEM((count, rows, width), jnp.float32),
            pltpu.SemaphoreType.DMA((1 + 2 * count,)),
        ],
        compiler_params=pltpu.CompilerParams(vmem_limit_bytes=VMEM_BYTES),
        cost_estimate=pl.CostEstimate(
            flops=2 * rows * half * width * count,
            bytes_accessed=2 * rows * half + count * width * (2 * half + 8 * rows),
            transcendentals=0,
        ),
    )(context, squares, *pieces, *parts)


def final_kernel(sources, late, plain, length, context, residual, squares, gain, flags, *refs):
    n_late = len(late)
    arrays = 1 + max(source for source, _, _, _ in sources)
    pieces, refs = refs[:n_late], refs[n_late:]
    hidden, refs = refs[:arrays], refs[arrays:]
    embedded, payload, second, weights, extra, blocks, scale_rows, sheet, sems = refs
    half, width = weights.shape[1:]
    rows = context.shape[0]
    total = len(sources)
    features = total * width
    copies = []
    first = [copy_in(copies, context.at[:, half_rows(True, half)], second, sems)]
    late_copies = []
    for i, slot in enumerate(late):
        source, entry, distance, same = sources[slot]
        late_copies.append(
            [
                copy_in(copies, pieces[i], weights.at[i], sems),
                copy_in(copies, hidden[source].at[entry], blocks.at[slot], sems),
                copy_in(copies, residual.at[:, columns(distance, same, width)], extra.at[i], sems),
            ]
        )
    plain_copies = []
    for i, slot in enumerate(plain):
        source, entry, distance, same = sources[slot]
        plain_copies.append(
            [
                copy_in(copies, hidden[source].at[entry], blocks.at[slot], sems),
                copy_in(copies, residual.at[:, columns(distance, same, width)], extra.at[n_late + i], sems),
            ]
        )
    rest = [slot for slot in range(total) if slot not in late + plain]
    rest_copies = [
        copy_in(copies, hidden[sources[slot][0]].at[sources[slot][1]], blocks.at[slot], sems) for slot in rest
    ]
    for copy in first:
        copy.wait()
    for i, slot in enumerate(late):
        for copy in late_copies[i]:
            copy.wait()

        @pl.loop(0, rows // STEP)
        def _(k):
            at = pl.ds(pl.multiple_of(k * STEP, STEP), STEP)
            value = jnp.dot(second[at, :], weights[i], preferred_element_type=jnp.float32)
            value += blocks[slot, at, :] + extra[i, at, :].astype(jnp.float32)
            blocks[slot, at, :] = value
            add_squares(squares, at, value)

    for i, slot in enumerate(plain):
        for copy in plain_copies[i]:
            copy.wait()

        @pl.loop(0, rows // STEP)
        def _(k):
            at = pl.ds(pl.multiple_of(k * STEP, STEP), STEP)
            value = blocks[slot, at, :] + extra[n_late + i, at, :].astype(jnp.float32)
            blocks[slot, at, :] = value
            add_squares(squares, at, value)

    mean = jnp.sum(squares[...], axis=1, keepdims=True) * (1.0 / features)
    row = lax.broadcasted_iota(jnp.int32, mean.shape, 0)
    scale = jnp.where(row < length[0], lax.rsqrt(mean + 1e-05), 0.0)
    scale_rows[...] = jnp.broadcast_to(scale, scale_rows.shape)
    for copy in rest_copies:
        copy.wait()
    inverse = 1.0 / jnp.full((1, width), length[0], jnp.int32).astype(jnp.float32)
    for slot, (_, _, distance, same) in enumerate(sources):
        parts = [
            jnp.sum(blocks[slot, :, lane : lane + LANES] * scale_rows[...], axis=0, keepdims=True)
            for lane in range(0, width, LANES)
        ]
        where = columns(distance, same, width)
        embedded[:, where] = jnp.concatenate(parts, axis=1) * gain[:, where] * inverse
    pooled = embedded[...]
    mean = jnp.sum(pooled * pooled, axis=1, keepdims=True) * (1.0 / features)
    embedded[...] = pooled * lax.rsqrt(mean + 1e-06)
    lines = features // LANES
    sheet[lines:, :] = jnp.zeros((sheet.shape[0] - lines, LANES), jnp.float32)
    for line in range(lines):
        sheet[line : line + 1, :] = embedded[:, line * LANES : (line + 1) * LANES]
    sheet[lines : lines + 1, :] = flags[...]
    rounded = sheet[...].astype(jnp.bfloat16)
    for rank in range(payload.shape[0]):
        payload[rank] = rounded


def finish(sources, late, plain, lengths, context, residual, squares, gain, flags, pieces, hidden, ranks):
    rows = context.shape[0]
    half, width = pieces[0].shape
    total = len(sources)
    features = total * width
    lines = -(-(features // LANES + 1) // 16) * 16
    return pl.pallas_call(
        functools.partial(final_kernel, sources, late, plain),
        out_shape=(
            jax.ShapeDtypeStruct((1, features), jnp.float32),
            jax.ShapeDtypeStruct((ranks, lines, LANES), jnp.bfloat16),
        ),
        in_specs=[pl.BlockSpec(memory_space=pltpu.SMEM)]
        + [pl.BlockSpec(memory_space=pl.ANY)] * 2
        + [pl.BlockSpec(memory_space=pltpu.VMEM)] * 3
        + [pl.BlockSpec(memory_space=pl.ANY)] * (len(pieces) + len(hidden)),
        out_specs=(pl.BlockSpec(memory_space=pltpu.VMEM), pl.BlockSpec(memory_space=pltpu.VMEM)),
        scratch_shapes=[
            pltpu.VMEM((rows, half), jnp.bfloat16),
            pltpu.VMEM((len(late), half, width), jnp.bfloat16),
            pltpu.VMEM((len(late) + len(plain), rows, width), jnp.bfloat16),
            pltpu.VMEM((total, rows, width), jnp.float32),
            pltpu.VMEM((rows, LANES), jnp.float32),
            pltpu.VMEM((lines, LANES), jnp.float32),
            pltpu.SemaphoreType.DMA((1 + total + 2 * len(late) + len(plain),)),
        ],
        compiler_params=pltpu.CompilerParams(vmem_limit_bytes=VMEM_BYTES),
    )(lengths, context, residual, squares, gain, flags, *pieces, *hidden)


def score_kernel(lines, blocks, got, queries, other_queries, out, wide, emb, mix):
    me = lax.axis_index("dp")
    ranks = got.shape[0]
    count = queries.shape[0]
    wide[...] = got[...].astype(jnp.float32)
    for line in range(lines):
        emb[:, line * LANES : (line + 1) * LANES] = wide[:, line, :]
    half = emb[...].astype(jnp.bfloat16)
    flags = wide[:, lines, :].astype(jnp.bfloat16)
    temper = 1.0 / (0.02 * math.sqrt(lines * LANES))
    scores, masks = [], []
    for owner, rows in ((me, queries), (me + 1 - 2 * lax.rem(me, CORES), other_queries)):
        score = lax.dot_general(
            half, rows[...], (((1,), (1,)), ((), ())), preferred_element_type=jnp.float32
        )
        scores.append(score * temper)
        block = lax.broadcasted_iota(jnp.int32, (LANES, count), 0)
        row = owner * count + lax.broadcasted_iota(jnp.int32, (LANES, count), 1)
        pick = (row >= block * QB) & (row < block * QB + QB) & (block < blocks)
        pick = jnp.where(pick, 1.0, 0.0).astype(jnp.bfloat16)
        masks.append(jnp.dot(flags, pick, preferred_element_type=jnp.float32) > 0.5)
    peaks = [
        jnp.max(jnp.where(mask, score, LOW), axis=1, keepdims=True) for score, mask in zip(scores, masks)
    ]
    peak = jnp.maximum(*peaks)
    weights = [jnp.where(mask, jnp.exp(score - peak), 0.0) for score, mask in zip(scores, masks)]
    total = sum(jnp.sum(weight, axis=1, keepdims=True) for weight in weights)
    mix[...] = jnp.dot(
        weights[0].astype(jnp.bfloat16), queries[...], preferred_element_type=jnp.float32
    ) + jnp.dot(weights[1].astype(jnp.bfloat16), other_queries[...], preferred_element_type=jnp.float32)
    for line in range(lines):
        out[:, line, :] = mix[:, line * LANES : (line + 1) * LANES]
    lane = lax.broadcasted_iota(jnp.int32, (ranks, LANES), 1)
    out[:, lines, :] = jnp.where(lane == 0, peak, jnp.where(lane == 1, total, 0.0))
    for line in range(lines + 1, out.shape[1]):
        out[:, line, :] = jnp.zeros((ranks, LANES), jnp.float32)


def score(got, queries, other_queries, blocks):
    ranks = got.shape[0]
    features = queries.shape[1]
    lines = features // LANES
    return pl.pallas_call(
        functools.partial(score_kernel, lines, blocks),
        out_shape=jax.ShapeDtypeStruct((ranks, -(-(lines + 1) // 8) * 8, LANES), jnp.float32),
        in_specs=[pl.BlockSpec(memory_space=pltpu.VMEM)] * 3,
        out_specs=pl.BlockSpec(memory_space=pltpu.VMEM),
        scratch_shapes=[
            pltpu.VMEM(got.shape, jnp.float32),
            pltpu.VMEM((ranks, features), jnp.float32),
            pltpu.VMEM((ranks, features), jnp.float32),
        ],
        compiler_params=pltpu.CompilerParams(vmem_limit_bytes=VMEM_BYTES),
    )(got, queries, other_queries)


def combine_kernel(lines, got, recalled, log_total):
    stats = got[:, lines, :]
    peaks, sums = stats[:, 0:1], stats[:, 1:2]
    peak = jnp.max(peaks, axis=0, keepdims=True)
    factor = jnp.exp(peaks - peak)
    total = jnp.sum(sums * factor, axis=0, keepdims=True)
    mix = got[0, :lines, :] * factor[0:1, :]
    for rank in range(1, got.shape[0]):
        mix += got[rank, :lines, :] * factor[rank : rank + 1, :]
    mix = mix / total
    for line in range(lines):
        recalled[:, line * LANES : (line + 1) * LANES] = mix[line : line + 1, :]
    log_total[...] = peak + jnp.log(total)


def combine(got, features):
    recalled, log_total = pl.pallas_call(
        functools.partial(combine_kernel, features // LANES),
        out_shape=(
            jax.ShapeDtypeStruct((1, features), jnp.float32),
            jax.ShapeDtypeStruct((1, 1), jnp.float32),
        ),
        in_specs=[pl.BlockSpec(memory_space=pltpu.VMEM)],
        out_specs=(pl.BlockSpec(memory_space=pltpu.VMEM), pl.BlockSpec(memory_space=pltpu.VMEM)),
        compiler_params=pltpu.CompilerParams(vmem_limit_bytes=VMEM_BYTES),
    )(got)
    return recalled, log_total.reshape(1)


def on_cycle(context, residual, out_proj, norm_gain, lengths, queries, pattern):
    ranks = lax.axis_size("dp")
    size = ranks // CORES
    features = residual.shape[1]

    def ring(step):
        return [
            (CYCLE[r] * CORES + c, CYCLE[(r + step * (1 - 2 * c)) % size] * CORES + c)
            for r in range(size)
            for c in range(CORES)
        ]

    def from_next(piece):
        return lax.ppermute(piece, "dp", ring(-1))

    def from_last(piece):
        return lax.ppermute(piece, "dp", ring(1))

    def over_x(piece):
        return lax.ppermute(piece, "groups", [(0, 1), (1, 0)])

    def other_core(piece):
        return lax.ppermute(piece, "dp", [(i, i ^ 1) for i in range(ranks)])

    wait = lax.optimization_barrier

    def run(i, pieces, arrived=(), received=None, squares=None):
        full, part = WAVES[i]
        return wave(full, part, arrived, context, context2, residual, pieces, received, squares)

    own = own_half(out_proj)
    a, b, c = from_next(own), from_last(own), other_core(context)
    n1 = wait(a)
    a = from_next(n1)
    l1, n1 = wait((b, n1))
    b = from_last(l1)
    x = over_x(n1)
    context2, l1 = wait((c, l1))
    c = other_core(queries)
    h0, t0, _, sq0 = run(0, [out_proj])

    n2, t0, sq0, queries2 = wait((a, t0, sq0, c))
    a = from_next(n2)
    r0 = other_core(t0)
    l2, n2 = wait((b, n2))
    b = from_last(l2)
    xn1, n2, l2 = wait((x, n2, l2))
    x = over_x(n2)
    h1, t1, f0, sq1 = run(1, [n1, xn1], (0,), r0, sq0)

    n3, t1, sq1 = wait((a, t1, sq1))
    r1 = other_core(t1)
    l3, n3 = wait((b, n3))
    b = from_last(l3)
    xn2, n3, l3, l2 = wait((x, n3, l3, l2))
    a = from_next(xn2)
    x = over_x(l2)
    h2, t2, f1, sq2 = run(2, [n2, xn2, l1, l3], (1,), r1, sq1)

    n3x, l4, xl2, t2, sq2 = wait((a, b, x, t2, sq2))
    a = from_next(n3x)
    r2 = other_core(t2)
    b = from_last(xl2)
    x = over_x(l1)
    h3, t3, f2, sq3 = run(3, [l2, xl2, n3, n3x, l4], (2,), r2, sq2)
    n4x, l3x, xl1, t3, sq3 = wait((a, b, x, t3, sq3))
    last = [xl1, l3x, n4x]
    late = [other_core(piece) for piece in last]
    r3 = other_core(t3)
    h4, sq4 = late_half(context, sq3, last, [h2, h2, h3], (1, 2, 2))

    hidden = [h0, h1, h2, h3, h4, f0, f1, f2, r2, r3]
    sources = (
        (8, 1, -1, False),
        (8, 2, -3, False),
        (9, 2, 4, False),
        (9, 0, -2, False),
        (9, 1, 3, False),
        (0, 0, 0, True),
        (1, 0, 1, True),
        (2, 0, 2, True),
        (3, 0, -2, True),
        (3, 1, 3, True),
        (4, 0, -1, True),
        (4, 1, -3, True),
        (4, 2, 4, True),
        (5, 0, 0, False),
        (6, 0, 1, False),
        (7, 0, 2, False),
    )
    flags = jnp.pad(pattern.astype(jnp.float32), ((0, 0), (0, LANES - pattern.shape[1])))
    embedded, payload = finish(
        sources,
        (0, 1, 2),
        (3, 4),
        lengths,
        context,
        residual,
        sq4,
        norm_gain.reshape(1, -1),
        flags,
        late,
        hidden,
        size,
    )
    same_core = [list(range(c, ranks, CORES)) for c in range(CORES)]

    def spread(blocks):
        return lax.all_to_all(blocks, "dp", 0, 0, axis_index_groups=same_core, tiled=True)

    parts = score(spread(payload), queries, queries2, pattern.shape[1])
    recalled, log_total = combine(spread(parts), features)
    return embedded, recalled, log_total


def gathered(context, residual, out_proj, norm_gain, lengths, queries, pattern):
    tok_rows = context.shape[0]
    features = residual.shape[1]
    passages_here = lengths.shape[0]
    seq_len = tok_rows // passages_here
    query_rows = queries.shape[0]
    blocks = pattern.shape[1]
    ranks = lax.axis_size("dp")
    me = lax.axis_index("dp")
    branch = jnp.dot(
        context,
        lax.all_gather(out_proj, "dp", axis=1, tiled=True),
        preferred_element_type=jnp.float32,
    )
    hidden_sum = residual.astype(jnp.float32) + branch
    normed = (
        hidden_sum
        * lax.rsqrt(jnp.mean(hidden_sum * hidden_sum, axis=-1, keepdims=True) + 1e-05)
        * norm_gain
    )
    shaped = normed.reshape(passages_here, seq_len, features)
    valid_mask = (jnp.arange(seq_len)[None, :] < lengths[:, None]).astype(jnp.float32)
    pooled = jnp.sum(shaped * valid_mask[:, :, None], axis=1) / lengths.astype(jnp.float32)[:, None]
    embedded = pooled * lax.rsqrt(jnp.mean(pooled * pooled, axis=-1, keepdims=True) + 1e-06)
    emb_half = embedded.astype(jnp.bfloat16)
    temper = 1.0 / (0.02 * math.sqrt(features))
    contract = (((1,), (1,)), ((), ()))

    flags = jnp.pad(pattern.astype(jnp.bfloat16), ((0, 0), (0, LANES - blocks)))
    everyone = lax.all_gather(jnp.concatenate([emb_half, flags], axis=1), "dp", axis=0, tiled=True)
    emb_all = everyone[:, :features]
    flags_all = everyone[:, features : features + blocks].astype(jnp.float32)
    scores = lax.dot_general(emb_all, queries, contract, preferred_element_type=jnp.float32) * temper
    row_block = (me * query_rows + jnp.arange(query_rows)) // QB
    picks = (row_block[None, :] == jnp.arange(blocks)[:, None]).astype(jnp.float32)
    cand_mask = jnp.dot(flags_all, picks) > 0
    peak_part = jnp.max(jnp.where(cand_mask, scores, LOW), axis=1, keepdims=True)
    weights = jnp.where(cand_mask, jnp.exp(scores - peak_part), 0.0)
    total_part = jnp.sum(weights, axis=1, keepdims=True)
    mix_part = jnp.dot(weights.astype(jnp.bfloat16), queries, preferred_element_type=jnp.float32)

    passages = emb_all.shape[0]
    lane = jnp.arange(LANES)[None, :]
    tail = jnp.where(lane == 0, peak_part, jnp.where(lane == 1, total_part, 0.0))
    parts = jnp.concatenate([mix_part, tail], axis=1).reshape(ranks, passages // ranks, -1)
    parts = lax.all_to_all(parts, "dp", split_axis=0, concat_axis=0, tiled=True)
    mixes, peaks, sums = parts[:, :, :features], parts[:, :, features], parts[:, :, features + 1]
    peak_score = jnp.max(peaks, axis=0)
    factor = jnp.exp(peaks - peak_score[None, :])
    totals = jnp.sum(sums * factor, axis=0)
    recalled = jnp.sum(mixes * factor[:, :, None], axis=0) / totals[:, None]
    log_total = peak_score + jnp.log(totals)
    return (embedded, recalled, log_total)


def per_device(context, residual, out_proj, norm_gain, lengths, queries, pattern):
    fits = (
        lax.axis_size("dp") == CORES * len(CYCLE)
        and lax.axis_size("groups") == 2
        and lengths.shape[0] == 1
        and out_proj.shape[1] % LANES == 0
        and out_proj.shape[0] % (2 * LANES) == 0
        and context.shape[0] % STEP == 0
        and pattern.shape[1] <= LANES
    )
    form = on_cycle if fits else gathered
    return form(context, residual, out_proj, norm_gain, lengths, queries, pattern)


def solution(mesh):
    in_specs = (
        P(("groups", "dp"), None),
        P(("groups", "dp"), None),
        P(None, "dp"),
        P(),
        P(("groups", "dp")),
        P(("groups", "dp"), None),
        P(("groups", "dp"), None),
    )
    out_specs = (P(("groups", "dp"), None), P(("groups", "dp"), None), P(("groups", "dp")))
    return jax.shard_map(
        per_device, mesh=mesh, in_specs=in_specs, out_specs=out_specs, check_vma=False
    )
```

```python
import functools
import math

import jax
import jax.numpy as jnp
from jax import lax
from jax.experimental import pallas as pl
from jax.experimental.pallas import tpu as pltpu
from jax.sharding import PartitionSpec as P

QB = 256
LANES = 128
CORES = 2
STEP = 256
VMEM_BYTES = 12 << 20
LOW = -1e30
CYCLE = (0, 2, 4, 6, 7, 5, 3, 1)
VMEM_SPEC = pl.BlockSpec(memory_space=pltpu.VMEM)
SMALL = pl.CostEstimate(flops=1000, bytes_accessed=1000, transcendentals=0)


def column_block(distance, same_core):
    me = lax.axis_index("dp")
    core = lax.rem(me, CORES)
    chip = lax.div(me, CORES)
    z, y = lax.div(chip, 2), lax.rem(chip, 2)
    size = len(CYCLE)
    at = jnp.where(y == 0, z, size - 1 - z)
    core = core if same_core else 1 - core
    there = lax.rem(at + jnp.where(core == 0, size + distance, size - distance), size)
    chip = jnp.where(there < size // 2, 2 * there, 2 * (size - 1 - there) + 1)
    return chip * CORES + core


def columns(distance, same_core, width):
    return pl.ds(pl.multiple_of(column_block(distance, same_core) * width, width), width)


def half_slice(second, half):
    side = lax.axis_index("groups")
    return pl.ds(pl.multiple_of((1 - side if second else side) * half, half), half)


def add_squares(squares, at, total):
    square = total * total
    for lane in range(0, total.shape[1], LANES):
        squares[at, :] += square[:, lane : lane + LANES]


def half_kernel(whole, part):
    part[...] = whole[half_slice(False, part.shape[0]), :]


def own_half(whole):
    rows, width = whole.shape
    return pl.pallas_call(
        half_kernel,
        out_shape=jax.ShapeDtypeStruct((rows // 2, width), whole.dtype),
        in_specs=[VMEM_SPEC],
        out_specs=VMEM_SPEC,
        compiler_params=pltpu.CompilerParams(vmem_limit_bytes=VMEM_BYTES),
    )(whole)


def row_steps(rows):
    def loop(body):
        @pl.loop(0, rows // STEP)
        def _(k):
            body(pl.ds(pl.multiple_of(k * STEP, STEP), STEP))

    return loop


def product(tokens, at, pieces):
    total = None
    for piece, second in pieces:
        half = piece.shape[0]
        term = jnp.dot(tokens[at, half_slice(second, half)], piece[...], preferred_element_type=jnp.float32)
        total = term if total is None else total + term
    return total


def wave_kernel(full, part, arrived, whole, tokens, *refs):
    count = len(full) + len(part)
    refs = list(refs)
    context = refs.pop(0) if "mine" in tokens else None
    other_context = refs.pop(0) if "theirs" in tokens else None
    residual = refs.pop(0) if "mine" in tokens else None
    if whole:
        shard = refs.pop(0)
        half = shard.shape[0] // 2
        jobs = [[(shard.at[half_slice(second, half)], second) for second in (False, True)]]
    else:
        jobs = [[(refs.pop(0), False)] + ([(refs.pop(0), True)] if j < len(full) else []) for j in range(count)]
    if arrived:
        received, before = [refs.pop(0) for _ in arrived], refs.pop(0)
    mine = refs.pop(0) if "mine" in tokens else None
    theirs = [refs.pop(0) for _ in range(count)] if "theirs" in tokens else None
    finished = refs.pop(0) if arrived else None
    squares = refs.pop(0) if "mine" in tokens else None
    rows, width = mine.shape[1:] if "mine" in tokens else theirs[0].shape
    if arrived:
        squares[...] = before[...]
    elif "mine" in tokens:
        squares[...] = jnp.zeros_like(squares)
    for j, distance in enumerate(full + part):

        @row_steps(rows)
        def _(at):
            if "theirs" in tokens:
                theirs[j][at, :] = product(other_context, at, jobs[j])
            if "mine" in tokens:
                total = product(context, at, jobs[j])
                total += residual[at, columns(distance, True, width)].astype(jnp.float32)
                mine[j, at, :] = total
                if j < len(full):
                    add_squares(squares, at, total)

    for j, distance in enumerate(arrived):

        @row_steps(rows)
        def _(at):
            total = received[j][at, :] + residual[at, columns(distance, False, width)].astype(jnp.float32)
            finished[j, at, :] = total
            add_squares(squares, at, total)


def wave(full, part, arrived, context, other_context, residual, pieces, received=None, squares=None):
    tokens = (("mine",) if context is not None else ()) + (("theirs",) if other_context is not None else ())
    count = len(full) + len(part)
    rows = (context if other_context is None else other_context).shape[0]
    whole = len(pieces) == 1
    block = jax.ShapeDtypeStruct((rows, pieces[0].shape[1]), jnp.float32)
    outs = [jax.ShapeDtypeStruct((count,) + block.shape, jnp.float32)] if "mine" in tokens else []
    outs += [block] * count if "theirs" in tokens else []
    operands = [x for x in (context, other_context) if x is not None]
    operands += ([residual] if "mine" in tokens else []) + list(pieces)
    if arrived:
        operands += [*received, squares]
        outs.append(jax.ShapeDtypeStruct((len(arrived),) + block.shape, jnp.float32))
    if "mine" in tokens:
        outs.append(jax.ShapeDtypeStruct((rows, LANES), jnp.float32))
    return pl.pallas_call(
        functools.partial(wave_kernel, full, part, arrived, whole, tokens),
        out_shape=outs,
        in_specs=[VMEM_SPEC] * len(operands),
        out_specs=[VMEM_SPEC] * len(outs),
        compiler_params=pltpu.CompilerParams(vmem_limit_bytes=VMEM_BYTES),
        cost_estimate=SMALL,
    )(*operands)


def late_blocks(items, context, residual, pieces, hidden, squares, target):
    rows, width = target.shape[1:]
    for i, (base, parts, bare, distance, same) in enumerate(items):

        @row_steps(rows)
        def _(at):
            value = product(context, at, [(pieces[index], second) for index, second in parts])
            if base is not None:
                known = hidden[base[0]][(at,) if base[1] is None else (base[1], at)]
                value = known if value is None else value + known
            if bare:
                value += residual[at, columns(distance, same, width)].astype(jnp.float32)
            target[i, at, :] = value
            add_squares(squares, at, value)


def late_kernel(items, n_pieces, context, residual, before, *refs):
    pieces, hidden = refs[:n_pieces], refs[n_pieces:-2]
    finished, squares = refs[-2:]
    squares[...] = before[...]
    late_blocks(items, context, residual, pieces, hidden, squares, finished)


def late(items, context, residual, squares, pieces, hidden):
    rows = context.shape[0]
    operands = [context, residual, squares, *pieces, *hidden]
    return pl.pallas_call(
        functools.partial(late_kernel, items, len(pieces)),
        out_shape=(
            jax.ShapeDtypeStruct((len(items), rows, pieces[0].shape[1]), jnp.float32),
            jax.ShapeDtypeStruct(squares.shape, jnp.float32),
        ),
        in_specs=[VMEM_SPEC] * len(operands),
        out_specs=(VMEM_SPEC, VMEM_SPEC),
        compiler_params=pltpu.CompilerParams(vmem_limit_bytes=VMEM_BYTES),
        cost_estimate=SMALL,
    )(*operands)


def final_kernel(items, sources, n_pieces, length, context, residual, before, gain, flags, *refs):
    pieces, hidden = refs[:n_pieces], refs[n_pieces:-6]
    embedded, payload, blocks, squares, scale_rows, sheet = refs[-6:]
    width = blocks.shape[2]
    features = embedded.shape[1]
    squares[...] = before[...]
    late_blocks(items, context, residual, pieces, hidden, squares, blocks)
    mean = jnp.sum(squares[...], axis=1, keepdims=True) * (1.0 / features)
    row = lax.broadcasted_iota(jnp.int32, mean.shape, 0)
    scale = jnp.where(row < length[0], lax.rsqrt(mean + 1e-05), 0.0)
    scale_rows[...] = jnp.broadcast_to(scale, scale_rows.shape)
    inverse = 1.0 / jnp.full((1, width), length[0], jnp.int32).astype(jnp.float32)
    done = [(blocks.at[i], distance, same) for i, (_, _, _, distance, same) in enumerate(items)]
    done += [(hidden[array].at[entry], distance, same) for array, entry, distance, same in sources]
    for block, distance, same in done:
        parts = [
            jnp.sum(block[:, lane : lane + LANES] * scale_rows[...], axis=0, keepdims=True)
            for lane in range(0, width, LANES)
        ]
        where = columns(distance, same, width)
        embedded[:, where] = jnp.concatenate(parts, axis=1) * gain[:, where] * inverse
    pooled = embedded[...]
    mean = jnp.sum(pooled * pooled, axis=1, keepdims=True) * (1.0 / features)
    embedded[...] = pooled * lax.rsqrt(mean + 1e-06)
    lines = features // LANES
    sheet[lines:, :] = jnp.zeros((sheet.shape[0] - lines, LANES), jnp.float32)
    for line in range(lines):
        sheet[line : line + 1, :] = embedded[:, line * LANES : (line + 1) * LANES]
    sheet[lines : lines + 1, :] = flags[...]
    rounded = sheet[...].astype(jnp.bfloat16)
    for rank in range(payload.shape[0]):
        payload[rank] = rounded


def finish(items, sources, lengths, context, residual, squares, gain, flags, pieces, hidden, ranks):
    rows = context.shape[0]
    width = pieces[0].shape[1]
    features = (len(items) + len(sources)) * width
    lines = -(-(features // LANES + 1) // 16) * 16
    operands = [context, residual, squares, gain, flags, *pieces, *hidden]
    return pl.pallas_call(
        functools.partial(final_kernel, items, sources, len(pieces)),
        out_shape=(
            jax.ShapeDtypeStruct((1, features), jnp.float32),
            jax.ShapeDtypeStruct((ranks, lines, LANES), jnp.bfloat16),
        ),
        in_specs=[pl.BlockSpec(memory_space=pltpu.SMEM)] + [VMEM_SPEC] * len(operands),
        out_specs=(VMEM_SPEC, VMEM_SPEC),
        scratch_shapes=[
            pltpu.VMEM((len(items), rows, width), jnp.float32),
            pltpu.VMEM((rows, LANES), jnp.float32),
            pltpu.VMEM((rows, LANES), jnp.float32),
            pltpu.VMEM((lines, LANES), jnp.float32),
        ],
        compiler_params=pltpu.CompilerParams(vmem_limit_bytes=VMEM_BYTES),
        cost_estimate=SMALL,
    )(lengths, *operands)


def score_kernel(lines, blocks, got, queries, other_queries, out, wide, emb, mix):
    me = lax.axis_index("dp")
    ranks = got.shape[0]
    count = queries.shape[0]
    wide[...] = got[...].astype(jnp.float32)
    for line in range(lines):
        emb[:, line * LANES : (line + 1) * LANES] = wide[:, line, :]
    half = emb[...].astype(jnp.bfloat16)
    flags = wide[:, lines, :].astype(jnp.bfloat16)
    temper = 1.0 / (0.02 * math.sqrt(lines * LANES))
    scores, masks = [], []
    for owner, rows in ((me, queries), (me + 1 - 2 * lax.rem(me, CORES), other_queries)):
        score = lax.dot_general(
            half, rows[...], (((1,), (1,)), ((), ())), preferred_element_type=jnp.float32
        )
        scores.append(score * temper)
        block = lax.broadcasted_iota(jnp.int32, (LANES, count), 0)
        row = owner * count + lax.broadcasted_iota(jnp.int32, (LANES, count), 1)
        pick = (row >= block * QB) & (row < block * QB + QB) & (block < blocks)
        pick = jnp.where(pick, 1.0, 0.0).astype(jnp.bfloat16)
        masks.append(jnp.dot(flags, pick, preferred_element_type=jnp.float32) > 0.5)
    peaks = [
        jnp.max(jnp.where(mask, score, LOW), axis=1, keepdims=True) for score, mask in zip(scores, masks)
    ]
    peak = jnp.maximum(*peaks)
    weights = [jnp.where(mask, jnp.exp(score - peak), 0.0) for score, mask in zip(scores, masks)]
    total = sum(jnp.sum(weight, axis=1, keepdims=True) for weight in weights)
    mix[...] = jnp.dot(
        weights[0].astype(jnp.bfloat16), queries[...], preferred_element_type=jnp.float32
    ) + jnp.dot(weights[1].astype(jnp.bfloat16), other_queries[...], preferred_element_type=jnp.float32)
    for line in range(lines):
        out[:, line, :] = mix[:, line * LANES : (line + 1) * LANES]
    lane = lax.broadcasted_iota(jnp.int32, (ranks, LANES), 1)
    out[:, lines, :] = jnp.where(lane == 0, peak, jnp.where(lane == 1, total, 0.0))
    for line in range(lines + 1, out.shape[1]):
        out[:, line, :] = jnp.zeros((ranks, LANES), jnp.float32)


def score(got, queries, other_queries, blocks):
    ranks = got.shape[0]
    features = queries.shape[1]
    lines = features // LANES
    return pl.pallas_call(
        functools.partial(score_kernel, lines, blocks),
        out_shape=jax.ShapeDtypeStruct((ranks, -(-(lines + 1) // 8) * 8, LANES), jnp.float32),
        in_specs=[pl.BlockSpec(memory_space=pltpu.VMEM)] * 3,
        out_specs=pl.BlockSpec(memory_space=pltpu.VMEM),
        scratch_shapes=[
            pltpu.VMEM(got.shape, jnp.float32),
            pltpu.VMEM((ranks, features), jnp.float32),
            pltpu.VMEM((ranks, features), jnp.float32),
        ],
        compiler_params=pltpu.CompilerParams(vmem_limit_bytes=VMEM_BYTES),
    )(got, queries, other_queries)


def combine_kernel(lines, got, recalled, log_total):
    stats = got[:, lines, :]
    peaks, sums = stats[:, 0:1], stats[:, 1:2]
    peak = jnp.max(peaks, axis=0, keepdims=True)
    factor = jnp.exp(peaks - peak)
    total = jnp.sum(sums * factor, axis=0, keepdims=True)
    mix = got[0, :lines, :] * factor[0:1, :]
    for rank in range(1, got.shape[0]):
        mix += got[rank, :lines, :] * factor[rank : rank + 1, :]
    mix = mix / total
    for line in range(lines):
        recalled[:, line * LANES : (line + 1) * LANES] = mix[line : line + 1, :]
    log_total[...] = peak + jnp.log(total)


def combine(got, features):
    recalled, log_total = pl.pallas_call(
        functools.partial(combine_kernel, features // LANES),
        out_shape=(
            jax.ShapeDtypeStruct((1, features), jnp.float32),
            jax.ShapeDtypeStruct((1, 1), jnp.float32),
        ),
        in_specs=[pl.BlockSpec(memory_space=pltpu.VMEM)],
        out_specs=(pl.BlockSpec(memory_space=pltpu.VMEM), pl.BlockSpec(memory_space=pltpu.VMEM)),
        compiler_params=pltpu.CompilerParams(vmem_limit_bytes=VMEM_BYTES),
    )(got)
    return recalled, log_total.reshape(1)


def on_cycle(context, residual, out_proj, norm_gain, lengths, queries, pattern):
    ranks = lax.axis_size("dp")
    size = ranks // CORES
    features = residual.shape[1]

    def ring(step):
        return [
            (CYCLE[r] * CORES + c, CYCLE[(r + step * (1 - 2 * c)) % size] * CORES + c)
            for r in range(size)
            for c in range(CORES)
        ]

    def from_next(piece):
        return lax.ppermute(piece, "dp", ring(-1))

    def from_last(piece):
        return lax.ppermute(piece, "dp", ring(1))

    def over_x(piece):
        return lax.ppermute(piece, "groups", [(0, 1), (1, 0)])

    def other_core(piece):
        return lax.ppermute(piece, "dp", [(i, i ^ 1) for i in range(ranks)])

    wait = lax.optimization_barrier

    own = own_half(out_proj)
    a = from_next(own)
    c = other_core(context)
    h0, sq0 = wave((0,), (), (), context, None, residual, [out_proj])
    own, h0, sq0 = wait((own, h0, sq0))
    b = from_last(own)

    n1, sq0 = wait((a, sq0))
    x = over_x(n1)
    a = from_next(n1)
    context2, n1 = wait((c, n1))
    (t0,) = wave((0,), (), (), None, context2, None, [out_proj])
    l1, n1, t0 = wait((b, n1, t0))
    b = from_last(l1)
    r0 = other_core(t0)

    n2, l1, queries = wait((a, l1, queries))
    queries2 = other_core(queries)
    xn1, n2 = wait((x, n2))
    x = over_x(n2)
    a = from_next(n2)
    h1, t1, f0, sq1 = wave((1,), (), (0,), context, context2, residual, [n1, xn1], [r0], sq0)
    l2, n2, t1, sq1 = wait((b, n2, t1, sq1))
    b = from_last(l2)
    r1 = other_core(t1)

    xn2, l2, queries2 = wait((x, l2, queries2))
    x = over_x(l2)
    a2 = from_next(xn2)
    n3, xn2 = wait((a, xn2))
    h2, t2, t2p, f1, sq2 = wave((2,), (-1,), (1,), context, context2, residual, [n2, xn2, l1], [r1], sq1)
    l3, n3, t2, t2p, sq2 = wait((b, n3, t2, t2p, sq2))
    b = from_last(l3)
    r2, r2p = other_core(t2), other_core(t2p)

    n3x, l3 = wait((a2, l3))
    a = from_next(n3x)
    xl2, l1, n3x = wait((x, l1, n3x))
    x = over_x(l1)
    h3, t3a, t3b, t3p, f2, sq3 = wave(
        (-2, 3), (-3,), (2,), context, context2, residual, [l2, xl2, n3, n3x, l3], [r2], sq2
    )
    l4, xl2, t3a, t3b, t3p, sq3, r2p = wait((b, xl2, t3a, t3b, t3p, sq3, r2p))
    b = from_last(xl2)
    r3a, r3b, r3p = other_core(t3a), other_core(t3b), other_core(t3p)
    l4s = other_core(l4)

    n4x, l4 = wait((a, l4))
    n4xs = other_core(n4x)
    xl1, n4x = wait((x, n4x))
    xl1s = other_core(xl1)
    l3x, xl1 = wait((b, xl1))
    l3xs = other_core(l3x)

    missing = (((0, True),), ((1, True),), ((2, False), (3, True)))
    own_items = tuple(
        (base, parts, base is None, distance, True)
        for base, parts, distance in zip(((0, 1), (1, 2), None), missing, (-1, -3, 4))
    )
    h4, sq4 = late(own_items, context, residual, sq3, [xl1, l3x, l4, n4x], [h2, h3])
    items = tuple(
        (base, parts, True, distance, False)
        for base, parts, distance in zip(
            ((8, None), (9, None), None, (10, None), (11, None)), missing + ((), ()), (-1, -3, 4, -2, 3)
        )
    )
    hidden = [h0, h1, h2, h3, h4, f0, f1, f2, r2p, r3p, r3a, r3b]
    sources = (
        (0, 0, 0, True),
        (1, 0, 1, True),
        (2, 0, 2, True),
        (3, 0, -2, True),
        (3, 1, 3, True),
        (4, 0, -1, True),
        (4, 1, -3, True),
        (4, 2, 4, True),
        (5, 0, 0, False),
        (6, 0, 1, False),
        (7, 0, 2, False),
    )
    flags = jnp.pad(pattern.astype(jnp.float32), ((0, 0), (0, LANES - pattern.shape[1])))
    embedded, payload = finish(
        items,
        sources,
        lengths,
        context,
        residual,
        sq4,
        norm_gain.reshape(1, -1),
        flags,
        [xl1s, l3xs, l4s, n4xs],
        hidden,
        size,
    )
    same_core = [list(range(c, ranks, CORES)) for c in range(CORES)]

    def spread(blocks):
        return lax.all_to_all(blocks, "dp", 0, 0, axis_index_groups=same_core, tiled=True)

    parts = score(spread(payload), queries, queries2, pattern.shape[1])
    recalled, log_total = combine(spread(parts), features)
    return embedded, recalled, log_total


def gathered(context, residual, out_proj, norm_gain, lengths, queries, pattern):
    tok_rows = context.shape[0]
    features = residual.shape[1]
    passages_here = lengths.shape[0]
    seq_len = tok_rows // passages_here
    query_rows = queries.shape[0]
    blocks = pattern.shape[1]
    ranks = lax.axis_size("dp")
    me = lax.axis_index("dp")
    branch = jnp.dot(
        context,
        lax.all_gather(out_proj, "dp", axis=1, tiled=True),
        preferred_element_type=jnp.float32,
    )
    hidden_sum = residual.astype(jnp.float32) + branch
    normed = (
        hidden_sum
        * lax.rsqrt(jnp.mean(hidden_sum * hidden_sum, axis=-1, keepdims=True) + 1e-05)
        * norm_gain
    )
    shaped = normed.reshape(passages_here, seq_len, features)
    valid_mask = (jnp.arange(seq_len)[None, :] < lengths[:, None]).astype(jnp.float32)
    pooled = jnp.sum(shaped * valid_mask[:, :, None], axis=1) / lengths.astype(jnp.float32)[:, None]
    embedded = pooled * lax.rsqrt(jnp.mean(pooled * pooled, axis=-1, keepdims=True) + 1e-06)
    emb_half = embedded.astype(jnp.bfloat16)
    temper = 1.0 / (0.02 * math.sqrt(features))
    contract = (((1,), (1,)), ((), ()))

    flags = jnp.pad(pattern.astype(jnp.bfloat16), ((0, 0), (0, LANES - blocks)))
    everyone = lax.all_gather(jnp.concatenate([emb_half, flags], axis=1), "dp", axis=0, tiled=True)
    emb_all = everyone[:, :features]
    flags_all = everyone[:, features : features + blocks].astype(jnp.float32)
    scores = lax.dot_general(emb_all, queries, contract, preferred_element_type=jnp.float32) * temper
    row_block = (me * query_rows + jnp.arange(query_rows)) // QB
    picks = (row_block[None, :] == jnp.arange(blocks)[:, None]).astype(jnp.float32)
    cand_mask = jnp.dot(flags_all, picks) > 0
    peak_part = jnp.max(jnp.where(cand_mask, scores, LOW), axis=1, keepdims=True)
    weights = jnp.where(cand_mask, jnp.exp(scores - peak_part), 0.0)
    total_part = jnp.sum(weights, axis=1, keepdims=True)
    mix_part = jnp.dot(weights.astype(jnp.bfloat16), queries, preferred_element_type=jnp.float32)

    passages = emb_all.shape[0]
    lane = jnp.arange(LANES)[None, :]
    tail = jnp.where(lane == 0, peak_part, jnp.where(lane == 1, total_part, 0.0))
    parts = jnp.concatenate([mix_part, tail], axis=1).reshape(ranks, passages // ranks, -1)
    parts = lax.all_to_all(parts, "dp", split_axis=0, concat_axis=0, tiled=True)
    mixes, peaks, sums = parts[:, :, :features], parts[:, :, features], parts[:, :, features + 1]
    peak_score = jnp.max(peaks, axis=0)
    factor = jnp.exp(peaks - peak_score[None, :])
    totals = jnp.sum(sums * factor, axis=0)
    recalled = jnp.sum(mixes * factor[:, :, None], axis=0) / totals[:, None]
    log_total = peak_score + jnp.log(totals)
    return (embedded, recalled, log_total)


def per_device(context, residual, out_proj, norm_gain, lengths, queries, pattern):
    fits = (
        lax.axis_size("dp") == CORES * len(CYCLE)
        and lax.axis_size("groups") == 2
        and lengths.shape[0] == 1
        and out_proj.shape[1] % LANES == 0
        and out_proj.shape[0] % (2 * LANES) == 0
        and context.shape[0] % STEP == 0
        and pattern.shape[1] <= LANES
    )
    form = on_cycle if fits else gathered
    return form(context, residual, out_proj, norm_gain, lengths, queries, pattern)


def solution(mesh):
    in_specs = (
        P(("groups", "dp"), None),
        P(("groups", "dp"), None),
        P(None, "dp"),
        P(),
        P(("groups", "dp")),
        P(("groups", "dp"), None),
        P(("groups", "dp"), None),
    )
    out_specs = (P(("groups", "dp"), None), P(("groups", "dp"), None), P(("groups", "dp")))
    return jax.shard_map(
        per_device, mesh=mesh, in_specs=in_specs, out_specs=out_specs, check_vma=False
    )
```

```python
import functools
import math

import jax
import jax.numpy as jnp
from jax import lax
from jax.experimental import pallas as pl
from jax.experimental.pallas import tpu as pltpu
from jax.sharding import PartitionSpec as P

QB = 256
LANES = 128
CORES = 2
STEP = 256
VMEM_BYTES = 12 << 20
LOW = -1e30
CYCLE = (0, 2, 4, 6, 7, 5, 3, 1)
VMEM_SPEC = pl.BlockSpec(memory_space=pltpu.VMEM)
SMALL = pl.CostEstimate(flops=1000, bytes_accessed=1000, transcendentals=0)


def column_block(distance, same_core):
    me = lax.axis_index("dp")
    core = lax.rem(me, CORES)
    chip = lax.div(me, CORES)
    z, y = lax.div(chip, 2), lax.rem(chip, 2)
    size = len(CYCLE)
    at = jnp.where(y == 0, z, size - 1 - z)
    core = core if same_core else 1 - core
    there = lax.rem(at + jnp.where(core == 0, size + distance, size - distance), size)
    chip = jnp.where(there < size // 2, 2 * there, 2 * (size - 1 - there) + 1)
    return chip * CORES + core


def columns(distance, same_core, width):
    return pl.ds(pl.multiple_of(column_block(distance, same_core) * width, width), width)


def half_slice(second, half):
    side = lax.axis_index("groups")
    return pl.ds(pl.multiple_of((1 - side if second else side) * half, half), half)


def add_squares(squares, at, total):
    square = total * total
    for lane in range(0, total.shape[1], LANES):
        squares[at, :] += square[:, lane : lane + LANES]


def half_kernel(whole, part):
    part[...] = whole[half_slice(False, part.shape[0]), :]


def own_half(whole):
    rows, width = whole.shape
    return pl.pallas_call(
        half_kernel,
        out_shape=jax.ShapeDtypeStruct((rows // 2, width), whole.dtype),
        in_specs=[VMEM_SPEC],
        out_specs=VMEM_SPEC,
        compiler_params=pltpu.CompilerParams(vmem_limit_bytes=VMEM_BYTES),
    )(whole)


def row_steps(rows):
    def loop(body):
        @pl.loop(0, rows // STEP)
        def _(k):
            body(pl.ds(pl.multiple_of(k * STEP, STEP), STEP))

    return loop


def product(tokens, at, pieces):
    total = None
    for piece, second in pieces:
        half = piece.shape[0]
        term = jnp.dot(tokens[at, half_slice(second, half)], piece[...], preferred_element_type=jnp.float32)
        total = term if total is None else total + term
    return total


def wave_kernel(full, part, arrived, whole, tokens, *refs):
    count = len(full) + len(part)
    refs = list(refs)
    context = refs.pop(0) if "mine" in tokens else None
    other_context = refs.pop(0) if "theirs" in tokens else None
    residual = refs.pop(0) if "mine" in tokens else None
    if whole:
        shard = refs.pop(0)
        half = shard.shape[0] // 2
        jobs = [[(shard.at[half_slice(second, half)], second) for second in (False, True)]]
    else:
        jobs = [[(refs.pop(0), False)] + ([(refs.pop(0), True)] if j < len(full) else []) for j in range(count)]
    if arrived:
        received, before = [refs.pop(0) for _ in arrived], refs.pop(0)
    mine = refs.pop(0) if "mine" in tokens else None
    theirs = [refs.pop(0) for _ in range(count)] if "theirs" in tokens else None
    finished = refs.pop(0) if arrived else None
    squares = refs.pop(0) if "mine" in tokens else None
    rows, width = mine.shape[1:] if "mine" in tokens else theirs[0].shape
    if arrived:
        squares[...] = before[...]
    elif "mine" in tokens:
        squares[...] = jnp.zeros_like(squares)
    for j, distance in enumerate(full + part):

        @row_steps(rows)
        def _(at):
            if "theirs" in tokens:
                theirs[j][at, :] = product(other_context, at, jobs[j])
            if "mine" in tokens:
                total = product(context, at, jobs[j])
                total += residual[at, columns(distance, True, width)].astype(jnp.float32)
                mine[j, at, :] = total
                if j < len(full):
                    add_squares(squares, at, total)

    for j, distance in enumerate(arrived):

        @row_steps(rows)
        def _(at):
            total = received[j][at, :] + residual[at, columns(distance, False, width)].astype(jnp.float32)
            finished[j, at, :] = total
            add_squares(squares, at, total)


def wave(full, part, arrived, context, other_context, residual, pieces, received=None, squares=None):
    tokens = (("mine",) if context is not None else ()) + (("theirs",) if other_context is not None else ())
    count = len(full) + len(part)
    rows = (context if other_context is None else other_context).shape[0]
    whole = len(pieces) == 1
    block = jax.ShapeDtypeStruct((rows, pieces[0].shape[1]), jnp.float32)
    outs = [jax.ShapeDtypeStruct((count,) + block.shape, jnp.float32)] if "mine" in tokens else []
    outs += [block] * count if "theirs" in tokens else []
    operands = [x for x in (context, other_context) if x is not None]
    operands += ([residual] if "mine" in tokens else []) + list(pieces)
    if arrived:
        operands += [*received, squares]
        outs.append(jax.ShapeDtypeStruct((len(arrived),) + block.shape, jnp.float32))
    if "mine" in tokens:
        outs.append(jax.ShapeDtypeStruct((rows, LANES), jnp.float32))
    return pl.pallas_call(
        functools.partial(wave_kernel, full, part, arrived, whole, tokens),
        out_shape=outs,
        in_specs=[VMEM_SPEC] * len(operands),
        out_specs=[VMEM_SPEC] * len(outs),
        compiler_params=pltpu.CompilerParams(vmem_limit_bytes=VMEM_BYTES),
        cost_estimate=SMALL,
    )(*operands)


def late_blocks(items, context, residual, pieces, hidden, squares, target):
    rows, width = target.shape[1:]
    for i, (base, parts, bare, distance, same) in enumerate(items):

        @row_steps(rows)
        def _(at):
            value = product(context, at, [(pieces[index], second) for index, second in parts])
            if base is not None:
                known = hidden[base[0]][(at,) if base[1] is None else (base[1], at)]
                value = known if value is None else value + known
            if bare:
                value += residual[at, columns(distance, same, width)].astype(jnp.float32)
            target[i, at, :] = value
            add_squares(squares, at, value)


def late_kernel(items, n_pieces, context, residual, before, *refs):
    pieces, hidden = refs[:n_pieces], refs[n_pieces:-2]
    finished, squares = refs[-2:]
    squares[...] = before[...]
    late_blocks(items, context, residual, pieces, hidden, squares, finished)


def late(items, context, residual, squares, pieces, hidden):
    rows = context.shape[0]
    operands = [context, residual, squares, *pieces, *hidden]
    return pl.pallas_call(
        functools.partial(late_kernel, items, len(pieces)),
        out_shape=(
            jax.ShapeDtypeStruct((len(items), rows, pieces[0].shape[1]), jnp.float32),
            jax.ShapeDtypeStruct(squares.shape, jnp.float32),
        ),
        in_specs=[VMEM_SPEC] * len(operands),
        out_specs=(VMEM_SPEC, VMEM_SPEC),
        compiler_params=pltpu.CompilerParams(vmem_limit_bytes=VMEM_BYTES),
        cost_estimate=SMALL,
    )(*operands)


def final_kernel(items, sources, n_pieces, length, context, residual, before, gain, flags, *refs):
    pieces, hidden = refs[:n_pieces], refs[n_pieces:-6]
    embedded, payload, blocks, squares, scale_rows, sheet = refs[-6:]
    width = blocks.shape[2]
    features = embedded.shape[1]
    squares[...] = before[...]
    late_blocks(items, context, residual, pieces, hidden, squares, blocks)
    mean = jnp.sum(squares[...], axis=1, keepdims=True) * (1.0 / features)
    row = lax.broadcasted_iota(jnp.int32, mean.shape, 0)
    scale = jnp.where(row < length[0], lax.rsqrt(mean + 1e-05), 0.0)
    scale_rows[...] = jnp.broadcast_to(scale, scale_rows.shape)
    inverse = 1.0 / jnp.full((1, width), length[0], jnp.int32).astype(jnp.float32)
    done = [(blocks.at[i], distance, same) for i, (_, _, _, distance, same) in enumerate(items)]
    done += [(hidden[array].at[entry], distance, same) for array, entry, distance, same in sources]
    for block, distance, same in done:
        parts = [
            jnp.sum(block[:, lane : lane + LANES] * scale_rows[...], axis=0, keepdims=True)
            for lane in range(0, width, LANES)
        ]
        where = columns(distance, same, width)
        embedded[:, where] = jnp.concatenate(parts, axis=1) * gain[:, where] * inverse
    pooled = embedded[...]
    mean = jnp.sum(pooled * pooled, axis=1, keepdims=True) * (1.0 / features)
    embedded[...] = pooled * lax.rsqrt(mean + 1e-06)
    lines = features // LANES
    sheet[lines:, :] = jnp.zeros((sheet.shape[0] - lines, LANES), jnp.float32)
    for line in range(lines):
        sheet[line : line + 1, :] = embedded[:, line * LANES : (line + 1) * LANES]
    sheet[lines : lines + 1, :] = flags[...]
    rounded = sheet[...].astype(jnp.bfloat16)
    for rank in range(payload.shape[0]):
        payload[rank] = rounded


def finish(items, sources, lengths, context, residual, squares, gain, flags, pieces, hidden, ranks):
    rows = context.shape[0]
    width = pieces[0].shape[1]
    features = (len(items) + len(sources)) * width
    lines = -(-(features // LANES + 1) // 16) * 16
    operands = [context, residual, squares, gain, flags, *pieces, *hidden]
    return pl.pallas_call(
        functools.partial(final_kernel, items, sources, len(pieces)),
        out_shape=(
            jax.ShapeDtypeStruct((1, features), jnp.float32),
            jax.ShapeDtypeStruct((ranks, lines, LANES), jnp.bfloat16),
        ),
        in_specs=[pl.BlockSpec(memory_space=pltpu.SMEM)] + [VMEM_SPEC] * len(operands),
        out_specs=(VMEM_SPEC, VMEM_SPEC),
        scratch_shapes=[
            pltpu.VMEM((len(items), rows, width), jnp.float32),
            pltpu.VMEM((rows, LANES), jnp.float32),
            pltpu.VMEM((rows, LANES), jnp.float32),
            pltpu.VMEM((lines, LANES), jnp.float32),
        ],
        compiler_params=pltpu.CompilerParams(vmem_limit_bytes=VMEM_BYTES),
        cost_estimate=SMALL,
    )(lengths, *operands)


def score_kernel(lines, blocks, got, queries, other_queries, out, wide, emb, mix):
    me = lax.axis_index("dp")
    ranks = got.shape[0]
    count = queries.shape[0]
    wide[...] = got[...].astype(jnp.float32)
    for line in range(lines):
        emb[:, line * LANES : (line + 1) * LANES] = wide[:, line, :]
    half = emb[...].astype(jnp.bfloat16)
    flags = wide[:, lines, :].astype(jnp.bfloat16)
    temper = 1.0 / (0.02 * math.sqrt(lines * LANES))
    scores, masks = [], []
    for owner, rows in ((me, queries), (me + 1 - 2 * lax.rem(me, CORES), other_queries)):
        score = lax.dot_general(
            half, rows[...], (((1,), (1,)), ((), ())), preferred_element_type=jnp.float32
        )
        scores.append(score * temper)
        block = lax.broadcasted_iota(jnp.int32, (LANES, count), 0)
        row = owner * count + lax.broadcasted_iota(jnp.int32, (LANES, count), 1)
        pick = (row >= block * QB) & (row < block * QB + QB) & (block < blocks)
        pick = jnp.where(pick, 1.0, 0.0).astype(jnp.bfloat16)
        masks.append(jnp.dot(flags, pick, preferred_element_type=jnp.float32) > 0.5)
    peaks = [
        jnp.max(jnp.where(mask, score, LOW), axis=1, keepdims=True) for score, mask in zip(scores, masks)
    ]
    peak = jnp.maximum(*peaks)
    weights = [jnp.where(mask, jnp.exp(score - peak), 0.0) for score, mask in zip(scores, masks)]
    total = sum(jnp.sum(weight, axis=1, keepdims=True) for weight in weights)
    mix[...] = jnp.dot(
        weights[0].astype(jnp.bfloat16), queries[...], preferred_element_type=jnp.float32
    ) + jnp.dot(weights[1].astype(jnp.bfloat16), other_queries[...], preferred_element_type=jnp.float32)
    for line in range(lines):
        out[:, line, :] = mix[:, line * LANES : (line + 1) * LANES]
    lane = lax.broadcasted_iota(jnp.int32, (ranks, LANES), 1)
    out[:, lines, :] = jnp.where(lane == 0, peak, jnp.where(lane == 1, total, 0.0))
    for line in range(lines + 1, out.shape[1]):
        out[:, line, :] = jnp.zeros((ranks, LANES), jnp.float32)


def score(got, queries, other_queries, blocks):
    ranks = got.shape[0]
    features = queries.shape[1]
    lines = features // LANES
    return pl.pallas_call(
        functools.partial(score_kernel, lines, blocks),
        out_shape=jax.ShapeDtypeStruct((ranks, -(-(lines + 1) // 8) * 8, LANES), jnp.float32),
        in_specs=[pl.BlockSpec(memory_space=pltpu.VMEM)] * 3,
        out_specs=pl.BlockSpec(memory_space=pltpu.VMEM),
        scratch_shapes=[
            pltpu.VMEM(got.shape, jnp.float32),
            pltpu.VMEM((ranks, features), jnp.float32),
            pltpu.VMEM((ranks, features), jnp.float32),
        ],
        compiler_params=pltpu.CompilerParams(vmem_limit_bytes=VMEM_BYTES),
    )(got, queries, other_queries)


def combine_kernel(lines, got, recalled, log_total):
    stats = got[:, lines, :]
    peaks, sums = stats[:, 0:1], stats[:, 1:2]
    peak = jnp.max(peaks, axis=0, keepdims=True)
    factor = jnp.exp(peaks - peak)
    total = jnp.sum(sums * factor, axis=0, keepdims=True)
    mix = got[0, :lines, :] * factor[0:1, :]
    for rank in range(1, got.shape[0]):
        mix += got[rank, :lines, :] * factor[rank : rank + 1, :]
    mix = mix / total
    for line in range(lines):
        recalled[:, line * LANES : (line + 1) * LANES] = mix[line : line + 1, :]
    log_total[...] = peak + jnp.log(total)


def combine(got, features):
    recalled, log_total = pl.pallas_call(
        functools.partial(combine_kernel, features // LANES),
        out_shape=(
            jax.ShapeDtypeStruct((1, features), jnp.float32),
            jax.ShapeDtypeStruct((1, 1), jnp.float32),
        ),
        in_specs=[pl.BlockSpec(memory_space=pltpu.VMEM)],
        out_specs=(pl.BlockSpec(memory_space=pltpu.VMEM), pl.BlockSpec(memory_space=pltpu.VMEM)),
        compiler_params=pltpu.CompilerParams(vmem_limit_bytes=VMEM_BYTES),
    )(got)
    return recalled, log_total.reshape(1)


def on_cycle(context, residual, out_proj, norm_gain, lengths, queries, pattern):
    ranks = lax.axis_size("dp")
    size = ranks // CORES
    features = residual.shape[1]

    def ring(step):
        return [
            (CYCLE[r] * CORES + c, CYCLE[(r + step * (1 - 2 * c)) % size] * CORES + c)
            for r in range(size)
            for c in range(CORES)
        ]

    def from_next(piece):
        return lax.ppermute(piece, "dp", ring(-1))

    def from_last(piece):
        return lax.ppermute(piece, "dp", ring(1))

    def over_x(piece):
        return lax.ppermute(piece, "groups", [(0, 1), (1, 0)])

    def other_core(piece):
        return lax.ppermute(piece, "dp", [(i, i ^ 1) for i in range(ranks)])

    wait = lax.optimization_barrier

    own = own_half(out_proj)
    a = from_next(own)
    c = other_core(context)
    q = other_core(queries)
    h0, sq0 = wave((0,), (), (), context, None, residual, [out_proj])
    own, h0, sq0 = wait((own, h0, sq0))
    b = from_last(own)

    n1, sq0 = wait((a, sq0))
    x1 = over_x(n1)
    a = from_next(n1)
    context2, n1 = wait((c, n1))
    (t0,) = wave((0,), (), (), None, context2, None, [out_proj])
    l1, n1, t0, queries2 = wait((b, n1, t0, q))
    b = from_last(l1)
    r0 = other_core(t0)

    n2, l1 = wait((a, l1))
    x2 = over_x(n2)
    a = from_next(n2)
    xn1, n2 = wait((x1, n2))
    h1, t1, f0, sq1 = wave((1,), (), (0,), context, context2, residual, [n1, xn1], [r0], sq0)
    l2, n2, t1, sq1 = wait((b, n2, t1, sq1))
    b = from_last(l2)
    x3 = over_x(l2)
    r1 = other_core(t1)

    n3, l2 = wait((a, l2))
    xn2, l2, n3 = wait((x2, l2, n3))
    a = from_next(xn2)
    h2, t2, t2p, f1, sq2 = wave((2,), (-1,), (1,), context, context2, residual, [n2, xn2, l1], [r1], sq1)
    l3, n3, t2, t2p, sq2 = wait((b, n3, t2, t2p, sq2))
    b = from_last(l3)
    r2, r2p = other_core(t2), other_core(t2p)

    n3x, l3 = wait((a, l3))
    a = from_next(n3x)
    xl2, l1, n3x = wait((x3, l1, n3x))
    x4 = over_x(l1)
    h3, t3a, t3b, t3p, f2, sq3 = wave(
        (-2, 3), (-3,), (2,), context, context2, residual, [l2, xl2, n3, n3x, l3], [r2], sq2
    )
    l4, xl2, t3a, t3b, t3p, sq3, r2p = wait((b, xl2, t3a, t3b, t3p, sq3, r2p))
    b2 = from_last(xl2)
    l4s = other_core(l4)
    r3a, r3b, r3p = other_core(t3a), other_core(t3b), other_core(t3p)
    n4x, l4 = wait((a, l4))
    n4xs = other_core(n4x)
    xl1, n4x, r3a, r3b = wait((x4, n4x, r3a, r3b))
    xl1s = other_core(xl1)
    l3x, xl1, r3p, l4s = wait((b2, xl1, r3p, l4s))
    l3xs = other_core(l3x)

    missing = (((0, True),), ((1, True),), ((2, False), (3, True)))
    own_items = tuple(
        (base, parts, base is None, distance, True)
        for base, parts, distance in zip(((0, 1), (1, 2), None), missing, (-1, -3, 4))
    )
    h4, sq4 = late(own_items, context, residual, sq3, [xl1, l3x, l4, n4x], [h2, h3])
    items = tuple(
        (base, parts, True, distance, False)
        for base, parts, distance in zip(
            ((8, None), (9, None), None, (10, None), (11, None)), missing + ((), ()), (-1, -3, 4, -2, 3)
        )
    )
    hidden = [h0, h1, h2, h3, h4, f0, f1, f2, r2p, r3p, r3a, r3b]
    sources = (
        (0, 0, 0, True),
        (1, 0, 1, True),
        (2, 0, 2, True),
        (3, 0, -2, True),
        (3, 1, 3, True),
        (4, 0, -1, True),
        (4, 1, -3, True),
        (4, 2, 4, True),
        (5, 0, 0, False),
        (6, 0, 1, False),
        (7, 0, 2, False),
    )
    flags = jnp.pad(pattern.astype(jnp.float32), ((0, 0), (0, LANES - pattern.shape[1])))
    embedded, payload = finish(
        items,
        sources,
        lengths,
        context,
        residual,
        sq4,
        norm_gain.reshape(1, -1),
        flags,
        [xl1s, l3xs, l4s, n4xs],
        hidden,
        size,
    )
    same_core = [list(range(c, ranks, CORES)) for c in range(CORES)]

    def spread(blocks):
        return lax.all_to_all(blocks, "dp", 0, 0, axis_index_groups=same_core, tiled=True)

    parts = score(spread(payload), queries, queries2, pattern.shape[1])
    recalled, log_total = combine(spread(parts), features)
    return embedded, recalled, log_total


def gathered(context, residual, out_proj, norm_gain, lengths, queries, pattern):
    tok_rows = context.shape[0]
    features = residual.shape[1]
    passages_here = lengths.shape[0]
    seq_len = tok_rows // passages_here
    query_rows = queries.shape[0]
    blocks = pattern.shape[1]
    ranks = lax.axis_size("dp")
    me = lax.axis_index("dp")
    branch = jnp.dot(
        context,
        lax.all_gather(out_proj, "dp", axis=1, tiled=True),
        preferred_element_type=jnp.float32,
    )
    hidden_sum = residual.astype(jnp.float32) + branch
    normed = (
        hidden_sum
        * lax.rsqrt(jnp.mean(hidden_sum * hidden_sum, axis=-1, keepdims=True) + 1e-05)
        * norm_gain
    )
    shaped = normed.reshape(passages_here, seq_len, features)
    valid_mask = (jnp.arange(seq_len)[None, :] < lengths[:, None]).astype(jnp.float32)
    pooled = jnp.sum(shaped * valid_mask[:, :, None], axis=1) / lengths.astype(jnp.float32)[:, None]
    embedded = pooled * lax.rsqrt(jnp.mean(pooled * pooled, axis=-1, keepdims=True) + 1e-06)
    emb_half = embedded.astype(jnp.bfloat16)
    temper = 1.0 / (0.02 * math.sqrt(features))
    contract = (((1,), (1,)), ((), ()))

    flags = jnp.pad(pattern.astype(jnp.bfloat16), ((0, 0), (0, LANES - blocks)))
    everyone = lax.all_gather(jnp.concatenate([emb_half, flags], axis=1), "dp", axis=0, tiled=True)
    emb_all = everyone[:, :features]
    flags_all = everyone[:, features : features + blocks].astype(jnp.float32)
    scores = lax.dot_general(emb_all, queries, contract, preferred_element_type=jnp.float32) * temper
    row_block = (me * query_rows + jnp.arange(query_rows)) // QB
    picks = (row_block[None, :] == jnp.arange(blocks)[:, None]).astype(jnp.float32)
    cand_mask = jnp.dot(flags_all, picks) > 0
    peak_part = jnp.max(jnp.where(cand_mask, scores, LOW), axis=1, keepdims=True)
    weights = jnp.where(cand_mask, jnp.exp(scores - peak_part), 0.0)
    total_part = jnp.sum(weights, axis=1, keepdims=True)
    mix_part = jnp.dot(weights.astype(jnp.bfloat16), queries, preferred_element_type=jnp.float32)

    passages = emb_all.shape[0]
    lane = jnp.arange(LANES)[None, :]
    tail = jnp.where(lane == 0, peak_part, jnp.where(lane == 1, total_part, 0.0))
    parts = jnp.concatenate([mix_part, tail], axis=1).reshape(ranks, passages // ranks, -1)
    parts = lax.all_to_all(parts, "dp", split_axis=0, concat_axis=0, tiled=True)
    mixes, peaks, sums = parts[:, :, :features], parts[:, :, features], parts[:, :, features + 1]
    peak_score = jnp.max(peaks, axis=0)
    factor = jnp.exp(peaks - peak_score[None, :])
    totals = jnp.sum(sums * factor, axis=0)
    recalled = jnp.sum(mixes * factor[:, :, None], axis=0) / totals[:, None]
    log_total = peak_score + jnp.log(totals)
    return (embedded, recalled, log_total)


def per_device(context, residual, out_proj, norm_gain, lengths, queries, pattern):
    fits = (
        lax.axis_size("dp") == CORES * len(CYCLE)
        and lax.axis_size("groups") == 2
        and lengths.shape[0] == 1
        and out_proj.shape[1] % LANES == 0
        and out_proj.shape[0] % (2 * LANES) == 0
        and context.shape[0] % STEP == 0
        and pattern.shape[1] <= LANES
    )
    form = on_cycle if fits else gathered
    return form(context, residual, out_proj, norm_gain, lengths, queries, pattern)


def solution(mesh):
    in_specs = (
        P(("groups", "dp"), None),
        P(("groups", "dp"), None),
        P(None, "dp"),
        P(),
        P(("groups", "dp")),
        P(("groups", "dp"), None),
        P(("groups", "dp"), None),
    )
    out_specs = (P(("groups", "dp"), None), P(("groups", "dp"), None), P(("groups", "dp")))
    return jax.shard_map(
        per_device, mesh=mesh, in_specs=in_specs, out_specs=out_specs, check_vma=False
    )
```

```python
import functools
import math

import jax
import jax.numpy as jnp
from jax import lax
from jax.experimental import pallas as pl
from jax.experimental.pallas import tpu as pltpu
from jax.sharding import PartitionSpec as P

QB = 256
LANES = 128
CORES = 2
STEP = 256
VMEM_BYTES = 12 << 20
LOW = -1e30
CYCLE = (0, 2, 4, 6, 7, 5, 3, 1)
VMEM_SPEC = pl.BlockSpec(memory_space=pltpu.VMEM)
SMALL = pl.CostEstimate(flops=1000, bytes_accessed=1000, transcendentals=0)


def column_block(distance, same_core):
    me = lax.axis_index("dp")
    core = lax.rem(me, CORES)
    chip = lax.div(me, CORES)
    z, y = lax.div(chip, 2), lax.rem(chip, 2)
    size = len(CYCLE)
    at = jnp.where(y == 0, z, size - 1 - z)
    core = core if same_core else 1 - core
    there = lax.rem(at + jnp.where(core == 0, size + distance, size - distance), size)
    chip = jnp.where(there < size // 2, 2 * there, 2 * (size - 1 - there) + 1)
    return chip * CORES + core


def columns(distance, same_core, width):
    return pl.ds(pl.multiple_of(column_block(distance, same_core) * width, width), width)


def half_slice(second, half):
    side = lax.axis_index("groups")
    return pl.ds(pl.multiple_of((1 - side if second else side) * half, half), half)


def add_squares(squares, at, total):
    square = total * total
    for lane in range(0, total.shape[1], LANES):
        squares[at, :] += square[:, lane : lane + LANES]


def half_kernel(whole, part):
    part[...] = whole[half_slice(False, part.shape[0]), :]


def own_half(whole):
    rows, width = whole.shape
    return pl.pallas_call(
        half_kernel,
        out_shape=jax.ShapeDtypeStruct((rows // 2, width), whole.dtype),
        in_specs=[VMEM_SPEC],
        out_specs=VMEM_SPEC,
        compiler_params=pltpu.CompilerParams(vmem_limit_bytes=VMEM_BYTES),
    )(whole)


def row_steps(rows):
    def loop(body):
        @pl.loop(0, rows // STEP)
        def _(k):
            body(pl.ds(pl.multiple_of(k * STEP, STEP), STEP))

    return loop


def product(tokens, at, pieces):
    total = None
    for piece, second in pieces:
        half = piece.shape[0]
        term = jnp.dot(tokens[at, half_slice(second, half)], piece[...], preferred_element_type=jnp.float32)
        total = term if total is None else total + term
    return total


def wave_kernel(full, part, arrived, whole, tokens, stacked, *refs):
    count = len(full) + len(part)
    refs = list(refs)
    context = refs.pop(0) if "mine" in tokens else None
    other_context = refs.pop(0) if "theirs" in tokens else None
    residual = refs.pop(0) if "mine" in tokens else None
    if whole:
        shard = refs.pop(0)
        half = shard.shape[0] // 2
        jobs = [[(shard.at[half_slice(second, half)], second) for second in (False, True)]]
    else:
        jobs = [[(refs.pop(0), False)] + ([(refs.pop(0), True)] if j < len(full) else []) for j in range(count)]
    if arrived:
        received, before = [refs.pop(0) for _ in arrived], refs.pop(0)
    mine = refs.pop(0) if "mine" in tokens else None
    theirs = None
    if "theirs" in tokens:
        stacks = [refs.pop(0) for _ in range(2 if stacked else count)]
        theirs = stacks
        if stacked:
            theirs = [stacks[0].at[j] for j in range(len(full))] + [stacks[1].at[j] for j in range(len(part))]
    finished = refs.pop(0) if arrived else None
    squares = refs.pop(0) if "mine" in tokens else None
    rows, width = mine.shape[1:] if "mine" in tokens else theirs[0].shape
    if arrived:
        squares[...] = before[...]
    elif "mine" in tokens:
        squares[...] = jnp.zeros_like(squares)
    for j, distance in enumerate(full + part):

        @row_steps(rows)
        def _(at):
            if "theirs" in tokens:
                theirs[j][at, :] = product(other_context, at, jobs[j])
            if "mine" in tokens:
                total = product(context, at, jobs[j])
                total += residual[at, columns(distance, True, width)].astype(jnp.float32)
                mine[j, at, :] = total
                if j < len(full):
                    add_squares(squares, at, total)

    for j, distance in enumerate(arrived):

        @row_steps(rows)
        def _(at):
            total = received[j][at, :] + residual[at, columns(distance, False, width)].astype(jnp.float32)
            finished[j, at, :] = total
            add_squares(squares, at, total)


def wave(
    full, part, arrived, context, other_context, residual, pieces, received=None, squares=None, stacked=False
):
    tokens = (("mine",) if context is not None else ()) + (("theirs",) if other_context is not None else ())
    count = len(full) + len(part)
    rows = (context if other_context is None else other_context).shape[0]
    whole = len(pieces) == 1
    block = jax.ShapeDtypeStruct((rows, pieces[0].shape[1]), jnp.float32)

    def stack(n):
        return jax.ShapeDtypeStruct((n,) + block.shape, jnp.float32)

    outs = [stack(count)] if "mine" in tokens else []
    if "theirs" in tokens:
        outs += [stack(len(full)), stack(len(part))] if stacked else [block] * count
    operands = [x for x in (context, other_context) if x is not None]
    operands += ([residual] if "mine" in tokens else []) + list(pieces)
    if arrived:
        operands += [*received, squares]
        outs.append(jax.ShapeDtypeStruct((len(arrived),) + block.shape, jnp.float32))
    if "mine" in tokens:
        outs.append(jax.ShapeDtypeStruct((rows, LANES), jnp.float32))
    return pl.pallas_call(
        functools.partial(wave_kernel, full, part, arrived, whole, tokens, stacked),
        out_shape=outs,
        in_specs=[VMEM_SPEC] * len(operands),
        out_specs=[VMEM_SPEC] * len(outs),
        compiler_params=pltpu.CompilerParams(vmem_limit_bytes=VMEM_BYTES),
        cost_estimate=SMALL,
    )(*operands)


def late_blocks(items, context, residual, pieces, hidden, squares, target):
    rows, width = target.shape[1:]
    for i, (base, parts, bare, distance, same) in enumerate(items):

        @row_steps(rows)
        def _(at):
            value = product(context, at, [(pieces[index], second) for index, second in parts])
            if base is not None:
                known = hidden[base[0]][(at,) if base[1] is None else (base[1], at)]
                value = known if value is None else value + known
            if bare:
                value += residual[at, columns(distance, same, width)].astype(jnp.float32)
            target[i, at, :] = value
            add_squares(squares, at, value)


def late_kernel(items, n_pieces, context, residual, before, *refs):
    pieces, hidden = refs[:n_pieces], refs[n_pieces:-2]
    finished, squares = refs[-2:]
    squares[...] = before[...]
    late_blocks(items, context, residual, pieces, hidden, squares, finished)


def late(items, context, residual, squares, pieces, hidden):
    rows = context.shape[0]
    operands = [context, residual, squares, *pieces, *hidden]
    return pl.pallas_call(
        functools.partial(late_kernel, items, len(pieces)),
        out_shape=(
            jax.ShapeDtypeStruct((len(items), rows, pieces[0].shape[1]), jnp.float32),
            jax.ShapeDtypeStruct(squares.shape, jnp.float32),
        ),
        in_specs=[VMEM_SPEC] * len(operands),
        out_specs=(VMEM_SPEC, VMEM_SPEC),
        compiler_params=pltpu.CompilerParams(vmem_limit_bytes=VMEM_BYTES),
        cost_estimate=SMALL,
    )(*operands)


def final_kernel(items, sources, n_pieces, length, context, residual, before, gain, flags, *refs):
    pieces, hidden = refs[:n_pieces], refs[n_pieces:-6]
    embedded, payload, blocks, squares, scale_rows, sheet = refs[-6:]
    width = blocks.shape[2]
    features = embedded.shape[1]
    squares[...] = before[...]
    late_blocks(items, context, residual, pieces, hidden, squares, blocks)
    mean = jnp.sum(squares[...], axis=1, keepdims=True) * (1.0 / features)
    row = lax.broadcasted_iota(jnp.int32, mean.shape, 0)
    scale = jnp.where(row < length[0], lax.rsqrt(mean + 1e-05), 0.0)
    scale_rows[...] = jnp.broadcast_to(scale, scale_rows.shape)
    inverse = 1.0 / jnp.full((1, width), length[0], jnp.int32).astype(jnp.float32)
    done = [(blocks.at[i], distance, same) for i, (_, _, _, distance, same) in enumerate(items)]
    done += [(hidden[array].at[entry], distance, same) for array, entry, distance, same in sources]
    for block, distance, same in done:
        parts = [
            jnp.sum(block[:, lane : lane + LANES] * scale_rows[...], axis=0, keepdims=True)
            for lane in range(0, width, LANES)
        ]
        where = columns(distance, same, width)
        embedded[:, where] = jnp.concatenate(parts, axis=1) * gain[:, where] * inverse
    pooled = embedded[...]
    mean = jnp.sum(pooled * pooled, axis=1, keepdims=True) * (1.0 / features)
    embedded[...] = pooled * lax.rsqrt(mean + 1e-06)
    lines = features // LANES
    sheet[lines:, :] = jnp.zeros((sheet.shape[0] - lines, LANES), jnp.float32)
    for line in range(lines):
        sheet[line : line + 1, :] = embedded[:, line * LANES : (line + 1) * LANES]
    sheet[lines : lines + 1, :] = flags[...]
    rounded = sheet[...].astype(jnp.bfloat16)
    for rank in range(payload.shape[0]):
        payload[rank] = rounded


def finish(items, sources, lengths, context, residual, squares, gain, flags, pieces, hidden, ranks):
    rows = context.shape[0]
    width = pieces[0].shape[1]
    features = (len(items) + len(sources)) * width
    lines = -(-(features // LANES + 1) // 16) * 16
    operands = [context, residual, squares, gain, flags, *pieces, *hidden]
    return pl.pallas_call(
        functools.partial(final_kernel, items, sources, len(pieces)),
        out_shape=(
            jax.ShapeDtypeStruct((1, features), jnp.float32),
            jax.ShapeDtypeStruct((ranks, lines, LANES), jnp.bfloat16),
        ),
        in_specs=[pl.BlockSpec(memory_space=pltpu.SMEM)] + [VMEM_SPEC] * len(operands),
        out_specs=(VMEM_SPEC, VMEM_SPEC),
        scratch_shapes=[
            pltpu.VMEM((len(items), rows, width), jnp.float32),
            pltpu.VMEM((rows, LANES), jnp.float32),
            pltpu.VMEM((rows, LANES), jnp.float32),
            pltpu.VMEM((lines, LANES), jnp.float32),
        ],
        compiler_params=pltpu.CompilerParams(vmem_limit_bytes=VMEM_BYTES),
        cost_estimate=SMALL,
    )(lengths, *operands)


def score_kernel(lines, blocks, got, queries, other_queries, out, wide, emb, mix):
    me = lax.axis_index("dp")
    ranks = got.shape[0]
    count = queries.shape[0]
    wide[...] = got[...].astype(jnp.float32)
    for line in range(lines):
        emb[:, line * LANES : (line + 1) * LANES] = wide[:, line, :]
    half = emb[...].astype(jnp.bfloat16)
    flags = wide[:, lines, :].astype(jnp.bfloat16)
    temper = 1.0 / (0.02 * math.sqrt(lines * LANES))
    scores, masks = [], []
    for owner, rows in ((me, queries), (me + 1 - 2 * lax.rem(me, CORES), other_queries)):
        score = lax.dot_general(
            half, rows[...], (((1,), (1,)), ((), ())), preferred_element_type=jnp.float32
        )
        scores.append(score * temper)
        block = lax.broadcasted_iota(jnp.int32, (LANES, count), 0)
        row = owner * count + lax.broadcasted_iota(jnp.int32, (LANES, count), 1)
        pick = (row >= block * QB) & (row < block * QB + QB) & (block < blocks)
        pick = jnp.where(pick, 1.0, 0.0).astype(jnp.bfloat16)
        masks.append(jnp.dot(flags, pick, preferred_element_type=jnp.float32) > 0.5)
    peaks = [
        jnp.max(jnp.where(mask, score, LOW), axis=1, keepdims=True) for score, mask in zip(scores, masks)
    ]
    peak = jnp.maximum(*peaks)
    weights = [jnp.where(mask, jnp.exp(score - peak), 0.0) for score, mask in zip(scores, masks)]
    total = sum(jnp.sum(weight, axis=1, keepdims=True) for weight in weights)
    mix[...] = jnp.dot(
        weights[0].astype(jnp.bfloat16), queries[...], preferred_element_type=jnp.float32
    ) + jnp.dot(weights[1].astype(jnp.bfloat16), other_queries[...], preferred_element_type=jnp.float32)
    for line in range(lines):
        out[:, line, :] = mix[:, line * LANES : (line + 1) * LANES]
    lane = lax.broadcasted_iota(jnp.int32, (ranks, LANES), 1)
    out[:, lines, :] = jnp.where(lane == 0, peak, jnp.where(lane == 1, total, 0.0))
    for line in range(lines + 1, out.shape[1]):
        out[:, line, :] = jnp.zeros((ranks, LANES), jnp.float32)


def score(got, queries, other_queries, blocks):
    ranks = got.shape[0]
    features = queries.shape[1]
    lines = features // LANES
    return pl.pallas_call(
        functools.partial(score_kernel, lines, blocks),
        out_shape=jax.ShapeDtypeStruct((ranks, -(-(lines + 1) // 8) * 8, LANES), jnp.float32),
        in_specs=[pl.BlockSpec(memory_space=pltpu.VMEM)] * 3,
        out_specs=pl.BlockSpec(memory_space=pltpu.VMEM),
        scratch_shapes=[
            pltpu.VMEM(got.shape, jnp.float32),
            pltpu.VMEM((ranks, features), jnp.float32),
            pltpu.VMEM((ranks, features), jnp.float32),
        ],
        compiler_params=pltpu.CompilerParams(vmem_limit_bytes=VMEM_BYTES),
    )(got, queries, other_queries)


def combine_kernel(lines, got, recalled, log_total):
    stats = got[:, lines, :]
    peaks, sums = stats[:, 0:1], stats[:, 1:2]
    peak = jnp.max(peaks, axis=0, keepdims=True)
    factor = jnp.exp(peaks - peak)
    total = jnp.sum(sums * factor, axis=0, keepdims=True)
    mix = got[0, :lines, :] * factor[0:1, :]
    for rank in range(1, got.shape[0]):
        mix += got[rank, :lines, :] * factor[rank : rank + 1, :]
    mix = mix / total
    for line in range(lines):
        recalled[:, line * LANES : (line + 1) * LANES] = mix[line : line + 1, :]
    log_total[...] = peak + jnp.log(total)


def combine(got, features):
    recalled, log_total = pl.pallas_call(
        functools.partial(combine_kernel, features // LANES),
        out_shape=(
            jax.ShapeDtypeStruct((1, features), jnp.float32),
            jax.ShapeDtypeStruct((1, 1), jnp.float32),
        ),
        in_specs=[pl.BlockSpec(memory_space=pltpu.VMEM)],
        out_specs=(pl.BlockSpec(memory_space=pltpu.VMEM), pl.BlockSpec(memory_space=pltpu.VMEM)),
        compiler_params=pltpu.CompilerParams(vmem_limit_bytes=VMEM_BYTES),
    )(got)
    return recalled, log_total.reshape(1)


def on_cycle(context, residual, out_proj, norm_gain, lengths, queries, pattern):
    ranks = lax.axis_size("dp")
    size = ranks // CORES
    features = residual.shape[1]

    def ring(step):
        return [
            (CYCLE[r] * CORES + c, CYCLE[(r + step * (1 - 2 * c)) % size] * CORES + c)
            for r in range(size)
            for c in range(CORES)
        ]

    def from_next(piece):
        return lax.ppermute(piece, "dp", ring(-1))

    def from_last(piece):
        return lax.ppermute(piece, "dp", ring(1))

    def over_x(piece):
        return lax.ppermute(piece, "groups", [(0, 1), (1, 0)])

    def other_core(piece):
        return lax.ppermute(piece, "dp", [(i, i ^ 1) for i in range(ranks)])

    wait = lax.optimization_barrier

    own = own_half(out_proj)
    a, b = from_next(own), from_last(own)
    c, q = other_core(context), other_core(queries)
    h0, sq0 = wave((0,), (), (), context, None, residual, [out_proj])

    n1, sq0 = wait((a, sq0))
    x1 = over_x(n1)
    a = from_next(n1)
    l1, n1, context2 = wait((b, n1, c))
    b = from_last(l1)
    (t0,) = wave((0,), (), (), None, context2, None, [out_proj])

    n2, t0, queries2 = wait((a, t0, q))
    x2 = over_x(n2)
    a = from_next(n2)
    r0 = other_core(t0)
    l2, n2 = wait((b, n2))
    b = from_last(l2)
    xn1, n2, l2 = wait((x1, n2, l2))
    h1, t1, f0, sq1 = wave((1,), (), (0,), context, context2, residual, [n1, xn1], [r0], sq0)

    xn2, l2, t1, sq1 = wait((x2, l2, t1, sq1))
    x3 = over_x(l2)
    a2 = from_next(xn2)
    r1 = other_core(t1)
    n3, xn2 = wait((a, xn2))
    l3, n3, xn2 = wait((b, n3, xn2))
    b = from_last(l3)
    h2, t2, t2p, f1, sq2 = wave((2,), (-1,), (1,), context, context2, residual, [n2, xn2, l1], [r1], sq1)

    n3x, t2, t2p, sq2 = wait((a2, t2, t2p, sq2))
    a = from_next(n3x)
    r2, r2p = other_core(t2), other_core(t2p)
    xl2, n3x, l1 = wait((x3, n3x, l1))
    x4 = over_x(l1)
    l4, xl2, n3x = wait((b, xl2, n3x))
    b = from_last(xl2)
    h3, t3a, t3b, f2, sq3 = wave(
        (-2, 3), (-3, 4), (2,), context, context2, residual, [l2, xl2, n3, n3x, l3, l4], [r2], sq2, stacked=True
    )

    r3a, r3b = other_core(t3a), other_core(t3b)
    n4x, sq3, r2p = wait((a, sq3, r2p))
    n4xs = other_core(n4x)
    xl1, n4x = wait((x4, n4x))
    xl1s = other_core(xl1)
    l3x, xl1 = wait((b, xl1))
    l3xs = other_core(l3x)

    first_items = (
        ((0, 1), ((0, True),), False, -1, True),
        ((1, 2), ((1, True),), False, -3, True),
        ((1, 3), ((2, True),), False, 4, True),
    )
    h4, sq4 = late(first_items, context, residual, sq3, [xl1, l3x, n4x], [h2, h3])
    items = (
        ((8, None), ((0, True),), True, -1, False),
        ((10, 0), ((1, True),), True, -3, False),
        ((10, 1), ((2, True),), True, 4, False),
        ((9, 0), (), True, -2, False),
        ((9, 1), (), True, 3, False),
    )
    hidden = [h0, h1, h2, h3, h4, f0, f1, f2, r2p, r3a, r3b]
    sources = (
        (0, 0, 0, True),
        (1, 0, 1, True),
        (2, 0, 2, True),
        (3, 0, -2, True),
        (3, 1, 3, True),
        (5, 0, 0, False),
        (6, 0, 1, False),
        (7, 0, 2, False),
        (4, 0, -1, True),
        (4, 1, -3, True),
        (4, 2, 4, True),
    )
    flags = jnp.pad(pattern.astype(jnp.float32), ((0, 0), (0, LANES - pattern.shape[1])))
    embedded, payload = finish(
        items,
        sources,
        lengths,
        context,
        residual,
        sq4,
        norm_gain.reshape(1, -1),
        flags,
        [xl1s, l3xs, n4xs],
        hidden,
        size,
    )
    same_core = [list(range(c, ranks, CORES)) for c in range(CORES)]

    def spread(blocks):
        return lax.all_to_all(blocks, "dp", 0, 0, axis_index_groups=same_core, tiled=True)

    parts = score(spread(payload), queries, queries2, pattern.shape[1])
    recalled, log_total = combine(spread(parts), features)
    return embedded, recalled, log_total


def gathered(context, residual, out_proj, norm_gain, lengths, queries, pattern):
    tok_rows = context.shape[0]
    features = residual.shape[1]
    passages_here = lengths.shape[0]
    seq_len = tok_rows // passages_here
    query_rows = queries.shape[0]
    blocks = pattern.shape[1]
    ranks = lax.axis_size("dp")
    me = lax.axis_index("dp")
    branch = jnp.dot(
        context,
        lax.all_gather(out_proj, "dp", axis=1, tiled=True),
        preferred_element_type=jnp.float32,
    )
    hidden_sum = residual.astype(jnp.float32) + branch
    normed = (
        hidden_sum
        * lax.rsqrt(jnp.mean(hidden_sum * hidden_sum, axis=-1, keepdims=True) + 1e-05)
        * norm_gain
    )
    shaped = normed.reshape(passages_here, seq_len, features)
    valid_mask = (jnp.arange(seq_len)[None, :] < lengths[:, None]).astype(jnp.float32)
    pooled = jnp.sum(shaped * valid_mask[:, :, None], axis=1) / lengths.astype(jnp.float32)[:, None]
    embedded = pooled * lax.rsqrt(jnp.mean(pooled * pooled, axis=-1, keepdims=True) + 1e-06)
    emb_half = embedded.astype(jnp.bfloat16)
    temper = 1.0 / (0.02 * math.sqrt(features))
    contract = (((1,), (1,)), ((), ()))

    flags = jnp.pad(pattern.astype(jnp.bfloat16), ((0, 0), (0, LANES - blocks)))
    everyone = lax.all_gather(jnp.concatenate([emb_half, flags], axis=1), "dp", axis=0, tiled=True)
    emb_all = everyone[:, :features]
    flags_all = everyone[:, features : features + blocks].astype(jnp.float32)
    scores = lax.dot_general(emb_all, queries, contract, preferred_element_type=jnp.float32) * temper
    row_block = (me * query_rows + jnp.arange(query_rows)) // QB
    picks = (row_block[None, :] == jnp.arange(blocks)[:, None]).astype(jnp.float32)
    cand_mask = jnp.dot(flags_all, picks) > 0
    peak_part = jnp.max(jnp.where(cand_mask, scores, LOW), axis=1, keepdims=True)
    weights = jnp.where(cand_mask, jnp.exp(scores - peak_part), 0.0)
    total_part = jnp.sum(weights, axis=1, keepdims=True)
    mix_part = jnp.dot(weights.astype(jnp.bfloat16), queries, preferred_element_type=jnp.float32)

    passages = emb_all.shape[0]
    lane = jnp.arange(LANES)[None, :]
    tail = jnp.where(lane == 0, peak_part, jnp.where(lane == 1, total_part, 0.0))
    parts = jnp.concatenate([mix_part, tail], axis=1).reshape(ranks, passages // ranks, -1)
    parts = lax.all_to_all(parts, "dp", split_axis=0, concat_axis=0, tiled=True)
    mixes, peaks, sums = parts[:, :, :features], parts[:, :, features], parts[:, :, features + 1]
    peak_score = jnp.max(peaks, axis=0)
    factor = jnp.exp(peaks - peak_score[None, :])
    totals = jnp.sum(sums * factor, axis=0)
    recalled = jnp.sum(mixes * factor[:, :, None], axis=0) / totals[:, None]
    log_total = peak_score + jnp.log(totals)
    return (embedded, recalled, log_total)


def per_device(context, residual, out_proj, norm_gain, lengths, queries, pattern):
    fits = (
        lax.axis_size("dp") == CORES * len(CYCLE)
        and lax.axis_size("groups") == 2
        and lengths.shape[0] == 1
        and out_proj.shape[1] % LANES == 0
        and out_proj.shape[0] % (2 * LANES) == 0
        and context.shape[0] % STEP == 0
        and pattern.shape[1] <= LANES
    )
    form = on_cycle if fits else gathered
    return form(context, residual, out_proj, norm_gain, lengths, queries, pattern)


def solution(mesh):
    in_specs = (
        P(("groups", "dp"), None),
        P(("groups", "dp"), None),
        P(None, "dp"),
        P(),
        P(("groups", "dp")),
        P(("groups", "dp"), None),
        P(("groups", "dp"), None),
    )
    out_specs = (P(("groups", "dp"), None), P(("groups", "dp"), None), P(("groups", "dp")))
    return jax.shard_map(
        per_device, mesh=mesh, in_specs=in_specs, out_specs=out_specs, check_vma=False
    )
```

```python
import functools
import math

import jax
import jax.numpy as jnp
from jax import lax
from jax.experimental import pallas as pl
from jax.experimental.pallas import tpu as pltpu
from jax.sharding import PartitionSpec as P

QB = 256
LANES = 128
CORES = 2
STEP = 256
VMEM_BYTES = 12 << 20
LOW = -1e30
CYCLE = (0, 2, 4, 6, 7, 5, 3, 1)
VMEM_SPEC = pl.BlockSpec(memory_space=pltpu.VMEM)
SMALL = pl.CostEstimate(flops=1000, bytes_accessed=1000, transcendentals=0)


def column_block(distance, same_core):
    me = lax.axis_index("dp")
    core = lax.rem(me, CORES)
    chip = lax.div(me, CORES)
    z, y = lax.div(chip, 2), lax.rem(chip, 2)
    size = len(CYCLE)
    at = jnp.where(y == 0, z, size - 1 - z)
    core = core if same_core else 1 - core
    there = lax.rem(at + jnp.where(core == 0, size + distance, size - distance), size)
    chip = jnp.where(there < size // 2, 2 * there, 2 * (size - 1 - there) + 1)
    return chip * CORES + core


def columns(distance, same_core, width):
    return pl.ds(pl.multiple_of(column_block(distance, same_core) * width, width), width)


def half_slice(second, half):
    side = lax.axis_index("groups")
    return pl.ds(pl.multiple_of((1 - side if second else side) * half, half), half)


def add_squares(squares, at, total):
    square = total * total
    for lane in range(0, total.shape[1], LANES):
        squares[at, :] += square[:, lane : lane + LANES]


def half_kernel(whole, part):
    part[...] = whole[half_slice(False, part.shape[0]), :]


def own_half(whole):
    rows, width = whole.shape
    return pl.pallas_call(
        half_kernel,
        out_shape=jax.ShapeDtypeStruct((rows // 2, width), whole.dtype),
        in_specs=[VMEM_SPEC],
        out_specs=VMEM_SPEC,
        compiler_params=pltpu.CompilerParams(vmem_limit_bytes=VMEM_BYTES),
    )(whole)


def row_steps(rows):
    def loop(body):
        @pl.loop(0, rows // STEP)
        def _(k):
            body(pl.ds(pl.multiple_of(k * STEP, STEP), STEP))

    return loop


def product(tokens, at, pieces):
    total = None
    for piece, second in pieces:
        half = piece.shape[0]
        term = jnp.dot(tokens[at, half_slice(second, half)], piece[...], preferred_element_type=jnp.float32)
        total = term if total is None else total + term
    return total


def wave_kernel(full, part, arrived, whole, tokens, chained, stacked, *refs):
    count = len(full) + len(part)
    refs = list(refs)
    context = refs.pop(0) if "mine" in tokens else None
    other_context = refs.pop(0) if "theirs" in tokens else None
    residual = refs.pop(0) if "mine" in tokens else None
    if whole:
        shard = refs.pop(0)
        half = shard.shape[0] // 2
        jobs = [[(shard.at[half_slice(second, half)], second) for second in (False, True)]]
    else:
        jobs = [[(refs.pop(0), False)] + ([(refs.pop(0), True)] if j < len(full) else []) for j in range(count)]
    received = [refs.pop(0) for _ in arrived]
    before = refs.pop(0) if chained else None
    mine = refs.pop(0) if "mine" in tokens else None
    theirs = None
    if "theirs" in tokens:
        stacks = [refs.pop(0) for _ in range(2 if stacked else count)]
        theirs = stacks
        if stacked:
            theirs = [stacks[0].at[j] for j in range(len(full))] + [stacks[1].at[j] for j in range(len(part))]
    finished = refs.pop(0) if arrived else None
    squares = refs.pop(0) if "mine" in tokens else None
    rows, width = mine.shape[1:] if "mine" in tokens else theirs[0].shape
    if chained:
        squares[...] = before[...]
    elif "mine" in tokens:
        squares[...] = jnp.zeros_like(squares)
    for j, distance in enumerate(full + part):

        @row_steps(rows)
        def _(at):
            if "theirs" in tokens:
                theirs[j][at, :] = product(other_context, at, jobs[j])
            if "mine" in tokens:
                total = product(context, at, jobs[j])
                total += residual[at, columns(distance, True, width)].astype(jnp.float32)
                mine[j, at, :] = total
                if j < len(full):
                    add_squares(squares, at, total)

    for j, (distance, same) in enumerate(arrived):

        @row_steps(rows)
        def _(at):
            total = received[j][at, :] + residual[at, columns(distance, same, width)].astype(jnp.float32)
            finished[j, at, :] = total
            add_squares(squares, at, total)


def wave(
    full, part, arrived, context, other_context, residual, pieces, received=None, squares=None, stacked=False
):
    tokens = (("mine",) if context is not None else ()) + (("theirs",) if other_context is not None else ())
    count = len(full) + len(part)
    rows = (context if other_context is None else other_context).shape[0]
    whole = len(pieces) == 1
    block = jax.ShapeDtypeStruct((rows, pieces[0].shape[1]), jnp.float32)

    def stack(n):
        return jax.ShapeDtypeStruct((n,) + block.shape, jnp.float32)

    outs = [stack(count)] if "mine" in tokens else []
    if "theirs" in tokens:
        outs += [stack(len(full)), stack(len(part))] if stacked else [block] * count
    operands = [x for x in (context, other_context) if x is not None]
    operands += ([residual] if "mine" in tokens else []) + list(pieces)
    if arrived:
        operands += [*received] + ([] if squares is None else [squares])
        outs.append(jax.ShapeDtypeStruct((len(arrived),) + block.shape, jnp.float32))
    if "mine" in tokens:
        outs.append(jax.ShapeDtypeStruct((rows, LANES), jnp.float32))
    return pl.pallas_call(
        functools.partial(wave_kernel, full, part, arrived, whole, tokens, squares is not None, stacked),
        out_shape=outs,
        in_specs=[VMEM_SPEC] * len(operands),
        out_specs=[VMEM_SPEC] * len(outs),
        compiler_params=pltpu.CompilerParams(vmem_limit_bytes=VMEM_BYTES),
        cost_estimate=SMALL,
    )(*operands)


def late_blocks(items, context, residual, pieces, hidden, squares, target):
    rows, width = target.shape[1:]
    for i, (base, parts, bare, distance, same) in enumerate(items):

        @row_steps(rows)
        def _(at):
            value = product(context, at, [(pieces[index], second) for index, second in parts])
            if base is not None:
                known = hidden[base[0]][(at,) if base[1] is None else (base[1], at)]
                value = known if value is None else value + known
            if bare:
                value += residual[at, columns(distance, same, width)].astype(jnp.float32)
            target[i, at, :] = value
            add_squares(squares, at, value)


def late_kernel(items, n_pieces, context, residual, before, *refs):
    pieces, hidden = refs[:n_pieces], refs[n_pieces:-2]
    finished, squares = refs[-2:]
    squares[...] = before[...]
    late_blocks(items, context, residual, pieces, hidden, squares, finished)


def late(items, context, residual, squares, pieces, hidden):
    rows = context.shape[0]
    operands = [context, residual, squares, *pieces, *hidden]
    return pl.pallas_call(
        functools.partial(late_kernel, items, len(pieces)),
        out_shape=(
            jax.ShapeDtypeStruct((len(items), rows, pieces[0].shape[1]), jnp.float32),
            jax.ShapeDtypeStruct(squares.shape, jnp.float32),
        ),
        in_specs=[VMEM_SPEC] * len(operands),
        out_specs=(VMEM_SPEC, VMEM_SPEC),
        compiler_params=pltpu.CompilerParams(vmem_limit_bytes=VMEM_BYTES),
        cost_estimate=SMALL,
    )(*operands)


def final_kernel(items, sources, n_pieces, length, context, residual, before, gain, flags, *refs):
    pieces, hidden = refs[:n_pieces], refs[n_pieces:-6]
    embedded, payload, blocks, squares, scale_rows, sheet = refs[-6:]
    width = blocks.shape[2]
    features = embedded.shape[1]
    squares[...] = before[...]
    late_blocks(items, context, residual, pieces, hidden, squares, blocks)
    mean = jnp.sum(squares[...], axis=1, keepdims=True) * (1.0 / features)
    row = lax.broadcasted_iota(jnp.int32, mean.shape, 0)
    scale = jnp.where(row < length[0], lax.rsqrt(mean + 1e-05), 0.0)
    scale_rows[...] = jnp.broadcast_to(scale, scale_rows.shape)
    inverse = 1.0 / jnp.full((1, width), length[0], jnp.int32).astype(jnp.float32)
    done = [(blocks.at[i], distance, same) for i, (_, _, _, distance, same) in enumerate(items)]
    done += [(hidden[array].at[entry], distance, same) for array, entry, distance, same in sources]
    for block, distance, same in done:
        parts = [
            jnp.sum(block[:, lane : lane + LANES] * scale_rows[...], axis=0, keepdims=True)
            for lane in range(0, width, LANES)
        ]
        where = columns(distance, same, width)
        embedded[:, where] = jnp.concatenate(parts, axis=1) * gain[:, where] * inverse
    pooled = embedded[...]
    mean = jnp.sum(pooled * pooled, axis=1, keepdims=True) * (1.0 / features)
    embedded[...] = pooled * lax.rsqrt(mean + 1e-06)
    lines = features // LANES
    sheet[lines:, :] = jnp.zeros((sheet.shape[0] - lines, LANES), jnp.float32)
    for line in range(lines):
        sheet[line : line + 1, :] = embedded[:, line * LANES : (line + 1) * LANES]
    sheet[lines : lines + 1, :] = flags[...]
    rounded = sheet[...].astype(jnp.bfloat16)
    for rank in range(payload.shape[0]):
        payload[rank] = rounded


def finish(items, sources, lengths, context, residual, squares, gain, flags, pieces, hidden, ranks):
    rows = context.shape[0]
    width = pieces[0].shape[1]
    features = (len(items) + len(sources)) * width
    lines = -(-(features // LANES + 1) // 16) * 16
    operands = [context, residual, squares, gain, flags, *pieces, *hidden]
    return pl.pallas_call(
        functools.partial(final_kernel, items, sources, len(pieces)),
        out_shape=(
            jax.ShapeDtypeStruct((1, features), jnp.float32),
            jax.ShapeDtypeStruct((ranks, lines, LANES), jnp.bfloat16),
        ),
        in_specs=[pl.BlockSpec(memory_space=pltpu.SMEM)] + [VMEM_SPEC] * len(operands),
        out_specs=(VMEM_SPEC, VMEM_SPEC),
        scratch_shapes=[
            pltpu.VMEM((len(items), rows, width), jnp.float32),
            pltpu.VMEM((rows, LANES), jnp.float32),
            pltpu.VMEM((rows, LANES), jnp.float32),
            pltpu.VMEM((lines, LANES), jnp.float32),
        ],
        compiler_params=pltpu.CompilerParams(vmem_limit_bytes=VMEM_BYTES),
        cost_estimate=SMALL,
    )(lengths, *operands)


def score_kernel(lines, blocks, got, queries, other_queries, out, wide, emb, mix):
    me = lax.axis_index("dp")
    ranks = got.shape[0]
    count = queries.shape[0]
    wide[...] = got[...].astype(jnp.float32)
    for line in range(lines):
        emb[:, line * LANES : (line + 1) * LANES] = wide[:, line, :]
    half = emb[...].astype(jnp.bfloat16)
    flags = wide[:, lines, :].astype(jnp.bfloat16)
    temper = 1.0 / (0.02 * math.sqrt(lines * LANES))
    scores, masks = [], []
    for owner, rows in ((me, queries), (me + 1 - 2 * lax.rem(me, CORES), other_queries)):
        score = lax.dot_general(
            half, rows[...], (((1,), (1,)), ((), ())), preferred_element_type=jnp.float32
        )
        scores.append(score * temper)
        block = lax.broadcasted_iota(jnp.int32, (LANES, count), 0)
        row = owner * count + lax.broadcasted_iota(jnp.int32, (LANES, count), 1)
        pick = (row >= block * QB) & (row < block * QB + QB) & (block < blocks)
        pick = jnp.where(pick, 1.0, 0.0).astype(jnp.bfloat16)
        masks.append(jnp.dot(flags, pick, preferred_element_type=jnp.float32) > 0.5)
    peaks = [
        jnp.max(jnp.where(mask, score, LOW), axis=1, keepdims=True) for score, mask in zip(scores, masks)
    ]
    peak = jnp.maximum(*peaks)
    weights = [jnp.where(mask, jnp.exp(score - peak), 0.0) for score, mask in zip(scores, masks)]
    total = sum(jnp.sum(weight, axis=1, keepdims=True) for weight in weights)
    mix[...] = jnp.dot(
        weights[0].astype(jnp.bfloat16), queries[...], preferred_element_type=jnp.float32
    ) + jnp.dot(weights[1].astype(jnp.bfloat16), other_queries[...], preferred_element_type=jnp.float32)
    for line in range(lines):
        out[:, line, :] = mix[:, line * LANES : (line + 1) * LANES]
    lane = lax.broadcasted_iota(jnp.int32, (ranks, LANES), 1)
    out[:, lines, :] = jnp.where(lane == 0, peak, jnp.where(lane == 1, total, 0.0))
    for line in range(lines + 1, out.shape[1]):
        out[:, line, :] = jnp.zeros((ranks, LANES), jnp.float32)


def score(got, queries, other_queries, blocks):
    ranks = got.shape[0]
    features = queries.shape[1]
    lines = features // LANES
    return pl.pallas_call(
        functools.partial(score_kernel, lines, blocks),
        out_shape=jax.ShapeDtypeStruct((ranks, -(-(lines + 1) // 8) * 8, LANES), jnp.float32),
        in_specs=[pl.BlockSpec(memory_space=pltpu.VMEM)] * 3,
        out_specs=pl.BlockSpec(memory_space=pltpu.VMEM),
        scratch_shapes=[
            pltpu.VMEM(got.shape, jnp.float32),
            pltpu.VMEM((ranks, features), jnp.float32),
            pltpu.VMEM((ranks, features), jnp.float32),
        ],
        compiler_params=pltpu.CompilerParams(vmem_limit_bytes=VMEM_BYTES),
    )(got, queries, other_queries)


def combine_kernel(lines, got, recalled, log_total):
    stats = got[:, lines, :]
    peaks, sums = stats[:, 0:1], stats[:, 1:2]
    peak = jnp.max(peaks, axis=0, keepdims=True)
    factor = jnp.exp(peaks - peak)
    total = jnp.sum(sums * factor, axis=0, keepdims=True)
    mix = got[0, :lines, :] * factor[0:1, :]
    for rank in range(1, got.shape[0]):
        mix += got[rank, :lines, :] * factor[rank : rank + 1, :]
    mix = mix / total
    for line in range(lines):
        recalled[:, line * LANES : (line + 1) * LANES] = mix[line : line + 1, :]
    log_total[...] = peak + jnp.log(total)


def combine(got, features):
    recalled, log_total = pl.pallas_call(
        functools.partial(combine_kernel, features // LANES),
        out_shape=(
            jax.ShapeDtypeStruct((1, features), jnp.float32),
            jax.ShapeDtypeStruct((1, 1), jnp.float32),
        ),
        in_specs=[pl.BlockSpec(memory_space=pltpu.VMEM)],
        out_specs=(pl.BlockSpec(memory_space=pltpu.VMEM), pl.BlockSpec(memory_space=pltpu.VMEM)),
        compiler_params=pltpu.CompilerParams(vmem_limit_bytes=VMEM_BYTES),
    )(got)
    return recalled, log_total.reshape(1)


def on_cycle(context, residual, out_proj, norm_gain, lengths, queries, pattern):
    ranks = lax.axis_size("dp")
    size = ranks // CORES
    features = residual.shape[1]

    def ring(step):
        return [
            (CYCLE[r] * CORES + c, CYCLE[(r + step * (1 - 2 * c)) % size] * CORES + c)
            for r in range(size)
            for c in range(CORES)
        ]

    def from_next(piece):
        return lax.ppermute(piece, "dp", ring(-1))

    def from_last(piece):
        return lax.ppermute(piece, "dp", ring(1))

    def over_x(piece):
        return lax.ppermute(piece, "groups", [(0, 1), (1, 0)])

    def other_core(piece):
        return lax.ppermute(piece, "dp", [(i, i ^ 1) for i in range(ranks)])

    wait = lax.optimization_barrier

    own = own_half(out_proj)
    a = from_next(own)
    c, q = other_core(context), other_core(queries)
    (p0,) = wave((0,), (), (), None, context, None, [out_proj])
    own, p0 = wait((own, p0))
    b = from_last(own)

    n1, p0 = wait((a, p0))
    x = over_x(n1)
    a = from_next(n1)
    context2, n1 = wait((c, n1))
    (t0,) = wave((0,), (), (), None, context2, None, [out_proj])
    l1, n1, t0, queries2 = wait((b, n1, t0, q))
    b = from_last(l1)
    r0 = other_core(t0)

    n2, l1 = wait((a, l1))
    xn1, n2 = wait((x, n2))
    x = over_x(n2)
    a = from_next(n2)
    h1, t1, f0, sq1 = wave(
        (1,), (), ((0, True), (0, False)), context, context2, residual, [n1, xn1], [p0, r0], None
    )
    l2, n2, t1, sq1 = wait((b, n2, t1, sq1))
    b = from_last(l2)
    r1 = other_core(t1)

    xn2, l2 = wait((x, l2))
    x = over_x(l2)
    a2 = from_next(xn2)
    n3, xn2 = wait((a, xn2))
    h2, t2, t2p, f1, sq2 = wave((2,), (-1,), ((1, False),), context, context2, residual, [n2, xn2, l1], [r1], sq1)
    l3, n3, t2, t2p, sq2 = wait((b, n3, t2, t2p, sq2))
    b = from_last(l3)
    r2, r2p = other_core(t2), other_core(t2p)

    n3x, l3 = wait((a2, l3))
    a = from_next(n3x)
    xl2, l1, n3x = wait((x, l1, n3x))
    x = over_x(l1)
    h3, t3a, t3p, f2, sq3 = wave(
        (-2, 3), (-3,), ((2, False),), context, context2, residual, [l2, xl2, n3, n3x, l3], [r2], sq2, stacked=True
    )
    l4, xl2, t3a, t3p, sq3, r2p = wait((b, xl2, t3a, t3p, sq3, r2p))
    b = from_last(xl2)
    r3a, r3p = other_core(t3a), other_core(t3p)
    l4s = other_core(l4)

    n4x, l4 = wait((a, l4))
    n4xs = other_core(n4x)
    xl1, n4x, r3p, l4s = wait((x, n4x, r3p, l4s))
    xl1s = other_core(xl1)
    l3x, xl1 = wait((b, xl1))
    l3xs = other_core(l3x)

    missing = (((0, True),), ((1, True),), ((2, False), (3, True)))
    own_items = tuple(
        (base, parts, base is None, distance, True)
        for base, parts, distance in zip(((0, 1), (1, 2), None), missing, (-1, -3, 4))
    )
    h4, sq4 = late(own_items, context, residual, sq3, [xl1, l3x, l4, n4x], [h2, h3])
    items = tuple(
        (base, parts, True, distance, False)
        for base, parts, distance in zip(
            ((8, None), (9, 0), None, (10, 0), (10, 1)), missing + ((), ()), (-1, -3, 4, -2, 3)
        )
    )
    hidden = [f0, h1, h2, h3, h4, f0, f1, f2, r2p, r3p, r3a]
    sources = (
        (0, 0, 0, True),
        (1, 0, 1, True),
        (2, 0, 2, True),
        (3, 0, -2, True),
        (3, 1, 3, True),
        (4, 0, -1, True),
        (4, 1, -3, True),
        (4, 2, 4, True),
        (0, 1, 0, False),
        (6, 0, 1, False),
        (7, 0, 2, False),
    )
    flags = jnp.pad(pattern.astype(jnp.float32), ((0, 0), (0, LANES - pattern.shape[1])))
    embedded, payload = finish(
        items,
        sources,
        lengths,
        context,
        residual,
        sq4,
        norm_gain.reshape(1, -1),
        flags,
        [xl1s, l3xs, l4s, n4xs],
        hidden,
        size,
    )
    same_core = [list(range(c, ranks, CORES)) for c in range(CORES)]

    def spread(blocks):
        return lax.all_to_all(blocks, "dp", 0, 0, axis_index_groups=same_core, tiled=True)

    parts = score(spread(payload), queries, queries2, pattern.shape[1])
    recalled, log_total = combine(spread(parts), features)
    return embedded, recalled, log_total


def gathered(context, residual, out_proj, norm_gain, lengths, queries, pattern):
    tok_rows = context.shape[0]
    features = residual.shape[1]
    passages_here = lengths.shape[0]
    seq_len = tok_rows // passages_here
    query_rows = queries.shape[0]
    blocks = pattern.shape[1]
    ranks = lax.axis_size("dp")
    me = lax.axis_index("dp")
    branch = jnp.dot(
        context,
        lax.all_gather(out_proj, "dp", axis=1, tiled=True),
        preferred_element_type=jnp.float32,
    )
    hidden_sum = residual.astype(jnp.float32) + branch
    normed = (
        hidden_sum
        * lax.rsqrt(jnp.mean(hidden_sum * hidden_sum, axis=-1, keepdims=True) + 1e-05)
        * norm_gain
    )
    shaped = normed.reshape(passages_here, seq_len, features)
    valid_mask = (jnp.arange(seq_len)[None, :] < lengths[:, None]).astype(jnp.float32)
    pooled = jnp.sum(shaped * valid_mask[:, :, None], axis=1) / lengths.astype(jnp.float32)[:, None]
    embedded = pooled * lax.rsqrt(jnp.mean(pooled * pooled, axis=-1, keepdims=True) + 1e-06)
    emb_half = embedded.astype(jnp.bfloat16)
    temper = 1.0 / (0.02 * math.sqrt(features))
    contract = (((1,), (1,)), ((), ()))

    flags = jnp.pad(pattern.astype(jnp.bfloat16), ((0, 0), (0, LANES - blocks)))
    everyone = lax.all_gather(jnp.concatenate([emb_half, flags], axis=1), "dp", axis=0, tiled=True)
    emb_all = everyone[:, :features]
    flags_all = everyone[:, features : features + blocks].astype(jnp.float32)
    scores = lax.dot_general(emb_all, queries, contract, preferred_element_type=jnp.float32) * temper
    row_block = (me * query_rows + jnp.arange(query_rows)) // QB
    picks = (row_block[None, :] == jnp.arange(blocks)[:, None]).astype(jnp.float32)
    cand_mask = jnp.dot(flags_all, picks) > 0
    peak_part = jnp.max(jnp.where(cand_mask, scores, LOW), axis=1, keepdims=True)
    weights = jnp.where(cand_mask, jnp.exp(scores - peak_part), 0.0)
    total_part = jnp.sum(weights, axis=1, keepdims=True)
    mix_part = jnp.dot(weights.astype(jnp.bfloat16), queries, preferred_element_type=jnp.float32)

    passages = emb_all.shape[0]
    lane = jnp.arange(LANES)[None, :]
    tail = jnp.where(lane == 0, peak_part, jnp.where(lane == 1, total_part, 0.0))
    parts = jnp.concatenate([mix_part, tail], axis=1).reshape(ranks, passages // ranks, -1)
    parts = lax.all_to_all(parts, "dp", split_axis=0, concat_axis=0, tiled=True)
    mixes, peaks, sums = parts[:, :, :features], parts[:, :, features], parts[:, :, features + 1]
    peak_score = jnp.max(peaks, axis=0)
    factor = jnp.exp(peaks - peak_score[None, :])
    totals = jnp.sum(sums * factor, axis=0)
    recalled = jnp.sum(mixes * factor[:, :, None], axis=0) / totals[:, None]
    log_total = peak_score + jnp.log(totals)
    return (embedded, recalled, log_total)


def per_device(context, residual, out_proj, norm_gain, lengths, queries, pattern):
    fits = (
        lax.axis_size("dp") == CORES * len(CYCLE)
        and lax.axis_size("groups") == 2
        and lengths.shape[0] == 1
        and out_proj.shape[1] % LANES == 0
        and out_proj.shape[0] % (2 * LANES) == 0
        and context.shape[0] % STEP == 0
        and pattern.shape[1] <= LANES
    )
    form = on_cycle if fits else gathered
    return form(context, residual, out_proj, norm_gain, lengths, queries, pattern)


def solution(mesh):
    in_specs = (
        P(("groups", "dp"), None),
        P(("groups", "dp"), None),
        P(None, "dp"),
        P(),
        P(("groups", "dp")),
        P(("groups", "dp"), None),
        P(("groups", "dp"), None),
    )
    out_specs = (P(("groups", "dp"), None), P(("groups", "dp"), None), P(("groups", "dp")))
    return jax.shard_map(
        per_device, mesh=mesh, in_specs=in_specs, out_specs=out_specs, check_vma=False
    )
```

```python
import functools
import math

import jax
import jax.numpy as jnp
from jax import lax
from jax.experimental import pallas as pl
from jax.experimental.pallas import tpu as pltpu
from jax.sharding import PartitionSpec as P

QB = 256
LANES = 128
CORES = 2
STEP = 256
VMEM_BYTES = 12 << 20
LOW = -1e30
CYCLE = (0, 2, 4, 6, 7, 5, 3, 1)
VMEM_SPEC = pl.BlockSpec(memory_space=pltpu.VMEM)
SMALL = pl.CostEstimate(flops=1000, bytes_accessed=1000, transcendentals=0)


def column_block(distance, same_core):
    me = lax.axis_index("dp")
    core = lax.rem(me, CORES)
    chip = lax.div(me, CORES)
    z, y = lax.div(chip, 2), lax.rem(chip, 2)
    size = len(CYCLE)
    at = jnp.where(y == 0, z, size - 1 - z)
    core = core if same_core else 1 - core
    there = lax.rem(at + jnp.where(core == 0, size + distance, size - distance), size)
    chip = jnp.where(there < size // 2, 2 * there, 2 * (size - 1 - there) + 1)
    return chip * CORES + core


def columns(distance, same_core, width):
    return pl.ds(pl.multiple_of(column_block(distance, same_core) * width, width), width)


def half_slice(second, half):
    side = lax.axis_index("groups")
    return pl.ds(pl.multiple_of((1 - side if second else side) * half, half), half)


def add_squares(squares, at, total):
    square = total * total
    for lane in range(0, total.shape[1], LANES):
        squares[at, :] += square[:, lane : lane + LANES]


def half_kernel(whole, part):
    part[...] = whole[half_slice(False, part.shape[0]), :]


def own_half(whole):
    rows, width = whole.shape
    return pl.pallas_call(
        half_kernel,
        out_shape=jax.ShapeDtypeStruct((rows // 2, width), whole.dtype),
        in_specs=[VMEM_SPEC],
        out_specs=VMEM_SPEC,
        compiler_params=pltpu.CompilerParams(vmem_limit_bytes=VMEM_BYTES),
    )(whole)


def row_steps(rows):
    def loop(body):
        @pl.loop(0, rows // STEP)
        def _(k):
            body(pl.ds(pl.multiple_of(k * STEP, STEP), STEP))

    return loop


def product(tokens, at, pieces):
    total = None
    for piece, second in pieces:
        half = piece.shape[0]
        term = jnp.dot(tokens[at, half_slice(second, half)], piece[...], preferred_element_type=jnp.float32)
        total = term if total is None else total + term
    return total


def wave_kernel(full, part, arrived, whole, tokens, chained, stacked, *refs):
    count = len(full) + len(part)
    refs = list(refs)
    context = refs.pop(0) if "mine" in tokens else None
    other_context = refs.pop(0) if "theirs" in tokens else None
    residual = refs.pop(0) if "mine" in tokens else None
    if whole:
        shard = refs.pop(0)
        half = shard.shape[0] // 2
        jobs = [[(shard.at[half_slice(second, half)], second) for second in (False, True)]]
    else:
        jobs = [[(refs.pop(0), False)] + ([(refs.pop(0), True)] if j < len(full) else []) for j in range(count)]
    received = [refs.pop(0) for _ in arrived]
    before = refs.pop(0) if chained else None
    mine = refs.pop(0) if "mine" in tokens else None
    theirs = None
    if "theirs" in tokens:
        stacks = [refs.pop(0) for _ in range(2 if stacked else count)]
        theirs = stacks
        if stacked:
            theirs = [stacks[0].at[j] for j in range(len(full))] + [stacks[1].at[j] for j in range(len(part))]
    finished = refs.pop(0) if arrived else None
    squares = refs.pop(0) if "mine" in tokens else None
    rows, width = mine.shape[1:] if "mine" in tokens else theirs[0].shape
    if chained:
        squares[...] = before[...]
    elif "mine" in tokens:
        squares[...] = jnp.zeros_like(squares)
    for j, distance in enumerate(full + part):

        @row_steps(rows)
        def _(at):
            if "theirs" in tokens:
                theirs[j][at, :] = product(other_context, at, jobs[j])
            if "mine" in tokens:
                total = product(context, at, jobs[j])
                total += residual[at, columns(distance, True, width)].astype(jnp.float32)
                mine[j, at, :] = total
                if j < len(full):
                    add_squares(squares, at, total)

    for j, (distance, same) in enumerate(arrived):

        @row_steps(rows)
        def _(at):
            total = received[j][at, :] + residual[at, columns(distance, same, width)].astype(jnp.float32)
            finished[j, at, :] = total
            add_squares(squares, at, total)


def wave(
    full, part, arrived, context, other_context, residual, pieces, received=None, squares=None, stacked=False
):
    tokens = (("mine",) if context is not None else ()) + (("theirs",) if other_context is not None else ())
    count = len(full) + len(part)
    rows = (context if other_context is None else other_context).shape[0]
    whole = len(pieces) == 1
    block = jax.ShapeDtypeStruct((rows, pieces[0].shape[1]), jnp.float32)

    def stack(n):
        return jax.ShapeDtypeStruct((n,) + block.shape, jnp.float32)

    outs = [stack(count)] if "mine" in tokens else []
    if "theirs" in tokens:
        outs += [stack(len(full)), stack(len(part))] if stacked else [block] * count
    operands = [x for x in (context, other_context) if x is not None]
    operands += ([residual] if "mine" in tokens else []) + list(pieces)
    if arrived:
        operands += [*received] + ([] if squares is None else [squares])
        outs.append(jax.ShapeDtypeStruct((len(arrived),) + block.shape, jnp.float32))
    if "mine" in tokens:
        outs.append(jax.ShapeDtypeStruct((rows, LANES), jnp.float32))
    return pl.pallas_call(
        functools.partial(wave_kernel, full, part, arrived, whole, tokens, squares is not None, stacked),
        out_shape=outs,
        in_specs=[VMEM_SPEC] * len(operands),
        out_specs=[VMEM_SPEC] * len(outs),
        compiler_params=pltpu.CompilerParams(vmem_limit_bytes=VMEM_BYTES),
        cost_estimate=SMALL,
    )(*operands)


def late_blocks(items, context, residual, pieces, hidden, squares, target):
    rows, width = target.shape[1:]
    for i, (base, parts, bare, distance, same) in enumerate(items):

        @row_steps(rows)
        def _(at):
            value = product(context, at, [(pieces[index], second) for index, second in parts])
            if base is not None:
                known = hidden[base[0]][(at,) if base[1] is None else (base[1], at)]
                value = known if value is None else value + known
            if bare:
                value += residual[at, columns(distance, same, width)].astype(jnp.float32)
            target[i, at, :] = value
            add_squares(squares, at, value)


def late_kernel(items, n_pieces, context, residual, before, *refs):
    pieces, hidden = refs[:n_pieces], refs[n_pieces:-2]
    finished, squares = refs[-2:]
    squares[...] = before[...]
    late_blocks(items, context, residual, pieces, hidden, squares, finished)


def late(items, context, residual, squares, pieces, hidden):
    rows = context.shape[0]
    operands = [context, residual, squares, *pieces, *hidden]
    return pl.pallas_call(
        functools.partial(late_kernel, items, len(pieces)),
        out_shape=(
            jax.ShapeDtypeStruct((len(items), rows, pieces[0].shape[1]), jnp.float32),
            jax.ShapeDtypeStruct(squares.shape, jnp.float32),
        ),
        in_specs=[VMEM_SPEC] * len(operands),
        out_specs=(VMEM_SPEC, VMEM_SPEC),
        compiler_params=pltpu.CompilerParams(vmem_limit_bytes=VMEM_BYTES),
        cost_estimate=SMALL,
    )(*operands)


def final_kernel(items, sources, n_pieces, length, context, residual, before, gain, flags, *refs):
    pieces, hidden = refs[:n_pieces], refs[n_pieces:-6]
    embedded, payload, blocks, squares, scale_rows, sheet = refs[-6:]
    width = blocks.shape[2]
    features = embedded.shape[1]
    squares[...] = before[...]
    late_blocks(items, context, residual, pieces, hidden, squares, blocks)
    mean = jnp.sum(squares[...], axis=1, keepdims=True) * (1.0 / features)
    row = lax.broadcasted_iota(jnp.int32, mean.shape, 0)
    scale = jnp.where(row < length[0], lax.rsqrt(mean + 1e-05), 0.0)
    scale_rows[...] = jnp.broadcast_to(scale, scale_rows.shape)
    inverse = 1.0 / jnp.full((1, width), length[0], jnp.int32).astype(jnp.float32)
    done = [(blocks.at[i], distance, same) for i, (_, _, _, distance, same) in enumerate(items)]
    done += [(hidden[array].at[entry], distance, same) for array, entry, distance, same in sources]
    for block, distance, same in done:
        parts = [
            jnp.sum(block[:, lane : lane + LANES] * scale_rows[...], axis=0, keepdims=True)
            for lane in range(0, width, LANES)
        ]
        where = columns(distance, same, width)
        embedded[:, where] = jnp.concatenate(parts, axis=1) * gain[:, where] * inverse
    pooled = embedded[...]
    mean = jnp.sum(pooled * pooled, axis=1, keepdims=True) * (1.0 / features)
    embedded[...] = pooled * lax.rsqrt(mean + 1e-06)
    lines = features // LANES
    sheet[lines:, :] = jnp.zeros((sheet.shape[0] - lines, LANES), jnp.float32)
    for line in range(lines):
        sheet[line : line + 1, :] = embedded[:, line * LANES : (line + 1) * LANES]
    sheet[lines : lines + 1, :] = flags[...]
    rounded = sheet[...].astype(jnp.bfloat16)
    for rank in range(payload.shape[0]):
        payload[rank] = rounded


def finish(items, sources, lengths, context, residual, squares, gain, flags, pieces, hidden, ranks):
    rows = context.shape[0]
    width = pieces[0].shape[1]
    features = (len(items) + len(sources)) * width
    lines = -(-(features // LANES + 1) // 16) * 16
    operands = [context, residual, squares, gain, flags, *pieces, *hidden]
    return pl.pallas_call(
        functools.partial(final_kernel, items, sources, len(pieces)),
        out_shape=(
            jax.ShapeDtypeStruct((1, features), jnp.float32),
            jax.ShapeDtypeStruct((ranks, lines, LANES), jnp.bfloat16),
        ),
        in_specs=[pl.BlockSpec(memory_space=pltpu.SMEM)] + [VMEM_SPEC] * len(operands),
        out_specs=(VMEM_SPEC, VMEM_SPEC),
        scratch_shapes=[
            pltpu.VMEM((len(items), rows, width), jnp.float32),
            pltpu.VMEM((rows, LANES), jnp.float32),
            pltpu.VMEM((rows, LANES), jnp.float32),
            pltpu.VMEM((lines, LANES), jnp.float32),
        ],
        compiler_params=pltpu.CompilerParams(vmem_limit_bytes=VMEM_BYTES),
        cost_estimate=SMALL,
    )(lengths, *operands)


def score_kernel(lines, blocks, got, queries, other_queries, out, wide, emb, mix):
    me = lax.axis_index("dp")
    ranks = got.shape[0]
    count = queries.shape[0]
    wide[...] = got[...].astype(jnp.float32)
    for line in range(lines):
        emb[:, line * LANES : (line + 1) * LANES] = wide[:, line, :]
    half = emb[...].astype(jnp.bfloat16)
    flags = wide[:, lines, :].astype(jnp.bfloat16)
    temper = 1.0 / (0.02 * math.sqrt(lines * LANES))
    scores, masks = [], []
    for owner, rows in ((me, queries), (me + 1 - 2 * lax.rem(me, CORES), other_queries)):
        score = lax.dot_general(
            half, rows[...], (((1,), (1,)), ((), ())), preferred_element_type=jnp.float32
        )
        scores.append(score * temper)
        block = lax.broadcasted_iota(jnp.int32, (LANES, count), 0)
        row = owner * count + lax.broadcasted_iota(jnp.int32, (LANES, count), 1)
        pick = (row >= block * QB) & (row < block * QB + QB) & (block < blocks)
        pick = jnp.where(pick, 1.0, 0.0).astype(jnp.bfloat16)
        masks.append(jnp.dot(flags, pick, preferred_element_type=jnp.float32) > 0.5)
    peaks = [
        jnp.max(jnp.where(mask, score, LOW), axis=1, keepdims=True) for score, mask in zip(scores, masks)
    ]
    peak = jnp.maximum(*peaks)
    weights = [jnp.where(mask, jnp.exp(score - peak), 0.0) for score, mask in zip(scores, masks)]
    total = sum(jnp.sum(weight, axis=1, keepdims=True) for weight in weights)
    mix[...] = jnp.dot(
        weights[0].astype(jnp.bfloat16), queries[...], preferred_element_type=jnp.float32
    ) + jnp.dot(weights[1].astype(jnp.bfloat16), other_queries[...], preferred_element_type=jnp.float32)
    for line in range(lines):
        out[:, line, :] = mix[:, line * LANES : (line + 1) * LANES]
    lane = lax.broadcasted_iota(jnp.int32, (ranks, LANES), 1)
    out[:, lines, :] = jnp.where(lane == 0, peak, jnp.where(lane == 1, total, 0.0))
    for line in range(lines + 1, out.shape[1]):
        out[:, line, :] = jnp.zeros((ranks, LANES), jnp.float32)


def score(got, queries, other_queries, blocks):
    ranks = got.shape[0]
    features = queries.shape[1]
    lines = features // LANES
    return pl.pallas_call(
        functools.partial(score_kernel, lines, blocks),
        out_shape=jax.ShapeDtypeStruct((ranks, -(-(lines + 1) // 8) * 8, LANES), jnp.float32),
        in_specs=[pl.BlockSpec(memory_space=pltpu.VMEM)] * 3,
        out_specs=pl.BlockSpec(memory_space=pltpu.VMEM),
        scratch_shapes=[
            pltpu.VMEM(got.shape, jnp.float32),
            pltpu.VMEM((ranks, features), jnp.float32),
            pltpu.VMEM((ranks, features), jnp.float32),
        ],
        compiler_params=pltpu.CompilerParams(vmem_limit_bytes=VMEM_BYTES),
    )(got, queries, other_queries)


def combine_kernel(lines, got, recalled, log_total):
    stats = got[:, lines, :]
    peaks, sums = stats[:, 0:1], stats[:, 1:2]
    peak = jnp.max(peaks, axis=0, keepdims=True)
    factor = jnp.exp(peaks - peak)
    total = jnp.sum(sums * factor, axis=0, keepdims=True)
    mix = got[0, :lines, :] * factor[0:1, :]
    for rank in range(1, got.shape[0]):
        mix += got[rank, :lines, :] * factor[rank : rank + 1, :]
    mix = mix / total
    for line in range(lines):
        recalled[:, line * LANES : (line + 1) * LANES] = mix[line : line + 1, :]
    log_total[...] = peak + jnp.log(total)


def combine(got, features):
    recalled, log_total = pl.pallas_call(
        functools.partial(combine_kernel, features // LANES),
        out_shape=(
            jax.ShapeDtypeStruct((1, features), jnp.float32),
            jax.ShapeDtypeStruct((1, 1), jnp.float32),
        ),
        in_specs=[pl.BlockSpec(memory_space=pltpu.VMEM)],
        out_specs=(pl.BlockSpec(memory_space=pltpu.VMEM), pl.BlockSpec(memory_space=pltpu.VMEM)),
        compiler_params=pltpu.CompilerParams(vmem_limit_bytes=VMEM_BYTES),
    )(got)
    return recalled, log_total.reshape(1)


def on_cycle(context, residual, out_proj, norm_gain, lengths, queries, pattern):
    ranks = lax.axis_size("dp")
    size = ranks // CORES
    features = residual.shape[1]

    def ring(step):
        return [
            (CYCLE[r] * CORES + c, CYCLE[(r + step * (1 - 2 * c)) % size] * CORES + c)
            for r in range(size)
            for c in range(CORES)
        ]

    def from_next(piece):
        return lax.ppermute(piece, "dp", ring(-1))

    def from_last(piece):
        return lax.ppermute(piece, "dp", ring(1))

    def over_x(piece):
        return lax.ppermute(piece, "groups", [(0, 1), (1, 0)])

    def other_core(piece):
        return lax.ppermute(piece, "dp", [(i, i ^ 1) for i in range(ranks)])

    wait = lax.optimization_barrier

    own = own_half(out_proj)
    a = from_next(own)
    c, q = other_core(context), other_core(queries)
    (p0,) = wave((0,), (), (), None, context, None, [out_proj])
    own, p0 = wait((own, p0))
    b = from_last(own)

    n1, p0 = wait((a, p0))
    x = over_x(n1)
    a = from_next(n1)
    context2, n1 = wait((c, n1))
    (t0,) = wave((0,), (), (), None, context2, None, [out_proj])
    l1, n1, t0, queries2 = wait((b, n1, t0, q))
    b = from_last(l1)
    r0 = other_core(t0)

    n2, l1 = wait((a, l1))
    x2 = over_x(n2)
    a = from_next(n2)
    xn1, n2 = wait((x, n2))
    x = x2
    h1, t1, f0, sq1 = wave(
        (1,), (), ((0, True), (0, False)), context, context2, residual, [n1, xn1], [p0, r0], None
    )
    l2, n2, t1, sq1 = wait((b, n2, t1, sq1))
    b = from_last(l2)
    r1 = other_core(t1)

    xn2, l2 = wait((x, l2))
    x = over_x(l2)
    a2 = from_next(xn2)
    n3, xn2 = wait((a, xn2))
    h2, t2, t2p, f1, sq2 = wave((2,), (-1,), ((1, False),), context, context2, residual, [n2, xn2, l1], [r1], sq1)
    l3, n3, t2, t2p, sq2 = wait((b, n3, t2, t2p, sq2))
    b = from_last(l3)
    r2, r2p = other_core(t2), other_core(t2p)

    n3x, l3 = wait((a2, l3))
    a = from_next(n3x)
    xl2, l1, n3x = wait((x, l1, n3x))
    x = over_x(l1)
    h3, t3a, t3p, f2, sq3 = wave(
        (-2, 3), (-3,), ((2, False),), context, context2, residual, [l2, xl2, n3, n3x, l3], [r2], sq2, stacked=True
    )
    l4, xl2, t3a, t3p, sq3, r2p = wait((b, xl2, t3a, t3p, sq3, r2p))
    b = from_last(xl2)
    r3a, r3p = other_core(t3a), other_core(t3p)
    l4s = other_core(l4)

    n4x, l4 = wait((a, l4))
    n4xs = other_core(n4x)
    xl1, n4x = wait((x, n4x))
    xl1s = other_core(xl1)
    l3x, xl1 = wait((b, xl1))
    l3xs = other_core(l3x)

    missing = (((0, True),), ((1, True),), ((2, False), (3, True)))
    own_items = tuple(
        (base, parts, base is None, distance, True)
        for base, parts, distance in zip(((0, 1), (1, 2), None), missing, (-1, -3, 4))
    )
    h4, sq4 = late(own_items, context, residual, sq3, [xl1, l3x, l4, n4x], [h2, h3])
    items = tuple(
        (base, parts, True, distance, False)
        for base, parts, distance in zip(
            ((8, None), (9, 0), None, (10, 0), (10, 1)), missing + ((), ()), (-1, -3, 4, -2, 3)
        )
    )
    hidden = [f0, h1, h2, h3, h4, f0, f1, f2, r2p, r3p, r3a]
    sources = (
        (0, 0, 0, True),
        (1, 0, 1, True),
        (2, 0, 2, True),
        (3, 0, -2, True),
        (3, 1, 3, True),
        (4, 0, -1, True),
        (4, 1, -3, True),
        (4, 2, 4, True),
        (0, 1, 0, False),
        (6, 0, 1, False),
        (7, 0, 2, False),
    )
    flags = jnp.pad(pattern.astype(jnp.float32), ((0, 0), (0, LANES - pattern.shape[1])))
    embedded, payload = finish(
        items,
        sources,
        lengths,
        context,
        residual,
        sq4,
        norm_gain.reshape(1, -1),
        flags,
        [xl1s, l3xs, l4s, n4xs],
        hidden,
        size,
    )
    same_core = [list(range(c, ranks, CORES)) for c in range(CORES)]

    def spread(blocks):
        return lax.all_to_all(blocks, "dp", 0, 0, axis_index_groups=same_core, tiled=True)

    parts = score(spread(payload), queries, queries2, pattern.shape[1])
    recalled, log_total = combine(spread(parts), features)
    return embedded, recalled, log_total


def gathered(context, residual, out_proj, norm_gain, lengths, queries, pattern):
    tok_rows = context.shape[0]
    features = residual.shape[1]
    passages_here = lengths.shape[0]
    seq_len = tok_rows // passages_here
    query_rows = queries.shape[0]
    blocks = pattern.shape[1]
    ranks = lax.axis_size("dp")
    me = lax.axis_index("dp")
    branch = jnp.dot(
        context,
        lax.all_gather(out_proj, "dp", axis=1, tiled=True),
        preferred_element_type=jnp.float32,
    )
    hidden_sum = residual.astype(jnp.float32) + branch
    normed = (
        hidden_sum
        * lax.rsqrt(jnp.mean(hidden_sum * hidden_sum, axis=-1, keepdims=True) + 1e-05)
        * norm_gain
    )
    shaped = normed.reshape(passages_here, seq_len, features)
    valid_mask = (jnp.arange(seq_len)[None, :] < lengths[:, None]).astype(jnp.float32)
    pooled = jnp.sum(shaped * valid_mask[:, :, None], axis=1) / lengths.astype(jnp.float32)[:, None]
    embedded = pooled * lax.rsqrt(jnp.mean(pooled * pooled, axis=-1, keepdims=True) + 1e-06)
    emb_half = embedded.astype(jnp.bfloat16)
    temper = 1.0 / (0.02 * math.sqrt(features))
    contract = (((1,), (1,)), ((), ()))

    flags = jnp.pad(pattern.astype(jnp.bfloat16), ((0, 0), (0, LANES - blocks)))
    everyone = lax.all_gather(jnp.concatenate([emb_half, flags], axis=1), "dp", axis=0, tiled=True)
    emb_all = everyone[:, :features]
    flags_all = everyone[:, features : features + blocks].astype(jnp.float32)
    scores = lax.dot_general(emb_all, queries, contract, preferred_element_type=jnp.float32) * temper
    row_block = (me * query_rows + jnp.arange(query_rows)) // QB
    picks = (row_block[None, :] == jnp.arange(blocks)[:, None]).astype(jnp.float32)
    cand_mask = jnp.dot(flags_all, picks) > 0
    peak_part = jnp.max(jnp.where(cand_mask, scores, LOW), axis=1, keepdims=True)
    weights = jnp.where(cand_mask, jnp.exp(scores - peak_part), 0.0)
    total_part = jnp.sum(weights, axis=1, keepdims=True)
    mix_part = jnp.dot(weights.astype(jnp.bfloat16), queries, preferred_element_type=jnp.float32)

    passages = emb_all.shape[0]
    lane = jnp.arange(LANES)[None, :]
    tail = jnp.where(lane == 0, peak_part, jnp.where(lane == 1, total_part, 0.0))
    parts = jnp.concatenate([mix_part, tail], axis=1).reshape(ranks, passages // ranks, -1)
    parts = lax.all_to_all(parts, "dp", split_axis=0, concat_axis=0, tiled=True)
    mixes, peaks, sums = parts[:, :, :features], parts[:, :, features], parts[:, :, features + 1]
    peak_score = jnp.max(peaks, axis=0)
    factor = jnp.exp(peaks - peak_score[None, :])
    totals = jnp.sum(sums * factor, axis=0)
    recalled = jnp.sum(mixes * factor[:, :, None], axis=0) / totals[:, None]
    log_total = peak_score + jnp.log(totals)
    return (embedded, recalled, log_total)


def per_device(context, residual, out_proj, norm_gain, lengths, queries, pattern):
    fits = (
        lax.axis_size("dp") == CORES * len(CYCLE)
        and lax.axis_size("groups") == 2
        and lengths.shape[0] == 1
        and out_proj.shape[1] % LANES == 0
        and out_proj.shape[0] % (2 * LANES) == 0
        and context.shape[0] % STEP == 0
        and pattern.shape[1] <= LANES
    )
    form = on_cycle if fits else gathered
    return form(context, residual, out_proj, norm_gain, lengths, queries, pattern)


def solution(mesh):
    in_specs = (
        P(("groups", "dp"), None),
        P(("groups", "dp"), None),
        P(None, "dp"),
        P(),
        P(("groups", "dp")),
        P(("groups", "dp"), None),
        P(("groups", "dp"), None),
    )
    out_specs = (P(("groups", "dp"), None), P(("groups", "dp"), None), P(("groups", "dp")))
    return jax.shard_map(
        per_device, mesh=mesh, in_specs=in_specs, out_specs=out_specs, check_vma=False
    )
```

```python
import functools
import math

import jax
import jax.numpy as jnp
from jax import lax
from jax.experimental import pallas as pl
from jax.experimental.pallas import tpu as pltpu
from jax.sharding import PartitionSpec as P

QB = 256
LANES = 128
CORES = 2
STEP = 256
VMEM_BYTES = 12 << 20
LOW = -1e30
CYCLE = (0, 2, 4, 6, 7, 5, 3, 1)
VMEM_SPEC = pl.BlockSpec(memory_space=pltpu.VMEM)
SMALL = pl.CostEstimate(flops=1000, bytes_accessed=1000, transcendentals=0)


def column_block(distance, same_core):
    me = lax.axis_index("dp")
    core = lax.rem(me, CORES)
    chip = lax.div(me, CORES)
    z, y = lax.div(chip, 2), lax.rem(chip, 2)
    size = len(CYCLE)
    at = jnp.where(y == 0, z, size - 1 - z)
    core = core if same_core else 1 - core
    there = lax.rem(at + jnp.where(core == 0, size + distance, size - distance), size)
    chip = jnp.where(there < size // 2, 2 * there, 2 * (size - 1 - there) + 1)
    return chip * CORES + core


def columns(distance, same_core, width):
    return pl.ds(pl.multiple_of(column_block(distance, same_core) * width, width), width)


def half_slice(second, half):
    side = lax.axis_index("groups")
    return pl.ds(pl.multiple_of((1 - side if second else side) * half, half), half)


def add_squares(squares, at, total):
    square = total * total
    for lane in range(0, total.shape[1], LANES):
        squares[at, :] += square[:, lane : lane + LANES]


def half_kernel(whole, part):
    part[...] = whole[half_slice(False, part.shape[0]), :]


def own_half(whole):
    rows, width = whole.shape
    return pl.pallas_call(
        half_kernel,
        out_shape=jax.ShapeDtypeStruct((rows // 2, width), whole.dtype),
        in_specs=[VMEM_SPEC],
        out_specs=VMEM_SPEC,
        compiler_params=pltpu.CompilerParams(vmem_limit_bytes=VMEM_BYTES),
    )(whole)


def row_steps(rows):
    def loop(body):
        @pl.loop(0, rows // STEP)
        def _(k):
            body(pl.ds(pl.multiple_of(k * STEP, STEP), STEP))

    return loop


def product(tokens, at, pieces):
    total = None
    for piece, second in pieces:
        half = piece.shape[0]
        term = jnp.dot(tokens[at, half_slice(second, half)], piece[...], preferred_element_type=jnp.float32)
        total = term if total is None else total + term
    return total


def wave_kernel(full, part, arrived, whole, tokens, chained, stacked, *refs):
    count = len(full) + len(part)
    refs = list(refs)
    context = refs.pop(0) if "mine" in tokens else None
    other_context = refs.pop(0) if "theirs" in tokens else None
    residual = refs.pop(0) if "mine" in tokens else None
    if whole:
        shard = refs.pop(0)
        half = shard.shape[0] // 2
        jobs = [[(shard.at[half_slice(second, half)], second) for second in (False, True)]]
    else:
        jobs = [[(refs.pop(0), False)] + ([(refs.pop(0), True)] if j < len(full) else []) for j in range(count)]
    received = [refs.pop(0) for _ in arrived]
    before = refs.pop(0) if chained else None
    mine = refs.pop(0) if "mine" in tokens else None
    theirs = None
    if "theirs" in tokens:
        stacks = [refs.pop(0) for _ in range(2 if stacked else count)]
        theirs = stacks
        if stacked:
            theirs = [stacks[0].at[j] for j in range(len(full))] + [stacks[1].at[j] for j in range(len(part))]
    finished = refs.pop(0) if arrived else None
    squares = refs.pop(0) if "mine" in tokens else None
    rows, width = mine.shape[1:] if "mine" in tokens else theirs[0].shape
    if chained:
        squares[...] = before[...]
    elif "mine" in tokens:
        squares[...] = jnp.zeros_like(squares)
    for j, distance in enumerate(full + part):

        @row_steps(rows)
        def _(at):
            if "theirs" in tokens:
                theirs[j][at, :] = product(other_context, at, jobs[j])
            if "mine" in tokens:
                total = product(context, at, jobs[j])
                total += residual[at, columns(distance, True, width)].astype(jnp.float32)
                mine[j, at, :] = total
                if j < len(full):
                    add_squares(squares, at, total)

    for j, (distance, same) in enumerate(arrived):

        @row_steps(rows)
        def _(at):
            total = received[j][at, :] + residual[at, columns(distance, same, width)].astype(jnp.float32)
            finished[j, at, :] = total
            add_squares(squares, at, total)


def wave(
    full, part, arrived, context, other_context, residual, pieces, received=None, squares=None, stacked=False
):
    tokens = (("mine",) if context is not None else ()) + (("theirs",) if other_context is not None else ())
    count = len(full) + len(part)
    rows = (context if other_context is None else other_context).shape[0]
    whole = len(pieces) == 1
    block = jax.ShapeDtypeStruct((rows, pieces[0].shape[1]), jnp.float32)

    def stack(n):
        return jax.ShapeDtypeStruct((n,) + block.shape, jnp.float32)

    outs = [stack(count)] if "mine" in tokens else []
    if "theirs" in tokens:
        outs += [stack(len(full)), stack(len(part))] if stacked else [block] * count
    operands = [x for x in (context, other_context) if x is not None]
    operands += ([residual] if "mine" in tokens else []) + list(pieces)
    if arrived:
        operands += [*received] + ([] if squares is None else [squares])
        outs.append(jax.ShapeDtypeStruct((len(arrived),) + block.shape, jnp.float32))
    if "mine" in tokens:
        outs.append(jax.ShapeDtypeStruct((rows, LANES), jnp.float32))
    return pl.pallas_call(
        functools.partial(wave_kernel, full, part, arrived, whole, tokens, squares is not None, stacked),
        out_shape=outs,
        in_specs=[VMEM_SPEC] * len(operands),
        out_specs=[VMEM_SPEC] * len(outs),
        compiler_params=pltpu.CompilerParams(vmem_limit_bytes=VMEM_BYTES),
        cost_estimate=SMALL,
    )(*operands)


def late_blocks(items, context, residual, pieces, hidden, squares, target):
    rows, width = target.shape[1:]
    for i, (base, parts, bare, distance, same) in enumerate(items):

        @row_steps(rows)
        def _(at):
            value = product(context, at, [(pieces[index], second) for index, second in parts])
            if base is not None:
                known = hidden[base[0]][(at,) if base[1] is None else (base[1], at)]
                value = known if value is None else value + known
            if bare:
                value += residual[at, columns(distance, same, width)].astype(jnp.float32)
            target[i, at, :] = value
            add_squares(squares, at, value)


def late_kernel(items, n_pieces, context, residual, before, *refs):
    pieces, hidden = refs[:n_pieces], refs[n_pieces:-2]
    finished, squares = refs[-2:]
    squares[...] = before[...]
    late_blocks(items, context, residual, pieces, hidden, squares, finished)


def late(items, context, residual, squares, pieces, hidden):
    rows = context.shape[0]
    operands = [context, residual, squares, *pieces, *hidden]
    return pl.pallas_call(
        functools.partial(late_kernel, items, len(pieces)),
        out_shape=(
            jax.ShapeDtypeStruct((len(items), rows, pieces[0].shape[1]), jnp.float32),
            jax.ShapeDtypeStruct(squares.shape, jnp.float32),
        ),
        in_specs=[VMEM_SPEC] * len(operands),
        out_specs=(VMEM_SPEC, VMEM_SPEC),
        compiler_params=pltpu.CompilerParams(vmem_limit_bytes=VMEM_BYTES),
        cost_estimate=SMALL,
    )(*operands)


def final_kernel(items, sources, n_pieces, context, residual, before, gain, flags, *refs):
    pieces, hidden = refs[:n_pieces], refs[n_pieces:-6]
    embedded, payload, blocks, squares, scale_rows, sheet = refs[-6:]
    width = blocks.shape[2]
    features = embedded.shape[1]
    squares[...] = before[...]
    late_blocks(items, context, residual, pieces, hidden, squares, blocks)
    mean = jnp.sum(squares[...], axis=1, keepdims=True) * (1.0 / features)
    length = flags[:, LANES - 1 : LANES]
    row = lax.broadcasted_iota(jnp.int32, mean.shape, 0).astype(jnp.float32)
    scale = jnp.where(row < length, lax.rsqrt(mean + 1e-05), 0.0)
    scale_rows[...] = jnp.broadcast_to(scale, scale_rows.shape)
    inverse = 1.0 / length
    done = [(blocks.at[i], distance, same) for i, (_, _, _, distance, same) in enumerate(items)]
    done += [(hidden[array].at[entry], distance, same) for array, entry, distance, same in sources]
    for block, distance, same in done:
        parts = [
            jnp.sum(block[:, lane : lane + LANES] * scale_rows[...], axis=0, keepdims=True)
            for lane in range(0, width, LANES)
        ]
        where = columns(distance, same, width)
        embedded[:, where] = jnp.concatenate(parts, axis=1) * gain[:, where] * inverse
    pooled = embedded[...]
    mean = jnp.sum(pooled * pooled, axis=1, keepdims=True) * (1.0 / features)
    embedded[...] = pooled * lax.rsqrt(mean + 1e-06)
    lines = features // LANES
    sheet[lines:, :] = jnp.zeros((sheet.shape[0] - lines, LANES), jnp.float32)
    for line in range(lines):
        sheet[line : line + 1, :] = embedded[:, line * LANES : (line + 1) * LANES]
    sheet[lines : lines + 1, :] = flags[...]
    payload[...] = sheet[...].astype(jnp.bfloat16)


def finish(items, sources, context, residual, squares, gain, flags, pieces, hidden):
    rows = context.shape[0]
    width = pieces[0].shape[1]
    features = (len(items) + len(sources)) * width
    lines = -(-(features // LANES + 1) // 16) * 16
    operands = [context, residual, squares, gain, flags, *pieces, *hidden]
    return pl.pallas_call(
        functools.partial(final_kernel, items, sources, len(pieces)),
        out_shape=(
            jax.ShapeDtypeStruct((1, features), jnp.float32),
            jax.ShapeDtypeStruct((lines, LANES), jnp.bfloat16),
        ),
        in_specs=[VMEM_SPEC] * len(operands),
        out_specs=(VMEM_SPEC, VMEM_SPEC),
        scratch_shapes=[
            pltpu.VMEM((len(items), rows, width), jnp.float32),
            pltpu.VMEM((rows, LANES), jnp.float32),
            pltpu.VMEM((rows, LANES), jnp.float32),
            pltpu.VMEM((lines, LANES), jnp.float32),
        ],
        compiler_params=pltpu.CompilerParams(vmem_limit_bytes=VMEM_BYTES),
        cost_estimate=SMALL,
    )(*operands)


def score_kernel(lines, blocks, lists, *refs):
    got, (queries, other_queries), outs = refs[:lists], refs[lists : lists + 2], refs[lists + 2 : 2 * lists + 2]
    wide, emb, mix = refs[2 * lists + 2 :]
    me = lax.axis_index("dp")
    each = got[0].shape[0]
    count = queries.shape[0]
    for i in range(lists):
        wide[i * each : (i + 1) * each] = got[i][...].astype(jnp.float32)
    for line in range(lines):
        emb[:, line * LANES : (line + 1) * LANES] = wide[:, line, :]
    half = emb[...].astype(jnp.bfloat16)
    flags = wide[:, lines, :].astype(jnp.bfloat16)
    temper = 1.0 / (0.02 * math.sqrt(lines * LANES))
    scores, masks = [], []
    for owner, rows in ((me, queries), (me + 1 - 2 * lax.rem(me, CORES), other_queries)):
        score = lax.dot_general(
            half, rows[...], (((1,), (1,)), ((), ())), preferred_element_type=jnp.float32
        )
        scores.append(score * temper)
        block = lax.broadcasted_iota(jnp.int32, (LANES, count), 0)
        row = owner * count + lax.broadcasted_iota(jnp.int32, (LANES, count), 1)
        pick = (row >= block * QB) & (row < block * QB + QB) & (block < blocks)
        pick = jnp.where(pick, 1.0, 0.0).astype(jnp.bfloat16)
        masks.append(jnp.dot(flags, pick, preferred_element_type=jnp.float32) > 0.5)
    peaks = [
        jnp.max(jnp.where(mask, score, LOW), axis=1, keepdims=True) for score, mask in zip(scores, masks)
    ]
    peak = jnp.maximum(*peaks)
    weights = [jnp.where(mask, jnp.exp(score - peak), 0.0) for score, mask in zip(scores, masks)]
    total = sum(jnp.sum(weight, axis=1, keepdims=True) for weight in weights)
    mix[...] = jnp.dot(
        weights[0].astype(jnp.bfloat16), queries[...], preferred_element_type=jnp.float32
    ) + jnp.dot(weights[1].astype(jnp.bfloat16), other_queries[...], preferred_element_type=jnp.float32)
    lane = lax.broadcasted_iota(jnp.int32, (lists * each, LANES), 1)
    stats = jnp.where(lane == 0, peak, jnp.where(lane == 1, total, 0.0))
    for i in range(lists):
        here = slice(i * each, (i + 1) * each)
        for line in range(lines):
            outs[i][:, line, :] = mix[here, line * LANES : (line + 1) * LANES]
        outs[i][:, lines, :] = stats[here, :]
        for line in range(lines + 1, outs[i].shape[1]):
            outs[i][:, line, :] = jnp.zeros((each, LANES), jnp.float32)


def score(got, queries, other_queries, blocks):
    lists, each = len(got), got[0].shape[0]
    features = queries.shape[1]
    lines = features // LANES
    out = jax.ShapeDtypeStruct((each, -(-(lines + 1) // 8) * 8, LANES), jnp.float32)
    return pl.pallas_call(
        functools.partial(score_kernel, lines, blocks, lists),
        out_shape=[out] * lists,
        in_specs=[VMEM_SPEC] * (lists + 2),
        out_specs=[VMEM_SPEC] * lists,
        scratch_shapes=[
            pltpu.VMEM((lists * each,) + got[0].shape[1:], jnp.float32),
            pltpu.VMEM((lists * each, features), jnp.float32),
            pltpu.VMEM((lists * each, features), jnp.float32),
        ],
        compiler_params=pltpu.CompilerParams(vmem_limit_bytes=VMEM_BYTES),
    )(*got, queries, other_queries)


def joined(parts, lines):
    peaks = [part[lines : lines + 1, 0:1] for part in parts]
    peak = functools.reduce(jnp.maximum, peaks)
    factors = [jnp.exp(own - peak) for own in peaks]
    mix = sum(part[:lines, :] * factor for part, factor in zip(parts, factors))
    total = sum(part[lines : lines + 1, 1:2] * factor for part, factor in zip(parts, factors))
    return mix, peak, total


def join_kernel(lines, lists, *refs):
    for j, out in enumerate(refs[lists:]):
        mix, peak, total = joined([ref[j] for ref in refs[:lists]], lines)
        out[:lines, :] = mix
        lane = lax.broadcasted_iota(jnp.int32, (out.shape[0] - lines, LANES), 1)
        out[lines:, :] = jnp.where(lane == 0, peak, jnp.where(lane == 1, total, 0.0))


def join(parts, features):
    out = jax.ShapeDtypeStruct(parts[0].shape[1:], jnp.float32)
    return pl.pallas_call(
        functools.partial(join_kernel, features // LANES, len(parts)),
        out_shape=[out] * parts[0].shape[0],
        in_specs=[VMEM_SPEC] * len(parts),
        out_specs=[VMEM_SPEC] * parts[0].shape[0],
        compiler_params=pltpu.CompilerParams(vmem_limit_bytes=VMEM_BYTES),
    )(*parts)


def combine_kernel(lines, first, second, recalled, log_total):
    mix, peak, total = joined([first[...], second[...]], lines)
    mix = mix / total
    for line in range(lines):
        recalled[:, line * LANES : (line + 1) * LANES] = mix[line : line + 1, :]
    log_total[...] = peak + jnp.log(total)


def combine(first, second, features):
    recalled, log_total = pl.pallas_call(
        functools.partial(combine_kernel, features // LANES),
        out_shape=(
            jax.ShapeDtypeStruct((1, features), jnp.float32),
            jax.ShapeDtypeStruct((1, 1), jnp.float32),
        ),
        in_specs=[VMEM_SPEC] * 2,
        out_specs=(VMEM_SPEC, VMEM_SPEC),
        compiler_params=pltpu.CompilerParams(vmem_limit_bytes=VMEM_BYTES),
    )(first, second)
    return recalled, log_total.reshape(1)


def on_cycle(context, residual, out_proj, norm_gain, lengths, queries, pattern):
    ranks = lax.axis_size("dp")
    size = ranks // CORES
    features = residual.shape[1]

    def ring(step):
        return [
            (CYCLE[r] * CORES + c, CYCLE[(r + step * (1 - 2 * c)) % size] * CORES + c)
            for r in range(size)
            for c in range(CORES)
        ]

    def from_next(piece):
        return lax.ppermute(piece, "dp", ring(-1))

    def from_last(piece):
        return lax.ppermute(piece, "dp", ring(1))

    def over_x(piece):
        return lax.ppermute(piece, "groups", [(0, 1), (1, 0)])

    def other_core(piece):
        return lax.ppermute(piece, "dp", [(i, i ^ 1) for i in range(ranks)])

    wait = lax.optimization_barrier

    own = own_half(out_proj)
    a = from_next(own)
    c, q = other_core(context), other_core(queries)
    (p0,) = wave((0,), (), (), None, context, None, [out_proj])
    own, p0 = wait((own, p0))
    b = from_last(own)

    n1, p0 = wait((a, p0))
    x = over_x(n1)
    a = from_next(n1)
    context2, n1 = wait((c, n1))
    (t0,) = wave((0,), (), (), None, context2, None, [out_proj])
    l1, n1, t0, queries2 = wait((b, n1, t0, q))
    b = from_last(l1)
    r0 = other_core(t0)

    n2, l1 = wait((a, l1))
    x2 = over_x(n2)
    a = from_next(n2)
    xn1, n2 = wait((x, n2))
    x = x2
    h1, t1, f0, sq1 = wave(
        (1,), (), ((0, True), (0, False)), context, context2, residual, [n1, xn1], [p0, r0], None
    )
    l2, n2, t1, sq1 = wait((b, n2, t1, sq1))
    b = from_last(l2)
    r1 = other_core(t1)

    xn2, l2 = wait((x, l2))
    x = over_x(l2)
    a2 = from_next(xn2)
    n3, xn2 = wait((a, xn2))
    h2, t2, t2p, f1, sq2 = wave((2,), (-1,), ((1, False),), context, context2, residual, [n2, xn2, l1], [r1], sq1)
    l3, n3, t2, t2p, sq2 = wait((b, n3, t2, t2p, sq2))
    b = from_last(l3)
    r2, r2p = other_core(t2), other_core(t2p)

    n3x, l3 = wait((a2, l3))
    a = from_next(n3x)
    xl2, l1, n3x = wait((x, l1, n3x))
    x = over_x(l1)
    h3, t3a, t3p, f2, sq3 = wave(
        (-2, 3), (-3,), ((2, False),), context, context2, residual, [l2, xl2, n3, n3x, l3], [r2], sq2, stacked=True
    )
    l4, xl2, t3a, t3p, sq3, r2p = wait((b, xl2, t3a, t3p, sq3, r2p))
    b = from_last(xl2)
    r3a, r3p = other_core(t3a), other_core(t3p)
    l4s = other_core(l4)

    n4x, l4 = wait((a, l4))
    n4xs = other_core(n4x)
    items = ((None, ((0, False), (1, True)), True, 4, True),)
    h4, sq4 = late(items, context, residual, sq3, [l4, n4x], [])
    xl1, n4x, sq4 = wait((x, n4x, sq4))
    xl1s = other_core(xl1)
    items = (((0, 1), ((0, True),), False, -1, True),)
    h5, sq5 = late(items, context, residual, sq4, [xl1], [h2])
    l3x, xl1, sq5 = wait((b, xl1, sq5))
    l3xs = other_core(l3x)
    items = (
        ((0, 2), ((0, True),), False, -3, True),
        ((1, 0), (), True, -2, False),
        ((1, 1), (), True, 3, False),
        (None, ((1, False), (2, True)), True, 4, False),
    )
    h6, sq6 = late(items, context, residual, sq5, [l3x, l4s, n4xs], [h3, r3a])
    items = (((0, None), ((0, True),), True, -1, False), ((1, 0), ((1, True),), True, -3, False))
    hidden = [r2p, r3p, h1, h2, h3, h4, h5, h6, f0, f1, f2]
    sources = (
        (2, 0, 1, True),
        (3, 0, 2, True),
        (4, 0, -2, True),
        (4, 1, 3, True),
        (5, 0, 4, True),
        (6, 0, -1, True),
        (8, 0, 0, True),
        (8, 1, 0, False),
        (9, 0, 1, False),
        (10, 0, 2, False),
        (7, 0, -3, True),
        (7, 1, -2, False),
        (7, 2, 3, False),
        (7, 3, 4, False),
    )
    flags = jnp.pad(pattern.astype(jnp.float32), ((0, 0), (0, LANES - 1 - pattern.shape[1])))
    flags = jnp.concatenate([flags, lengths.astype(jnp.float32)[:, None]], axis=1)
    embedded, payload = finish(
        items, sources, context, residual, sq6, norm_gain.reshape(1, -1), flags, [xl1s, l3xs], hidden
    )

    line_z = size // 2

    def along_z(block, k):
        return lax.ppermute(block, "dp", [(i, (i + k * 2 * CORES) % ranks) for i in range(ranks)])

    def over_y(block):
        return lax.ppermute(block, "dp", [(i, i ^ CORES) for i in range(ranks)])

    both = jnp.stack([payload, over_y(payload)])
    got = [both] + [along_z(both, k) for k in range(1, line_z)]
    parts = score(got, queries, queries2, pattern.shape[1])
    parts = [parts[0]] + [along_z(parts[k], -k) for k in range(1, line_z)]
    mine, theirs = join(parts, features)
    recalled, log_total = combine(mine, over_y(theirs), features)
    return embedded, recalled, log_total


def gathered(context, residual, out_proj, norm_gain, lengths, queries, pattern):
    tok_rows = context.shape[0]
    features = residual.shape[1]
    passages_here = lengths.shape[0]
    seq_len = tok_rows // passages_here
    query_rows = queries.shape[0]
    blocks = pattern.shape[1]
    ranks = lax.axis_size("dp")
    me = lax.axis_index("dp")
    branch = jnp.dot(
        context,
        lax.all_gather(out_proj, "dp", axis=1, tiled=True),
        preferred_element_type=jnp.float32,
    )
    hidden_sum = residual.astype(jnp.float32) + branch
    normed = (
        hidden_sum
        * lax.rsqrt(jnp.mean(hidden_sum * hidden_sum, axis=-1, keepdims=True) + 1e-05)
        * norm_gain
    )
    shaped = normed.reshape(passages_here, seq_len, features)
    valid_mask = (jnp.arange(seq_len)[None, :] < lengths[:, None]).astype(jnp.float32)
    pooled = jnp.sum(shaped * valid_mask[:, :, None], axis=1) / lengths.astype(jnp.float32)[:, None]
    embedded = pooled * lax.rsqrt(jnp.mean(pooled * pooled, axis=-1, keepdims=True) + 1e-06)
    emb_half = embedded.astype(jnp.bfloat16)
    temper = 1.0 / (0.02 * math.sqrt(features))
    contract = (((1,), (1,)), ((), ()))

    flags = jnp.pad(pattern.astype(jnp.bfloat16), ((0, 0), (0, LANES - blocks)))
    everyone = lax.all_gather(jnp.concatenate([emb_half, flags], axis=1), "dp", axis=0, tiled=True)
    emb_all = everyone[:, :features]
    flags_all = everyone[:, features : features + blocks].astype(jnp.float32)
    scores = lax.dot_general(emb_all, queries, contract, preferred_element_type=jnp.float32) * temper
    row_block = (me * query_rows + jnp.arange(query_rows)) // QB
    picks = (row_block[None, :] == jnp.arange(blocks)[:, None]).astype(jnp.float32)
    cand_mask = jnp.dot(flags_all, picks) > 0
    peak_part = jnp.max(jnp.where(cand_mask, scores, LOW), axis=1, keepdims=True)
    weights = jnp.where(cand_mask, jnp.exp(scores - peak_part), 0.0)
    total_part = jnp.sum(weights, axis=1, keepdims=True)
    mix_part = jnp.dot(weights.astype(jnp.bfloat16), queries, preferred_element_type=jnp.float32)

    passages = emb_all.shape[0]
    lane = jnp.arange(LANES)[None, :]
    tail = jnp.where(lane == 0, peak_part, jnp.where(lane == 1, total_part, 0.0))
    parts = jnp.concatenate([mix_part, tail], axis=1).reshape(ranks, passages // ranks, -1)
    parts = lax.all_to_all(parts, "dp", split_axis=0, concat_axis=0, tiled=True)
    mixes, peaks, sums = parts[:, :, :features], parts[:, :, features], parts[:, :, features + 1]
    peak_score = jnp.max(peaks, axis=0)
    factor = jnp.exp(peaks - peak_score[None, :])
    totals = jnp.sum(sums * factor, axis=0)
    recalled = jnp.sum(mixes * factor[:, :, None], axis=0) / totals[:, None]
    log_total = peak_score + jnp.log(totals)
    return (embedded, recalled, log_total)


def per_device(context, residual, out_proj, norm_gain, lengths, queries, pattern):
    fits = (
        lax.axis_size("dp") == CORES * len(CYCLE)
        and lax.axis_size("groups") == 2
        and lengths.shape[0] == 1
        and out_proj.shape[1] % LANES == 0
        and out_proj.shape[0] % (2 * LANES) == 0
        and context.shape[0] % STEP == 0
        and pattern.shape[1] < LANES
    )
    form = on_cycle if fits else gathered
    return form(context, residual, out_proj, norm_gain, lengths, queries, pattern)


def solution(mesh):
    in_specs = (
        P(("groups", "dp"), None),
        P(("groups", "dp"), None),
        P(None, "dp"),
        P(),
        P(("groups", "dp")),
        P(("groups", "dp"), None),
        P(("groups", "dp"), None),
    )
    out_specs = (P(("groups", "dp"), None), P(("groups", "dp"), None), P(("groups", "dp")))
    return jax.shard_map(
        per_device, mesh=mesh, in_specs=in_specs, out_specs=out_specs, check_vma=False
    )
```

```python
import functools
import math

import jax
import jax.numpy as jnp
from jax import lax
from jax.experimental import pallas as pl
from jax.experimental.pallas import tpu as pltpu
from jax.sharding import PartitionSpec as P

QB = 256
LANES = 128
CORES = 2
STEP = 256
VMEM_BYTES = 12 << 20
LOW = -1e30
CYCLE = (0, 2, 4, 6, 7, 5, 3, 1)
VMEM_SPEC = pl.BlockSpec(memory_space=pltpu.VMEM)
SMALL = pl.CostEstimate(flops=1000, bytes_accessed=1000, transcendentals=0)


def column_block(distance, same_core):
    me = lax.axis_index("dp")
    core = lax.rem(me, CORES)
    chip = lax.div(me, CORES)
    z, y = lax.div(chip, 2), lax.rem(chip, 2)
    size = len(CYCLE)
    at = jnp.where(y == 0, z, size - 1 - z)
    core = core if same_core else 1 - core
    there = lax.rem(at + jnp.where(core == 0, size + distance, size - distance), size)
    chip = jnp.where(there < size // 2, 2 * there, 2 * (size - 1 - there) + 1)
    return chip * CORES + core


def columns(distance, same_core, width):
    return pl.ds(pl.multiple_of(column_block(distance, same_core) * width, width), width)


def half_slice(second, half):
    side = lax.axis_index("groups")
    return pl.ds(pl.multiple_of((1 - side if second else side) * half, half), half)


def add_squares(squares, at, total):
    square = total * total
    for lane in range(0, total.shape[1], LANES):
        squares[at, :] += square[:, lane : lane + LANES]


def half_kernel(whole, part):
    part[...] = whole[half_slice(False, part.shape[0]), :]


def own_half(whole):
    rows, width = whole.shape
    return pl.pallas_call(
        half_kernel,
        out_shape=jax.ShapeDtypeStruct((rows // 2, width), whole.dtype),
        in_specs=[VMEM_SPEC],
        out_specs=VMEM_SPEC,
        compiler_params=pltpu.CompilerParams(vmem_limit_bytes=VMEM_BYTES),
    )(whole)


def row_steps(rows):
    def loop(body):
        @pl.loop(0, rows // STEP)
        def _(k):
            body(pl.ds(pl.multiple_of(k * STEP, STEP), STEP))

    return loop


def product(tokens, at, pieces):
    total = None
    for piece, second in pieces:
        half = piece.shape[0]
        term = jnp.dot(tokens[at, half_slice(second, half)], piece[...], preferred_element_type=jnp.float32)
        total = term if total is None else total + term
    return total


def wave_kernel(full, part, arrived, whole, tokens, chained, stacked, *refs):
    count = len(full) + len(part)
    refs = list(refs)
    context = refs.pop(0) if "mine" in tokens else None
    other_context = refs.pop(0) if "theirs" in tokens else None
    residual = refs.pop(0) if "mine" in tokens else None
    if whole:
        shard = refs.pop(0)
        half = shard.shape[0] // 2
        jobs = [[(shard.at[half_slice(second, half)], second) for second in (False, True)]]
    else:
        jobs = [[(refs.pop(0), False)] + ([(refs.pop(0), True)] if j < len(full) else []) for j in range(count)]
    received = [refs.pop(0) for _ in arrived]
    before = refs.pop(0) if chained else None
    mine = refs.pop(0) if "mine" in tokens else None
    theirs = None
    if "theirs" in tokens:
        stacks = [refs.pop(0) for _ in range(2 if stacked else count)]
        theirs = stacks
        if stacked:
            theirs = [stacks[0].at[j] for j in range(len(full))] + [stacks[1].at[j] for j in range(len(part))]
    finished = refs.pop(0) if arrived else None
    squares = refs.pop(0) if "mine" in tokens else None
    rows, width = mine.shape[1:] if "mine" in tokens else theirs[0].shape
    if chained:
        squares[...] = before[...]
    elif "mine" in tokens:
        squares[...] = jnp.zeros_like(squares)
    for j, distance in enumerate(full + part):

        @row_steps(rows)
        def _(at):
            if "theirs" in tokens:
                theirs[j][at, :] = product(other_context, at, jobs[j])
            if "mine" in tokens:
                total = product(context, at, jobs[j])
                total += residual[at, columns(distance, True, width)].astype(jnp.float32)
                mine[j, at, :] = total
                if j < len(full):
                    add_squares(squares, at, total)

    for j, (distance, same) in enumerate(arrived):

        @row_steps(rows)
        def _(at):
            total = received[j][at, :] + residual[at, columns(distance, same, width)].astype(jnp.float32)
            finished[j, at, :] = total
            add_squares(squares, at, total)


def wave(
    full, part, arrived, context, other_context, residual, pieces, received=None, squares=None, stacked=False
):
    tokens = (("mine",) if context is not None else ()) + (("theirs",) if other_context is not None else ())
    count = len(full) + len(part)
    rows = (context if other_context is None else other_context).shape[0]
    whole = len(pieces) == 1
    block = jax.ShapeDtypeStruct((rows, pieces[0].shape[1]), jnp.float32)

    def stack(n):
        return jax.ShapeDtypeStruct((n,) + block.shape, jnp.float32)

    outs = [stack(count)] if "mine" in tokens else []
    if "theirs" in tokens:
        outs += [stack(len(full)), stack(len(part))] if stacked else [block] * count
    operands = [x for x in (context, other_context) if x is not None]
    operands += ([residual] if "mine" in tokens else []) + list(pieces)
    if arrived:
        operands += [*received] + ([] if squares is None else [squares])
        outs.append(jax.ShapeDtypeStruct((len(arrived),) + block.shape, jnp.float32))
    if "mine" in tokens:
        outs.append(jax.ShapeDtypeStruct((rows, LANES), jnp.float32))
    return pl.pallas_call(
        functools.partial(wave_kernel, full, part, arrived, whole, tokens, squares is not None, stacked),
        out_shape=outs,
        in_specs=[VMEM_SPEC] * len(operands),
        out_specs=[VMEM_SPEC] * len(outs),
        compiler_params=pltpu.CompilerParams(vmem_limit_bytes=VMEM_BYTES),
        cost_estimate=SMALL,
    )(*operands)


def late_blocks(items, context, residual, pieces, hidden, squares, target):
    rows, width = target.shape[1:]
    for i, (base, parts, bare, distance, same) in enumerate(items):

        @row_steps(rows)
        def _(at):
            value = product(context, at, [(pieces[index], second) for index, second in parts])
            if base is not None:
                known = hidden[base[0]][(at,) if base[1] is None else (base[1], at)]
                value = known if value is None else value + known
            if bare:
                value += residual[at, columns(distance, same, width)].astype(jnp.float32)
            target[i, at, :] = value
            add_squares(squares, at, value)


def late_kernel(items, n_pieces, context, residual, before, *refs):
    pieces, hidden = refs[:n_pieces], refs[n_pieces:-2]
    finished, squares = refs[-2:]
    squares[...] = before[...]
    late_blocks(items, context, residual, pieces, hidden, squares, finished)


def late(items, context, residual, squares, pieces, hidden):
    rows = context.shape[0]
    operands = [context, residual, squares, *pieces, *hidden]
    return pl.pallas_call(
        functools.partial(late_kernel, items, len(pieces)),
        out_shape=(
            jax.ShapeDtypeStruct((len(items), rows, pieces[0].shape[1]), jnp.float32),
            jax.ShapeDtypeStruct(squares.shape, jnp.float32),
        ),
        in_specs=[VMEM_SPEC] * len(operands),
        out_specs=(VMEM_SPEC, VMEM_SPEC),
        compiler_params=pltpu.CompilerParams(vmem_limit_bytes=VMEM_BYTES),
        cost_estimate=SMALL,
    )(*operands)


def final_kernel(items, sources, n_pieces, context, residual, before, gain, flags, *refs):
    pieces, hidden = refs[:n_pieces], refs[n_pieces:-6]
    embedded, payload, blocks, squares, scale_rows, sheet = refs[-6:]
    width = blocks.shape[2]
    features = embedded.shape[1]
    squares[...] = before[...]
    late_blocks(items, context, residual, pieces, hidden, squares, blocks)
    mean = jnp.sum(squares[...], axis=1, keepdims=True) * (1.0 / features)
    length = flags[:, LANES - 1 : LANES]
    row = lax.broadcasted_iota(jnp.int32, mean.shape, 0).astype(jnp.float32)
    scale = jnp.where(row < length, lax.rsqrt(mean + 1e-05), 0.0)
    scale_rows[...] = jnp.broadcast_to(scale, scale_rows.shape)
    inverse = 1.0 / length
    done = [(blocks.at[i], distance, same) for i, (_, _, _, distance, same) in enumerate(items)]
    done += [(hidden[array].at[entry], distance, same) for array, entry, distance, same in sources]
    for block, distance, same in done:
        parts = [
            jnp.sum(block[:, lane : lane + LANES] * scale_rows[...], axis=0, keepdims=True)
            for lane in range(0, width, LANES)
        ]
        where = columns(distance, same, width)
        embedded[:, where] = jnp.concatenate(parts, axis=1) * gain[:, where] * inverse
    pooled = embedded[...]
    mean = jnp.sum(pooled * pooled, axis=1, keepdims=True) * (1.0 / features)
    embedded[...] = pooled * lax.rsqrt(mean + 1e-06)
    lines = features // LANES
    sheet[lines:, :] = jnp.zeros((sheet.shape[0] - lines, LANES), jnp.float32)
    for line in range(lines):
        sheet[line : line + 1, :] = embedded[:, line * LANES : (line + 1) * LANES]
    sheet[lines : lines + 1, :] = flags[...]
    rounded = sheet[...].astype(jnp.bfloat16)
    for rank in range(payload.shape[0]):
        payload[rank] = rounded


def finish(items, sources, context, residual, squares, gain, flags, pieces, hidden, ranks):
    rows = context.shape[0]
    width = pieces[0].shape[1]
    features = (len(items) + len(sources)) * width
    lines = -(-(features // LANES + 1) // 16) * 16
    operands = [context, residual, squares, gain, flags, *pieces, *hidden]
    return pl.pallas_call(
        functools.partial(final_kernel, items, sources, len(pieces)),
        out_shape=(
            jax.ShapeDtypeStruct((1, features), jnp.float32),
            jax.ShapeDtypeStruct((ranks, lines, LANES), jnp.bfloat16),
        ),
        in_specs=[VMEM_SPEC] * len(operands),
        out_specs=(VMEM_SPEC, VMEM_SPEC),
        scratch_shapes=[
            pltpu.VMEM((len(items), rows, width), jnp.float32),
            pltpu.VMEM((rows, LANES), jnp.float32),
            pltpu.VMEM((rows, LANES), jnp.float32),
            pltpu.VMEM((lines, LANES), jnp.float32),
        ],
        compiler_params=pltpu.CompilerParams(vmem_limit_bytes=VMEM_BYTES),
        cost_estimate=SMALL,
    )(*operands)


def score_kernel(lines, blocks, got, queries, other_queries, out, wide, emb, mix):
    me = lax.axis_index("dp")
    ranks = got.shape[0]
    count = queries.shape[0]
    wide[...] = got[...].astype(jnp.float32)
    for line in range(lines):
        emb[:, line * LANES : (line + 1) * LANES] = wide[:, line, :]
    half = emb[...].astype(jnp.bfloat16)
    flags = wide[:, lines, :].astype(jnp.bfloat16)
    temper = 1.0 / (0.02 * math.sqrt(lines * LANES))
    scores, masks = [], []
    for owner, rows in ((me, queries), (me + 1 - 2 * lax.rem(me, CORES), other_queries)):
        score = lax.dot_general(
            half, rows[...], (((1,), (1,)), ((), ())), preferred_element_type=jnp.float32
        )
        scores.append(score * temper)
        block = lax.broadcasted_iota(jnp.int32, (LANES, count), 0)
        row = owner * count + lax.broadcasted_iota(jnp.int32, (LANES, count), 1)
        pick = (row >= block * QB) & (row < block * QB + QB) & (block < blocks)
        pick = jnp.where(pick, 1.0, 0.0).astype(jnp.bfloat16)
        masks.append(jnp.dot(flags, pick, preferred_element_type=jnp.float32) > 0.5)
    peaks = [
        jnp.max(jnp.where(mask, score, LOW), axis=1, keepdims=True) for score, mask in zip(scores, masks)
    ]
    peak = jnp.maximum(*peaks)
    weights = [jnp.where(mask, jnp.exp(score - peak), 0.0) for score, mask in zip(scores, masks)]
    total = sum(jnp.sum(weight, axis=1, keepdims=True) for weight in weights)
    mix[...] = jnp.dot(
        weights[0].astype(jnp.bfloat16), queries[...], preferred_element_type=jnp.float32
    ) + jnp.dot(weights[1].astype(jnp.bfloat16), other_queries[...], preferred_element_type=jnp.float32)
    for line in range(lines):
        out[:, line, :] = mix[:, line * LANES : (line + 1) * LANES]
    lane = lax.broadcasted_iota(jnp.int32, (ranks, LANES), 1)
    out[:, lines, :] = jnp.where(lane == 0, peak, jnp.where(lane == 1, total, 0.0))
    for line in range(lines + 1, out.shape[1]):
        out[:, line, :] = jnp.zeros((ranks, LANES), jnp.float32)


def score(got, queries, other_queries, blocks):
    ranks = got.shape[0]
    features = queries.shape[1]
    lines = features // LANES
    return pl.pallas_call(
        functools.partial(score_kernel, lines, blocks),
        out_shape=jax.ShapeDtypeStruct((ranks, -(-(lines + 1) // 8) * 8, LANES), jnp.float32),
        in_specs=[pl.BlockSpec(memory_space=pltpu.VMEM)] * 3,
        out_specs=pl.BlockSpec(memory_space=pltpu.VMEM),
        scratch_shapes=[
            pltpu.VMEM(got.shape, jnp.float32),
            pltpu.VMEM((ranks, features), jnp.float32),
            pltpu.VMEM((ranks, features), jnp.float32),
        ],
        compiler_params=pltpu.CompilerParams(vmem_limit_bytes=VMEM_BYTES),
    )(got, queries, other_queries)


def combine_kernel(lines, got, recalled, log_total):
    stats = got[:, lines, :]
    peaks, sums = stats[:, 0:1], stats[:, 1:2]
    peak = jnp.max(peaks, axis=0, keepdims=True)
    factor = jnp.exp(peaks - peak)
    total = jnp.sum(sums * factor, axis=0, keepdims=True)
    mix = got[0, :lines, :] * factor[0:1, :]
    for rank in range(1, got.shape[0]):
        mix += got[rank, :lines, :] * factor[rank : rank + 1, :]
    mix = mix / total
    for line in range(lines):
        recalled[:, line * LANES : (line + 1) * LANES] = mix[line : line + 1, :]
    log_total[...] = peak + jnp.log(total)


def combine(got, features):
    recalled, log_total = pl.pallas_call(
        functools.partial(combine_kernel, features // LANES),
        out_shape=(
            jax.ShapeDtypeStruct((1, features), jnp.float32),
            jax.ShapeDtypeStruct((1, 1), jnp.float32),
        ),
        in_specs=[pl.BlockSpec(memory_space=pltpu.VMEM)],
        out_specs=(pl.BlockSpec(memory_space=pltpu.VMEM), pl.BlockSpec(memory_space=pltpu.VMEM)),
        compiler_params=pltpu.CompilerParams(vmem_limit_bytes=VMEM_BYTES),
    )(got)
    return recalled, log_total.reshape(1)


def on_cycle(context, residual, out_proj, norm_gain, lengths, queries, pattern):
    ranks = lax.axis_size("dp")
    size = ranks // CORES
    features = residual.shape[1]

    def ring(step):
        return [
            (CYCLE[r] * CORES + c, CYCLE[(r + step * (1 - 2 * c)) % size] * CORES + c)
            for r in range(size)
            for c in range(CORES)
        ]

    def from_next(piece):
        return lax.ppermute(piece, "dp", ring(-1))

    def from_last(piece):
        return lax.ppermute(piece, "dp", ring(1))

    def over_x(piece):
        return lax.ppermute(piece, "groups", [(0, 1), (1, 0)])

    def other_core(piece):
        return lax.ppermute(piece, "dp", [(i, i ^ 1) for i in range(ranks)])

    wait = lax.optimization_barrier

    own = own_half(out_proj)
    a = from_next(own)
    c, q = other_core(context), other_core(queries)
    (p0,) = wave((0,), (), (), None, context, None, [out_proj])
    own, p0 = wait((own, p0))
    b = from_last(own)

    n1, p0 = wait((a, p0))
    x = over_x(n1)
    a = from_next(n1)
    context2, n1 = wait((c, n1))
    (t0,) = wave((0,), (), (), None, context2, None, [out_proj])
    l1, n1, t0, queries2 = wait((b, n1, t0, q))
    b = from_last(l1)
    r0 = other_core(t0)

    n2, l1 = wait((a, l1))
    x2 = over_x(n2)
    a = from_next(n2)
    xn1, n2 = wait((x, n2))
    x = x2
    h1, t1, f0, sq1 = wave(
        (1,), (), ((0, True), (0, False)), context, context2, residual, [n1, xn1], [p0, r0], None
    )
    l2, n2, t1, sq1 = wait((b, n2, t1, sq1))
    b = from_last(l2)
    r1 = other_core(t1)

    xn2, l2 = wait((x, l2))
    x = over_x(l2)
    a2 = from_next(xn2)
    n3, xn2 = wait((a, xn2))
    h2, t2, t2p, f1, sq2 = wave((2,), (-1,), ((1, False),), context, context2, residual, [n2, xn2, l1], [r1], sq1)
    l3, n3, t2, t2p, sq2 = wait((b, n3, t2, t2p, sq2))
    b = from_last(l3)
    r2, r2p = other_core(t2), other_core(t2p)

    n3x, l3 = wait((a2, l3))
    a = from_next(n3x)
    xl2, l1, n3x = wait((x, l1, n3x))
    x = over_x(l1)
    h3, t3a, t3p, f2, sq3 = wave(
        (-2, 3), (-3,), ((2, False),), context, context2, residual, [l2, xl2, n3, n3x, l3], [r2], sq2, stacked=True
    )
    l4, xl2, t3a, t3p, sq3, r2p = wait((b, xl2, t3a, t3p, sq3, r2p))
    b = from_last(xl2)
    r3a, r3p = other_core(t3a), other_core(t3p)
    l4s = other_core(l4)

    n4x, l4 = wait((a, l4))
    n4xs = other_core(n4x)
    items = ((None, ((0, False), (1, True)), True, 4, True),)
    h4, sq4 = late(items, context, residual, sq3, [l4, n4x], [])
    xl1, n4x, sq4 = wait((x, n4x, sq4))
    xl1s = other_core(xl1)
    items = (((0, 1), ((0, True),), False, -1, True),)
    h5, sq5 = late(items, context, residual, sq4, [xl1], [h2])
    l3x, xl1, sq5 = wait((b, xl1, sq5))
    l3xs = other_core(l3x)
    items = (
        ((0, 2), ((0, True),), False, -3, True),
        ((1, 0), (), True, -2, False),
        ((1, 1), (), True, 3, False),
        (None, ((1, False), (2, True)), True, 4, False),
    )
    h6, sq6 = late(items, context, residual, sq5, [l3x, l4s, n4xs], [h3, r3a])
    items = (((0, None), ((0, True),), True, -1, False), ((1, 0), ((1, True),), True, -3, False))
    hidden = [r2p, r3p, h1, h2, h3, h4, h5, h6, f0, f1, f2]
    sources = (
        (2, 0, 1, True),
        (3, 0, 2, True),
        (4, 0, -2, True),
        (4, 1, 3, True),
        (5, 0, 4, True),
        (6, 0, -1, True),
        (8, 0, 0, True),
        (8, 1, 0, False),
        (9, 0, 1, False),
        (10, 0, 2, False),
        (7, 0, -3, True),
        (7, 1, -2, False),
        (7, 2, 3, False),
        (7, 3, 4, False),
    )
    flags = jnp.pad(pattern.astype(jnp.float32), ((0, 0), (0, LANES - 1 - pattern.shape[1])))
    flags = jnp.concatenate([flags, lengths.astype(jnp.float32)[:, None]], axis=1)
    embedded, payload = finish(
        items, sources, context, residual, sq6, norm_gain.reshape(1, -1), flags, [xl1s, l3xs], hidden, size
    )

    same_core = [list(range(c, ranks, CORES)) for c in range(CORES)]

    def spread(blocks):
        return lax.all_to_all(blocks, "dp", 0, 0, axis_index_groups=same_core, tiled=True)

    parts = score(spread(payload), queries, queries2, pattern.shape[1])
    recalled, log_total = combine(spread(parts), features)
    return embedded, recalled, log_total


def gathered(context, residual, out_proj, norm_gain, lengths, queries, pattern):
    tok_rows = context.shape[0]
    features = residual.shape[1]
    passages_here = lengths.shape[0]
    seq_len = tok_rows // passages_here
    query_rows = queries.shape[0]
    blocks = pattern.shape[1]
    ranks = lax.axis_size("dp")
    me = lax.axis_index("dp")
    branch = jnp.dot(
        context,
        lax.all_gather(out_proj, "dp", axis=1, tiled=True),
        preferred_element_type=jnp.float32,
    )
    hidden_sum = residual.astype(jnp.float32) + branch
    normed = (
        hidden_sum
        * lax.rsqrt(jnp.mean(hidden_sum * hidden_sum, axis=-1, keepdims=True) + 1e-05)
        * norm_gain
    )
    shaped = normed.reshape(passages_here, seq_len, features)
    valid_mask = (jnp.arange(seq_len)[None, :] < lengths[:, None]).astype(jnp.float32)
    pooled = jnp.sum(shaped * valid_mask[:, :, None], axis=1) / lengths.astype(jnp.float32)[:, None]
    embedded = pooled * lax.rsqrt(jnp.mean(pooled * pooled, axis=-1, keepdims=True) + 1e-06)
    emb_half = embedded.astype(jnp.bfloat16)
    temper = 1.0 / (0.02 * math.sqrt(features))
    contract = (((1,), (1,)), ((), ()))

    flags = jnp.pad(pattern.astype(jnp.bfloat16), ((0, 0), (0, LANES - blocks)))
    everyone = lax.all_gather(jnp.concatenate([emb_half, flags], axis=1), "dp", axis=0, tiled=True)
    emb_all = everyone[:, :features]
    flags_all = everyone[:, features : features + blocks].astype(jnp.float32)
    scores = lax.dot_general(emb_all, queries, contract, preferred_element_type=jnp.float32) * temper
    row_block = (me * query_rows + jnp.arange(query_rows)) // QB
    picks = (row_block[None, :] == jnp.arange(blocks)[:, None]).astype(jnp.float32)
    cand_mask = jnp.dot(flags_all, picks) > 0
    peak_part = jnp.max(jnp.where(cand_mask, scores, LOW), axis=1, keepdims=True)
    weights = jnp.where(cand_mask, jnp.exp(scores - peak_part), 0.0)
    total_part = jnp.sum(weights, axis=1, keepdims=True)
    mix_part = jnp.dot(weights.astype(jnp.bfloat16), queries, preferred_element_type=jnp.float32)

    passages = emb_all.shape[0]
    lane = jnp.arange(LANES)[None, :]
    tail = jnp.where(lane == 0, peak_part, jnp.where(lane == 1, total_part, 0.0))
    parts = jnp.concatenate([mix_part, tail], axis=1).reshape(ranks, passages // ranks, -1)
    parts = lax.all_to_all(parts, "dp", split_axis=0, concat_axis=0, tiled=True)
    mixes, peaks, sums = parts[:, :, :features], parts[:, :, features], parts[:, :, features + 1]
    peak_score = jnp.max(peaks, axis=0)
    factor = jnp.exp(peaks - peak_score[None, :])
    totals = jnp.sum(sums * factor, axis=0)
    recalled = jnp.sum(mixes * factor[:, :, None], axis=0) / totals[:, None]
    log_total = peak_score + jnp.log(totals)
    return (embedded, recalled, log_total)


def per_device(context, residual, out_proj, norm_gain, lengths, queries, pattern):
    fits = (
        lax.axis_size("dp") == CORES * len(CYCLE)
        and lax.axis_size("groups") == 2
        and lengths.shape[0] == 1
        and out_proj.shape[1] % LANES == 0
        and out_proj.shape[0] % (2 * LANES) == 0
        and context.shape[0] % STEP == 0
        and pattern.shape[1] < LANES
    )
    form = on_cycle if fits else gathered
    return form(context, residual, out_proj, norm_gain, lengths, queries, pattern)


def solution(mesh):
    in_specs = (
        P(("groups", "dp"), None),
        P(("groups", "dp"), None),
        P(None, "dp"),
        P(),
        P(("groups", "dp")),
        P(("groups", "dp"), None),
        P(("groups", "dp"), None),
    )
    out_specs = (P(("groups", "dp"), None), P(("groups", "dp"), None), P(("groups", "dp")))
    return jax.shard_map(
        per_device, mesh=mesh, in_specs=in_specs, out_specs=out_specs, check_vma=False
    )
```

```python
import functools
import math

import jax
import jax.numpy as jnp
from jax import lax
from jax.experimental import pallas as pl
from jax.experimental.pallas import tpu as pltpu
from jax.sharding import PartitionSpec as P

QB = 256
LANES = 128
CORES = 2
STEP = 256
VMEM_BYTES = 12 << 20
LOW = -1e30
CYCLE = (0, 2, 4, 6, 7, 5, 3, 1)
VMEM_SPEC = pl.BlockSpec(memory_space=pltpu.VMEM)
SMALL = pl.CostEstimate(flops=1000, bytes_accessed=1000, transcendentals=0)


def column_block(distance, same_core):
    me = lax.axis_index("dp")
    core = lax.rem(me, CORES)
    chip = lax.div(me, CORES)
    z, y = lax.div(chip, 2), lax.rem(chip, 2)
    size = len(CYCLE)
    at = jnp.where(y == 0, z, size - 1 - z)
    core = core if same_core else 1 - core
    there = lax.rem(at + jnp.where(core == 0, size + distance, size - distance), size)
    chip = jnp.where(there < size // 2, 2 * there, 2 * (size - 1 - there) + 1)
    return chip * CORES + core


def columns(distance, same_core, width):
    return pl.ds(pl.multiple_of(column_block(distance, same_core) * width, width), width)


def half_slice(second, half):
    side = lax.axis_index("groups")
    return pl.ds(pl.multiple_of((1 - side if second else side) * half, half), half)


def add_squares(squares, at, total):
    square = total * total
    for lane in range(0, total.shape[1], LANES):
        squares[at, :] += square[:, lane : lane + LANES]


def half_kernel(whole, part):
    part[...] = whole[half_slice(False, part.shape[0]), :]


def own_half(whole):
    rows, width = whole.shape
    return pl.pallas_call(
        half_kernel,
        out_shape=jax.ShapeDtypeStruct((rows // 2, width), whole.dtype),
        in_specs=[VMEM_SPEC],
        out_specs=VMEM_SPEC,
        compiler_params=pltpu.CompilerParams(vmem_limit_bytes=VMEM_BYTES),
    )(whole)


def row_steps(rows):
    def loop(body):
        @pl.loop(0, rows // STEP)
        def _(k):
            body(pl.ds(pl.multiple_of(k * STEP, STEP), STEP))

    return loop


def product(tokens, at, pieces):
    total = None
    for piece, second in pieces:
        half = piece.shape[0]
        term = jnp.dot(tokens[at, half_slice(second, half)], piece[...], preferred_element_type=jnp.float32)
        total = term if total is None else total + term
    return total


def wave_kernel(full, part, arrived, whole, tokens, chained, stacked, *refs):
    count = len(full) + len(part)
    refs = list(refs)
    context = refs.pop(0) if "mine" in tokens else None
    other_context = refs.pop(0) if "theirs" in tokens else None
    residual = refs.pop(0) if "mine" in tokens else None
    if whole:
        shard = refs.pop(0)
        half = shard.shape[0] // 2
        jobs = [[(shard.at[half_slice(second, half)], second) for second in (False, True)]]
    else:
        jobs = [[(refs.pop(0), False)] + ([(refs.pop(0), True)] if j < len(full) else []) for j in range(count)]
    received = [refs.pop(0) for _ in arrived]
    before = refs.pop(0) if chained else None
    mine = refs.pop(0) if "mine" in tokens else None
    theirs = None
    if "theirs" in tokens:
        stacks = [refs.pop(0) for _ in range(2 if stacked else count)]
        theirs = stacks
        if stacked:
            theirs = [stacks[0].at[j] for j in range(len(full))] + [stacks[1].at[j] for j in range(len(part))]
    finished = refs.pop(0) if arrived else None
    squares = refs.pop(0) if "mine" in tokens else None
    rows, width = mine.shape[1:] if "mine" in tokens else theirs[0].shape
    if chained:
        squares[...] = before[...]
    elif "mine" in tokens:
        squares[...] = jnp.zeros_like(squares)
    for j, distance in enumerate(full + part):

        @row_steps(rows)
        def _(at):
            if "theirs" in tokens:
                theirs[j][at, :] = product(other_context, at, jobs[j])
            if "mine" in tokens:
                total = product(context, at, jobs[j])
                total += residual[at, columns(distance, True, width)].astype(jnp.float32)
                mine[j, at, :] = total
                if j < len(full):
                    add_squares(squares, at, total)

    for j, (distance, same) in enumerate(arrived):

        @row_steps(rows)
        def _(at):
            total = received[j][at, :] + residual[at, columns(distance, same, width)].astype(jnp.float32)
            finished[j, at, :] = total
            add_squares(squares, at, total)


def wave(
    full, part, arrived, context, other_context, residual, pieces, received=None, squares=None, stacked=False
):
    tokens = (("mine",) if context is not None else ()) + (("theirs",) if other_context is not None else ())
    count = len(full) + len(part)
    rows = (context if other_context is None else other_context).shape[0]
    whole = len(pieces) == 1
    block = jax.ShapeDtypeStruct((rows, pieces[0].shape[1]), jnp.float32)

    def stack(n):
        return jax.ShapeDtypeStruct((n,) + block.shape, jnp.float32)

    outs = [stack(count)] if "mine" in tokens else []
    if "theirs" in tokens:
        outs += [stack(len(full)), stack(len(part))] if stacked else [block] * count
    operands = [x for x in (context, other_context) if x is not None]
    operands += ([residual] if "mine" in tokens else []) + list(pieces)
    if arrived:
        operands += [*received] + ([] if squares is None else [squares])
        outs.append(jax.ShapeDtypeStruct((len(arrived),) + block.shape, jnp.float32))
    if "mine" in tokens:
        outs.append(jax.ShapeDtypeStruct((rows, LANES), jnp.float32))
    return pl.pallas_call(
        functools.partial(wave_kernel, full, part, arrived, whole, tokens, squares is not None, stacked),
        out_shape=outs,
        in_specs=[VMEM_SPEC] * len(operands),
        out_specs=[VMEM_SPEC] * len(outs),
        compiler_params=pltpu.CompilerParams(vmem_limit_bytes=VMEM_BYTES),
        cost_estimate=SMALL,
    )(*operands)


def late_blocks(items, context, residual, pieces, hidden, squares, target):
    rows, width = target.shape[1:]
    for i, (base, parts, bare, distance, same) in enumerate(items):

        @row_steps(rows)
        def _(at):
            value = product(context, at, [(pieces[index], second) for index, second in parts])
            if base is not None:
                known = hidden[base[0]][(at,) if base[1] is None else (base[1], at)]
                value = known if value is None else value + known
            if bare:
                value += residual[at, columns(distance, same, width)].astype(jnp.float32)
            target[i, at, :] = value
            add_squares(squares, at, value)


def late_kernel(items, n_pieces, context, residual, before, *refs):
    pieces, hidden = refs[:n_pieces], refs[n_pieces:-2]
    finished, squares = refs[-2:]
    squares[...] = before[...]
    late_blocks(items, context, residual, pieces, hidden, squares, finished)


def late(items, context, residual, squares, pieces, hidden):
    rows = context.shape[0]
    operands = [context, residual, squares, *pieces, *hidden]
    return pl.pallas_call(
        functools.partial(late_kernel, items, len(pieces)),
        out_shape=(
            jax.ShapeDtypeStruct((len(items), rows, pieces[0].shape[1]), jnp.float32),
            jax.ShapeDtypeStruct(squares.shape, jnp.float32),
        ),
        in_specs=[VMEM_SPEC] * len(operands),
        out_specs=(VMEM_SPEC, VMEM_SPEC),
        compiler_params=pltpu.CompilerParams(vmem_limit_bytes=VMEM_BYTES),
        cost_estimate=SMALL,
    )(*operands)


def final_kernel(items, sources, n_pieces, context, residual, before, gain, flags, *refs):
    pieces, hidden = refs[:n_pieces], refs[n_pieces:-6]
    embedded, payload, blocks, squares, scale_rows, sheet = refs[-6:]
    width = blocks.shape[2]
    features = embedded.shape[1]
    squares[...] = before[...]
    late_blocks(items, context, residual, pieces, hidden, squares, blocks)
    mean = jnp.sum(squares[...], axis=1, keepdims=True) * (1.0 / features)
    length = flags[:, LANES - 1 : LANES]
    row = lax.broadcasted_iota(jnp.int32, mean.shape, 0).astype(jnp.float32)
    scale = jnp.where(row < length, lax.rsqrt(mean + 1e-05), 0.0)
    scale_rows[...] = jnp.broadcast_to(scale, scale_rows.shape)
    inverse = 1.0 / length
    done = [(blocks.at[i], distance, same) for i, (_, _, _, distance, same) in enumerate(items)]
    done += [(hidden[array].at[entry], distance, same) for array, entry, distance, same in sources]
    for block, distance, same in done:
        parts = [
            jnp.sum(block[:, lane : lane + LANES] * scale_rows[...], axis=0, keepdims=True)
            for lane in range(0, width, LANES)
        ]
        where = columns(distance, same, width)
        embedded[:, where] = jnp.concatenate(parts, axis=1) * gain[:, where] * inverse
    pooled = embedded[...]
    mean = jnp.sum(pooled * pooled, axis=1, keepdims=True) * (1.0 / features)
    embedded[...] = pooled * lax.rsqrt(mean + 1e-06)
    lines = features // LANES
    sheet[lines:, :] = jnp.zeros((sheet.shape[0] - lines, LANES), jnp.float32)
    for line in range(lines):
        sheet[line : line + 1, :] = embedded[:, line * LANES : (line + 1) * LANES]
    sheet[lines : lines + 1, :] = flags[...]
    rounded = sheet[...].astype(jnp.bfloat16)
    for rank in range(payload.shape[0]):
        payload[rank] = rounded


def finish(items, sources, context, residual, squares, gain, flags, pieces, hidden, ranks):
    rows = context.shape[0]
    width = pieces[0].shape[1]
    features = (len(items) + len(sources)) * width
    lines = -(-(features // LANES + 1) // 16) * 16
    operands = [context, residual, squares, gain, flags, *pieces, *hidden]
    return pl.pallas_call(
        functools.partial(final_kernel, items, sources, len(pieces)),
        out_shape=(
            jax.ShapeDtypeStruct((1, features), jnp.float32),
            jax.ShapeDtypeStruct((ranks, lines, LANES), jnp.bfloat16),
        ),
        in_specs=[VMEM_SPEC] * len(operands),
        out_specs=(VMEM_SPEC, VMEM_SPEC),
        scratch_shapes=[
            pltpu.VMEM((len(items), rows, width), jnp.float32),
            pltpu.VMEM((rows, LANES), jnp.float32),
            pltpu.VMEM((rows, LANES), jnp.float32),
            pltpu.VMEM((lines, LANES), jnp.float32),
        ],
        compiler_params=pltpu.CompilerParams(vmem_limit_bytes=VMEM_BYTES),
        cost_estimate=SMALL,
    )(*operands)


def score_kernel(lines, blocks, got, queries, other_queries, out, wide, emb, mix):
    me = lax.axis_index("dp")
    ranks = got.shape[0]
    count = queries.shape[0]
    wide[...] = got[...].astype(jnp.float32)
    for line in range(lines):
        emb[:, line * LANES : (line + 1) * LANES] = wide[:, line, :]
    half = emb[...].astype(jnp.bfloat16)
    flags = wide[:, lines, :].astype(jnp.bfloat16)
    temper = 1.0 / (0.02 * math.sqrt(lines * LANES))
    scores, masks = [], []
    for owner, rows in ((me, queries), (me + 1 - 2 * lax.rem(me, CORES), other_queries)):
        score = lax.dot_general(
            half, rows[...], (((1,), (1,)), ((), ())), preferred_element_type=jnp.float32
        )
        scores.append(score * temper)
        block = lax.broadcasted_iota(jnp.int32, (LANES, count), 0)
        row = owner * count + lax.broadcasted_iota(jnp.int32, (LANES, count), 1)
        pick = (row >= block * QB) & (row < block * QB + QB) & (block < blocks)
        pick = jnp.where(pick, 1.0, 0.0).astype(jnp.bfloat16)
        masks.append(jnp.dot(flags, pick, preferred_element_type=jnp.float32) > 0.5)
    peaks = [
        jnp.max(jnp.where(mask, score, LOW), axis=1, keepdims=True) for score, mask in zip(scores, masks)
    ]
    peak = jnp.maximum(*peaks)
    weights = [jnp.where(mask, jnp.exp(score - peak), 0.0) for score, mask in zip(scores, masks)]
    total = sum(jnp.sum(weight, axis=1, keepdims=True) for weight in weights)
    mix[...] = jnp.dot(
        weights[0].astype(jnp.bfloat16), queries[...], preferred_element_type=jnp.float32
    ) + jnp.dot(weights[1].astype(jnp.bfloat16), other_queries[...], preferred_element_type=jnp.float32)
    for line in range(lines):
        out[:, line, :] = mix[:, line * LANES : (line + 1) * LANES]
    lane = lax.broadcasted_iota(jnp.int32, (ranks, LANES), 1)
    out[:, lines, :] = jnp.where(lane == 0, peak, jnp.where(lane == 1, total, 0.0))
    for line in range(lines + 1, out.shape[1]):
        out[:, line, :] = jnp.zeros((ranks, LANES), jnp.float32)


def score(got, queries, other_queries, blocks):
    ranks = got.shape[0]
    features = queries.shape[1]
    lines = features // LANES
    return pl.pallas_call(
        functools.partial(score_kernel, lines, blocks),
        out_shape=jax.ShapeDtypeStruct((ranks, -(-(lines + 1) // 8) * 8, LANES), jnp.float32),
        in_specs=[pl.BlockSpec(memory_space=pltpu.VMEM)] * 3,
        out_specs=pl.BlockSpec(memory_space=pltpu.VMEM),
        scratch_shapes=[
            pltpu.VMEM(got.shape, jnp.float32),
            pltpu.VMEM((ranks, features), jnp.float32),
            pltpu.VMEM((ranks, features), jnp.float32),
        ],
        compiler_params=pltpu.CompilerParams(vmem_limit_bytes=VMEM_BYTES),
    )(got, queries, other_queries)


def combine_kernel(lines, got, recalled, log_total):
    stats = got[:, lines, :]
    peaks, sums = stats[:, 0:1], stats[:, 1:2]
    peak = jnp.max(peaks, axis=0, keepdims=True)
    factor = jnp.exp(peaks - peak)
    total = jnp.sum(sums * factor, axis=0, keepdims=True)
    mix = got[0, :lines, :] * factor[0:1, :]
    for rank in range(1, got.shape[0]):
        mix += got[rank, :lines, :] * factor[rank : rank + 1, :]
    mix = mix / total
    for line in range(lines):
        recalled[:, line * LANES : (line + 1) * LANES] = mix[line : line + 1, :]
    log_total[...] = peak + jnp.log(total)


def combine(got, features):
    recalled, log_total = pl.pallas_call(
        functools.partial(combine_kernel, features // LANES),
        out_shape=(
            jax.ShapeDtypeStruct((1, features), jnp.float32),
            jax.ShapeDtypeStruct((1, 1), jnp.float32),
        ),
        in_specs=[pl.BlockSpec(memory_space=pltpu.VMEM)],
        out_specs=(pl.BlockSpec(memory_space=pltpu.VMEM), pl.BlockSpec(memory_space=pltpu.VMEM)),
        compiler_params=pltpu.CompilerParams(vmem_limit_bytes=VMEM_BYTES),
    )(got)
    return recalled, log_total.reshape(1)


def on_cycle(context, residual, out_proj, norm_gain, lengths, queries, pattern):
    ranks = lax.axis_size("dp")
    size = ranks // CORES
    features = residual.shape[1]

    def ring(step):
        return [
            (CYCLE[r] * CORES + c, CYCLE[(r + step * (1 - 2 * c)) % size] * CORES + c)
            for r in range(size)
            for c in range(CORES)
        ]

    def from_next(piece):
        return lax.ppermute(piece, "dp", ring(-1))

    def from_last(piece):
        return lax.ppermute(piece, "dp", ring(1))

    def over_x(piece):
        return lax.ppermute(piece, "groups", [(0, 1), (1, 0)])

    def other_core(piece):
        return lax.ppermute(piece, "dp", [(i, i ^ 1) for i in range(ranks)])

    wait = lax.optimization_barrier

    own = own_half(out_proj)
    a = from_next(own)
    c, q = other_core(context), other_core(queries)
    b = from_last(own)
    (p0,) = wave((0,), (), (), None, context, None, [out_proj])

    n1, p0 = wait((a, p0))
    x = over_x(n1)
    a = from_next(n1)
    context2, n1 = wait((c, n1))
    (t0,) = wave((0,), (), (), None, context2, None, [out_proj])
    l1, n1, t0, queries2 = wait((b, n1, t0, q))
    b = from_last(l1)
    r0 = other_core(t0)

    n2, l1 = wait((a, l1))
    x2 = over_x(n2)
    a = from_next(n2)
    xn1, n2 = wait((x, n2))
    x = x2
    h1, t1, f0, sq1 = wave(
        (1,), (), ((0, True), (0, False)), context, context2, residual, [n1, xn1], [p0, r0], None
    )
    l2, n2, t1, sq1 = wait((b, n2, t1, sq1))
    b = from_last(l2)
    r1 = other_core(t1)

    xn2, l2 = wait((x, l2))
    x = over_x(l2)
    a2 = from_next(xn2)
    n3, xn2 = wait((a, xn2))
    h2, t2, t2p, f1, sq2 = wave((2,), (-1,), ((1, False),), context, context2, residual, [n2, xn2, l1], [r1], sq1)
    l3, n3, t2, t2p, sq2 = wait((b, n3, t2, t2p, sq2))
    b = from_last(l3)
    r2, r2p = other_core(t2), other_core(t2p)

    n3x, l3 = wait((a2, l3))
    a = from_next(n3x)
    xl2, l1, n3x = wait((x, l1, n3x))
    x = over_x(l1)
    h3, t3a, t3p, f2, sq3 = wave(
        (-2, 3), (-3,), ((2, False),), context, context2, residual, [l2, xl2, n3, n3x, l3], [r2], sq2, stacked=True
    )
    l4, xl2, t3a, t3p, sq3, r2p = wait((b, xl2, t3a, t3p, sq3, r2p))
    b = from_last(xl2)
    r3a, r3p = other_core(t3a), other_core(t3p)
    l4s = other_core(l4)

    n4x, l4 = wait((a, l4))
    n4xs = other_core(n4x)
    items = ((None, ((0, False), (1, True)), True, 4, True),)
    h4, sq4 = late(items, context, residual, sq3, [l4, n4x], [])
    xl1, n4x, sq4 = wait((x, n4x, sq4))
    xl1s = other_core(xl1)
    items = (((0, 1), ((0, True),), False, -1, True),)
    h5, sq5 = late(items, context, residual, sq4, [xl1], [h2])
    l3x, xl1, sq5 = wait((b, xl1, sq5))
    l3xs = other_core(l3x)
    items = (
        ((0, 2), ((0, True),), False, -3, True),
        ((1, 0), (), True, -2, False),
        ((1, 1), (), True, 3, False),
        (None, ((1, False), (2, True)), True, 4, False),
    )
    h6, sq6 = late(items, context, residual, sq5, [l3x, l4s, n4xs], [h3, r3a])
    items = (((0, None), ((0, True),), True, -1, False), ((1, 0), ((1, True),), True, -3, False))
    hidden = [r2p, r3p, h1, h2, h3, h4, h5, h6, f0, f1, f2]
    sources = (
        (2, 0, 1, True),
        (3, 0, 2, True),
        (4, 0, -2, True),
        (4, 1, 3, True),
        (5, 0, 4, True),
        (6, 0, -1, True),
        (8, 0, 0, True),
        (8, 1, 0, False),
        (9, 0, 1, False),
        (10, 0, 2, False),
        (7, 0, -3, True),
        (7, 1, -2, False),
        (7, 2, 3, False),
        (7, 3, 4, False),
    )
    flags = jnp.pad(pattern.astype(jnp.float32), ((0, 0), (0, LANES - 1 - pattern.shape[1])))
    flags = jnp.concatenate([flags, lengths.astype(jnp.float32)[:, None]], axis=1)
    embedded, payload = finish(
        items, sources, context, residual, sq6, norm_gain.reshape(1, -1), flags, [xl1s, l3xs], hidden, size
    )

    same_core = [list(range(c, ranks, CORES)) for c in range(CORES)]

    def spread(blocks):
        return lax.all_to_all(blocks, "dp", 0, 0, axis_index_groups=same_core, tiled=True)

    parts = score(spread(payload), queries, queries2, pattern.shape[1])
    recalled, log_total = combine(spread(parts), features)
    return embedded, recalled, log_total


def gathered(context, residual, out_proj, norm_gain, lengths, queries, pattern):
    tok_rows = context.shape[0]
    features = residual.shape[1]
    passages_here = lengths.shape[0]
    seq_len = tok_rows // passages_here
    query_rows = queries.shape[0]
    blocks = pattern.shape[1]
    ranks = lax.axis_size("dp")
    me = lax.axis_index("dp")
    branch = jnp.dot(
        context,
        lax.all_gather(out_proj, "dp", axis=1, tiled=True),
        preferred_element_type=jnp.float32,
    )
    hidden_sum = residual.astype(jnp.float32) + branch
    normed = (
        hidden_sum
        * lax.rsqrt(jnp.mean(hidden_sum * hidden_sum, axis=-1, keepdims=True) + 1e-05)
        * norm_gain
    )
    shaped = normed.reshape(passages_here, seq_len, features)
    valid_mask = (jnp.arange(seq_len)[None, :] < lengths[:, None]).astype(jnp.float32)
    pooled = jnp.sum(shaped * valid_mask[:, :, None], axis=1) / lengths.astype(jnp.float32)[:, None]
    embedded = pooled * lax.rsqrt(jnp.mean(pooled * pooled, axis=-1, keepdims=True) + 1e-06)
    emb_half = embedded.astype(jnp.bfloat16)
    temper = 1.0 / (0.02 * math.sqrt(features))
    contract = (((1,), (1,)), ((), ()))

    flags = jnp.pad(pattern.astype(jnp.bfloat16), ((0, 0), (0, LANES - blocks)))
    everyone = lax.all_gather(jnp.concatenate([emb_half, flags], axis=1), "dp", axis=0, tiled=True)
    emb_all = everyone[:, :features]
    flags_all = everyone[:, features : features + blocks].astype(jnp.float32)
    scores = lax.dot_general(emb_all, queries, contract, preferred_element_type=jnp.float32) * temper
    row_block = (me * query_rows + jnp.arange(query_rows)) // QB
    picks = (row_block[None, :] == jnp.arange(blocks)[:, None]).astype(jnp.float32)
    cand_mask = jnp.dot(flags_all, picks) > 0
    peak_part = jnp.max(jnp.where(cand_mask, scores, LOW), axis=1, keepdims=True)
    weights = jnp.where(cand_mask, jnp.exp(scores - peak_part), 0.0)
    total_part = jnp.sum(weights, axis=1, keepdims=True)
    mix_part = jnp.dot(weights.astype(jnp.bfloat16), queries, preferred_element_type=jnp.float32)

    passages = emb_all.shape[0]
    lane = jnp.arange(LANES)[None, :]
    tail = jnp.where(lane == 0, peak_part, jnp.where(lane == 1, total_part, 0.0))
    parts = jnp.concatenate([mix_part, tail], axis=1).reshape(ranks, passages // ranks, -1)
    parts = lax.all_to_all(parts, "dp", split_axis=0, concat_axis=0, tiled=True)
    mixes, peaks, sums = parts[:, :, :features], parts[:, :, features], parts[:, :, features + 1]
    peak_score = jnp.max(peaks, axis=0)
    factor = jnp.exp(peaks - peak_score[None, :])
    totals = jnp.sum(sums * factor, axis=0)
    recalled = jnp.sum(mixes * factor[:, :, None], axis=0) / totals[:, None]
    log_total = peak_score + jnp.log(totals)
    return (embedded, recalled, log_total)


def per_device(context, residual, out_proj, norm_gain, lengths, queries, pattern):
    fits = (
        lax.axis_size("dp") == CORES * len(CYCLE)
        and lax.axis_size("groups") == 2
        and lengths.shape[0] == 1
        and out_proj.shape[1] % LANES == 0
        and out_proj.shape[0] % (2 * LANES) == 0
        and context.shape[0] % STEP == 0
        and pattern.shape[1] < LANES
    )
    form = on_cycle if fits else gathered
    return form(context, residual, out_proj, norm_gain, lengths, queries, pattern)


def solution(mesh):
    in_specs = (
        P(("groups", "dp"), None),
        P(("groups", "dp"), None),
        P(None, "dp"),
        P(),
        P(("groups", "dp")),
        P(("groups", "dp"), None),
        P(("groups", "dp"), None),
    )
    out_specs = (P(("groups", "dp"), None), P(("groups", "dp"), None), P(("groups", "dp")))
    return jax.shard_map(
        per_device, mesh=mesh, in_specs=in_specs, out_specs=out_specs, check_vma=False
    )
```

```python
import functools
import math

import jax
import jax.numpy as jnp
from jax import lax
from jax.experimental import pallas as pl
from jax.experimental.pallas import tpu as pltpu
from jax.sharding import PartitionSpec as P

QB = 256
LANES = 128
CORES = 2
STEP = 256
VMEM_BYTES = 12 << 20
LOW = -1e30
CYCLE = (0, 2, 4, 6, 7, 5, 3, 1)
VMEM_SPEC = pl.BlockSpec(memory_space=pltpu.VMEM)
SMALL = pl.CostEstimate(flops=1000, bytes_accessed=1000, transcendentals=0)


def column_block(distance, same_core):
    me = lax.axis_index("dp")
    core = lax.rem(me, CORES)
    chip = lax.div(me, CORES)
    z, y = lax.div(chip, 2), lax.rem(chip, 2)
    size = len(CYCLE)
    at = jnp.where(y == 0, z, size - 1 - z)
    core = core if same_core else 1 - core
    there = lax.rem(at + jnp.where(core == 0, size + distance, size - distance), size)
    chip = jnp.where(there < size // 2, 2 * there, 2 * (size - 1 - there) + 1)
    return chip * CORES + core


def columns(distance, same_core, width):
    return pl.ds(pl.multiple_of(column_block(distance, same_core) * width, width), width)


def half_slice(second, half):
    side = lax.axis_index("groups")
    return pl.ds(pl.multiple_of((1 - side if second else side) * half, half), half)


def add_squares(squares, at, total):
    square = total * total
    for lane in range(0, total.shape[1], LANES):
        squares[at, :] += square[:, lane : lane + LANES]


def half_kernel(whole, part):
    part[...] = whole[half_slice(False, part.shape[0]), :]


def own_half(whole):
    rows, width = whole.shape
    return pl.pallas_call(
        half_kernel,
        out_shape=jax.ShapeDtypeStruct((rows // 2, width), whole.dtype),
        in_specs=[VMEM_SPEC],
        out_specs=VMEM_SPEC,
        compiler_params=pltpu.CompilerParams(vmem_limit_bytes=VMEM_BYTES),
    )(whole)


def row_steps(rows):
    def loop(body):
        @pl.loop(0, rows // STEP)
        def _(k):
            body(pl.ds(pl.multiple_of(k * STEP, STEP), STEP))

    return loop


def product(tokens, at, pieces):
    total = None
    for piece, second in pieces:
        half = piece.shape[0]
        term = jnp.dot(tokens[at, half_slice(second, half)], piece[...], preferred_element_type=jnp.float32)
        total = term if total is None else total + term
    return total


def wave_kernel(full, part, arrived, whole, tokens, chained, stacked, *refs):
    count = len(full) + len(part)
    refs = list(refs)
    context = refs.pop(0) if "mine" in tokens else None
    other_context = refs.pop(0) if "theirs" in tokens else None
    residual = refs.pop(0) if "mine" in tokens else None
    if whole:
        shard = refs.pop(0)
        half = shard.shape[0] // 2
        jobs = [[(shard.at[half_slice(second, half)], second) for second in (False, True)]]
    else:
        jobs = [[(refs.pop(0), False)] + ([(refs.pop(0), True)] if j < len(full) else []) for j in range(count)]
    received = [refs.pop(0) for _ in arrived]
    before = refs.pop(0) if chained else None
    mine = refs.pop(0) if "mine" in tokens else None
    theirs = None
    if "theirs" in tokens:
        stacks = [refs.pop(0) for _ in range(2 if stacked else count)]
        theirs = stacks
        if stacked:
            theirs = [stacks[0].at[j] for j in range(len(full))] + [stacks[1].at[j] for j in range(len(part))]
    finished = refs.pop(0) if arrived else None
    squares = refs.pop(0) if "mine" in tokens else None
    rows, width = mine.shape[1:] if "mine" in tokens else theirs[0].shape
    if chained:
        squares[...] = before[...]
    elif "mine" in tokens:
        squares[...] = jnp.zeros_like(squares)
    for j, distance in enumerate(full + part):

        @row_steps(rows)
        def _(at):
            if "theirs" in tokens:
                theirs[j][at, :] = product(other_context, at, jobs[j])
            if "mine" in tokens:
                total = product(context, at, jobs[j])
                total += residual[at, columns(distance, True, width)].astype(jnp.float32)
                mine[j, at, :] = total
                if j < len(full):
                    add_squares(squares, at, total)

    for j, (distance, same) in enumerate(arrived):

        @row_steps(rows)
        def _(at):
            total = received[j][at, :] + residual[at, columns(distance, same, width)].astype(jnp.float32)
            finished[j, at, :] = total
            add_squares(squares, at, total)


def wave(
    full, part, arrived, context, other_context, residual, pieces, received=None, squares=None, stacked=False
):
    tokens = (("mine",) if context is not None else ()) + (("theirs",) if other_context is not None else ())
    count = len(full) + len(part)
    rows = (context if other_context is None else other_context).shape[0]
    whole = len(pieces) == 1
    block = jax.ShapeDtypeStruct((rows, pieces[0].shape[1]), jnp.float32)

    def stack(n):
        return jax.ShapeDtypeStruct((n,) + block.shape, jnp.float32)

    outs = [stack(count)] if "mine" in tokens else []
    if "theirs" in tokens:
        outs += [stack(len(full)), stack(len(part))] if stacked else [block] * count
    operands = [x for x in (context, other_context) if x is not None]
    operands += ([residual] if "mine" in tokens else []) + list(pieces)
    if arrived:
        operands += [*received] + ([] if squares is None else [squares])
        outs.append(jax.ShapeDtypeStruct((len(arrived),) + block.shape, jnp.float32))
    if "mine" in tokens:
        outs.append(jax.ShapeDtypeStruct((rows, LANES), jnp.float32))
    return pl.pallas_call(
        functools.partial(wave_kernel, full, part, arrived, whole, tokens, squares is not None, stacked),
        out_shape=outs,
        in_specs=[VMEM_SPEC] * len(operands),
        out_specs=[VMEM_SPEC] * len(outs),
        compiler_params=pltpu.CompilerParams(vmem_limit_bytes=VMEM_BYTES),
        cost_estimate=SMALL,
    )(*operands)


def late_blocks(items, context, residual, pieces, hidden, squares, target):
    rows, width = target.shape[1:]
    for i, (base, parts, bare, distance, same) in enumerate(items):

        @row_steps(rows)
        def _(at):
            value = product(context, at, [(pieces[index], second) for index, second in parts])
            if base is not None:
                known = hidden[base[0]][(at,) if base[1] is None else (base[1], at)]
                value = known if value is None else value + known
            if bare:
                value += residual[at, columns(distance, same, width)].astype(jnp.float32)
            target[i, at, :] = value
            add_squares(squares, at, value)


def late_kernel(items, n_pieces, context, residual, before, *refs):
    pieces, hidden = refs[:n_pieces], refs[n_pieces:-2]
    finished, squares = refs[-2:]
    squares[...] = before[...]
    late_blocks(items, context, residual, pieces, hidden, squares, finished)


def late(items, context, residual, squares, pieces, hidden):
    rows = context.shape[0]
    operands = [context, residual, squares, *pieces, *hidden]
    return pl.pallas_call(
        functools.partial(late_kernel, items, len(pieces)),
        out_shape=(
            jax.ShapeDtypeStruct((len(items), rows, pieces[0].shape[1]), jnp.float32),
            jax.ShapeDtypeStruct(squares.shape, jnp.float32),
        ),
        in_specs=[VMEM_SPEC] * len(operands),
        out_specs=(VMEM_SPEC, VMEM_SPEC),
        compiler_params=pltpu.CompilerParams(vmem_limit_bytes=VMEM_BYTES),
        cost_estimate=SMALL,
    )(*operands)


def final_kernel(items, sources, n_pieces, context, residual, before, gain, flags, *refs):
    pieces, hidden = refs[:n_pieces], refs[n_pieces:-6]
    embedded, payload, blocks, squares, scale_rows, sheet = refs[-6:]
    width = blocks.shape[2]
    features = embedded.shape[1]
    squares[...] = before[...]
    late_blocks(items, context, residual, pieces, hidden, squares, blocks)
    mean = jnp.sum(squares[...], axis=1, keepdims=True) * (1.0 / features)
    length = flags[:, LANES - 1 : LANES]
    row = lax.broadcasted_iota(jnp.int32, mean.shape, 0).astype(jnp.float32)
    scale = jnp.where(row < length, lax.rsqrt(mean + 1e-05), 0.0)
    scale_rows[...] = jnp.broadcast_to(scale, scale_rows.shape)
    inverse = 1.0 / length
    done = [(blocks.at[i], distance, same) for i, (_, _, _, distance, same) in enumerate(items)]
    done += [(hidden[array].at[entry], distance, same) for array, entry, distance, same in sources]
    for block, distance, same in done:
        parts = [
            jnp.sum(block[:, lane : lane + LANES] * scale_rows[...], axis=0, keepdims=True)
            for lane in range(0, width, LANES)
        ]
        where = columns(distance, same, width)
        embedded[:, where] = jnp.concatenate(parts, axis=1) * gain[:, where] * inverse
    pooled = embedded[...]
    mean = jnp.sum(pooled * pooled, axis=1, keepdims=True) * (1.0 / features)
    embedded[...] = pooled * lax.rsqrt(mean + 1e-06)
    lines = features // LANES
    sheet[lines:, :] = jnp.zeros((sheet.shape[0] - lines, LANES), jnp.float32)
    for line in range(lines):
        sheet[line : line + 1, :] = embedded[:, line * LANES : (line + 1) * LANES]
    sheet[lines : lines + 1, :] = flags[...]
    rounded = sheet[...].astype(jnp.bfloat16)
    for rank in range(payload.shape[0]):
        payload[rank] = rounded


def finish(items, sources, context, residual, squares, gain, flags, pieces, hidden, ranks):
    rows = context.shape[0]
    width = pieces[0].shape[1]
    features = (len(items) + len(sources)) * width
    lines = -(-(features // LANES + 1) // 16) * 16
    operands = [context, residual, squares, gain, flags, *pieces, *hidden]
    return pl.pallas_call(
        functools.partial(final_kernel, items, sources, len(pieces)),
        out_shape=(
            jax.ShapeDtypeStruct((1, features), jnp.float32),
            jax.ShapeDtypeStruct((ranks, lines, LANES), jnp.bfloat16),
        ),
        in_specs=[VMEM_SPEC] * len(operands),
        out_specs=(VMEM_SPEC, VMEM_SPEC),
        scratch_shapes=[
            pltpu.VMEM((len(items), rows, width), jnp.float32),
            pltpu.VMEM((rows, LANES), jnp.float32),
            pltpu.VMEM((rows, LANES), jnp.float32),
            pltpu.VMEM((lines, LANES), jnp.float32),
        ],
        compiler_params=pltpu.CompilerParams(vmem_limit_bytes=VMEM_BYTES),
        cost_estimate=SMALL,
    )(*operands)


def score_kernel(lines, blocks, got, queries, other_queries, out, wide, emb, mix):
    me = lax.axis_index("dp")
    ranks = got.shape[0]
    count = queries.shape[0]
    wide[...] = got[...].astype(jnp.float32)
    for line in range(lines):
        emb[:, line * LANES : (line + 1) * LANES] = wide[:, line, :]
    half = emb[...].astype(jnp.bfloat16)
    flags = wide[:, lines, :].astype(jnp.bfloat16)
    temper = 1.0 / (0.02 * math.sqrt(lines * LANES))
    scores, masks = [], []
    for owner, rows in ((me, queries), (me + 1 - 2 * lax.rem(me, CORES), other_queries)):
        score = lax.dot_general(
            half, rows[...], (((1,), (1,)), ((), ())), preferred_element_type=jnp.float32
        )
        scores.append(score * temper)
        block = lax.broadcasted_iota(jnp.int32, (LANES, count), 0)
        row = owner * count + lax.broadcasted_iota(jnp.int32, (LANES, count), 1)
        pick = (row >= block * QB) & (row < block * QB + QB) & (block < blocks)
        pick = jnp.where(pick, 1.0, 0.0).astype(jnp.bfloat16)
        masks.append(jnp.dot(flags, pick, preferred_element_type=jnp.float32) > 0.5)
    peaks = [
        jnp.max(jnp.where(mask, score, LOW), axis=1, keepdims=True) for score, mask in zip(scores, masks)
    ]
    peak = jnp.maximum(*peaks)
    weights = [jnp.where(mask, jnp.exp(score - peak), 0.0) for score, mask in zip(scores, masks)]
    total = sum(jnp.sum(weight, axis=1, keepdims=True) for weight in weights)
    mix[...] = jnp.dot(
        weights[0].astype(jnp.bfloat16), queries[...], preferred_element_type=jnp.float32
    ) + jnp.dot(weights[1].astype(jnp.bfloat16), other_queries[...], preferred_element_type=jnp.float32)
    for line in range(lines):
        out[:, line, :] = mix[:, line * LANES : (line + 1) * LANES]
    lane = lax.broadcasted_iota(jnp.int32, (ranks, LANES), 1)
    out[:, lines, :] = jnp.where(lane == 0, peak, jnp.where(lane == 1, total, 0.0))
    for line in range(lines + 1, out.shape[1]):
        out[:, line, :] = jnp.zeros((ranks, LANES), jnp.float32)


def score(got, queries, other_queries, blocks):
    ranks = got.shape[0]
    features = queries.shape[1]
    lines = features // LANES
    return pl.pallas_call(
        functools.partial(score_kernel, lines, blocks),
        out_shape=jax.ShapeDtypeStruct((ranks, -(-(lines + 1) // 8) * 8, LANES), jnp.float32),
        in_specs=[pl.BlockSpec(memory_space=pltpu.VMEM)] * 3,
        out_specs=pl.BlockSpec(memory_space=pltpu.VMEM),
        scratch_shapes=[
            pltpu.VMEM(got.shape, jnp.float32),
            pltpu.VMEM((ranks, features), jnp.float32),
            pltpu.VMEM((ranks, features), jnp.float32),
        ],
        compiler_params=pltpu.CompilerParams(vmem_limit_bytes=VMEM_BYTES),
    )(got, queries, other_queries)


def combine_kernel(lines, got, recalled, log_total):
    stats = got[:, lines, :]
    peaks, sums = stats[:, 0:1], stats[:, 1:2]
    peak = jnp.max(peaks, axis=0, keepdims=True)
    factor = jnp.exp(peaks - peak)
    total = jnp.sum(sums * factor, axis=0, keepdims=True)
    mix = got[0, :lines, :] * factor[0:1, :]
    for rank in range(1, got.shape[0]):
        mix += got[rank, :lines, :] * factor[rank : rank + 1, :]
    mix = mix / total
    for line in range(lines):
        recalled[:, line * LANES : (line + 1) * LANES] = mix[line : line + 1, :]
    log_total[...] = peak + jnp.log(total)


def combine(got, features):
    recalled, log_total = pl.pallas_call(
        functools.partial(combine_kernel, features // LANES),
        out_shape=(
            jax.ShapeDtypeStruct((1, features), jnp.float32),
            jax.ShapeDtypeStruct((1, 1), jnp.float32),
        ),
        in_specs=[pl.BlockSpec(memory_space=pltpu.VMEM)],
        out_specs=(pl.BlockSpec(memory_space=pltpu.VMEM), pl.BlockSpec(memory_space=pltpu.VMEM)),
        compiler_params=pltpu.CompilerParams(vmem_limit_bytes=VMEM_BYTES),
    )(got)
    return recalled, log_total.reshape(1)


def on_cycle(context, residual, out_proj, norm_gain, lengths, queries, pattern):
    ranks = lax.axis_size("dp")
    size = ranks // CORES
    features = residual.shape[1]

    def ring(step):
        return [
            (CYCLE[r] * CORES + c, CYCLE[(r + step * (1 - 2 * c)) % size] * CORES + c)
            for r in range(size)
            for c in range(CORES)
        ]

    def from_next(piece):
        return lax.ppermute(piece, "dp", ring(-1))

    def from_last(piece):
        return lax.ppermute(piece, "dp", ring(1))

    def over_x(piece):
        return lax.ppermute(piece, "groups", [(0, 1), (1, 0)])

    def other_core(piece):
        return lax.ppermute(piece, "dp", [(i, i ^ 1) for i in range(ranks)])

    wait = lax.optimization_barrier

    own = own_half(out_proj)
    a = from_next(own)
    c, q = other_core(context), other_core(queries)
    (p0,) = wave((0,), (), (), None, context, None, [out_proj])
    own, p0 = wait((own, p0))
    b = from_last(own)

    n1, p0 = wait((a, p0))
    x = over_x(n1)
    a = from_next(n1)
    context2, n1 = wait((c, n1))
    (t0,) = wave((0,), (), (), None, context2, None, [out_proj])
    l1, n1, t0, queries2 = wait((b, n1, t0, q))
    b = from_last(l1)
    r0 = other_core(t0)

    n2, l1 = wait((a, l1))
    x2 = over_x(n2)
    a = from_next(n2)
    xn1, n2 = wait((x, n2))
    x = x2
    h1, t1, f0, sq1 = wave(
        (1,), (), ((0, True), (0, False)), context, context2, residual, [n1, xn1], [p0, r0], None
    )
    l2, n2, t1, sq1, own_pattern, lengths = wait((b, n2, t1, sq1, pattern, lengths))
    b = from_last(l2)
    r1 = other_core(t1)
    flags = jnp.pad(own_pattern.astype(jnp.float32), ((0, 0), (0, LANES - 1 - pattern.shape[1])))
    flags = jnp.concatenate([flags, lengths.astype(jnp.float32)[:, None]], axis=1)

    xn2, l2, flags = wait((x, l2, flags))
    x = over_x(l2)
    a2 = from_next(xn2)
    n3, xn2 = wait((a, xn2))
    h2, t2, t2p, f1, sq2 = wave((2,), (-1,), ((1, False),), context, context2, residual, [n2, xn2, l1], [r1], sq1)
    l3, n3, t2, t2p, sq2 = wait((b, n3, t2, t2p, sq2))
    b = from_last(l3)
    r2, r2p = other_core(t2), other_core(t2p)

    n3x, l3 = wait((a2, l3))
    a = from_next(n3x)
    xl2, l1, n3x = wait((x, l1, n3x))
    x = over_x(l1)
    l4, xl2, n3x, r2p = wait((b, xl2, n3x, r2p))
    b = from_last(xl2)
    h3, t3a, t3p, f2, sq3 = wave(
        (-2, 3), (-3,), ((2, False),), context, context2, residual, [l2, xl2, n3, n3x, l3], [r2], sq2, stacked=True
    )
    r3a, r3p = other_core(t3a), other_core(t3p)
    l4s = other_core(l4)

    n4x, l4 = wait((a, l4))
    n4xs = other_core(n4x)
    items = ((None, ((0, False), (1, True)), True, 4, True),)
    h4, sq4 = late(items, context, residual, sq3, [l4, n4x], [])
    xl1, n4x, sq4 = wait((x, n4x, sq4))
    xl1s = other_core(xl1)
    items = (((0, 1), ((0, True),), False, -1, True),)
    h5, sq5 = late(items, context, residual, sq4, [xl1], [h2])
    l3x, xl1, sq5 = wait((b, xl1, sq5))
    l3xs = other_core(l3x)
    items = (
        ((0, 2), ((0, True),), False, -3, True),
        ((1, 0), (), True, -2, False),
        ((1, 1), (), True, 3, False),
        (None, ((1, False), (2, True)), True, 4, False),
    )
    h6, sq6 = late(items, context, residual, sq5, [l3x, l4s, n4xs], [h3, r3a])
    items = (((0, None), ((0, True),), True, -1, False), ((1, 0), ((1, True),), True, -3, False))
    hidden = [r2p, r3p, h1, h2, h3, h4, h5, h6, f0, f1, f2]
    sources = (
        (2, 0, 1, True),
        (3, 0, 2, True),
        (4, 0, -2, True),
        (4, 1, 3, True),
        (5, 0, 4, True),
        (6, 0, -1, True),
        (8, 0, 0, True),
        (8, 1, 0, False),
        (9, 0, 1, False),
        (10, 0, 2, False),
        (7, 0, -3, True),
        (7, 1, -2, False),
        (7, 2, 3, False),
        (7, 3, 4, False),
    )
    embedded, payload = finish(
        items, sources, context, residual, sq6, norm_gain.reshape(1, -1), flags, [xl1s, l3xs], hidden, size
    )

    same_core = [list(range(c, ranks, CORES)) for c in range(CORES)]

    def spread(blocks):
        return lax.all_to_all(blocks, "dp", 0, 0, axis_index_groups=same_core, tiled=True)

    parts = score(spread(payload), queries, queries2, pattern.shape[1])
    recalled, log_total = combine(spread(parts), features)
    return embedded, recalled, log_total


def gathered(context, residual, out_proj, norm_gain, lengths, queries, pattern):
    tok_rows = context.shape[0]
    features = residual.shape[1]
    passages_here = lengths.shape[0]
    seq_len = tok_rows // passages_here
    query_rows = queries.shape[0]
    blocks = pattern.shape[1]
    ranks = lax.axis_size("dp")
    me = lax.axis_index("dp")
    branch = jnp.dot(
        context,
        lax.all_gather(out_proj, "dp", axis=1, tiled=True),
        preferred_element_type=jnp.float32,
    )
    hidden_sum = residual.astype(jnp.float32) + branch
    normed = (
        hidden_sum
        * lax.rsqrt(jnp.mean(hidden_sum * hidden_sum, axis=-1, keepdims=True) + 1e-05)
        * norm_gain
    )
    shaped = normed.reshape(passages_here, seq_len, features)
    valid_mask = (jnp.arange(seq_len)[None, :] < lengths[:, None]).astype(jnp.float32)
    pooled = jnp.sum(shaped * valid_mask[:, :, None], axis=1) / lengths.astype(jnp.float32)[:, None]
    embedded = pooled * lax.rsqrt(jnp.mean(pooled * pooled, axis=-1, keepdims=True) + 1e-06)
    emb_half = embedded.astype(jnp.bfloat16)
    temper = 1.0 / (0.02 * math.sqrt(features))
    contract = (((1,), (1,)), ((), ()))

    flags = jnp.pad(pattern.astype(jnp.bfloat16), ((0, 0), (0, LANES - blocks)))
    everyone = lax.all_gather(jnp.concatenate([emb_half, flags], axis=1), "dp", axis=0, tiled=True)
    emb_all = everyone[:, :features]
    flags_all = everyone[:, features : features + blocks].astype(jnp.float32)
    scores = lax.dot_general(emb_all, queries, contract, preferred_element_type=jnp.float32) * temper
    row_block = (me * query_rows + jnp.arange(query_rows)) // QB
    picks = (row_block[None, :] == jnp.arange(blocks)[:, None]).astype(jnp.float32)
    cand_mask = jnp.dot(flags_all, picks) > 0
    peak_part = jnp.max(jnp.where(cand_mask, scores, LOW), axis=1, keepdims=True)
    weights = jnp.where(cand_mask, jnp.exp(scores - peak_part), 0.0)
    total_part = jnp.sum(weights, axis=1, keepdims=True)
    mix_part = jnp.dot(weights.astype(jnp.bfloat16), queries, preferred_element_type=jnp.float32)

    passages = emb_all.shape[0]
    lane = jnp.arange(LANES)[None, :]
    tail = jnp.where(lane == 0, peak_part, jnp.where(lane == 1, total_part, 0.0))
    parts = jnp.concatenate([mix_part, tail], axis=1).reshape(ranks, passages // ranks, -1)
    parts = lax.all_to_all(parts, "dp", split_axis=0, concat_axis=0, tiled=True)
    mixes, peaks, sums = parts[:, :, :features], parts[:, :, features], parts[:, :, features + 1]
    peak_score = jnp.max(peaks, axis=0)
    factor = jnp.exp(peaks - peak_score[None, :])
    totals = jnp.sum(sums * factor, axis=0)
    recalled = jnp.sum(mixes * factor[:, :, None], axis=0) / totals[:, None]
    log_total = peak_score + jnp.log(totals)
    return (embedded, recalled, log_total)


def per_device(context, residual, out_proj, norm_gain, lengths, queries, pattern):
    fits = (
        lax.axis_size("dp") == CORES * len(CYCLE)
        and lax.axis_size("groups") == 2
        and lengths.shape[0] == 1
        and out_proj.shape[1] % LANES == 0
        and out_proj.shape[0] % (2 * LANES) == 0
        and context.shape[0] % STEP == 0
        and pattern.shape[1] < LANES
    )
    form = on_cycle if fits else gathered
    return form(context, residual, out_proj, norm_gain, lengths, queries, pattern)


def solution(mesh):
    in_specs = (
        P(("groups", "dp"), None),
        P(("groups", "dp"), None),
        P(None, "dp"),
        P(),
        P(("groups", "dp")),
        P(("groups", "dp"), None),
        P(("groups", "dp"), None),
    )
    out_specs = (P(("groups", "dp"), None), P(("groups", "dp"), None), P(("groups", "dp")))
    return jax.shard_map(
        per_device, mesh=mesh, in_specs=in_specs, out_specs=out_specs, check_vma=False
    )
```

```python
import functools
import math

import jax
import jax.numpy as jnp
from jax import lax
from jax.experimental import pallas as pl
from jax.experimental.pallas import tpu as pltpu
from jax.sharding import PartitionSpec as P

QB = 256
LANES = 128
CORES = 2
STEP = 256
VMEM_BYTES = 12 << 20
LOW = -1e30
CYCLE = (0, 2, 4, 6, 7, 5, 3, 1)
VMEM_SPEC = pl.BlockSpec(memory_space=pltpu.VMEM)
SMALL = pl.CostEstimate(flops=1000, bytes_accessed=1000, transcendentals=0)


def column_block(distance, same_core):
    me = lax.axis_index("dp")
    core = lax.rem(me, CORES)
    chip = lax.div(me, CORES)
    z, y = lax.div(chip, 2), lax.rem(chip, 2)
    size = len(CYCLE)
    at = jnp.where(y == 0, z, size - 1 - z)
    core = core if same_core else 1 - core
    there = lax.rem(at + jnp.where(core == 0, size + distance, size - distance), size)
    chip = jnp.where(there < size // 2, 2 * there, 2 * (size - 1 - there) + 1)
    return chip * CORES + core


def columns(distance, same_core, width):
    return pl.ds(pl.multiple_of(column_block(distance, same_core) * width, width), width)


def half_slice(second, half):
    side = lax.axis_index("groups")
    return pl.ds(pl.multiple_of((1 - side if second else side) * half, half), half)


def add_squares(squares, at, total):
    square = total * total
    for lane in range(0, total.shape[1], LANES):
        squares[at, :] += square[:, lane : lane + LANES]


def half_kernel(whole, part):
    part[...] = whole[half_slice(False, part.shape[0]), :]


def own_half(whole):
    rows, width = whole.shape
    return pl.pallas_call(
        half_kernel,
        out_shape=jax.ShapeDtypeStruct((rows // 2, width), whole.dtype),
        in_specs=[VMEM_SPEC],
        out_specs=VMEM_SPEC,
        compiler_params=pltpu.CompilerParams(vmem_limit_bytes=VMEM_BYTES),
    )(whole)


def row_steps(rows):
    def loop(body):
        @pl.loop(0, rows // STEP)
        def _(k):
            body(pl.ds(pl.multiple_of(k * STEP, STEP), STEP))

    return loop


def product(tokens, at, pieces):
    total = None
    for piece, second in pieces:
        half = piece.shape[0]
        term = jnp.dot(tokens[at, half_slice(second, half)], piece[...], preferred_element_type=jnp.float32)
        total = term if total is None else total + term
    return total


def wave_kernel(full, part, arrived, whole, tokens, chained, stacked, *refs):
    count = len(full) + len(part)
    refs = list(refs)
    context = refs.pop(0) if "mine" in tokens else None
    other_context = refs.pop(0) if "theirs" in tokens else None
    residual = refs.pop(0) if "mine" in tokens else None
    if whole:
        shard = refs.pop(0)
        half = shard.shape[0] // 2
        jobs = [[(shard.at[half_slice(second, half)], second) for second in (False, True)]]
    else:
        jobs = [[(refs.pop(0), False)] + ([(refs.pop(0), True)] if j < len(full) else []) for j in range(count)]
    received = [refs.pop(0) for _ in arrived]
    before = refs.pop(0) if chained else None
    mine = refs.pop(0) if "mine" in tokens else None
    theirs = None
    if "theirs" in tokens:
        theirs = [refs.pop(0) for _ in range(1 if stacked else count)]
        if stacked:
            theirs = [theirs[0].at[j] for j in range(count)]
    finished = refs.pop(0) if arrived else None
    squares = refs.pop(0) if "mine" in tokens else None
    rows, width = mine.shape[1:] if "mine" in tokens else theirs[0].shape
    if chained:
        squares[...] = before[...]
    elif "mine" in tokens:
        squares[...] = jnp.zeros_like(squares)
    for j, distance in enumerate(full + part):

        @row_steps(rows)
        def _(at):
            if "theirs" in tokens:
                theirs[j][at, :] = product(other_context, at, jobs[j])
            if "mine" in tokens:
                total = product(context, at, jobs[j])
                total += residual[at, columns(distance, True, width)].astype(jnp.float32)
                mine[j, at, :] = total
                if j < len(full):
                    add_squares(squares, at, total)

    for j, (distance, same) in enumerate(arrived):

        @row_steps(rows)
        def _(at):
            total = received[j][at, :] + residual[at, columns(distance, same, width)].astype(jnp.float32)
            finished[j, at, :] = total
            add_squares(squares, at, total)


def wave(
    full, part, arrived, context, other_context, residual, pieces, received=None, squares=None, stacked=False
):
    tokens = (("mine",) if context is not None else ()) + (("theirs",) if other_context is not None else ())
    count = len(full) + len(part)
    rows = (context if other_context is None else other_context).shape[0]
    whole = len(pieces) == 1 and bool(full)
    block = jax.ShapeDtypeStruct((rows, pieces[0].shape[1]), jnp.float32)

    def stack(n):
        return jax.ShapeDtypeStruct((n,) + block.shape, jnp.float32)

    outs = [stack(count)] if "mine" in tokens else []
    if "theirs" in tokens:
        outs += [stack(count)] if stacked else [block] * count
    operands = [x for x in (context, other_context) if x is not None]
    operands += ([residual] if "mine" in tokens else []) + list(pieces)
    if arrived:
        operands += [*received]
        outs.append(jax.ShapeDtypeStruct((len(arrived),) + block.shape, jnp.float32))
    if squares is not None:
        operands.append(squares)
    if "mine" in tokens:
        outs.append(jax.ShapeDtypeStruct((rows, LANES), jnp.float32))
    return pl.pallas_call(
        functools.partial(wave_kernel, full, part, arrived, whole, tokens, squares is not None, stacked),
        out_shape=outs,
        in_specs=[VMEM_SPEC] * len(operands),
        out_specs=[VMEM_SPEC] * len(outs),
        compiler_params=pltpu.CompilerParams(vmem_limit_bytes=VMEM_BYTES),
        cost_estimate=SMALL,
    )(*operands)


def late_blocks(items, context, residual, pieces, hidden, squares, target):
    rows, width = target.shape[1:]
    for i, (base, parts, bare, distance, same) in enumerate(items):

        @row_steps(rows)
        def _(at):
            value = product(context, at, [(pieces[index], second) for index, second in parts])
            if base is not None:
                known = hidden[base[0]][(at,) if base[1] is None else (base[1], at)]
                value = known if value is None else value + known
            if bare:
                value += residual[at, columns(distance, same, width)].astype(jnp.float32)
            target[i, at, :] = value
            add_squares(squares, at, value)


def late_kernel(items, n_pieces, context, residual, before, *refs):
    pieces, hidden = refs[:n_pieces], refs[n_pieces:-2]
    finished, squares = refs[-2:]
    squares[...] = before[...]
    late_blocks(items, context, residual, pieces, hidden, squares, finished)


def late(items, context, residual, squares, pieces, hidden):
    rows = context.shape[0]
    operands = [context, residual, squares, *pieces, *hidden]
    return pl.pallas_call(
        functools.partial(late_kernel, items, len(pieces)),
        out_shape=(
            jax.ShapeDtypeStruct((len(items), rows, pieces[0].shape[1]), jnp.float32),
            jax.ShapeDtypeStruct(squares.shape, jnp.float32),
        ),
        in_specs=[VMEM_SPEC] * len(operands),
        out_specs=(VMEM_SPEC, VMEM_SPEC),
        compiler_params=pltpu.CompilerParams(vmem_limit_bytes=VMEM_BYTES),
        cost_estimate=SMALL,
    )(*operands)


def final_kernel(items, sources, n_pieces, context, residual, before, gain, flags, *refs):
    pieces, hidden = refs[:n_pieces], refs[n_pieces:-6]
    embedded, payload, blocks, squares, scale_rows, sheet = refs[-6:]
    width = blocks.shape[2]
    features = embedded.shape[1]
    squares[...] = before[...]
    late_blocks(items, context, residual, pieces, hidden, squares, blocks)
    mean = jnp.sum(squares[...], axis=1, keepdims=True) * (1.0 / features)
    length = flags[:, LANES - 1 : LANES]
    row = lax.broadcasted_iota(jnp.int32, mean.shape, 0).astype(jnp.float32)
    scale = jnp.where(row < length, lax.rsqrt(mean + 1e-05), 0.0)
    scale_rows[...] = jnp.broadcast_to(scale, scale_rows.shape)
    inverse = 1.0 / length
    done = [(blocks.at[i], distance, same) for i, (_, _, _, distance, same) in enumerate(items)]
    done += [(hidden[array].at[entry], distance, same) for array, entry, distance, same in sources]
    for block, distance, same in done:
        parts = [
            jnp.sum(block[:, lane : lane + LANES] * scale_rows[...], axis=0, keepdims=True)
            for lane in range(0, width, LANES)
        ]
        where = columns(distance, same, width)
        embedded[:, where] = jnp.concatenate(parts, axis=1) * gain[:, where] * inverse
    pooled = embedded[...]
    mean = jnp.sum(pooled * pooled, axis=1, keepdims=True) * (1.0 / features)
    embedded[...] = pooled * lax.rsqrt(mean + 1e-06)
    lines = features // LANES
    sheet[lines:, :] = jnp.zeros((sheet.shape[0] - lines, LANES), jnp.float32)
    for line in range(lines):
        sheet[line : line + 1, :] = embedded[:, line * LANES : (line + 1) * LANES]
    sheet[lines : lines + 1, :] = flags[...]
    rounded = sheet[...].astype(jnp.bfloat16)
    for rank in range(payload.shape[0]):
        payload[rank] = rounded


def finish(items, sources, context, residual, squares, gain, flags, pieces, hidden, ranks):
    rows = context.shape[0]
    width = pieces[0].shape[1]
    features = (len(items) + len(sources)) * width
    lines = -(-(features // LANES + 1) // 16) * 16
    operands = [context, residual, squares, gain, flags, *pieces, *hidden]
    return pl.pallas_call(
        functools.partial(final_kernel, items, sources, len(pieces)),
        out_shape=(
            jax.ShapeDtypeStruct((1, features), jnp.float32),
            jax.ShapeDtypeStruct((ranks, lines, LANES), jnp.bfloat16),
        ),
        in_specs=[VMEM_SPEC] * len(operands),
        out_specs=(VMEM_SPEC, VMEM_SPEC),
        scratch_shapes=[
            pltpu.VMEM((len(items), rows, width), jnp.float32),
            pltpu.VMEM((rows, LANES), jnp.float32),
            pltpu.VMEM((rows, LANES), jnp.float32),
            pltpu.VMEM((lines, LANES), jnp.float32),
        ],
        compiler_params=pltpu.CompilerParams(vmem_limit_bytes=VMEM_BYTES),
        cost_estimate=SMALL,
    )(*operands)


def score_kernel(lines, blocks, got, queries, other_queries, out, wide, emb, mix):
    me = lax.axis_index("dp")
    ranks = got.shape[0]
    count = queries.shape[0]
    wide[...] = got[...].astype(jnp.float32)
    for line in range(lines):
        emb[:, line * LANES : (line + 1) * LANES] = wide[:, line, :]
    half = emb[...].astype(jnp.bfloat16)
    flags = wide[:, lines, :].astype(jnp.bfloat16)
    temper = 1.0 / (0.02 * math.sqrt(lines * LANES))
    scores, masks = [], []
    for owner, rows in ((me, queries), (me + 1 - 2 * lax.rem(me, CORES), other_queries)):
        score = lax.dot_general(
            half, rows[...], (((1,), (1,)), ((), ())), preferred_element_type=jnp.float32
        )
        scores.append(score * temper)
        block = lax.broadcasted_iota(jnp.int32, (LANES, count), 0)
        row = owner * count + lax.broadcasted_iota(jnp.int32, (LANES, count), 1)
        pick = (row >= block * QB) & (row < block * QB + QB) & (block < blocks)
        pick = jnp.where(pick, 1.0, 0.0).astype(jnp.bfloat16)
        masks.append(jnp.dot(flags, pick, preferred_element_type=jnp.float32) > 0.5)
    peaks = [
        jnp.max(jnp.where(mask, score, LOW), axis=1, keepdims=True) for score, mask in zip(scores, masks)
    ]
    peak = jnp.maximum(*peaks)
    weights = [jnp.where(mask, jnp.exp(score - peak), 0.0) for score, mask in zip(scores, masks)]
    total = sum(jnp.sum(weight, axis=1, keepdims=True) for weight in weights)
    mix[...] = jnp.dot(
        weights[0].astype(jnp.bfloat16), queries[...], preferred_element_type=jnp.float32
    ) + jnp.dot(weights[1].astype(jnp.bfloat16), other_queries[...], preferred_element_type=jnp.float32)
    for line in range(lines):
        out[:, line, :] = mix[:, line * LANES : (line + 1) * LANES]
    lane = lax.broadcasted_iota(jnp.int32, (ranks, LANES), 1)
    out[:, lines, :] = jnp.where(lane == 0, peak, jnp.where(lane == 1, total, 0.0))
    for line in range(lines + 1, out.shape[1]):
        out[:, line, :] = jnp.zeros((ranks, LANES), jnp.float32)


def score(got, queries, other_queries, blocks):
    ranks = got.shape[0]
    features = queries.shape[1]
    lines = features // LANES
    return pl.pallas_call(
        functools.partial(score_kernel, lines, blocks),
        out_shape=jax.ShapeDtypeStruct((ranks, -(-(lines + 1) // 8) * 8, LANES), jnp.float32),
        in_specs=[pl.BlockSpec(memory_space=pltpu.VMEM)] * 3,
        out_specs=pl.BlockSpec(memory_space=pltpu.VMEM),
        scratch_shapes=[
            pltpu.VMEM(got.shape, jnp.float32),
            pltpu.VMEM((ranks, features), jnp.float32),
            pltpu.VMEM((ranks, features), jnp.float32),
        ],
        compiler_params=pltpu.CompilerParams(vmem_limit_bytes=VMEM_BYTES),
    )(got, queries, other_queries)


def combine_kernel(lines, got, recalled, log_total):
    stats = got[:, lines, :]
    peaks, sums = stats[:, 0:1], stats[:, 1:2]
    peak = jnp.max(peaks, axis=0, keepdims=True)
    factor = jnp.exp(peaks - peak)
    total = jnp.sum(sums * factor, axis=0, keepdims=True)
    mix = got[0, :lines, :] * factor[0:1, :]
    for rank in range(1, got.shape[0]):
        mix += got[rank, :lines, :] * factor[rank : rank + 1, :]
    mix = mix / total
    for line in range(lines):
        recalled[:, line * LANES : (line + 1) * LANES] = mix[line : line + 1, :]
    log_total[...] = peak + jnp.log(total)


def combine(got, features):
    recalled, log_total = pl.pallas_call(
        functools.partial(combine_kernel, features // LANES),
        out_shape=(
            jax.ShapeDtypeStruct((1, features), jnp.float32),
            jax.ShapeDtypeStruct((1, 1), jnp.float32),
        ),
        in_specs=[pl.BlockSpec(memory_space=pltpu.VMEM)],
        out_specs=(pl.BlockSpec(memory_space=pltpu.VMEM), pl.BlockSpec(memory_space=pltpu.VMEM)),
        compiler_params=pltpu.CompilerParams(vmem_limit_bytes=VMEM_BYTES),
    )(got)
    return recalled, log_total.reshape(1)


def on_cycle(context, residual, out_proj, norm_gain, lengths, queries, pattern):
    ranks = lax.axis_size("dp")
    size = ranks // CORES
    features = residual.shape[1]

    def ring(step):
        return [
            (CYCLE[r] * CORES + c, CYCLE[(r + step * (1 - 2 * c)) % size] * CORES + c)
            for r in range(size)
            for c in range(CORES)
        ]

    def from_next(piece):
        return lax.ppermute(piece, "dp", ring(-1))

    def from_last(piece):
        return lax.ppermute(piece, "dp", ring(1))

    def over_x(piece):
        return lax.ppermute(piece, "groups", [(0, 1), (1, 0)])

    def other_core(piece):
        return lax.ppermute(piece, "dp", [(i, i ^ 1) for i in range(ranks)])

    wait = lax.optimization_barrier

    own = own_half(out_proj)
    a = from_next(own)
    c, q = other_core(context), other_core(queries)
    (p0,) = wave((0,), (), (), None, context, None, [out_proj])
    own, p0 = wait((own, p0))
    b = from_last(own)

    n1, p0 = wait((a, p0))
    x = over_x(n1)
    a = from_next(n1)
    context2, n1 = wait((c, n1))
    (t0,) = wave((0,), (), (), None, context2, None, [out_proj])
    l1, n1, t0, queries2 = wait((b, n1, t0, q))
    b = from_last(l1)
    r0 = other_core(t0)

    n2, l1 = wait((a, l1))
    x2 = over_x(n2)
    a = from_next(n2)
    xn1, n2 = wait((x, n2))
    x = x2
    h1, t1, f0, sq1 = wave(
        (1,), (), ((0, True), (0, False)), context, context2, residual, [n1, xn1], [p0, r0], None
    )
    l2, n2, t1, sq1, own_pattern, lengths = wait((b, n2, t1, sq1, pattern, lengths))
    b = from_last(l2)
    r1 = other_core(t1)
    flags = jnp.pad(own_pattern.astype(jnp.float32), ((0, 0), (0, LANES - 1 - pattern.shape[1])))
    flags = jnp.concatenate([flags, lengths.astype(jnp.float32)[:, None]], axis=1)

    xn2, l2, flags = wait((x, l2, flags))
    x = over_x(l2)
    a2 = from_next(xn2)
    n3, xn2 = wait((a, xn2))
    h2, t2, t2p, f1, sq2 = wave((2,), (-1,), ((1, False),), context, context2, residual, [n2, xn2, l1], [r1], sq1)
    l3, n3, t2, t2p, sq2 = wait((b, n3, t2, t2p, sq2))
    b = from_last(l3)
    r2, r2p = other_core(t2), other_core(t2p)

    n3x, l3 = wait((a2, l3))
    a = from_next(n3x)
    xl2, l1, n3x = wait((x, l1, n3x))
    x = over_x(l1)
    h3, t3a, sq3 = wave(
        (-2, 3), (), (), context, context2, residual, [l2, xl2, n3, n3x], (), sq2, stacked=True
    )
    l4, xl2, t3a, sq3, l3, r2p = wait((b, xl2, t3a, sq3, l3, r2p))
    b = from_last(xl2)
    h3p, t3p, f2, sq3 = wave((), (-3,), ((2, False),), context, context2, residual, [l3], [r2], sq3)
    r3a, r3p = other_core(t3a), other_core(t3p)
    l4s = other_core(l4)

    n4x, l4 = wait((a, l4))
    n4xs = other_core(n4x)
    items = ((None, ((0, False), (1, True)), True, 4, True),)
    h4, sq4 = late(items, context, residual, sq3, [l4, n4x], [])
    xl1, n4x, sq4 = wait((x, n4x, sq4))
    xl1s = other_core(xl1)
    items = (((0, 1), ((0, True),), False, -1, True),)
    h5, sq5 = late(items, context, residual, sq4, [xl1], [h2])
    l3x, xl1, sq5 = wait((b, xl1, sq5))
    l3xs = other_core(l3x)
    items = (
        ((0, 0), ((0, True),), False, -3, True),
        ((1, 0), (), True, -2, False),
        ((1, 1), (), True, 3, False),
        (None, ((1, False), (2, True)), True, 4, False),
    )
    h6, sq6 = late(items, context, residual, sq5, [l3x, l4s, n4xs], [h3p, r3a])
    items = (((0, None), ((0, True),), True, -1, False), ((1, None), ((1, True),), True, -3, False))
    hidden = [r2p, r3p, h1, h2, h3, h4, h5, h6, f0, f1, f2]
    sources = (
        (2, 0, 1, True),
        (3, 0, 2, True),
        (4, 0, -2, True),
        (4, 1, 3, True),
        (5, 0, 4, True),
        (6, 0, -1, True),
        (8, 0, 0, True),
        (8, 1, 0, False),
        (9, 0, 1, False),
        (10, 0, 2, False),
        (7, 0, -3, True),
        (7, 1, -2, False),
        (7, 2, 3, False),
        (7, 3, 4, False),
    )
    embedded, payload = finish(
        items, sources, context, residual, sq6, norm_gain.reshape(1, -1), flags, [xl1s, l3xs], hidden, size
    )

    same_core = [list(range(c, ranks, CORES)) for c in range(CORES)]

    def spread(blocks):
        return lax.all_to_all(blocks, "dp", 0, 0, axis_index_groups=same_core, tiled=True)

    parts = score(spread(payload), queries, queries2, pattern.shape[1])
    recalled, log_total = combine(spread(parts), features)
    return embedded, recalled, log_total


def gathered(context, residual, out_proj, norm_gain, lengths, queries, pattern):
    tok_rows = context.shape[0]
    features = residual.shape[1]
    passages_here = lengths.shape[0]
    seq_len = tok_rows // passages_here
    query_rows = queries.shape[0]
    blocks = pattern.shape[1]
    ranks = lax.axis_size("dp")
    me = lax.axis_index("dp")
    branch = jnp.dot(
        context,
        lax.all_gather(out_proj, "dp", axis=1, tiled=True),
        preferred_element_type=jnp.float32,
    )
    hidden_sum = residual.astype(jnp.float32) + branch
    normed = (
        hidden_sum
        * lax.rsqrt(jnp.mean(hidden_sum * hidden_sum, axis=-1, keepdims=True) + 1e-05)
        * norm_gain
    )
    shaped = normed.reshape(passages_here, seq_len, features)
    valid_mask = (jnp.arange(seq_len)[None, :] < lengths[:, None]).astype(jnp.float32)
    pooled = jnp.sum(shaped * valid_mask[:, :, None], axis=1) / lengths.astype(jnp.float32)[:, None]
    embedded = pooled * lax.rsqrt(jnp.mean(pooled * pooled, axis=-1, keepdims=True) + 1e-06)
    emb_half = embedded.astype(jnp.bfloat16)
    temper = 1.0 / (0.02 * math.sqrt(features))
    contract = (((1,), (1,)), ((), ()))

    flags = jnp.pad(pattern.astype(jnp.bfloat16), ((0, 0), (0, LANES - blocks)))
    everyone = lax.all_gather(jnp.concatenate([emb_half, flags], axis=1), "dp", axis=0, tiled=True)
    emb_all = everyone[:, :features]
    flags_all = everyone[:, features : features + blocks].astype(jnp.float32)
    scores = lax.dot_general(emb_all, queries, contract, preferred_element_type=jnp.float32) * temper
    row_block = (me * query_rows + jnp.arange(query_rows)) // QB
    picks = (row_block[None, :] == jnp.arange(blocks)[:, None]).astype(jnp.float32)
    cand_mask = jnp.dot(flags_all, picks) > 0
    peak_part = jnp.max(jnp.where(cand_mask, scores, LOW), axis=1, keepdims=True)
    weights = jnp.where(cand_mask, jnp.exp(scores - peak_part), 0.0)
    total_part = jnp.sum(weights, axis=1, keepdims=True)
    mix_part = jnp.dot(weights.astype(jnp.bfloat16), queries, preferred_element_type=jnp.float32)

    passages = emb_all.shape[0]
    lane = jnp.arange(LANES)[None, :]
    tail = jnp.where(lane == 0, peak_part, jnp.where(lane == 1, total_part, 0.0))
    parts = jnp.concatenate([mix_part, tail], axis=1).reshape(ranks, passages // ranks, -1)
    parts = lax.all_to_all(parts, "dp", split_axis=0, concat_axis=0, tiled=True)
    mixes, peaks, sums = parts[:, :, :features], parts[:, :, features], parts[:, :, features + 1]
    peak_score = jnp.max(peaks, axis=0)
    factor = jnp.exp(peaks - peak_score[None, :])
    totals = jnp.sum(sums * factor, axis=0)
    recalled = jnp.sum(mixes * factor[:, :, None], axis=0) / totals[:, None]
    log_total = peak_score + jnp.log(totals)
    return (embedded, recalled, log_total)


def per_device(context, residual, out_proj, norm_gain, lengths, queries, pattern):
    fits = (
        lax.axis_size("dp") == CORES * len(CYCLE)
        and lax.axis_size("groups") == 2
        and lengths.shape[0] == 1
        and out_proj.shape[1] % LANES == 0
        and out_proj.shape[0] % (2 * LANES) == 0
        and context.shape[0] % STEP == 0
        and pattern.shape[1] < LANES
    )
    form = on_cycle if fits else gathered
    return form(context, residual, out_proj, norm_gain, lengths, queries, pattern)


def solution(mesh):
    in_specs = (
        P(("groups", "dp"), None),
        P(("groups", "dp"), None),
        P(None, "dp"),
        P(),
        P(("groups", "dp")),
        P(("groups", "dp"), None),
        P(("groups", "dp"), None),
    )
    out_specs = (P(("groups", "dp"), None), P(("groups", "dp"), None), P(("groups", "dp")))
    return jax.shard_map(
        per_device, mesh=mesh, in_specs=in_specs, out_specs=out_specs, check_vma=False
    )
```

```python
import functools
import math

import jax
import jax.numpy as jnp
from jax import lax
from jax.experimental import pallas as pl
from jax.experimental.pallas import tpu as pltpu
from jax.sharding import PartitionSpec as P

QB = 256
LANES = 128
SUBLANES = 8
CORES = 2
STEP = 256
VMEM_BYTES = 12 << 20
LOW = -1e30
CYCLE = (0, 2, 4, 6, 7, 5, 3, 1)
VMEM_SPEC = pl.BlockSpec(memory_space=pltpu.VMEM)
SMALL = pl.CostEstimate(flops=1000, bytes_accessed=1000, transcendentals=0)


def column_block(distance, same_core):
    me = lax.axis_index("dp")
    core = lax.rem(me, CORES)
    chip = lax.div(me, CORES)
    z, y = lax.div(chip, 2), lax.rem(chip, 2)
    size = len(CYCLE)
    at = jnp.where(y == 0, z, size - 1 - z)
    core = core if same_core else 1 - core
    there = lax.rem(at + jnp.where(core == 0, size + distance, size - distance), size)
    chip = jnp.where(there < size // 2, 2 * there, 2 * (size - 1 - there) + 1)
    return chip * CORES + core


def columns(distance, same_core, width):
    return pl.ds(pl.multiple_of(column_block(distance, same_core) * width, width), width)


def half_slice(second, half):
    side = lax.axis_index("groups")
    return pl.ds(pl.multiple_of((1 - side if second else side) * half, half), half)


def add_squares(squares, at, total):
    square = total * total
    for lane in range(0, total.shape[1], LANES):
        squares[at, :] += square[:, lane : lane + LANES]


def half_kernel(whole, part):
    part[...] = whole[half_slice(False, part.shape[0]), :]


def own_half(whole):
    rows, width = whole.shape
    return pl.pallas_call(
        half_kernel,
        out_shape=jax.ShapeDtypeStruct((rows // 2, width), whole.dtype),
        in_specs=[VMEM_SPEC],
        out_specs=VMEM_SPEC,
        compiler_params=pltpu.CompilerParams(vmem_limit_bytes=VMEM_BYTES),
    )(whole)


def row_steps(rows):
    def loop(body):
        @pl.loop(0, rows // STEP)
        def _(k):
            body(pl.ds(pl.multiple_of(k * STEP, STEP), STEP))

    return loop


def product(tokens, at, pieces):
    total = None
    for piece, second in pieces:
        half = piece.shape[0]
        term = jnp.dot(tokens[at, half_slice(second, half)], piece[...], preferred_element_type=jnp.float32)
        total = term if total is None else total + term
    return total


def wave_kernel(full, part, arrived, whole, tokens, chained, stacked, *refs):
    count = len(full) + len(part)
    refs = list(refs)
    context = refs.pop(0) if "mine" in tokens else None
    other_context = refs.pop(0) if "theirs" in tokens else None
    residual = refs.pop(0) if "mine" in tokens else None
    if whole:
        shard = refs.pop(0)
        half = shard.shape[0] // 2
        jobs = [[(shard.at[half_slice(second, half)], second) for second in (False, True)]]
    else:
        jobs = [[(refs.pop(0), False)] + ([(refs.pop(0), True)] if j < len(full) else []) for j in range(count)]
    received = [refs.pop(0) for _ in arrived]
    before = refs.pop(0) if chained else None
    mine = refs.pop(0) if "mine" in tokens else None
    theirs = None
    if "theirs" in tokens:
        stacks = [refs.pop(0) for _ in range(2 if stacked else count)]
        theirs = stacks
        if stacked:
            theirs = [stacks[0].at[j] for j in range(len(full))] + [stacks[1].at[j] for j in range(len(part))]
    finished = refs.pop(0) if arrived else None
    squares = refs.pop(0) if "mine" in tokens else None
    rows, width = mine.shape[1:] if "mine" in tokens else theirs[0].shape
    if chained:
        squares[...] = before[...]
    elif "mine" in tokens:
        squares[...] = jnp.zeros_like(squares)
    for j, distance in enumerate(full + part):

        @row_steps(rows)
        def _(at):
            if "theirs" in tokens:
                theirs[j][at, :] = product(other_context, at, jobs[j])
            if "mine" in tokens:
                total = product(context, at, jobs[j])
                total += residual[at, columns(distance, True, width)].astype(jnp.float32)
                mine[j, at, :] = total
                if j < len(full):
                    add_squares(squares, at, total)

    for j, (distance, same) in enumerate(arrived):

        @row_steps(rows)
        def _(at):
            total = received[j][at, :] + residual[at, columns(distance, same, width)].astype(jnp.float32)
            finished[j, at, :] = total
            add_squares(squares, at, total)


def wave(
    full, part, arrived, context, other_context, residual, pieces, received=None, squares=None, stacked=False
):
    tokens = (("mine",) if context is not None else ()) + (("theirs",) if other_context is not None else ())
    count = len(full) + len(part)
    rows = (context if other_context is None else other_context).shape[0]
    whole = len(pieces) == 1
    block = jax.ShapeDtypeStruct((rows, pieces[0].shape[1]), jnp.float32)

    def stack(n):
        return jax.ShapeDtypeStruct((n,) + block.shape, jnp.float32)

    outs = [stack(count)] if "mine" in tokens else []
    if "theirs" in tokens:
        outs += [stack(len(full)), stack(len(part))] if stacked else [block] * count
    operands = [x for x in (context, other_context) if x is not None]
    operands += ([residual] if "mine" in tokens else []) + list(pieces)
    if arrived:
        operands += [*received] + ([] if squares is None else [squares])
        outs.append(jax.ShapeDtypeStruct((len(arrived),) + block.shape, jnp.float32))
    if "mine" in tokens:
        outs.append(jax.ShapeDtypeStruct((rows, LANES), jnp.float32))
    return pl.pallas_call(
        functools.partial(wave_kernel, full, part, arrived, whole, tokens, squares is not None, stacked),
        out_shape=outs,
        in_specs=[VMEM_SPEC] * len(operands),
        out_specs=[VMEM_SPEC] * len(outs),
        compiler_params=pltpu.CompilerParams(vmem_limit_bytes=VMEM_BYTES),
        cost_estimate=SMALL,
    )(*operands)


def late_blocks(items, context, residual, pieces, hidden, squares, target):
    rows, width = target.shape[1:]
    for i, (base, parts, bare, distance, same) in enumerate(items):

        @row_steps(rows)
        def _(at):
            value = product(context, at, [(pieces[index], second) for index, second in parts])
            if base is not None:
                known = hidden[base[0]][(at,) if base[1] is None else (base[1], at)]
                value = known if value is None else value + known
            if bare:
                value += residual[at, columns(distance, same, width)].astype(jnp.float32)
            target[i, at, :] = value
            add_squares(squares, at, value)


def late_kernel(items, n_pieces, context, residual, before, *refs):
    pieces, hidden = refs[:n_pieces], refs[n_pieces:-2]
    finished, squares = refs[-2:]
    squares[...] = before[...]
    late_blocks(items, context, residual, pieces, hidden, squares, finished)


def late(items, context, residual, squares, pieces, hidden):
    rows = context.shape[0]
    operands = [context, residual, squares, *pieces, *hidden]
    return pl.pallas_call(
        functools.partial(late_kernel, items, len(pieces)),
        out_shape=(
            jax.ShapeDtypeStruct((len(items), rows, pieces[0].shape[1]), jnp.float32),
            jax.ShapeDtypeStruct(squares.shape, jnp.float32),
        ),
        in_specs=[VMEM_SPEC] * len(operands),
        out_specs=(VMEM_SPEC, VMEM_SPEC),
        compiler_params=pltpu.CompilerParams(vmem_limit_bytes=VMEM_BYTES),
        cost_estimate=SMALL,
    )(*operands)


def final_kernel(items, sources, n_pieces, context, residual, before, gain, flags, *refs):
    pieces, hidden = refs[:n_pieces], refs[n_pieces:-6]
    embedded, payload, blocks, squares, scale_rows, sheet = refs[-6:]
    width = blocks.shape[2]
    features = embedded.shape[1]
    squares[...] = before[...]
    late_blocks(items, context, residual, pieces, hidden, squares, blocks)
    mean = jnp.sum(squares[...], axis=1, keepdims=True) * (1.0 / features)
    length = flags[:, LANES - 1 : LANES]
    row = lax.broadcasted_iota(jnp.int32, mean.shape, 0).astype(jnp.float32)
    scale = jnp.where(row < length, lax.rsqrt(mean + 1e-05), 0.0)
    scale_rows[...] = jnp.broadcast_to(scale, scale_rows.shape)
    inverse = 1.0 / length
    done = [(blocks.at[i], distance, same) for i, (_, _, _, distance, same) in enumerate(items)]
    done += [(hidden[array].at[entry], distance, same) for array, entry, distance, same in sources]
    lanes = range(0, width, LANES)

    def add_rows(k, sums):
        at = pl.ds(pl.multiple_of(k * SUBLANES, SUBLANES), SUBLANES)
        weight = scale_rows[at, :]
        terms = [block[at, lane : lane + LANES] * weight for block, _, _ in done for lane in lanes]
        return tuple(total + term for total, term in zip(sums, terms))

    zero = jnp.zeros((SUBLANES, LANES), jnp.float32)
    sums = lax.fori_loop(0, scale_rows.shape[0] // SUBLANES, add_rows, (zero,) * (len(done) * len(lanes)))
    for i, (_, distance, same) in enumerate(done):
        parts = [jnp.sum(part, axis=0, keepdims=True) for part in sums[i * len(lanes) : (i + 1) * len(lanes)]]
        where = columns(distance, same, width)
        embedded[:, where] = jnp.concatenate(parts, axis=1) * gain[:, where] * inverse
    pooled = embedded[...]
    mean = jnp.sum(pooled * pooled, axis=1, keepdims=True) * (1.0 / features)
    embedded[...] = pooled * lax.rsqrt(mean + 1e-06)
    lines = features // LANES
    sheet[lines:, :] = jnp.zeros((sheet.shape[0] - lines, LANES), jnp.float32)
    for line in range(lines):
        sheet[line : line + 1, :] = embedded[:, line * LANES : (line + 1) * LANES]
    sheet[lines : lines + 1, :] = flags[...]
    rounded = sheet[...].astype(jnp.bfloat16)
    for rank in range(payload.shape[0]):
        payload[rank] = rounded


def finish(items, sources, context, residual, squares, gain, flags, pieces, hidden, ranks):
    rows = context.shape[0]
    width = pieces[0].shape[1]
    features = (len(items) + len(sources)) * width
    lines = -(-(features // LANES + 1) // 16) * 16
    operands = [context, residual, squares, gain, flags, *pieces, *hidden]
    return pl.pallas_call(
        functools.partial(final_kernel, items, sources, len(pieces)),
        out_shape=(
            jax.ShapeDtypeStruct((1, features), jnp.float32),
            jax.ShapeDtypeStruct((ranks, lines, LANES), jnp.bfloat16),
        ),
        in_specs=[VMEM_SPEC] * len(operands),
        out_specs=(VMEM_SPEC, VMEM_SPEC),
        scratch_shapes=[
            pltpu.VMEM((len(items), rows, width), jnp.float32),
            pltpu.VMEM((rows, LANES), jnp.float32),
            pltpu.VMEM((rows, LANES), jnp.float32),
            pltpu.VMEM((lines, LANES), jnp.float32),
        ],
        compiler_params=pltpu.CompilerParams(vmem_limit_bytes=VMEM_BYTES),
        cost_estimate=SMALL,
    )(*operands)


def score_kernel(lines, blocks, got, queries, other_queries, out, wide, emb, mix):
    me = lax.axis_index("dp")
    ranks = got.shape[0]
    count = queries.shape[0]
    wide[...] = got[...].astype(jnp.float32)
    for line in range(lines):
        emb[:, line * LANES : (line + 1) * LANES] = wide[:, line, :]
    half = emb[...].astype(jnp.bfloat16)
    flags = wide[:, lines, :].astype(jnp.bfloat16)
    temper = 1.0 / (0.02 * math.sqrt(lines * LANES))
    scores, masks = [], []
    for owner, rows in ((me, queries), (me + 1 - 2 * lax.rem(me, CORES), other_queries)):
        score = lax.dot_general(
            half, rows[...], (((1,), (1,)), ((), ())), preferred_element_type=jnp.float32
        )
        scores.append(score * temper)
        block = lax.broadcasted_iota(jnp.int32, (LANES, count), 0)
        row = owner * count + lax.broadcasted_iota(jnp.int32, (LANES, count), 1)
        pick = (row >= block * QB) & (row < block * QB + QB) & (block < blocks)
        pick = jnp.where(pick, 1.0, 0.0).astype(jnp.bfloat16)
        masks.append(jnp.dot(flags, pick, preferred_element_type=jnp.float32) > 0.5)
    peaks = [
        jnp.max(jnp.where(mask, score, LOW), axis=1, keepdims=True) for score, mask in zip(scores, masks)
    ]
    peak = jnp.maximum(*peaks)
    weights = [jnp.where(mask, jnp.exp(score - peak), 0.0) for score, mask in zip(scores, masks)]
    total = sum(jnp.sum(weight, axis=1, keepdims=True) for weight in weights)
    mix[...] = jnp.dot(
        weights[0].astype(jnp.bfloat16), queries[...], preferred_element_type=jnp.float32
    ) + jnp.dot(weights[1].astype(jnp.bfloat16), other_queries[...], preferred_element_type=jnp.float32)
    for line in range(lines):
        out[:, line, :] = mix[:, line * LANES : (line + 1) * LANES]
    lane = lax.broadcasted_iota(jnp.int32, (ranks, LANES), 1)
    out[:, lines, :] = jnp.where(lane == 0, peak, jnp.where(lane == 1, total, 0.0))
    for line in range(lines + 1, out.shape[1]):
        out[:, line, :] = jnp.zeros((ranks, LANES), jnp.float32)


def score(got, queries, other_queries, blocks):
    ranks = got.shape[0]
    features = queries.shape[1]
    lines = features // LANES
    return pl.pallas_call(
        functools.partial(score_kernel, lines, blocks),
        out_shape=jax.ShapeDtypeStruct((ranks, -(-(lines + 1) // 8) * 8, LANES), jnp.float32),
        in_specs=[pl.BlockSpec(memory_space=pltpu.VMEM)] * 3,
        out_specs=pl.BlockSpec(memory_space=pltpu.VMEM),
        scratch_shapes=[
            pltpu.VMEM(got.shape, jnp.float32),
            pltpu.VMEM((ranks, features), jnp.float32),
            pltpu.VMEM((ranks, features), jnp.float32),
        ],
        compiler_params=pltpu.CompilerParams(vmem_limit_bytes=VMEM_BYTES),
    )(got, queries, other_queries)


def combine_kernel(lines, got, recalled, log_total):
    stats = got[:, lines, :]
    peaks, sums = stats[:, 0:1], stats[:, 1:2]
    peak = jnp.max(peaks, axis=0, keepdims=True)
    factor = jnp.exp(peaks - peak)
    total = jnp.sum(sums * factor, axis=0, keepdims=True)
    mix = got[0, :lines, :] * factor[0:1, :]
    for rank in range(1, got.shape[0]):
        mix += got[rank, :lines, :] * factor[rank : rank + 1, :]
    mix = mix / total
    for line in range(lines):
        recalled[:, line * LANES : (line + 1) * LANES] = mix[line : line + 1, :]
    log_total[...] = peak + jnp.log(total)


def combine(got, features):
    recalled, log_total = pl.pallas_call(
        functools.partial(combine_kernel, features // LANES),
        out_shape=(
            jax.ShapeDtypeStruct((1, features), jnp.float32),
            jax.ShapeDtypeStruct((1, 1), jnp.float32),
        ),
        in_specs=[pl.BlockSpec(memory_space=pltpu.VMEM)],
        out_specs=(pl.BlockSpec(memory_space=pltpu.VMEM), pl.BlockSpec(memory_space=pltpu.VMEM)),
        compiler_params=pltpu.CompilerParams(vmem_limit_bytes=VMEM_BYTES),
    )(got)
    return recalled, log_total.reshape(1)


def on_cycle(context, residual, out_proj, norm_gain, lengths, queries, pattern):
    ranks = lax.axis_size("dp")
    size = ranks // CORES
    features = residual.shape[1]

    def ring(step):
        return [
            (CYCLE[r] * CORES + c, CYCLE[(r + step * (1 - 2 * c)) % size] * CORES + c)
            for r in range(size)
            for c in range(CORES)
        ]

    def from_next(piece):
        return lax.ppermute(piece, "dp", ring(-1))

    def from_last(piece):
        return lax.ppermute(piece, "dp", ring(1))

    def over_x(piece):
        return lax.ppermute(piece, "groups", [(0, 1), (1, 0)])

    def other_core(piece):
        return lax.ppermute(piece, "dp", [(i, i ^ 1) for i in range(ranks)])

    wait = lax.optimization_barrier

    own = own_half(out_proj)
    a = from_next(own)
    c, q = other_core(context), other_core(queries)
    (p0,) = wave((0,), (), (), None, context, None, [out_proj])
    own, p0 = wait((own, p0))
    b = from_last(own)

    n1, p0 = wait((a, p0))
    x = over_x(n1)
    a = from_next(n1)
    context2, n1 = wait((c, n1))
    (t0,) = wave((0,), (), (), None, context2, None, [out_proj])
    l1, n1, t0, queries2 = wait((b, n1, t0, q))
    b = from_last(l1)
    r0 = other_core(t0)

    n2, l1 = wait((a, l1))
    x2 = over_x(n2)
    a = from_next(n2)
    xn1, n2 = wait((x, n2))
    x = x2
    h1, t1, f0, sq1 = wave(
        (1,), (), ((0, True), (0, False)), context, context2, residual, [n1, xn1], [p0, r0], None
    )
    l2, n2, t1, sq1 = wait((b, n2, t1, sq1))
    b = from_last(l2)
    r1 = other_core(t1)

    xn2, l2 = wait((x, l2))
    x = over_x(l2)
    a2 = from_next(xn2)
    n3, xn2 = wait((a, xn2))
    h2, t2, t2p, f1, sq2 = wave((2,), (-1,), ((1, False),), context, context2, residual, [n2, xn2, l1], [r1], sq1)
    l3, n3, t2, t2p, sq2 = wait((b, n3, t2, t2p, sq2))
    b = from_last(l3)
    r2, r2p = other_core(t2), other_core(t2p)

    n3x, l3 = wait((a2, l3))
    a = from_next(n3x)
    xl2, l1, n3x = wait((x, l1, n3x))
    x = over_x(l1)
    h3, t3a, t3p, f2, sq3 = wave(
        (-2, 3), (-3,), ((2, False),), context, context2, residual, [l2, xl2, n3, n3x, l3], [r2], sq2, stacked=True
    )
    l4, xl2, t3a, t3p, sq3, r2p = wait((b, xl2, t3a, t3p, sq3, r2p))
    b = from_last(xl2)
    r3a, r3p = other_core(t3a), other_core(t3p)
    l4s = other_core(l4)

    n4x, l4, own_pattern, lengths = wait((a, l4, pattern, lengths))
    flags = jnp.pad(own_pattern.astype(jnp.float32), ((0, 0), (0, LANES - 1 - pattern.shape[1])))
    flags = jnp.concatenate([flags, lengths.astype(jnp.float32)[:, None]], axis=1)
    n4xs = other_core(n4x)
    items = ((None, ((0, False), (1, True)), True, 4, True),)
    h4, sq4 = late(items, context, residual, sq3, [l4, n4x], [])
    xl1, n4x, sq4, flags = wait((x, n4x, sq4, flags))
    xl1s = other_core(xl1)
    items = (((0, 1), ((0, True),), False, -1, True),)
    h5, sq5 = late(items, context, residual, sq4, [xl1], [h2])
    l3x, xl1, sq5 = wait((b, xl1, sq5))
    l3xs = other_core(l3x)
    items = (
        ((0, 2), ((0, True),), False, -3, True),
        ((1, 0), (), True, -2, False),
        ((1, 1), (), True, 3, False),
        (None, ((1, False), (2, True)), True, 4, False),
    )
    h6, sq6 = late(items, context, residual, sq5, [l3x, l4s, n4xs], [h3, r3a])
    items = (((0, None), ((0, True),), True, -1, False), ((1, 0), ((1, True),), True, -3, False))
    hidden = [r2p, r3p, h1, h2, h3, h4, h5, h6, f0, f1, f2]
    sources = (
        (2, 0, 1, True),
        (3, 0, 2, True),
        (4, 0, -2, True),
        (4, 1, 3, True),
        (5, 0, 4, True),
        (6, 0, -1, True),
        (8, 0, 0, True),
        (8, 1, 0, False),
        (9, 0, 1, False),
        (10, 0, 2, False),
        (7, 0, -3, True),
        (7, 1, -2, False),
        (7, 2, 3, False),
        (7, 3, 4, False),
    )
    embedded, payload = finish(
        items, sources, context, residual, sq6, norm_gain.reshape(1, -1), flags, [xl1s, l3xs], hidden, size
    )

    same_core = [list(range(c, ranks, CORES)) for c in range(CORES)]

    def spread(blocks):
        return lax.all_to_all(blocks, "dp", 0, 0, axis_index_groups=same_core, tiled=True)

    parts = score(spread(payload), queries, queries2, pattern.shape[1])
    recalled, log_total = combine(spread(parts), features)
    return embedded, recalled, log_total


def gathered(context, residual, out_proj, norm_gain, lengths, queries, pattern):
    tok_rows = context.shape[0]
    features = residual.shape[1]
    passages_here = lengths.shape[0]
    seq_len = tok_rows // passages_here
    query_rows = queries.shape[0]
    blocks = pattern.shape[1]
    ranks = lax.axis_size("dp")
    me = lax.axis_index("dp")
    branch = jnp.dot(
        context,
        lax.all_gather(out_proj, "dp", axis=1, tiled=True),
        preferred_element_type=jnp.float32,
    )
    hidden_sum = residual.astype(jnp.float32) + branch
    normed = (
        hidden_sum
        * lax.rsqrt(jnp.mean(hidden_sum * hidden_sum, axis=-1, keepdims=True) + 1e-05)
        * norm_gain
    )
    shaped = normed.reshape(passages_here, seq_len, features)
    valid_mask = (jnp.arange(seq_len)[None, :] < lengths[:, None]).astype(jnp.float32)
    pooled = jnp.sum(shaped * valid_mask[:, :, None], axis=1) / lengths.astype(jnp.float32)[:, None]
    embedded = pooled * lax.rsqrt(jnp.mean(pooled * pooled, axis=-1, keepdims=True) + 1e-06)
    emb_half = embedded.astype(jnp.bfloat16)
    temper = 1.0 / (0.02 * math.sqrt(features))
    contract = (((1,), (1,)), ((), ()))

    flags = jnp.pad(pattern.astype(jnp.bfloat16), ((0, 0), (0, LANES - blocks)))
    everyone = lax.all_gather(jnp.concatenate([emb_half, flags], axis=1), "dp", axis=0, tiled=True)
    emb_all = everyone[:, :features]
    flags_all = everyone[:, features : features + blocks].astype(jnp.float32)
    scores = lax.dot_general(emb_all, queries, contract, preferred_element_type=jnp.float32) * temper
    row_block = (me * query_rows + jnp.arange(query_rows)) // QB
    picks = (row_block[None, :] == jnp.arange(blocks)[:, None]).astype(jnp.float32)
    cand_mask = jnp.dot(flags_all, picks) > 0
    peak_part = jnp.max(jnp.where(cand_mask, scores, LOW), axis=1, keepdims=True)
    weights = jnp.where(cand_mask, jnp.exp(scores - peak_part), 0.0)
    total_part = jnp.sum(weights, axis=1, keepdims=True)
    mix_part = jnp.dot(weights.astype(jnp.bfloat16), queries, preferred_element_type=jnp.float32)

    passages = emb_all.shape[0]
    lane = jnp.arange(LANES)[None, :]
    tail = jnp.where(lane == 0, peak_part, jnp.where(lane == 1, total_part, 0.0))
    parts = jnp.concatenate([mix_part, tail], axis=1).reshape(ranks, passages // ranks, -1)
    parts = lax.all_to_all(parts, "dp", split_axis=0, concat_axis=0, tiled=True)
    mixes, peaks, sums = parts[:, :, :features], parts[:, :, features], parts[:, :, features + 1]
    peak_score = jnp.max(peaks, axis=0)
    factor = jnp.exp(peaks - peak_score[None, :])
    totals = jnp.sum(sums * factor, axis=0)
    recalled = jnp.sum(mixes * factor[:, :, None], axis=0) / totals[:, None]
    log_total = peak_score + jnp.log(totals)
    return (embedded, recalled, log_total)


def per_device(context, residual, out_proj, norm_gain, lengths, queries, pattern):
    fits = (
        lax.axis_size("dp") == CORES * len(CYCLE)
        and lax.axis_size("groups") == 2
        and lengths.shape[0] == 1
        and out_proj.shape[1] % LANES == 0
        and out_proj.shape[0] % (2 * LANES) == 0
        and context.shape[0] % STEP == 0
        and pattern.shape[1] < LANES
    )
    form = on_cycle if fits else gathered
    return form(context, residual, out_proj, norm_gain, lengths, queries, pattern)


def solution(mesh):
    in_specs = (
        P(("groups", "dp"), None),
        P(("groups", "dp"), None),
        P(None, "dp"),
        P(),
        P(("groups", "dp")),
        P(("groups", "dp"), None),
        P(("groups", "dp"), None),
    )
    out_specs = (P(("groups", "dp"), None), P(("groups", "dp"), None), P(("groups", "dp")))
    return jax.shard_map(
        per_device, mesh=mesh, in_specs=in_specs, out_specs=out_specs, check_vma=False
    )
```

```python
import functools
import math

import jax
import jax.numpy as jnp
from jax import lax
from jax.experimental import pallas as pl
from jax.experimental.pallas import tpu as pltpu
from jax.sharding import PartitionSpec as P

QB = 256
LANES = 128
CORES = 2
STEP = 256
VMEM_BYTES = 12 << 20
LOW = -1e30
CYCLE = (0, 2, 4, 6, 7, 5, 3, 1)
VMEM_SPEC = pl.BlockSpec(memory_space=pltpu.VMEM)
SMALL = pl.CostEstimate(flops=1000, bytes_accessed=1000, transcendentals=0)


def column_block(distance, same_core):
    me = lax.axis_index("dp")
    core = lax.rem(me, CORES)
    chip = lax.div(me, CORES)
    z, y = lax.div(chip, 2), lax.rem(chip, 2)
    size = len(CYCLE)
    at = jnp.where(y == 0, z, size - 1 - z)
    core = core if same_core else 1 - core
    there = lax.rem(at + jnp.where(core == 0, size + distance, size - distance), size)
    chip = jnp.where(there < size // 2, 2 * there, 2 * (size - 1 - there) + 1)
    return chip * CORES + core


def columns(distance, same_core, width):
    return pl.ds(pl.multiple_of(column_block(distance, same_core) * width, width), width)


def half_slice(second, half):
    side = lax.axis_index("groups")
    return pl.ds(pl.multiple_of((1 - side if second else side) * half, half), half)


def add_squares(squares, at, total):
    square = total * total
    for lane in range(0, total.shape[1], LANES):
        squares[at, :] += square[:, lane : lane + LANES]


def half_kernel(whole, part):
    part[...] = whole[half_slice(False, part.shape[0]), :]


def own_half(whole):
    rows, width = whole.shape
    return pl.pallas_call(
        half_kernel,
        out_shape=jax.ShapeDtypeStruct((rows // 2, width), whole.dtype),
        in_specs=[VMEM_SPEC],
        out_specs=VMEM_SPEC,
        compiler_params=pltpu.CompilerParams(vmem_limit_bytes=VMEM_BYTES),
    )(whole)


def row_steps(rows):
    def loop(body):
        @pl.loop(0, rows // STEP)
        def _(k):
            body(pl.ds(pl.multiple_of(k * STEP, STEP), STEP))

    return loop


def product(tokens, at, pieces):
    total = None
    for piece, second in pieces:
        half = piece.shape[0]
        term = jnp.dot(tokens[at, half_slice(second, half)], piece[...], preferred_element_type=jnp.float32)
        total = term if total is None else total + term
    return total


def wave_kernel(full, part, arrived, whole, tokens, chained, stacked, *refs):
    count = len(full) + len(part)
    refs = list(refs)
    context = refs.pop(0) if "mine" in tokens else None
    other_context = refs.pop(0) if "theirs" in tokens else None
    residual = refs.pop(0) if "mine" in tokens else None
    if whole:
        shard = refs.pop(0)
        half = shard.shape[0] // 2
        jobs = [[(shard.at[half_slice(second, half)], second) for second in (False, True)]]
    else:
        jobs = [[(refs.pop(0), False)] + ([(refs.pop(0), True)] if j < len(full) else []) for j in range(count)]
    received = [refs.pop(0) for _ in arrived]
    before = refs.pop(0) if chained else None
    mine = refs.pop(0) if "mine" in tokens else None
    theirs = None
    if "theirs" in tokens:
        stacks = [refs.pop(0) for _ in range(2 if stacked else count)]
        theirs = stacks
        if stacked:
            theirs = [stacks[0].at[j] for j in range(len(full))] + [stacks[1].at[j] for j in range(len(part))]
    finished = refs.pop(0) if arrived else None
    squares = refs.pop(0) if "mine" in tokens else None
    rows, width = mine.shape[1:] if "mine" in tokens else theirs[0].shape
    if chained:
        squares[...] = before[...]
    elif "mine" in tokens:
        squares[...] = jnp.zeros_like(squares)
    for j, distance in enumerate(full + part):

        @row_steps(rows)
        def _(at):
            if "theirs" in tokens:
                theirs[j][at, :] = product(other_context, at, jobs[j])
            if "mine" in tokens:
                total = product(context, at, jobs[j])
                total += residual[at, columns(distance, True, width)].astype(jnp.float32)
                mine[j, at, :] = total
                if j < len(full):
                    add_squares(squares, at, total)

    for j, (distance, same) in enumerate(arrived):

        @row_steps(rows)
        def _(at):
            total = received[j][at, :] + residual[at, columns(distance, same, width)].astype(jnp.float32)
            finished[j, at, :] = total
            add_squares(squares, at, total)


def wave(
    full, part, arrived, context, other_context, residual, pieces, received=None, squares=None, stacked=False
):
    tokens = (("mine",) if context is not None else ()) + (("theirs",) if other_context is not None else ())
    count = len(full) + len(part)
    rows = (context if other_context is None else other_context).shape[0]
    whole = len(pieces) == 1
    block = jax.ShapeDtypeStruct((rows, pieces[0].shape[1]), jnp.float32)

    def stack(n):
        return jax.ShapeDtypeStruct((n,) + block.shape, jnp.float32)

    outs = [stack(count)] if "mine" in tokens else []
    if "theirs" in tokens:
        outs += [stack(len(full)), stack(len(part))] if stacked else [block] * count
    operands = [x for x in (context, other_context) if x is not None]
    operands += ([residual] if "mine" in tokens else []) + list(pieces)
    if arrived:
        operands += [*received] + ([] if squares is None else [squares])
        outs.append(jax.ShapeDtypeStruct((len(arrived),) + block.shape, jnp.float32))
    if "mine" in tokens:
        outs.append(jax.ShapeDtypeStruct((rows, LANES), jnp.float32))
    return pl.pallas_call(
        functools.partial(wave_kernel, full, part, arrived, whole, tokens, squares is not None, stacked),
        out_shape=outs,
        in_specs=[VMEM_SPEC] * len(operands),
        out_specs=[VMEM_SPEC] * len(outs),
        compiler_params=pltpu.CompilerParams(vmem_limit_bytes=VMEM_BYTES),
        cost_estimate=SMALL,
    )(*operands)


def late_blocks(items, context, residual, pieces, hidden, squares, target):
    rows, width = target.shape[1:]
    for i, (base, parts, bare, distance, same) in enumerate(items):

        @row_steps(rows)
        def _(at):
            value = product(context, at, [(pieces[index], second) for index, second in parts])
            if base is not None:
                known = hidden[base[0]][(at,) if base[1] is None else (base[1], at)]
                value = known if value is None else value + known
            if bare:
                value += residual[at, columns(distance, same, width)].astype(jnp.float32)
            target[i, at, :] = value
            add_squares(squares, at, value)


def late_kernel(items, n_pieces, context, residual, before, *refs):
    pieces, hidden = refs[:n_pieces], refs[n_pieces:-2]
    finished, squares = refs[-2:]
    squares[...] = before[...]
    late_blocks(items, context, residual, pieces, hidden, squares, finished)


def late(items, context, residual, squares, pieces, hidden):
    rows = context.shape[0]
    operands = [context, residual, squares, *pieces, *hidden]
    return pl.pallas_call(
        functools.partial(late_kernel, items, len(pieces)),
        out_shape=(
            jax.ShapeDtypeStruct((len(items), rows, pieces[0].shape[1]), jnp.float32),
            jax.ShapeDtypeStruct(squares.shape, jnp.float32),
        ),
        in_specs=[VMEM_SPEC] * len(operands),
        out_specs=(VMEM_SPEC, VMEM_SPEC),
        compiler_params=pltpu.CompilerParams(vmem_limit_bytes=VMEM_BYTES),
        cost_estimate=SMALL,
    )(*operands)


def final_kernel(items, sources, n_pieces, context, residual, before, gain, flags, *refs):
    pieces, hidden = refs[:n_pieces], refs[n_pieces:-6]
    embedded, payload, blocks, squares, scale_rows, sheet = refs[-6:]
    width = blocks.shape[2]
    features = embedded.shape[1]
    squares[...] = before[...]
    late_blocks(items, context, residual, pieces, hidden, squares, blocks)
    mean = jnp.sum(squares[...], axis=1, keepdims=True) * (1.0 / features)
    length = flags[:, LANES - 1 : LANES]
    row = lax.broadcasted_iota(jnp.int32, mean.shape, 0).astype(jnp.float32)
    scale = jnp.where(row < length, lax.rsqrt(mean + 1e-05), 0.0)
    scale_rows[...] = jnp.broadcast_to(scale, scale_rows.shape)
    inverse = 1.0 / length
    done = [(blocks.at[i], distance, same) for i, (_, _, _, distance, same) in enumerate(items)]
    done += [(hidden[array].at[entry], distance, same) for array, entry, distance, same in sources]
    for block, distance, same in done:
        parts = [
            jnp.sum(block[:, lane : lane + LANES] * scale_rows[...], axis=0, keepdims=True)
            for lane in range(0, width, LANES)
        ]
        where = columns(distance, same, width)
        embedded[:, where] = jnp.concatenate(parts, axis=1) * gain[:, where] * inverse
    pooled = embedded[...]
    mean = jnp.sum(pooled * pooled, axis=1, keepdims=True) * (1.0 / features)
    embedded[...] = pooled * lax.rsqrt(mean + 1e-06)
    lines = features // LANES
    sheet[lines:, :] = jnp.zeros((sheet.shape[0] - lines, LANES), jnp.float32)
    for line in range(lines):
        sheet[line : line + 1, :] = embedded[:, line * LANES : (line + 1) * LANES]
    sheet[lines : lines + 1, :] = flags[...]
    rounded = sheet[...].astype(jnp.bfloat16)
    for rank in range(payload.shape[0]):
        payload[rank] = rounded


def finish(items, sources, context, residual, squares, gain, flags, pieces, hidden, ranks):
    rows = context.shape[0]
    width = pieces[0].shape[1]
    features = (len(items) + len(sources)) * width
    lines = -(-(features // LANES + 1) // 16) * 16
    operands = [context, residual, squares, gain, flags, *pieces, *hidden]
    return pl.pallas_call(
        functools.partial(final_kernel, items, sources, len(pieces)),
        out_shape=(
            jax.ShapeDtypeStruct((1, features), jnp.float32),
            jax.ShapeDtypeStruct((ranks, lines, LANES), jnp.bfloat16),
        ),
        in_specs=[VMEM_SPEC] * len(operands),
        out_specs=(VMEM_SPEC, VMEM_SPEC),
        scratch_shapes=[
            pltpu.VMEM((len(items), rows, width), jnp.float32),
            pltpu.VMEM((rows, LANES), jnp.float32),
            pltpu.VMEM((rows, LANES), jnp.float32),
            pltpu.VMEM((lines, LANES), jnp.float32),
        ],
        compiler_params=pltpu.CompilerParams(vmem_limit_bytes=VMEM_BYTES),
        cost_estimate=SMALL,
    )(*operands)


def score_kernel(lines, blocks, got, queries, other_queries, out, wide, emb, mix):
    me = lax.axis_index("dp")
    ranks = got.shape[0]
    count = queries.shape[0]
    wide[...] = got[...].astype(jnp.float32)
    for line in range(lines):
        emb[:, line * LANES : (line + 1) * LANES] = wide[:, line, :]
    half = emb[...].astype(jnp.bfloat16)
    flags = wide[:, lines, :].astype(jnp.bfloat16)
    temper = 1.0 / (0.02 * math.sqrt(lines * LANES))
    scores, masks = [], []
    for owner, rows in ((me, queries), (me + 1 - 2 * lax.rem(me, CORES), other_queries)):
        score = lax.dot_general(
            half, rows[...], (((1,), (1,)), ((), ())), preferred_element_type=jnp.float32
        )
        scores.append(score * temper)
        block = lax.broadcasted_iota(jnp.int32, (LANES, count), 0)
        row = owner * count + lax.broadcasted_iota(jnp.int32, (LANES, count), 1)
        pick = (row >= block * QB) & (row < block * QB + QB) & (block < blocks)
        pick = jnp.where(pick, 1.0, 0.0).astype(jnp.bfloat16)
        masks.append(jnp.dot(flags, pick, preferred_element_type=jnp.float32) > 0.5)
    peaks = [
        jnp.max(jnp.where(mask, score, LOW), axis=1, keepdims=True) for score, mask in zip(scores, masks)
    ]
    peak = jnp.maximum(*peaks)
    weights = [jnp.where(mask, jnp.exp(score - peak), 0.0) for score, mask in zip(scores, masks)]
    total = sum(jnp.sum(weight, axis=1, keepdims=True) for weight in weights)
    mix[...] = jnp.dot(
        weights[0].astype(jnp.bfloat16), queries[...], preferred_element_type=jnp.float32
    ) + jnp.dot(weights[1].astype(jnp.bfloat16), other_queries[...], preferred_element_type=jnp.float32)
    for line in range(lines):
        out[:, line, :] = mix[:, line * LANES : (line + 1) * LANES]
    lane = lax.broadcasted_iota(jnp.int32, (ranks, LANES), 1)
    out[:, lines, :] = jnp.where(lane == 0, peak, jnp.where(lane == 1, total, 0.0))
    for line in range(lines + 1, out.shape[1]):
        out[:, line, :] = jnp.zeros((ranks, LANES), jnp.float32)


def score(got, queries, other_queries, blocks):
    ranks = got.shape[0]
    features = queries.shape[1]
    lines = features // LANES
    return pl.pallas_call(
        functools.partial(score_kernel, lines, blocks),
        out_shape=jax.ShapeDtypeStruct((ranks, -(-(lines + 1) // 8) * 8, LANES), jnp.float32),
        in_specs=[pl.BlockSpec(memory_space=pltpu.VMEM)] * 3,
        out_specs=pl.BlockSpec(memory_space=pltpu.VMEM),
        scratch_shapes=[
            pltpu.VMEM(got.shape, jnp.float32),
            pltpu.VMEM((ranks, features), jnp.float32),
            pltpu.VMEM((ranks, features), jnp.float32),
        ],
        compiler_params=pltpu.CompilerParams(vmem_limit_bytes=VMEM_BYTES),
    )(got, queries, other_queries)


def combine_kernel(lines, got, recalled, log_total):
    stats = got[:, lines, :]
    peaks, sums = stats[:, 0:1], stats[:, 1:2]
    peak = jnp.max(peaks, axis=0, keepdims=True)
    factor = jnp.exp(peaks - peak)
    total = jnp.sum(sums * factor, axis=0, keepdims=True)
    mix = got[0, :lines, :] * factor[0:1, :]
    for rank in range(1, got.shape[0]):
        mix += got[rank, :lines, :] * factor[rank : rank + 1, :]
    mix = mix / total
    for line in range(lines):
        recalled[:, line * LANES : (line + 1) * LANES] = mix[line : line + 1, :]
    log_total[...] = peak + jnp.log(total)


def combine(got, features):
    recalled, log_total = pl.pallas_call(
        functools.partial(combine_kernel, features // LANES),
        out_shape=(
            jax.ShapeDtypeStruct((1, features), jnp.float32),
            jax.ShapeDtypeStruct((1, 1), jnp.float32),
        ),
        in_specs=[pl.BlockSpec(memory_space=pltpu.VMEM)],
        out_specs=(pl.BlockSpec(memory_space=pltpu.VMEM), pl.BlockSpec(memory_space=pltpu.VMEM)),
        compiler_params=pltpu.CompilerParams(vmem_limit_bytes=VMEM_BYTES),
    )(got)
    return recalled, log_total.reshape(1)


def on_cycle(context, residual, out_proj, norm_gain, lengths, queries, pattern):
    ranks = lax.axis_size("dp")
    size = ranks // CORES
    features = residual.shape[1]

    def ring(step):
        return [
            (CYCLE[r] * CORES + c, CYCLE[(r + step * (1 - 2 * c)) % size] * CORES + c)
            for r in range(size)
            for c in range(CORES)
        ]

    def from_next(piece):
        return lax.ppermute(piece, "dp", ring(-1))

    def from_last(piece):
        return lax.ppermute(piece, "dp", ring(1))

    def over_x(piece):
        return lax.ppermute(piece, "groups", [(0, 1), (1, 0)])

    def other_core(piece):
        return lax.ppermute(piece, "dp", [(i, i ^ 1) for i in range(ranks)])

    wait = lax.optimization_barrier

    own = own_half(out_proj)
    a = from_next(own)
    c, q = other_core(context), other_core(queries)
    (p0,) = wave((0,), (), (), None, context, None, [out_proj])
    own, p0 = wait((own, p0))
    b = from_last(own)

    n1, p0 = wait((a, p0))
    x = over_x(n1)
    a = from_next(n1)
    context2, n1 = wait((c, n1))
    (t0,) = wave((0,), (), (), None, context2, None, [out_proj])
    l1, n1, t0, queries2 = wait((b, n1, t0, q))
    b = from_last(l1)
    r0 = other_core(t0)

    n2, l1 = wait((a, l1))
    x2 = over_x(n2)
    a = from_next(n2)
    xn1, n2 = wait((x, n2))
    x = x2
    h1, t1, f0, sq1 = wave(
        (1,), (), ((0, True), (0, False)), context, context2, residual, [n1, xn1], [p0, r0], None
    )
    l2, n2, t1, sq1 = wait((b, n2, t1, sq1))
    b = from_last(l2)
    r1 = other_core(t1)

    xn2, l2 = wait((x, l2))
    x = over_x(l2)
    a2 = from_next(xn2)
    n3, xn2 = wait((a, xn2))
    h2, t2, t2p, f1, sq2 = wave((2,), (-1,), ((1, False),), context, context2, residual, [n2, xn2, l1], [r1], sq1)
    l3, n3, t2, t2p, sq2 = wait((b, n3, t2, t2p, sq2))
    b = from_last(l3)
    r2, r2p = other_core(t2), other_core(t2p)

    n3x, l3 = wait((a2, l3))
    a = from_next(n3x)
    xl2, l1, n3x = wait((x, l1, n3x))
    x = over_x(l1)
    h3, t3a, t3p, f2, sq3 = wave(
        (-2, 3), (-3,), ((2, False),), context, context2, residual, [l2, xl2, n3, n3x, l3], [r2], sq2, stacked=True
    )
    l4, xl2, t3a, t3p, sq3, r2p = wait((b, xl2, t3a, t3p, sq3, r2p))
    b = from_last(xl2)
    r3a, r3p = other_core(t3a), other_core(t3p)
    l4s = other_core(l4)

    n4x, l4, own_pattern, lengths = wait((a, l4, pattern, lengths))
    flags = jnp.pad(own_pattern.astype(jnp.float32), ((0, 0), (0, LANES - 1 - pattern.shape[1])))
    flags = jnp.concatenate([flags, lengths.astype(jnp.float32)[:, None]], axis=1)
    n4xs = other_core(n4x)
    items = ((None, ((0, False), (1, True)), True, 4, True),)
    h4, sq4 = late(items, context, residual, sq3, [l4, n4x], [])
    xl1, n4x, sq4, flags = wait((x, n4x, sq4, flags))
    xl1s = other_core(xl1)
    items = (((0, 1), ((0, True),), False, -1, True),)
    h5, sq5 = late(items, context, residual, sq4, [xl1], [h2])
    l3x, xl1, sq5 = wait((b, xl1, sq5))
    l3xs = other_core(l3x)
    items = (
        ((0, 2), ((0, True),), False, -3, True),
        ((1, 0), (), True, -2, False),
        ((1, 1), (), True, 3, False),
        (None, ((1, False), (2, True)), True, 4, False),
    )
    h6, sq6 = late(items, context, residual, sq5, [l3x, l4s, n4xs], [h3, r3a])
    items = (((0, None), ((0, True),), True, -1, False), ((1, 0), ((1, True),), True, -3, False))
    hidden = [r2p, r3p, h1, h2, h3, h4, h5, h6, f0, f1, f2]
    sources = (
        (2, 0, 1, True),
        (3, 0, 2, True),
        (4, 0, -2, True),
        (4, 1, 3, True),
        (5, 0, 4, True),
        (6, 0, -1, True),
        (8, 0, 0, True),
        (8, 1, 0, False),
        (9, 0, 1, False),
        (10, 0, 2, False),
        (7, 0, -3, True),
        (7, 1, -2, False),
        (7, 2, 3, False),
        (7, 3, 4, False),
    )
    embedded, payload = finish(
        items, sources, context, residual, sq6, norm_gain.reshape(1, -1), flags, [xl1s, l3xs], hidden, size
    )

    same_core = [list(range(c, ranks, CORES)) for c in range(CORES)]

    def spread(blocks):
        return lax.all_to_all(blocks, "dp", 0, 0, axis_index_groups=same_core, tiled=True)

    parts = score(spread(payload), queries, queries2, pattern.shape[1])
    recalled, log_total = combine(spread(parts), features)
    return embedded, recalled, log_total


def gathered(context, residual, out_proj, norm_gain, lengths, queries, pattern):
    tok_rows = context.shape[0]
    features = residual.shape[1]
    passages_here = lengths.shape[0]
    seq_len = tok_rows // passages_here
    query_rows = queries.shape[0]
    blocks = pattern.shape[1]
    ranks = lax.axis_size("dp")
    me = lax.axis_index("dp")
    branch = jnp.dot(
        context,
        lax.all_gather(out_proj, "dp", axis=1, tiled=True),
        preferred_element_type=jnp.float32,
    )
    hidden_sum = residual.astype(jnp.float32) + branch
    normed = (
        hidden_sum
        * lax.rsqrt(jnp.mean(hidden_sum * hidden_sum, axis=-1, keepdims=True) + 1e-05)
        * norm_gain
    )
    shaped = normed.reshape(passages_here, seq_len, features)
    valid_mask = (jnp.arange(seq_len)[None, :] < lengths[:, None]).astype(jnp.float32)
    pooled = jnp.sum(shaped * valid_mask[:, :, None], axis=1) / lengths.astype(jnp.float32)[:, None]
    embedded = pooled * lax.rsqrt(jnp.mean(pooled * pooled, axis=-1, keepdims=True) + 1e-06)
    emb_half = embedded.astype(jnp.bfloat16)
    temper = 1.0 / (0.02 * math.sqrt(features))
    contract = (((1,), (1,)), ((), ()))

    flags = jnp.pad(pattern.astype(jnp.bfloat16), ((0, 0), (0, LANES - blocks)))
    everyone = lax.all_gather(jnp.concatenate([emb_half, flags], axis=1), "dp", axis=0, tiled=True)
    emb_all = everyone[:, :features]
    flags_all = everyone[:, features : features + blocks].astype(jnp.float32)
    scores = lax.dot_general(emb_all, queries, contract, preferred_element_type=jnp.float32) * temper
    row_block = (me * query_rows + jnp.arange(query_rows)) // QB
    picks = (row_block[None, :] == jnp.arange(blocks)[:, None]).astype(jnp.float32)
    cand_mask = jnp.dot(flags_all, picks) > 0
    peak_part = jnp.max(jnp.where(cand_mask, scores, LOW), axis=1, keepdims=True)
    weights = jnp.where(cand_mask, jnp.exp(scores - peak_part), 0.0)
    total_part = jnp.sum(weights, axis=1, keepdims=True)
    mix_part = jnp.dot(weights.astype(jnp.bfloat16), queries, preferred_element_type=jnp.float32)

    passages = emb_all.shape[0]
    lane = jnp.arange(LANES)[None, :]
    tail = jnp.where(lane == 0, peak_part, jnp.where(lane == 1, total_part, 0.0))
    parts = jnp.concatenate([mix_part, tail], axis=1).reshape(ranks, passages // ranks, -1)
    parts = lax.all_to_all(parts, "dp", split_axis=0, concat_axis=0, tiled=True)
    mixes, peaks, sums = parts[:, :, :features], parts[:, :, features], parts[:, :, features + 1]
    peak_score = jnp.max(peaks, axis=0)
    factor = jnp.exp(peaks - peak_score[None, :])
    totals = jnp.sum(sums * factor, axis=0)
    recalled = jnp.sum(mixes * factor[:, :, None], axis=0) / totals[:, None]
    log_total = peak_score + jnp.log(totals)
    return (embedded, recalled, log_total)


def per_device(context, residual, out_proj, norm_gain, lengths, queries, pattern):
    fits = (
        lax.axis_size("dp") == CORES * len(CYCLE)
        and lax.axis_size("groups") == 2
        and lengths.shape[0] == 1
        and out_proj.shape[1] % LANES == 0
        and out_proj.shape[0] % (2 * LANES) == 0
        and context.shape[0] % STEP == 0
        and pattern.shape[1] < LANES
    )
    form = on_cycle if fits else gathered
    return form(context, residual, out_proj, norm_gain, lengths, queries, pattern)


def solution(mesh):
    in_specs = (
        P(("groups", "dp"), None),
        P(("groups", "dp"), None),
        P(None, "dp"),
        P(),
        P(("groups", "dp")),
        P(("groups", "dp"), None),
        P(("groups", "dp"), None),
    )
    out_specs = (P(("groups", "dp"), None), P(("groups", "dp"), None), P(("groups", "dp")))
    return jax.shard_map(
        per_device, mesh=mesh, in_specs=in_specs, out_specs=out_specs, check_vma=False
    )
```

```python
import functools
import math

import jax
import jax.numpy as jnp
from jax import lax
from jax.experimental import pallas as pl
from jax.experimental.pallas import tpu as pltpu
from jax.sharding import PartitionSpec as P

QB = 256
LANES = 128
CORES = 2
STEP = 256
VMEM_BYTES = 12 << 20
LOW = -1e30
CYCLE = (0, 2, 4, 6, 7, 5, 3, 1)
VMEM_SPEC = pl.BlockSpec(memory_space=pltpu.VMEM)
SMALL = pl.CostEstimate(flops=1000, bytes_accessed=1000, transcendentals=0)


def column_block(distance, same_core):
    me = lax.axis_index("dp")
    core = lax.rem(me, CORES)
    chip = lax.div(me, CORES)
    z, y = lax.div(chip, 2), lax.rem(chip, 2)
    size = len(CYCLE)
    at = jnp.where(y == 0, z, size - 1 - z)
    core = core if same_core else 1 - core
    there = lax.rem(at + jnp.where(core == 0, size + distance, size - distance), size)
    chip = jnp.where(there < size // 2, 2 * there, 2 * (size - 1 - there) + 1)
    return chip * CORES + core


def columns(distance, same_core, width):
    return pl.ds(pl.multiple_of(column_block(distance, same_core) * width, width), width)


def half_slice(second, half):
    side = lax.axis_index("groups")
    return pl.ds(pl.multiple_of((1 - side if second else side) * half, half), half)


def add_squares(squares, at, total):
    square = total * total
    for lane in range(0, total.shape[1], LANES):
        squares[at, :] += square[:, lane : lane + LANES]


def half_kernel(whole, part):
    part[...] = whole[half_slice(False, part.shape[0]), :]


def own_half(whole):
    rows, width = whole.shape
    return pl.pallas_call(
        half_kernel,
        out_shape=jax.ShapeDtypeStruct((rows // 2, width), whole.dtype),
        in_specs=[VMEM_SPEC],
        out_specs=VMEM_SPEC,
        compiler_params=pltpu.CompilerParams(vmem_limit_bytes=VMEM_BYTES),
    )(whole)


def row_steps(rows):
    def loop(body):
        @pl.loop(0, rows // STEP)
        def _(k):
            body(pl.ds(pl.multiple_of(k * STEP, STEP), STEP))

    return loop


def product(tokens, at, pieces):
    total = None
    for piece, second in pieces:
        half = piece.shape[0]
        term = jnp.dot(tokens[at, half_slice(second, half)], piece[...], preferred_element_type=jnp.float32)
        total = term if total is None else total + term
    return total


def wave_kernel(full, part, arrived, whole, tokens, chained, stacked, *refs):
    count = len(full) + len(part)
    refs = list(refs)
    context = refs.pop(0) if "mine" in tokens else None
    other_context = refs.pop(0) if "theirs" in tokens else None
    residual = refs.pop(0) if "mine" in tokens else None
    if whole:
        shard = refs.pop(0)
        half = shard.shape[0] // 2
        jobs = [[(shard.at[half_slice(second, half)], second) for second in (False, True)]]
    else:
        jobs = [[(refs.pop(0), False)] + ([(refs.pop(0), True)] if j < len(full) else []) for j in range(count)]
    received = [refs.pop(0) for _ in arrived]
    before = refs.pop(0) if chained else None
    mine = refs.pop(0) if "mine" in tokens else None
    theirs = None
    if "theirs" in tokens:
        stacks = [refs.pop(0) for _ in range(2 if stacked else count)]
        theirs = stacks
        if stacked:
            theirs = [stacks[0].at[j] for j in range(len(full))] + [stacks[1].at[j] for j in range(len(part))]
    finished = refs.pop(0) if arrived else None
    squares = refs.pop(0) if "mine" in tokens else None
    rows, width = mine.shape[1:] if "mine" in tokens else theirs[0].shape
    if chained:
        squares[...] = before[...]
    elif "mine" in tokens:
        squares[...] = jnp.zeros_like(squares)
    for j, distance in enumerate(full + part):

        @row_steps(rows)
        def _(at):
            if "theirs" in tokens:
                theirs[j][at, :] = product(other_context, at, jobs[j])
            if "mine" in tokens:
                total = product(context, at, jobs[j])
                total += residual[at, columns(distance, True, width)].astype(jnp.float32)
                mine[j, at, :] = total
                if j < len(full):
                    add_squares(squares, at, total)

    for j, (distance, same) in enumerate(arrived):

        @row_steps(rows)
        def _(at):
            total = received[j][at, :] + residual[at, columns(distance, same, width)].astype(jnp.float32)
            finished[j, at, :] = total
            add_squares(squares, at, total)


def wave(
    full, part, arrived, context, other_context, residual, pieces, received=None, squares=None, stacked=False
):
    tokens = (("mine",) if context is not None else ()) + (("theirs",) if other_context is not None else ())
    count = len(full) + len(part)
    rows = (context if other_context is None else other_context).shape[0]
    whole = len(pieces) == 1
    block = jax.ShapeDtypeStruct((rows, pieces[0].shape[1]), jnp.float32)

    def stack(n):
        return jax.ShapeDtypeStruct((n,) + block.shape, jnp.float32)

    outs = [stack(count)] if "mine" in tokens else []
    if "theirs" in tokens:
        outs += [stack(len(full)), stack(len(part))] if stacked else [block] * count
    operands = [x for x in (context, other_context) if x is not None]
    operands += ([residual] if "mine" in tokens else []) + list(pieces)
    if arrived:
        operands += [*received] + ([] if squares is None else [squares])
        outs.append(jax.ShapeDtypeStruct((len(arrived),) + block.shape, jnp.float32))
    if "mine" in tokens:
        outs.append(jax.ShapeDtypeStruct((rows, LANES), jnp.float32))
    return pl.pallas_call(
        functools.partial(wave_kernel, full, part, arrived, whole, tokens, squares is not None, stacked),
        out_shape=outs,
        in_specs=[VMEM_SPEC] * len(operands),
        out_specs=[VMEM_SPEC] * len(outs),
        compiler_params=pltpu.CompilerParams(vmem_limit_bytes=VMEM_BYTES),
        cost_estimate=SMALL,
    )(*operands)


def late_blocks(items, context, residual, pieces, hidden, squares, target):
    rows, width = target.shape[1:]
    for i, (base, parts, bare, distance, same) in enumerate(items):

        @row_steps(rows)
        def _(at):
            value = product(context, at, [(pieces[index], second) for index, second in parts])
            if base is not None:
                known = hidden[base[0]][(at,) if base[1] is None else (base[1], at)]
                value = known if value is None else value + known
            if bare:
                value += residual[at, columns(distance, same, width)].astype(jnp.float32)
            target[i, at, :] = value
            add_squares(squares, at, value)


def late_kernel(items, n_pieces, context, residual, before, *refs):
    pieces, hidden = refs[:n_pieces], refs[n_pieces:-2]
    finished, squares = refs[-2:]
    squares[...] = before[...]
    late_blocks(items, context, residual, pieces, hidden, squares, finished)


def late(items, context, residual, squares, pieces, hidden):
    rows = context.shape[0]
    operands = [context, residual, squares, *pieces, *hidden]
    return pl.pallas_call(
        functools.partial(late_kernel, items, len(pieces)),
        out_shape=(
            jax.ShapeDtypeStruct((len(items), rows, pieces[0].shape[1]), jnp.float32),
            jax.ShapeDtypeStruct(squares.shape, jnp.float32),
        ),
        in_specs=[VMEM_SPEC] * len(operands),
        out_specs=(VMEM_SPEC, VMEM_SPEC),
        compiler_params=pltpu.CompilerParams(vmem_limit_bytes=VMEM_BYTES),
        cost_estimate=SMALL,
    )(*operands)


def final_kernel(items, sources, n_pieces, context, residual, before, gain, flags, *refs):
    pieces, hidden = refs[:n_pieces], refs[n_pieces:-6]
    embedded, payload, blocks, squares, scale_rows, sheet = refs[-6:]
    width = blocks.shape[2]
    features = embedded.shape[1]
    squares[...] = before[...]
    late_blocks(items, context, residual, pieces, hidden, squares, blocks)
    mean = jnp.sum(squares[...], axis=1, keepdims=True) * (1.0 / features)
    length = flags[:, LANES - 1 : LANES]
    row = lax.broadcasted_iota(jnp.int32, mean.shape, 0).astype(jnp.float32)
    scale = jnp.where(row < length, lax.rsqrt(mean + 1e-05), 0.0)
    scale_rows[...] = jnp.broadcast_to(scale, scale_rows.shape)
    inverse = 1.0 / length
    done = [(blocks.at[i], distance, same) for i, (_, _, _, distance, same) in enumerate(items)]
    done += [(hidden[array].at[entry], distance, same) for array, entry, distance, same in sources]
    for block, distance, same in done:
        parts = [
            jnp.sum(block[:, lane : lane + LANES] * scale_rows[...], axis=0, keepdims=True)
            for lane in range(0, width, LANES)
        ]
        where = columns(distance, same, width)
        embedded[:, where] = jnp.concatenate(parts, axis=1) * gain[:, where] * inverse
    pooled = embedded[...]
    mean = jnp.sum(pooled * pooled, axis=1, keepdims=True) * (1.0 / features)
    embedded[...] = pooled * lax.rsqrt(mean + 1e-06)
    lines = features // LANES
    sheet[lines:, :] = jnp.zeros((sheet.shape[0] - lines, LANES), jnp.float32)
    for line in range(lines):
        sheet[line : line + 1, :] = embedded[:, line * LANES : (line + 1) * LANES]
    sheet[lines : lines + 1, :] = flags[...]
    rounded = sheet[...].astype(jnp.bfloat16)
    for rank in range(payload.shape[0]):
        payload[rank] = rounded


def finish(items, sources, context, residual, squares, gain, flags, pieces, hidden, ranks):
    rows = context.shape[0]
    width = pieces[0].shape[1]
    features = (len(items) + len(sources)) * width
    lines = -(-(features // LANES + 1) // 16) * 16
    operands = [context, residual, squares, gain, flags, *pieces, *hidden]
    return pl.pallas_call(
        functools.partial(final_kernel, items, sources, len(pieces)),
        out_shape=(
            jax.ShapeDtypeStruct((1, features), jnp.float32),
            jax.ShapeDtypeStruct((ranks, lines, LANES), jnp.bfloat16),
        ),
        in_specs=[VMEM_SPEC] * len(operands),
        out_specs=(VMEM_SPEC, VMEM_SPEC),
        scratch_shapes=[
            pltpu.VMEM((len(items), rows, width), jnp.float32),
            pltpu.VMEM((rows, LANES), jnp.float32),
            pltpu.VMEM((rows, LANES), jnp.float32),
            pltpu.VMEM((lines, LANES), jnp.float32),
        ],
        compiler_params=pltpu.CompilerParams(vmem_limit_bytes=VMEM_BYTES),
        cost_estimate=SMALL,
    )(*operands)


def score_kernel(lines, blocks, got, queries, other_queries, out, wide, emb, mix):
    me = lax.axis_index("dp")
    ranks = got.shape[0]
    count = queries.shape[0]
    wide[...] = got[...].astype(jnp.float32)
    for line in range(lines):
        emb[:, line * LANES : (line + 1) * LANES] = wide[:, line, :]
    half = emb[...].astype(jnp.bfloat16)
    flags = wide[:, lines, :].astype(jnp.bfloat16)
    temper = 1.0 / (0.02 * math.sqrt(lines * LANES))
    scores, masks = [], []
    for owner, rows in ((me, queries), (me + 1 - 2 * lax.rem(me, CORES), other_queries)):
        score = lax.dot_general(
            half, rows[...], (((1,), (1,)), ((), ())), preferred_element_type=jnp.float32
        )
        scores.append(score * temper)
        block = lax.broadcasted_iota(jnp.int32, (LANES, count), 0)
        row = owner * count + lax.broadcasted_iota(jnp.int32, (LANES, count), 1)
        pick = (row >= block * QB) & (row < block * QB + QB) & (block < blocks)
        pick = jnp.where(pick, 1.0, 0.0).astype(jnp.bfloat16)
        masks.append(jnp.dot(flags, pick, preferred_element_type=jnp.float32) > 0.5)
    peaks = [
        jnp.max(jnp.where(mask, score, LOW), axis=1, keepdims=True) for score, mask in zip(scores, masks)
    ]
    peak = jnp.maximum(*peaks)
    weights = [jnp.where(mask, jnp.exp(score - peak), 0.0) for score, mask in zip(scores, masks)]
    total = sum(jnp.sum(weight, axis=1, keepdims=True) for weight in weights)
    mix[...] = jnp.dot(
        weights[0].astype(jnp.bfloat16), queries[...], preferred_element_type=jnp.float32
    ) + jnp.dot(weights[1].astype(jnp.bfloat16), other_queries[...], preferred_element_type=jnp.float32)
    for line in range(lines):
        out[:, line, :] = mix[:, line * LANES : (line + 1) * LANES]
    lane = lax.broadcasted_iota(jnp.int32, (ranks, LANES), 1)
    out[:, lines, :] = jnp.where(lane == 0, peak, jnp.where(lane == 1, total, 0.0))
    for line in range(lines + 1, out.shape[1]):
        out[:, line, :] = jnp.zeros((ranks, LANES), jnp.float32)


def score(got, queries, other_queries, blocks):
    ranks = got.shape[0]
    features = queries.shape[1]
    lines = features // LANES
    return pl.pallas_call(
        functools.partial(score_kernel, lines, blocks),
        out_shape=jax.ShapeDtypeStruct((ranks, -(-(lines + 1) // 8) * 8, LANES), jnp.float32),
        in_specs=[pl.BlockSpec(memory_space=pltpu.VMEM)] * 3,
        out_specs=pl.BlockSpec(memory_space=pltpu.VMEM),
        scratch_shapes=[
            pltpu.VMEM(got.shape, jnp.float32),
            pltpu.VMEM((ranks, features), jnp.float32),
            pltpu.VMEM((ranks, features), jnp.float32),
        ],
        compiler_params=pltpu.CompilerParams(vmem_limit_bytes=VMEM_BYTES),
    )(got, queries, other_queries)


def combine_kernel(lines, got, recalled, log_total):
    stats = got[:, lines, :]
    peaks, sums = stats[:, 0:1], stats[:, 1:2]
    peak = jnp.max(peaks, axis=0, keepdims=True)
    factor = jnp.exp(peaks - peak)
    total = jnp.sum(sums * factor, axis=0, keepdims=True)
    mix = got[0, :lines, :] * factor[0:1, :]
    for rank in range(1, got.shape[0]):
        mix += got[rank, :lines, :] * factor[rank : rank + 1, :]
    mix = mix / total
    for line in range(lines):
        recalled[:, line * LANES : (line + 1) * LANES] = mix[line : line + 1, :]
    log_total[...] = peak + jnp.log(total)


def combine(got, features):
    recalled, log_total = pl.pallas_call(
        functools.partial(combine_kernel, features // LANES),
        out_shape=(
            jax.ShapeDtypeStruct((1, features), jnp.float32),
            jax.ShapeDtypeStruct((1, 1), jnp.float32),
        ),
        in_specs=[pl.BlockSpec(memory_space=pltpu.VMEM)],
        out_specs=(pl.BlockSpec(memory_space=pltpu.VMEM), pl.BlockSpec(memory_space=pltpu.VMEM)),
        compiler_params=pltpu.CompilerParams(vmem_limit_bytes=VMEM_BYTES),
    )(got)
    return recalled, log_total.reshape(1)


def on_cycle(context, residual, out_proj, norm_gain, lengths, queries, pattern):
    ranks = lax.axis_size("dp")
    size = ranks // CORES
    features = residual.shape[1]

    def ring(step):
        return [
            (CYCLE[r] * CORES + c, CYCLE[(r + step * (1 - 2 * c)) % size] * CORES + c)
            for r in range(size)
            for c in range(CORES)
        ]

    def from_next(piece):
        return lax.ppermute(piece, "dp", ring(-1))

    def from_last(piece):
        return lax.ppermute(piece, "dp", ring(1))

    def over_x(piece):
        return lax.ppermute(piece, "groups", [(0, 1), (1, 0)])

    def other_core(piece):
        return lax.ppermute(piece, "dp", [(i, i ^ 1) for i in range(ranks)])

    wait = lax.optimization_barrier

    own = own_half(out_proj)
    a = from_next(own)
    c, q = other_core(context), other_core(queries)
    (p0,) = wave((0,), (), (), None, context, None, [out_proj])
    own, p0 = wait((own, p0))
    b = from_last(own)

    n1, p0 = wait((a, p0))
    x = over_x(n1)
    a = from_next(n1)
    context2, n1 = wait((c, n1))
    (t0,) = wave((0,), (), (), None, context2, None, [out_proj])
    l1, n1, t0, queries2 = wait((b, n1, t0, q))
    b = from_last(l1)
    r0 = other_core(t0)

    n2, l1 = wait((a, l1))
    x2 = over_x(n2)
    a = from_next(n2)
    xn1, n2 = wait((x, n2))
    x = x2
    h1, t1, f0, sq1 = wave(
        (1,), (), ((0, True), (0, False)), context, context2, residual, [n1, xn1], [p0, r0], None
    )
    l2, n2, t1, sq1 = wait((b, n2, t1, sq1))
    b = from_last(l2)
    r1 = other_core(t1)

    xn2, l2 = wait((x, l2))
    x = over_x(l2)
    a2 = from_next(xn2)
    n3, xn2 = wait((a, xn2))
    h2, t2, t2p, f1, sq2 = wave((2,), (-1,), ((1, False),), context, context2, residual, [n2, xn2, l1], [r1], sq1)
    l3, n3, t2, t2p, sq2, own_pattern, lengths = wait((b, n3, t2, t2p, sq2, pattern, lengths))
    b = from_last(l3)
    r2, r2p = other_core(t2), other_core(t2p)

    flags = jnp.pad(own_pattern.astype(jnp.float32), ((0, 0), (0, LANES - 1 - pattern.shape[1])))
    flags = jnp.concatenate([flags, lengths.astype(jnp.float32)[:, None]], axis=1)
    n3x, l3, flags = wait((a2, l3, flags))
    a = from_next(n3x)
    xl2, l1, n3x = wait((x, l1, n3x))
    x = over_x(l1)
    h3, t3a, t3p, f2, sq3 = wave(
        (-2, 3), (-3,), ((2, False),), context, context2, residual, [l2, xl2, n3, n3x, l3], [r2], sq2, stacked=True
    )
    l4, xl2, t3a, t3p, sq3, r2p = wait((b, xl2, t3a, t3p, sq3, r2p))
    b = from_last(xl2)
    r3a, r3p = other_core(t3a), other_core(t3p)
    l4s = other_core(l4)

    n4x, l4 = wait((a, l4))
    n4xs = other_core(n4x)
    items = ((None, ((0, False), (1, True)), True, 4, True),)
    h4, sq4 = late(items, context, residual, sq3, [l4, n4x], [])
    xl1, n4x, sq4 = wait((x, n4x, sq4))
    xl1s = other_core(xl1)
    items = (((0, 1), ((0, True),), False, -1, True),)
    h5, sq5 = late(items, context, residual, sq4, [xl1], [h2])
    l3x, xl1, sq5 = wait((b, xl1, sq5))
    l3xs = other_core(l3x)
    items = (
        ((0, 2), ((0, True),), False, -3, True),
        ((1, 0), (), True, -2, False),
        ((1, 1), (), True, 3, False),
        (None, ((1, False), (2, True)), True, 4, False),
    )
    h6, sq6 = late(items, context, residual, sq5, [l3x, l4s, n4xs], [h3, r3a])
    items = (((0, None), ((0, True),), True, -1, False), ((1, 0), ((1, True),), True, -3, False))
    hidden = [r2p, r3p, h1, h2, h3, h4, h5, h6, f0, f1, f2]
    sources = (
        (2, 0, 1, True),
        (3, 0, 2, True),
        (4, 0, -2, True),
        (4, 1, 3, True),
        (5, 0, 4, True),
        (6, 0, -1, True),
        (8, 0, 0, True),
        (8, 1, 0, False),
        (9, 0, 1, False),
        (10, 0, 2, False),
        (7, 0, -3, True),
        (7, 1, -2, False),
        (7, 2, 3, False),
        (7, 3, 4, False),
    )
    embedded, payload = finish(
        items, sources, context, residual, sq6, norm_gain.reshape(1, -1), flags, [xl1s, l3xs], hidden, size
    )

    same_core = [list(range(c, ranks, CORES)) for c in range(CORES)]

    def spread(blocks):
        return lax.all_to_all(blocks, "dp", 0, 0, axis_index_groups=same_core, tiled=True)

    parts = score(spread(payload), queries, queries2, pattern.shape[1])
    recalled, log_total = combine(spread(parts), features)
    return embedded, recalled, log_total


def gathered(context, residual, out_proj, norm_gain, lengths, queries, pattern):
    tok_rows = context.shape[0]
    features = residual.shape[1]
    passages_here = lengths.shape[0]
    seq_len = tok_rows // passages_here
    query_rows = queries.shape[0]
    blocks = pattern.shape[1]
    ranks = lax.axis_size("dp")
    me = lax.axis_index("dp")
    branch = jnp.dot(
        context,
        lax.all_gather(out_proj, "dp", axis=1, tiled=True),
        preferred_element_type=jnp.float32,
    )
    hidden_sum = residual.astype(jnp.float32) + branch
    normed = (
        hidden_sum
        * lax.rsqrt(jnp.mean(hidden_sum * hidden_sum, axis=-1, keepdims=True) + 1e-05)
        * norm_gain
    )
    shaped = normed.reshape(passages_here, seq_len, features)
    valid_mask = (jnp.arange(seq_len)[None, :] < lengths[:, None]).astype(jnp.float32)
    pooled = jnp.sum(shaped * valid_mask[:, :, None], axis=1) / lengths.astype(jnp.float32)[:, None]
    embedded = pooled * lax.rsqrt(jnp.mean(pooled * pooled, axis=-1, keepdims=True) + 1e-06)
    emb_half = embedded.astype(jnp.bfloat16)
    temper = 1.0 / (0.02 * math.sqrt(features))
    contract = (((1,), (1,)), ((), ()))

    flags = jnp.pad(pattern.astype(jnp.bfloat16), ((0, 0), (0, LANES - blocks)))
    everyone = lax.all_gather(jnp.concatenate([emb_half, flags], axis=1), "dp", axis=0, tiled=True)
    emb_all = everyone[:, :features]
    flags_all = everyone[:, features : features + blocks].astype(jnp.float32)
    scores = lax.dot_general(emb_all, queries, contract, preferred_element_type=jnp.float32) * temper
    row_block = (me * query_rows + jnp.arange(query_rows)) // QB
    picks = (row_block[None, :] == jnp.arange(blocks)[:, None]).astype(jnp.float32)
    cand_mask = jnp.dot(flags_all, picks) > 0
    peak_part = jnp.max(jnp.where(cand_mask, scores, LOW), axis=1, keepdims=True)
    weights = jnp.where(cand_mask, jnp.exp(scores - peak_part), 0.0)
    total_part = jnp.sum(weights, axis=1, keepdims=True)
    mix_part = jnp.dot(weights.astype(jnp.bfloat16), queries, preferred_element_type=jnp.float32)

    passages = emb_all.shape[0]
    lane = jnp.arange(LANES)[None, :]
    tail = jnp.where(lane == 0, peak_part, jnp.where(lane == 1, total_part, 0.0))
    parts = jnp.concatenate([mix_part, tail], axis=1).reshape(ranks, passages // ranks, -1)
    parts = lax.all_to_all(parts, "dp", split_axis=0, concat_axis=0, tiled=True)
    mixes, peaks, sums = parts[:, :, :features], parts[:, :, features], parts[:, :, features + 1]
    peak_score = jnp.max(peaks, axis=0)
    factor = jnp.exp(peaks - peak_score[None, :])
    totals = jnp.sum(sums * factor, axis=0)
    recalled = jnp.sum(mixes * factor[:, :, None], axis=0) / totals[:, None]
    log_total = peak_score + jnp.log(totals)
    return (embedded, recalled, log_total)


def per_device(context, residual, out_proj, norm_gain, lengths, queries, pattern):
    fits = (
        lax.axis_size("dp") == CORES * len(CYCLE)
        and lax.axis_size("groups") == 2
        and lengths.shape[0] == 1
        and out_proj.shape[1] % LANES == 0
        and out_proj.shape[0] % (2 * LANES) == 0
        and context.shape[0] % STEP == 0
        and pattern.shape[1] < LANES
    )
    form = on_cycle if fits else gathered
    return form(context, residual, out_proj, norm_gain, lengths, queries, pattern)


def solution(mesh):
    in_specs = (
        P(("groups", "dp"), None),
        P(("groups", "dp"), None),
        P(None, "dp"),
        P(),
        P(("groups", "dp")),
        P(("groups", "dp"), None),
        P(("groups", "dp"), None),
    )
    out_specs = (P(("groups", "dp"), None), P(("groups", "dp"), None), P(("groups", "dp")))
    return jax.shard_map(
        per_device, mesh=mesh, in_specs=in_specs, out_specs=out_specs, check_vma=False
    )
```
